32 devices in a mesh: group: 4 (over y, x), batch: 8 (over z, core).
Axes of the slice: x: 2, y: 2, z: 4, core: 2. Of those that a mesh axis runs over, the one named last changes fastest.
Arguments:
- pixels: bfloat16 [4, 32, 16, 196, 256], P('group', 'batch'), may hold values from -18 to 18, as said below
- band_count: int32 [4, 32], P('group', 'batch'), may hold values from 2 to 16, as said below
- band_bin: int32 [4, 32, 16], P('group', 'batch'), may hold values from 0 to 511, as said below
- bin_wave: float32 [512], replicated, may hold values from 0.4 to 14
- run_mean: float32 [512], replicated, may hold values from -4 to 4
- run_var: float32 [512], replicated, may hold values from 0.5 to 4
- weight_tokens: float32 [128, 128], replicated, may hold values from -5 to 5
- bias_token: float32 [128], replicated, may hold values from -5 to 5
- hyper_in: float32 [128, 384], replicated, may hold values from -0.5 to 0.5
- hyper_qv_bias: float32 [2, 128], replicated, may hold values from -2 to 2
- hyper_out: float32 [128, 128], replicated, may hold values from -1 to 1
- hyper_out_bias: float32 [128], replicated, may hold values from -2 to 2
- hyper_gain: float32 [2, 128], replicated, may hold values from 0.5 to 1.5
- hyper_shift: float32 [2, 128], replicated, may hold values from -2 to 2
- hyper_up: float32 [128, 2048], replicated, may hold values from -0.5 to 0.5
- hyper_up_bias: float32 [2048], replicated, may hold values from -2 to 2
- hyper_down: float32 [2048, 128], replicated, may hold values from -0.1875 to 0.1875
- hyper_down_bias: float32 [128], replicated, may hold values from -2 to 2
- kernel_weight: bfloat16 [256, 768, 128], P('batch'), may hold values from -0.01171875 to 0.01171875
- bias_weight: float32 [128, 768], replicated, may hold values from -0.5 to 0.5
- bias_offset: float32 [768], replicated, may hold values from -2 to 2
- norm_gain: float32 [2, 768], replicated, may hold values from 0.5 to 1.5
- norm_shift: float32 [2, 768], replicated, may hold values from -2 to 2
- w_qkv: bfloat16 [768, 2304], replicated, may hold values from -0.21875 to 0.21875
- qv_bias: float32 [2, 768], replicated, may hold values from -2 to 2
- w_out: bfloat16 [768, 768], replicated, may hold values from -0.875 to 0.875
- out_bias: float32 [768], replicated, may hold values from -2 to 2
- w_up: bfloat16 [768, 3072], replicated, may hold values from -0.21875 to 0.21875
- up_bias: float32 [3072], replicated, may hold values from -2 to 2
- w_down: bfloat16 [3072, 768], replicated, may hold values from -0.15625 to 0.15625
- down_bias: float32 [768], replicated, may hold values from -2 to 2
- cotangent: bfloat16 [4, 32, 196, 768], P('group', 'batch'), may hold values from -6 to 6
Outputs:
- block_out: bfloat16 [4, 32, 196, 768], P('group', 'batch')
- pixel_grad: bfloat16 [4, 32, 16, 196, 256], P('group', 'batch')
- batch_mean: float32 [512], replicated
- batch_var: float32 [512], replicated
- grad_weight_tokens: float32 [128, 128], replicated
- grad_bias_token: float32 [128], replicated
- grad_hyper_in: float32 [128, 384], replicated
- grad_hyper_qv_bias: float32 [2, 128], replicated
- grad_hyper_out: float32 [128, 128], replicated
- grad_hyper_out_bias: float32 [128], replicated
- grad_hyper_gain: float32 [2, 128], replicated
- grad_hyper_shift: float32 [2, 128], replicated
- grad_hyper_up: float32 [128, 2048], replicated
- grad_hyper_up_bias: float32 [2048], replicated
- grad_hyper_down: float32 [2048, 128], replicated
- grad_hyper_down_bias: float32 [128], replicated
- grad_kernel_weight: float32 [256, 768, 128], P('batch')
- grad_bias_weight: float32 [128, 768], replicated
- grad_bias_offset: float32 [768], replicated
- grad_norm_gain: float32 [2, 768], replicated
- grad_norm_shift: float32 [2, 768], replicated
- grad_w_qkv: float32 [768, 2304], P('group')
- grad_qv_bias: float32 [2, 768], replicated
- grad_w_out: float32 [768, 768], P('group')
- grad_out_bias: float32 [768], replicated
- grad_w_up: float32 [768, 3072], P('group')
- grad_up_bias: float32 [3072], replicated
- grad_w_down: float32 [3072, 768], P('group')
- grad_down_bias: float32 [768], replicated
The draws below stay inside these ranges and needn't reach their ends.
Inputs may be any that keep to these rules, and one draw needn't show every extreme that they name: `band_count`: live bands fill an image's first slots. With c = 2 for group 0 and c = max(2, (g + 1) * 4) for group g > 0, every image of group g has between c - c // 3 and c live bands, and in each group one image, drawn from the seed, has exactly c. `band_bin`: max(2, 32) bins, drawn from the seed, are named by no slot of any image. `pixels`: each band slot has its own offset and scale.
All inputs are finite; a program needn't handle non-finite values.
Results may differ from the reference program's by a relative error of at most 0.015.
Values may be sent and summed in bfloat16 or wider, within the bound.
No kernel may reach another device: no remote copies, remote signals or barrier semaphores. Data moves between devices by JAX's collectives and lax.ppermute only.
A program may use at most 512 MiB of HBM per device.

```python
import math
import jax
import jax.numpy as jnp
from jax import lax

D = 768
HEADS = 12
FF = 3072
WV = 128
WT = 128
HHEADS = 4
HFF = 2048
PIX = 256
PATCHES = 196
BANDS = 16
NBINS = 512
IMG_DEV = 4
GROUPS = 4
IMAGES = 32


def draw_pixels(key, part):
    key = jax.random.fold_in(key, 11)
    first_key, second_key, third_key = jax.random.split(key, 3)
    full_shape = (GROUPS, IMAGES, BANDS, PATCHES, PIX)
    offset = jax.random.uniform(first_key, (GROUPS, IMAGES, BANDS, 1, 1), jnp.float32, -2.0, 2.0)
    spread = jnp.exp(jax.random.uniform(second_key, (GROUPS, IMAGES, BANDS, 1, 1), jnp.float32, math.log(0.5), math.log(4.0)))
    noise_draw = jnp.clip(jax.random.normal(third_key, full_shape, jnp.float32), -4.0, 4.0)
    return (offset + spread * noise_draw).astype(jnp.bfloat16)


def draw_band_count(key, part):
    key = jax.random.fold_in(key, 23)
    first_key, second_key = jax.random.split(key)
    group_index = lax.broadcasted_iota(jnp.int32, (GROUPS, IMAGES), 0)
    image_index = lax.broadcasted_iota(jnp.int32, (GROUPS, IMAGES), 1)
    band_most = jnp.where(group_index == 0, 2, jnp.maximum(2, (group_index + 1) * BANDS // GROUPS))
    band_least = band_most - band_most // 3
    spread = jax.random.randint(first_key, (GROUPS, IMAGES), 0, 1 << 20)
    counts = band_least + spread % (band_most - band_least + 1)
    full_image = jax.random.randint(second_key, (GROUPS, 1), 0, IMAGES)
    return jnp.where(image_index == full_image, band_most, counts).astype(jnp.int32)


def draw_band_bin(key, part):
    key = jax.random.fold_in(key, 37)
    first_key, second_key = jax.random.split(key)
    unused_bins = max(2, NBINS // 16)
    shuffled = jax.random.permutation(first_key, NBINS).astype(jnp.int32)
    drawn_slots = jax.random.randint(second_key, (GROUPS, IMAGES, BANDS), unused_bins, NBINS)
    return jnp.take(shuffled, drawn_slots).astype(jnp.int32)


def shard_levels(stream_key, shape, shards, least, largest):
    factor_of = 1.0
    for axis_at, shards_of in shards:
        draws = jax.random.uniform(jax.random.fold_in(jax.random.fold_in(stream_key, 6), axis_at), (shards_of,), jnp.float32, least / len(shards), largest / len(shards))
        factor_of = factor_of * jnp.repeat(jnp.exp(draws), shape[axis_at] // shards_of).reshape((-1,) + (1,) * (len(shape) - 1 - axis_at))
    return factor_of


def centred(stream_key, shape, width, reach, shards=(), kind=jnp.bfloat16):
    entries = jax.random.normal(stream_key, shape, jnp.float32) * width
    if len(shards) > 0:
        entries = shard_levels(stream_key, shape, shards, -0.22, 0.18) * entries
    return jnp.clip(entries, min=-reach, max=reach).astype(kind)


def setup_inputs(seed: int = 0) -> dict:
    seeds = jax.random.split(jax.random.key(seed), 33)
    return {
        "pixels": draw_pixels(jax.random.fold_in(seeds[32], 71), 0),
        "band_count": draw_band_count(jax.random.fold_in(seeds[32], 71), 0),
        "band_bin": draw_band_bin(jax.random.fold_in(seeds[32], 71), 0),
        "bin_wave": jnp.clip(jnp.exp(jax.random.uniform(seeds[3], (NBINS,), jnp.float32, math.log(0.4), math.log(14.0))), 0.4, 14.0),
        "run_mean": centred(seeds[4], (NBINS,), 1.0, 4.0, (), jnp.float32),
        "run_var": jnp.clip(jnp.exp(jax.random.uniform(seeds[5], (NBINS,), jnp.float32, math.log(0.5), math.log(4.0))), 0.5, 4.0),
        "weight_tokens": centred(seeds[6], (WT, WV), 1.0, 5.0, (), jnp.float32),
        "bias_token": centred(seeds[7], (WV,), 1.0, 5.0, (), jnp.float32),
        "hyper_in": centred(seeds[8], (WV, 3 * WV), WV ** -0.5, 0.5, (), jnp.float32),
        "hyper_qv_bias": centred(seeds[9], (2, WV), 0.3, 2.0, (), jnp.float32),
        "hyper_out": centred(seeds[10], (WV, WV), (WV // 4) ** -0.5, 1.0, (), jnp.float32),
        "hyper_out_bias": centred(seeds[11], (WV,), 0.3, 2.0, (), jnp.float32),
        "hyper_gain": jnp.clip(1.0 + 0.1 * jax.random.normal(seeds[12], (2, WV), jnp.float32), 0.5, 1.5),
        "hyper_shift": centred(seeds[13], (2, WV), 0.3, 2.0, (), jnp.float32),
        "hyper_up": centred(seeds[14], (WV, HFF), WV ** -0.5, 0.5, (), jnp.float32),
        "hyper_up_bias": centred(seeds[15], (HFF,), 0.3, 2.0, (), jnp.float32),
        "hyper_down": centred(seeds[16], (HFF, WV), (HFF // 2) ** -0.5, 0.1875, (), jnp.float32),
        "hyper_down_bias": centred(seeds[17], (WV,), 0.3, 2.0, (), jnp.float32),
        "kernel_weight": centred(seeds[18], (PIX, D, WV), (WV * PIX * BANDS // 2) ** -0.5, 0.01171875, ((0, 8),)),
        "bias_weight": centred(seeds[19], (WV, D), WV ** -0.5, 0.5, (), jnp.float32),
        "bias_offset": centred(seeds[20], (D,), 0.3, 2.0, (), jnp.float32),
        "norm_gain": jnp.clip(1.0 + 0.1 * jax.random.normal(seeds[21], (2, D), jnp.float32), 0.5, 1.5),
        "norm_shift": centred(seeds[22], (2, D), 0.3, 2.0, (), jnp.float32),
        "w_qkv": centred(seeds[23], (D, 3 * D), D ** -0.5, 0.21875),
        "qv_bias": centred(seeds[24], (2, D), 0.3, 2.0, (), jnp.float32),
        "w_out": centred(seeds[25], (D, D), (D // 14) ** -0.5, 0.875),
        "out_bias": centred(seeds[26], (D,), 0.3, 2.0, (), jnp.float32),
        "w_up": centred(seeds[27], (D, FF), D ** -0.5, 0.21875),
        "up_bias": centred(seeds[28], (FF,), 0.3, 2.0, (), jnp.float32),
        "w_down": centred(seeds[29], (FF, D), (FF // 2) ** -0.5, 0.15625),
        "down_bias": centred(seeds[30], (D,), 0.3, 2.0, (), jnp.float32),
        "cotangent": centred(seeds[31], (GROUPS, IMAGES, PATCHES, D), 1.0, 6.0, ((0, 4), (1, 8))),
    }


highest = lax.Precision.HIGHEST
stat_eps = 1e-05
hyper_eps = 1e-05
block_eps = 1e-06
wave_scale = 1000.0

@jax.custom_vjp
def low(v):
    return lax.optimization_barrier(v.astype(jnp.bfloat16)).astype(jnp.float32)

@jax.custom_vjp
def low_back(v):
    return v

def low_keep(v):
    return (low(v), None)

def low_pass(kept, grad):
    return (grad,)

def back_keep(v):
    return (v, None)

def back_low(kept, grad):
    return (low(grad),)
low.defvjp(low_keep, low_pass)
low_back.defvjp(back_keep, back_low)

def layer_norm(values, gain, shift, epsilon):
    center = values - lax.optimization_barrier(jnp.mean(values, axis=-1, keepdims=True))
    return center * lax.rsqrt(lax.optimization_barrier(jnp.mean(center * center, axis=-1, keepdims=True)) + epsilon) * gain + shift

def wave_embed(band_wave, model_width):
    half_width = model_width // 2
    ladder = jnp.arange(half_width, dtype=jnp.float32) / half_width
    frequency = 1.0 / 10000.0 ** ladder
    phase_arg = band_wave[..., None] * wave_scale * frequency
    return jnp.concatenate([jnp.sin(phase_arg), jnp.cos(phase_arg)], axis=-1)

def bin_stats(total_sums, squares, counts, cell_count):
    scaled = jnp.maximum(counts * cell_count, 1.0)
    bin_mean = total_sums / scaled
    bin_var = squares / scaled - bin_mean * bin_mean
    return (bin_mean, bin_var)

def hypernet(params, wave_emb, live_band):
    tokens_w, token_b, w_in, in_bias, w_proj, proj_bias, gain_pair, shifts, w_expand, expand_bias, w_reduce, reduce_bias = params
    image_count = wave_emb.shape[0]
    band_slots = wave_emb.shape[1]
    model_width = wave_emb.shape[2]
    head_count = HHEADS
    head_size = model_width // head_count
    token_rows = tokens_w.shape[0]
    sequence = jnp.concatenate([jnp.broadcast_to(tokens_w[None], (image_count, token_rows, model_width)), wave_emb, jnp.broadcast_to(token_b[None, None, :], (image_count, 1, model_width))], axis=1)
    key_live = jnp.concatenate([jnp.ones((image_count, token_rows), jnp.float32), live_band, jnp.ones((image_count, 1), jnp.float32)], axis=1) > 0.5
    projected = jnp.einsum('nsk,kj->nsj', sequence, w_in, precision=highest)
    query_heads = (projected[..., :model_width] + in_bias[0]).reshape(image_count, -1, head_count, head_size)
    keyed = projected[..., model_width:2 * model_width].reshape(image_count, -1, head_count, head_size)
    valued = (projected[..., 2 * model_width:] + in_bias[1]).reshape(image_count, -1, head_count, head_size)
    scores = jnp.einsum('nqhd,nkhd->nhqk', query_heads, keyed, precision=highest) * head_size ** (-0.5)
    scores = jnp.where(key_live[:, None, None, :], scores, -1e+30)
    attn_probs = jax.nn.softmax(scores, axis=-1)
    mixed_heads = jnp.einsum('nhqk,nkhd->nqhd', attn_probs, valued, precision=highest).reshape(image_count, -1, model_width)
    first_out = layer_norm(sequence + jnp.einsum('nsk,kj->nsj', mixed_heads, w_proj, precision=highest) + proj_bias, gain_pair[0], shifts[0], hyper_eps)
    inner_act = jax.nn.gelu(jnp.einsum('nsk,kf->nsf', first_out, w_expand, precision=highest) + expand_bias, approximate=False)
    second_out = layer_norm(first_out + jnp.einsum('nsf,fk->nsk', inner_act, w_reduce, precision=highest) + reduce_bias, gain_pair[1], shifts[1], hyper_eps)
    return (second_out[:, token_rows:token_rows + band_slots] + wave_emb, second_out[:, token_rows + band_slots])

def image_block(hyper_params, dense_params, block_pixels, block_mean, block_rstd, block_wave, block_live):
    kernel_w, bias_w, bias_o, gain_pair, shifts, joint_w, joint_bias, out_w, out_b, up_w, up_b, down_w, down_b = dense_params
    image_count = block_pixels.shape[0]
    patch_count = block_pixels.shape[2]
    model_width = joint_w.shape[0]
    head_size = model_width // HEADS
    normed = low((block_pixels - block_mean[:, :, None, None]) * block_rstd[:, :, None, None])
    band_vec, bias_vec = hypernet(hyper_params, block_wave, block_live)
    kernels = low(low_back(jnp.einsum('ibk,xek->ibxe', low(band_vec), kernel_w, precision=highest)))
    embed_conv = jnp.einsum('ibpx,ibxe->ipe', normed, kernels, precision=highest)
    embedded = low_back(embed_conv + (jnp.dot(bias_vec, bias_w, precision=highest) + bias_o)[:, None, :])
    normed1 = low(layer_norm(embedded, gain_pair[0], shifts[0], block_eps))
    joint_proj = jnp.einsum('ipd,dj->ipj', normed1, joint_w, precision=highest)
    query_heads = low(low_back(joint_proj[..., :model_width] + joint_bias[0])).reshape(image_count, patch_count, HEADS, head_size)
    keyed = low(low_back(joint_proj[..., model_width:2 * model_width])).reshape(image_count, patch_count, HEADS, head_size)
    valued = low(low_back(joint_proj[..., 2 * model_width:] + joint_bias[1])).reshape(image_count, patch_count, HEADS, head_size)
    scores = low_back(jnp.einsum('iqhd,ikhd->ihqk', query_heads, keyed, precision=highest) * head_size ** (-0.5))
    attn_probs = low(jax.nn.softmax(scores, axis=-1))
    attended = low(low_back(jnp.einsum('ihqk,ikhd->iqhd', attn_probs, valued, precision=highest))).reshape(image_count, patch_count, model_width)
    branch = low_back(jnp.einsum('ipd,de->ipe', attended, out_w, precision=highest) + out_b)
    residual = embedded + branch
    normed2 = low(layer_norm(residual, gain_pair[1], shifts[1], block_eps))
    pre_act = low_back(jnp.einsum('ipd,df->ipf', normed2, up_w, precision=highest) + up_b)
    activated = low(jax.nn.gelu(pre_act, approximate=False))
    return residual + jnp.einsum('ipf,fd->ipd', activated, down_w, precision=highest) + down_b

def reference(pixels, band_count, band_bin, bin_wave, run_mean, run_var, weight_tokens, bias_token, hyper_in, hyper_qv_bias, hyper_out, hyper_out_bias, hyper_gain, hyper_shift, hyper_up, hyper_up_bias, hyper_down, hyper_down_bias, kernel_weight, bias_weight, bias_offset, norm_gain, norm_shift, w_qkv, qv_bias, w_out, out_bias, w_up, up_bias, w_down, down_bias, cotangent):
    live_band = (lax.broadcasted_iota(jnp.int32, (GROUPS, IMAGES, BANDS), 2) < band_count[:, :, None]).astype(jnp.float32)
    bin_onehot = (band_bin[..., None] == lax.broadcasted_iota(jnp.int32, (GROUPS, IMAGES, BANDS, NBINS), 3)).astype(jnp.float32)
    chosen = bin_onehot * live_band[..., None]
    band_wave = bin_wave[band_bin]
    blocks = GROUPS * IMAGES // IMG_DEV
    wave_blocks = wave_embed(band_wave, WV).reshape(blocks, IMG_DEV, BANDS, WV)
    live_blocks = live_band.reshape(blocks, IMG_DEV, BANDS)
    hyper_params = (weight_tokens, bias_token, hyper_in, hyper_qv_bias, hyper_out, hyper_out_bias, hyper_gain, hyper_shift, hyper_up, hyper_up_bias, hyper_down, hyper_down_bias)
    dense_params = (kernel_weight.astype(jnp.float32), bias_weight, bias_offset, norm_gain, norm_shift, w_qkv.astype(jnp.float32), qv_bias, w_out.astype(jnp.float32), out_bias, w_up.astype(jnp.float32), up_bias, w_down.astype(jnp.float32), down_bias)
    values32 = pixels.astype(jnp.float32)
    total_sums = jnp.einsum('gib,gibn->n', lax.optimization_barrier(jnp.sum(values32, axis=(3, 4))), chosen, precision=highest)
    squares = jnp.einsum('gib,gibn->n', lax.optimization_barrier(jnp.sum(values32 * values32, axis=(3, 4))), chosen, precision=highest)
    counts = lax.optimization_barrier(jnp.sum(chosen, axis=(0, 1, 2)))
    batch_mean, batch_var = bin_stats(total_sums, squares, counts, PATCHES * PIX)
    run_rstd = lax.rsqrt(run_var + stat_eps)
    band_mean = jnp.einsum('gibn,n->gib', chosen, run_mean, precision=highest).reshape(blocks, IMG_DEV, BANDS)
    band_rstd = jnp.einsum('gibn,n->gib', chosen, run_rstd, precision=highest).reshape(blocks, IMG_DEV, BANDS)

    def forward(hyper_params, dense_params, values32):

        def scan_step(state, block_data):
            return (state, image_block(hyper_params, dense_params, block_data[0], block_data[1], block_data[2], block_data[3], block_data[4]))
        state, outputs = lax.scan(jax.checkpoint(scan_step), jnp.zeros((), jnp.float32), (values32.reshape(blocks, IMG_DEV, BANDS, PATCHES, PIX), band_mean, band_rstd, wave_blocks, live_blocks))
        return outputs.reshape(GROUPS, IMAGES, PATCHES, D)
    block_out, backward = jax.vjp(forward, hyper_params, dense_params, values32)
    grad_hyper, grad_dense, grad_pixels = backward(cotangent.astype(jnp.float32))
    return (block_out.astype(jnp.bfloat16), grad_pixels.astype(jnp.bfloat16), batch_mean, batch_var, grad_hyper[0], grad_hyper[1], grad_hyper[2], grad_hyper[3], grad_hyper[4], grad_hyper[5], grad_hyper[6], grad_hyper[7], grad_hyper[8], grad_hyper[9], grad_hyper[10], grad_hyper[11], grad_dense[0], grad_dense[1], grad_dense[2], grad_dense[3], grad_dense[4], grad_dense[5], grad_dense[6], grad_dense[7], grad_dense[8], grad_dense[9], grad_dense[10], grad_dense[11], grad_dense[12])
```

```python
from functools import partial

import jax
import jax.numpy as jnp
from jax import lax
from jax.experimental import pallas as pl
from jax.experimental.pallas import tpu as pltpu
from jax.sharding import PartitionSpec as P

HEADS = 12
HHEADS = 4


highest = lax.Precision.HIGHEST
high = lax.Precision.HIGH
stat_eps = 1e-05
hyper_eps = 1e-05
block_eps = 1e-06
wave_scale = 1000.0


def layer_norm(values, gain, shift, epsilon):
    center = values - jnp.mean(values, axis=-1, keepdims=True)
    return (
        center * lax.rsqrt(jnp.mean(center * center, axis=-1, keepdims=True) + epsilon) * gain
        + shift
    )


def norm_parts(values, epsilon):
    center = values - jnp.mean(values, axis=-1, keepdims=True)
    factor = lax.rsqrt(jnp.mean(center * center, axis=-1, keepdims=True) + epsilon)
    return (center * factor, factor)


def norm_back(grad_hat, normal_hat, factor):
    return factor * (
        grad_hat
        - jnp.mean(grad_hat, axis=-1, keepdims=True)
        - normal_hat * jnp.mean(grad_hat * normal_hat, axis=-1, keepdims=True)
    )


def wave_embed(band_wave, model_width):
    half_width = model_width // 2
    ladder = jnp.arange(half_width, dtype=jnp.float32) / half_width
    frequency = 1.0 / 10000.0**ladder
    phase_arg = band_wave[..., None] * wave_scale * frequency
    return jnp.concatenate([jnp.sin(phase_arg), jnp.cos(phase_arg)], axis=-1)


def bin_stats(total_sums, squares, counts, cell_count):
    scaled = jnp.maximum(counts * cell_count, 1.0)
    bin_mean = total_sums / scaled
    bin_var = squares / scaled - bin_mean * bin_mean
    return (bin_mean, bin_var)


def hypernet(params, wave_emb, live_band):
    (
        tokens_w,
        token_b,
        w_in,
        in_bias,
        w_proj,
        proj_bias,
        gain_pair,
        shifts,
        w_expand,
        expand_bias,
        w_reduce,
        reduce_bias,
    ) = params
    image_count = wave_emb.shape[0]
    band_slots = wave_emb.shape[1]
    model_width = wave_emb.shape[2]
    head_count = HHEADS
    head_size = model_width // head_count
    token_rows = tokens_w.shape[0]
    sequence = jnp.concatenate(
        [
            jnp.broadcast_to(tokens_w[None], (image_count, token_rows, model_width)),
            wave_emb,
            jnp.broadcast_to(token_b[None, None, :], (image_count, 1, model_width)),
        ],
        axis=1,
    )
    key_live = (
        jnp.concatenate(
            [
                jnp.ones((image_count, token_rows), jnp.float32),
                live_band,
                jnp.ones((image_count, 1), jnp.float32),
            ],
            axis=1,
        )
        > 0.5
    )
    projected = jnp.einsum("nsk,kj->nsj", sequence, w_in, precision=high)
    query_heads = (projected[..., :model_width] + in_bias[0]).reshape(
        image_count, -1, head_count, head_size
    )
    keyed = projected[..., model_width : 2 * model_width].reshape(
        image_count, -1, head_count, head_size
    )
    valued = (projected[..., 2 * model_width :] + in_bias[1]).reshape(
        image_count, -1, head_count, head_size
    )
    scores = jnp.einsum("nqhd,nkhd->nhqk", query_heads, keyed, precision=high) * head_size ** (
        -0.5
    )
    scores = jnp.where(key_live[:, None, None, :], scores, -1e30)
    attn_probs = jax.nn.softmax(scores, axis=-1)
    mixed_heads = jnp.einsum("nhqk,nkhd->nqhd", attn_probs, valued, precision=high).reshape(
        image_count, -1, model_width
    )
    first_out = layer_norm(
        sequence + jnp.einsum("nsk,kj->nsj", mixed_heads, w_proj, precision=high) + proj_bias,
        gain_pair[0],
        shifts[0],
        hyper_eps,
    )
    inner_act = jax.nn.gelu(
        jnp.einsum("nsk,kf->nsf", first_out, w_expand, precision=high) + expand_bias,
        approximate=False,
    )
    second_out = layer_norm(
        first_out + jnp.einsum("nsf,fk->nsk", inner_act, w_reduce, precision=high) + reduce_bias,
        gain_pair[1],
        shifts[1],
        hyper_eps,
    )
    return (
        second_out[:, token_rows : token_rows + band_slots] + wave_emb,
        second_out[:, token_rows + band_slots],
    )


def swap_group(value, bits):
    return lax.ppermute(value, "group", [(at, at ^ bits) for at in range(4)])


def swap_batch(value, bits):
    count = lax.axis_size("batch")
    return lax.ppermute(value, "batch", [(at, at ^ bits) for at in range(count)])


def tuned_mesh():
    return lax.axis_size("group") == 4 and lax.axis_size("batch") == 8


def same_core():
    count = lax.axis_size("batch")
    return [list(range(0, count, 2)), list(range(1, count, 2))]


def in_order(bit, first, second):
    return jnp.where(
        bit == 0, jnp.concatenate([first, second]), jnp.concatenate([second, first])
    )


def four_in_order(index, pieces):
    low, high = (index & 1, index >> 1)
    return in_order(
        high, in_order(low, pieces[0], pieces[1]), in_order(low, pieces[2], pieces[3])
    )


def part_of(value, index, parts):
    rows = value.shape[0] // parts
    return lax.dynamic_slice_in_dim(value, index * rows, rows)


def tie(*values):
    return lax.optimization_barrier(values)


def along_line(value, step):
    count = lax.axis_size("batch")
    pairs = [(at, at + 2 * step) for at in range(count) if 0 <= at + 2 * step < count]
    return lax.ppermute(value, "batch", pairs)


def of_chip(chip, values):
    return jnp.array(values, jnp.int32)[chip]


def plain_weight_pieces(weight):
    core = lax.axis_index("batch") & 1
    shards = lax.all_gather(weight, "batch", axis=0)
    shards = shards.reshape((-1, 2) + weight.shape)
    mine = lax.dynamic_index_in_dim(shards, core, 1, keepdims=False)
    return mine.reshape((4, -1) + weight.shape[1:])


def plain_line_cells(pixels):
    pieces, images, rows, lanes = pixels.shape
    chips = lax.axis_size("batch") // 2
    parts = pixels.reshape(pieces, images, rows, chips // pieces, -1)
    parts = parts.transpose(0, 3, 1, 2, 4).reshape(chips, images, rows, -1)
    came = lax.all_to_all(parts, "batch", 0, 0, axis_index_groups=same_core(), tiled=True)
    return [came.reshape((chips * images,) + came.shape[2:])]


def plain_line_images(value, beside):
    both = jnp.concatenate([value, beside])
    return [lax.all_gather(both, "batch", axis=0, axis_index_groups=same_core(), tiled=True)]


def line_rows(low):
    if not tuned_mesh():
        return lax.all_gather(low, "batch", axis=0, axis_index_groups=same_core(), tiled=True)
    return jnp.concatenate([low] + [swap_batch(low, 2 * hop) for hop in (1, 2, 3)])


def core_sum(grad):
    core = lax.axis_index("batch") & 1
    split = grad.reshape(4, 2, -1, grad.shape[1])
    keep = lax.dynamic_index_in_dim(split, core, 1, keepdims=False)
    send = lax.dynamic_index_in_dim(split, 1 - core, 1, keepdims=False)
    came = swap_batch(send, 1)
    return (
        (keep.astype(jnp.float32) + came.astype(jnp.float32))
        .astype(jnp.bfloat16)
        .reshape(-1, grad.shape[1])
    )


def row_share(half):
    return lax.psum_scatter(half, "group", scatter_dimension=0, tiled=True)


def row_mine(share):
    return lax.psum(share, "batch", axis_index_groups=same_core())


def row_both(mine):
    core = lax.axis_index("batch") & 1
    return in_order(core, mine, swap_batch(mine, 1)).astype(jnp.float32)


def add_low(left, right):
    return (left.astype(jnp.float32) + right.astype(jnp.float32)).astype(left.dtype)


def ring_sides():
    group = lax.axis_index("group")
    side, level = (group & 1, group >> 1)
    return (1, side), (2, level)


def sum_out(parts, flip):
    order = ring_sides()[::-1] if flip else ring_sides()
    return [swap_group(part_of(part, 1 - bit, 2), way) for part, (way, bit) in zip(parts, order)]


def sum_in(parts, came, flip):
    order = ring_sides()[::-1] if flip else ring_sides()
    return [
        add_low(part_of(part, bit, 2), other)
        for part, other, (way, bit) in zip(parts, came, order)
    ]


def share_out(parts, flip):
    order = ring_sides()[::-1] if flip else ring_sides()
    return [swap_group(part, way) for part, (way, bit) in zip(parts, order)]


def share_in(parts, came, flip):
    order = ring_sides()[::-1] if flip else ring_sides()
    return [in_order(bit, part, other) for part, other, (way, bit) in zip(parts, came, order)]


def block_rows(value):
    rows, lanes = value.shape
    return value.reshape(rows, lanes // 128, 128).transpose(1, 0, 2).reshape(-1, 128)


def unblock_rows(value, rows):
    return value.reshape(-1, rows, 128).transpose(1, 0, 2).reshape(rows, -1)


def grid_params(mebibytes, semantics=1):
    return pltpu.CompilerParams(
        dimension_semantics=("arbitrary",) * semantics,
        vmem_limit_bytes=mebibytes * 1024 * 1024,
    )


def dot_nn(left, right):
    return lax.dot_general(
        left, right, (((1,), (0,)), ((), ())), preferred_element_type=jnp.float32
    )


def dot_nt(left, right):
    return lax.dot_general(
        left, right, (((1,), (1,)), ((), ())), preferred_element_type=jnp.float32
    )


def dot_tn(left, right):
    return lax.dot_general(
        left, right, (((0,), (0,)), ((), ())), preferred_element_type=jnp.float32
    )


def split_kernel(cells, core_ref, pixel_ref, mean_ref, rate_ref, *refs):
    out_refs, scratch = (refs[:2], refs[2:])
    patches, bands, lanes = pixel_ref.shape[1:]
    pieces, _, rows, _ = out_refs[0].shape
    share = lanes // (2 * pieces * cells)
    span = cells * bands
    tile = 128
    columns, tiles = (lanes // tile, -(-rows // tile))
    flat, turned = (scratch[:columns], scratch[columns:])
    values = (pixel_ref[0].astype(jnp.float32) - mean_ref[0]) * rate_ref[0]
    values = values.astype(jnp.bfloat16).astype(jnp.float32).reshape(patches * bands, lanes)
    for column in range(columns):
        flat[column][: patches * bands] = values[:, column * tile : (column + 1) * tile]
        flat[column][patches * bands :] = jnp.zeros(
            (flat[column].shape[0] - patches * bands, tile), jnp.float32
        )
    for band in range(bands):
        for column in range(columns):
            for at in range(tiles):
                block = flat[column][pl.ds(at * tile * bands + band, tile, stride=bands), :]
                turned[at][pl.ds(column * tile * bands + band, tile, stride=bands), :] = block.T
    for out_ref, side in zip(out_refs, (core_ref[0], 1 - core_ref[0])):
        for piece in range(pieces):
            for at in range(tiles):
                count = min(tile, rows - at * tile)
                parts = []
                for one in range(share):
                    first = ((piece * share + one) * 2 + side) * span
                    place = pl.ds(pl.multiple_of(first, span), span)
                    parts.append(turned[at][place, :].T[:count])
                block = parts[0] if share == 1 else jnp.concatenate(parts, axis=1)
                out_ref[piece, 0, at * tile : at * tile + count, :] = block.astype(jnp.bfloat16)


def turn_scratch(rows, bands, lanes):
    tiles = -(-rows // 128)
    return [pltpu.VMEM((tiles * 128 * bands, 128), jnp.float32)] * (lanes // 128) + [
        pltpu.VMEM((lanes * bands, 128), jnp.float32)
    ] * tiles


def split_pixels(pixels, means, rates, core, rows, cells):
    images, bands, patches, lanes = pixels.shape
    wide = bands * lanes // 8
    side = jax.ShapeDtypeStruct((4, images, rows, wide), jnp.bfloat16)
    return pl.pallas_call(
        partial(split_kernel, cells),
        grid_spec=pltpu.PrefetchScalarGridSpec(
            num_scalar_prefetch=1,
            grid=(images,),
            in_specs=[
                pl.BlockSpec((1, patches, bands, lanes), lambda i, core: (i, 0, 0, 0)),
                pl.BlockSpec((1, bands, 1), lambda i, core: (i, 0, 0)),
                pl.BlockSpec((1, bands, 1), lambda i, core: (i, 0, 0)),
            ],
            out_specs=[pl.BlockSpec((4, 1, rows, wide), lambda i, core: (0, i, 0, 0))] * 2,
            scratch_shapes=turn_scratch(rows, bands, lanes),
        ),
        out_shape=[side, side],
        compiler_params=grid_params(40),
        cost_estimate=pl.CostEstimate(flops=1, bytes_accessed=1, transcendentals=0),
        name="split_pixels",
    )(core.reshape(1), pixels.transpose(0, 2, 1, 3), means[:, :, None], rates[:, :, None])


def join_kernel(cells, patches, core_ref, mine_ref, other_ref, out_ref, *scratch):
    rows = mine_ref.shape[2]
    bands, lanes = out_ref.shape[2:]
    pieces = mine_ref.shape[0]
    share = lanes // (2 * pieces * cells)
    span = cells * bands
    tile = 128
    columns, tiles = (lanes // tile, -(-rows // tile))
    flat, turned = (scratch[:columns], scratch[columns:])
    core = core_ref[0]
    for piece in range(pieces):
        for ref, flip in ((mine_ref, core), (other_ref, 1 - core)):
            for one in range(share):
                first = ((piece * share + one) * 2 + flip) * span
                place = pl.ds(pl.multiple_of(first, span), span)
                for at in range(tiles):
                    count = min(tile, rows - at * tile)
                    block = ref[
                        piece, 0, at * tile : at * tile + count, one * span : (one + 1) * span
                    ].astype(jnp.float32)
                    if count < tile:
                        block = jnp.concatenate(
                            [block, jnp.zeros((tile - count, span), jnp.float32)]
                        )
                    turned[at][place, :] = block.T
    for band in range(bands):
        for column in range(columns):
            for at in range(tiles):
                block = turned[at][pl.ds(column * tile * bands + band, tile, stride=bands), :]
                flat[column][pl.ds(at * tile * bands + band, tile, stride=bands), :] = block.T
    for column in range(columns):
        out_ref[0, :, :, column * tile : (column + 1) * tile] = (
            flat[column][: patches * bands].reshape(patches, bands, tile).astype(jnp.bfloat16)
        )


def join_pixels(mine, other, core, patches, cells, lanes, bands):
    pieces, images, rows, wide = mine.shape
    block = pl.BlockSpec((pieces, 1, rows, wide), lambda i, core: (0, i, 0, 0))
    joined = pl.pallas_call(
        partial(join_kernel, cells, patches),
        grid_spec=pltpu.PrefetchScalarGridSpec(
            num_scalar_prefetch=1,
            grid=(images,),
            in_specs=[block, block],
            out_specs=pl.BlockSpec((1, patches, bands, lanes), lambda i, core: (i, 0, 0, 0)),
            scratch_shapes=turn_scratch(rows, bands, lanes),
        ),
        out_shape=jax.ShapeDtypeStruct((images, patches, bands, lanes), jnp.bfloat16),
        compiler_params=grid_params(40),
        cost_estimate=pl.CostEstimate(flops=1, bytes_accessed=1, transcendentals=0),
        name="join_pixels",
    )(core.reshape(1), mine, other)
    return joined.transpose(0, 2, 1, 3)


def embed_kernel(first, count, at_ref, low_ref, *refs):
    weight_refs, pixel_refs = refs[:count], refs[count : count + 2]
    if first:
        total_ref, kernel_ref, weight_now = refs[count + 2 :]
    else:
        before_ref, _, total_ref, kernel_ref, weight_now = refs[count + 2 :]
    share = pixel_refs[0].shape[1]
    images = 2 * share
    cells = weight_now.shape[0]
    bands = pixel_refs[0].shape[3] // cells

    @pl.when(pl.program_id(0) == 0)
    def _():
        if first:
            total_ref[...] = jnp.zeros_like(total_ref)
        else:
            total_ref[...] = before_ref[...]

    for at in range(count):

        @pl.when((pl.program_id(0) == at) | (count == 1))
        def _(at=at):
            weight_now[...] = weight_refs[at][...]

    low = low_ref[...]
    for cell in range(cells):
        made = dot_nt(low, weight_now[cell]).astype(jnp.bfloat16)
        for image in range(images):
            kernel_ref[0, image, cell * bands : (cell + 1) * bands, :] = made[
                image * bands : (image + 1) * bands
            ]
    for image in range(images):
        block = pixel_refs[image // share][0, image % share]
        total_ref[image] += dot_nn(block, kernel_ref[0, image])


def embed_piece(place, low, weights, pixels, total, kernels):
    pieces, share, rows, lanes = pixels[0].shape
    images = 2 * share
    cells, width, depth = weights[0].shape
    step = lanes // (4 * 16)
    count = len(weights)
    steps = max(count, cells // step)
    bands = lanes // (4 * step)
    first = total is None
    any_spec = pl.BlockSpec(memory_space=pl.ANY)
    whole_total = pl.BlockSpec((images, rows, width), lambda t, at: (0, 0, 0))
    if count == 1:
        weight_specs = [pl.BlockSpec((step, width, depth), lambda t, at: (t, 0, 0))]
    else:
        weight_specs = [pl.BlockSpec((step, width, depth), lambda t, at: (0, 0, 0))] * count
    return pl.pallas_call(
        partial(embed_kernel, first, count),
        grid_spec=pltpu.PrefetchScalarGridSpec(
            num_scalar_prefetch=1,
            grid=(steps,),
            in_specs=[pl.BlockSpec(low.shape, lambda t, at: (0, 0))]
            + weight_specs
            + [
                pl.BlockSpec(
                    (1, share, rows, step * bands), lambda t, at: (at[0], 0, 0, at[1 + t])
                ),
            ]
            * 2
            + ([] if first else [whole_total, any_spec]),
            out_specs=[
                whole_total,
                pl.BlockSpec(
                    (1, images, step * bands, width), lambda t, at: (at[0], 0, at[1 + t], 0)
                ),
            ],
            scratch_shapes=[pltpu.VMEM((step, width, depth), jnp.bfloat16)],
        ),
        out_shape=[
            jax.ShapeDtypeStruct((images, rows, width), jnp.float32),
            jax.ShapeDtypeStruct((pieces, images, lanes, width), jnp.bfloat16),
        ],
        input_output_aliases={} if first else {4 + count: 0, 5 + count: 1},
        compiler_params=grid_params(48),
        cost_estimate=pl.CostEstimate(flops=1, bytes_accessed=1, transcendentals=0),
        name="embed_piece",
    )(place, low, *weights, *pixels, *(() if first else (total, kernels)))


def pixel_grad_kernel(grad_ref, kernel_ref, rate_ref, out_ref):
    for image in range(grad_ref.shape[0]):
        out_ref[0, image] = (
            dot_nt(grad_ref[image], kernel_ref[0, image]) * rate_ref[image]
        ).astype(jnp.bfloat16)


def pixel_grads(grads, kernels, rates):
    pieces, images, lanes, width = kernels.shape
    rows = grads.shape[1]
    share = images // 2
    return pl.pallas_call(
        pixel_grad_kernel,
        grid=(2, pieces),
        in_specs=[
            pl.BlockSpec((share, rows, width), lambda i, j: (i, 0, 0)),
            pl.BlockSpec((1, share, lanes, width), lambda i, j: (j, i, 0, 0)),
            pl.BlockSpec((share, 1, lanes), lambda i, j: (i, 0, 0)),
        ],
        out_specs=pl.BlockSpec((1, share, rows, lanes), lambda i, j: (j, i, 0, 0)),
        out_shape=jax.ShapeDtypeStruct((pieces, images, rows, lanes), jnp.bfloat16),
        compiler_params=grid_params(40, 2),
        cost_estimate=pl.CostEstimate(flops=1, bytes_accessed=1, transcendentals=0),
        name="pixel_grads",
    )(grads, kernels, rates)


def line_kernel(half, halves, low_ref, pixel_refs, grad_refs, out_ref, made):
    cells = out_ref.shape[0]
    lanes = pixel_refs[0].shape[2] // halves
    bands = lanes // cells
    columns = slice(half * lanes, (half + 1) * lanes)
    image = 0
    for pixel_ref, grad_ref in zip(pixel_refs, grad_refs):
        count = pixel_ref.shape[0]

        @pl.loop(0, count, unroll=count if count <= 4 else 2)
        def _(at, image=image):
            grads = dot_tn(pixel_ref[at, :, columns], grad_ref[at]).astype(jnp.bfloat16)
            row = pl.multiple_of((image + at) * bands, bands)
            for cell in range(cells):
                made[cell, pl.ds(row, bands), :] = grads[cell * bands : (cell + 1) * bands]

        image += count

    @pl.loop(0, cells, unroll=4)
    def _(cell):
        out_ref[cell] = dot_nn(low_ref[...], made[cell]).T.astype(jnp.bfloat16)


def line_grads(low_turned, cells, pixels, grads, half, halves):
    step_cells = cells // halves
    depth = low_turned.shape[0]
    width = grads[0].shape[2]
    bands = pixels[0].shape[2] // cells
    images = sum(piece.shape[0] for piece in pixels)
    vmem = pl.BlockSpec(memory_space=pltpu.VMEM)

    def body(*refs):
        pixel_refs = refs[1 : 1 + len(pixels)]
        grad_refs = refs[1 + len(pixels) : 1 + 2 * len(pixels)]
        line_kernel(half, halves, refs[0], pixel_refs, grad_refs, *refs[-2:])

    return pl.pallas_call(
        body,
        in_specs=[vmem] * (1 + 2 * len(pixels)),
        out_specs=vmem,
        out_shape=jax.ShapeDtypeStruct((step_cells, width, depth), jnp.bfloat16),
        scratch_shapes=[pltpu.VMEM((step_cells, images * bands, width), jnp.bfloat16)],
        compiler_params=pltpu.CompilerParams(vmem_limit_bytes=48 * 1024 * 1024),
        cost_estimate=pl.CostEstimate(flops=1, bytes_accessed=1, transcendentals=0),
        name="line_grads",
    )(low_turned, *pixels, *grads)


def band_kernel(first, count, at_ref, grad_ref, *refs):
    weight_refs, pixel_refs = refs[:count], refs[count : count + 2]
    if first:
        total_ref, weight_now, made = refs[count + 2 :]
    else:
        before_ref, total_ref, weight_now, made = refs[count + 2 :]
    share = pixel_refs[0].shape[1]
    images = 2 * share
    cells = weight_now.shape[0]
    bands = pixel_refs[0].shape[3] // cells

    @pl.when(pl.program_id(0) == 0)
    def _():
        if first:
            total_ref[...] = jnp.zeros_like(total_ref)
        else:
            total_ref[...] = before_ref[...]

    for at in range(count):

        @pl.when((pl.program_id(0) == at) | (count == 1))
        def _(at=at):
            weight_now[...] = weight_refs[at][...]

    for image in range(images):
        block = pixel_refs[image // share][0, image % share]
        grads = dot_tn(block, grad_ref[image]).astype(jnp.bfloat16)
        for cell in range(cells):
            made[cell, image * bands : (image + 1) * bands, :] = grads[
                cell * bands : (cell + 1) * bands
            ]
    for cell in range(cells):
        total_ref[...] += dot_nn(made[cell], weight_now[cell])


def band_piece(place, grads, weights, pixels, total):
    pieces, share, rows, lanes = pixels[0].shape
    images = 2 * share
    cells, width, depth = weights[0].shape
    step = lanes // (4 * 16)
    count = len(weights)
    steps = max(count, cells // step)
    bands = lanes // (4 * step)
    first = total is None
    whole_total = pl.BlockSpec((images * bands, depth), lambda t, at: (0, 0))
    if count == 1:
        weight_specs = [pl.BlockSpec((step, width, depth), lambda t, at: (t, 0, 0))]
    else:
        weight_specs = [pl.BlockSpec((step, width, depth), lambda t, at: (0, 0, 0))] * count
    return pl.pallas_call(
        partial(band_kernel, first, count),
        grid_spec=pltpu.PrefetchScalarGridSpec(
            num_scalar_prefetch=1,
            grid=(steps,),
            in_specs=[pl.BlockSpec(grads.shape, lambda t, at: (0, 0, 0))]
            + weight_specs
            + [
                pl.BlockSpec(
                    (1, share, rows, step * bands), lambda t, at: (at[0], 0, 0, at[1 + t])
                ),
            ]
            * 2
            + ([] if first else [whole_total]),
            out_specs=whole_total,
            scratch_shapes=[
                pltpu.VMEM((step, width, depth), jnp.bfloat16),
                pltpu.VMEM((step, images * bands, width), jnp.bfloat16),
            ],
        ),
        out_shape=jax.ShapeDtypeStruct((images * bands, depth), jnp.float32),
        compiler_params=grid_params(40),
        cost_estimate=pl.CostEstimate(flops=1, bytes_accessed=1, transcendentals=0),
        name="band_piece",
    )(place, grads, *weights, *pixels, *(() if first else (total,)))


def head_probs(patches, query, keyed, mine):
    rows = query.shape[0]
    scores = dot_nt(jnp.where(mine, query, jnp.zeros_like(query)), keyed)
    column = lax.broadcasted_iota(jnp.int32, (1, rows), 1)
    scores = jnp.where(column < patches, scores, -1e30)
    powers = jnp.exp(scores - jnp.max(scores, axis=-1, keepdims=True))
    return powers * (1.0 / jnp.sum(powers, axis=-1, keepdims=True))


def attend_kernel(patches, head_size, joint_ref, out_ref):
    width = out_ref.shape[2]
    pair = 2 * head_size
    lane = lax.broadcasted_iota(jnp.int32, (1, pair), 1)
    scale = jnp.asarray(head_size ** (-0.5), jnp.bfloat16)
    for at in range(0, width, pair):
        query = joint_ref[0, :, at : at + pair] * scale
        keyed = joint_ref[0, :, width + at : width + at + pair]
        valued = joint_ref[0, :, 2 * width + at : 2 * width + at + pair]
        mixed = []
        for head in range(2):
            mine = (lane >= head * head_size) & (lane < (head + 1) * head_size)
            probs = head_probs(patches, query, keyed, mine)
            mixed.append(dot_nn(probs.astype(jnp.bfloat16), valued))
        out_ref[0, :, at : at + pair] = jnp.where(lane < head_size, mixed[0], mixed[1]).astype(
            jnp.bfloat16
        )


def attend(joint, patches, head_size):
    images, rows, triple = joint.shape
    width = triple // 3
    return pl.pallas_call(
        partial(attend_kernel, patches, head_size),
        grid=(images,),
        in_specs=[pl.BlockSpec((1, rows, triple), lambda i: (i, 0, 0))],
        out_specs=pl.BlockSpec((1, rows, width), lambda i: (i, 0, 0)),
        out_shape=jax.ShapeDtypeStruct((images, rows, width), jnp.bfloat16),
        compiler_params=grid_params(24),
        cost_estimate=pl.CostEstimate(flops=1, bytes_accessed=1, transcendentals=0),
        name="attend",
    )(joint)


def attend_back_kernel(patches, head_size, joint_ref, grad_ref, out_ref, sum_ref):
    width = grad_ref.shape[2]
    pair = 2 * head_size
    lane = lax.broadcasted_iota(jnp.int32, (1, pair), 1)
    scale = jnp.asarray(head_size ** (-0.5), jnp.bfloat16)

    @pl.when(pl.program_id(0) == 0)
    def _():
        sum_ref[...] = jnp.zeros_like(sum_ref)

    for at in range(0, width, pair):
        query = joint_ref[0, :, at : at + pair] * scale
        keyed = joint_ref[0, :, width + at : width + at + pair]
        valued = joint_ref[0, :, 2 * width + at : 2 * width + at + pair]
        grads = grad_ref[0, :, at : at + pair]
        none = jnp.zeros_like(grads)
        parts = []
        for head in range(2):
            mine = (lane >= head * head_size) & (lane < (head + 1) * head_size)
            probs = head_probs(patches, query, keyed, mine)
            grad = jnp.where(mine, grads, none)
            to_probs = dot_nt(grad, valued)
            inner = jnp.sum(probs * to_probs, axis=-1, keepdims=True)
            to_scores = (probs * (to_probs - inner)).astype(jnp.bfloat16)
            parts.append(
                (
                    dot_nn(to_scores, jnp.where(mine, keyed, none)),
                    dot_tn(to_scores, jnp.where(mine, query, none)),
                    dot_tn(probs.astype(jnp.bfloat16), grad),
                )
            )
        to_query = (parts[0][0] + parts[1][0]) * (head_size ** (-0.5))
        to_keyed = parts[0][1] + parts[1][1]
        to_valued = parts[0][2] + parts[1][2]
        for slot, value in enumerate((to_query, to_keyed, to_valued)):
            value = value.astype(jnp.bfloat16)
            out_ref[0, :, slot * width + at : slot * width + at + pair] = value
            sum_ref[:, slot * width + at : slot * width + at + pair] += jnp.sum(
                value.astype(jnp.float32), axis=0, keepdims=True
            )


def attend_back(joint, grads, patches, head_size):
    images, rows, triple = joint.shape
    width = triple // 3
    return pl.pallas_call(
        partial(attend_back_kernel, patches, head_size),
        grid=(images,),
        in_specs=[
            pl.BlockSpec((1, rows, triple), lambda i: (i, 0, 0)),
            pl.BlockSpec((1, rows, width), lambda i: (i, 0, 0)),
        ],
        out_specs=[
            pl.BlockSpec((1, rows, triple), lambda i: (i, 0, 0)),
            pl.BlockSpec((1, triple), lambda i: (0, 0)),
        ],
        out_shape=[
            jax.ShapeDtypeStruct((images, rows, triple), jnp.bfloat16),
            jax.ShapeDtypeStruct((1, triple), jnp.float32),
        ],
        compiler_params=grid_params(24),
        cost_estimate=pl.CostEstimate(flops=1, bytes_accessed=1, transcendentals=0),
        name="attend_back",
    )(joint, grads)


def norm_inside(values, epsilon):
    center = values - jnp.mean(values, axis=-1, keepdims=True)
    factor = lax.rsqrt(jnp.mean(center * center, axis=-1, keepdims=True) + epsilon)
    return center * factor, factor


def small_call(kernel, name, grid, in_specs, out_specs, out_shape, scratch=(), limit=40):
    return pl.pallas_call(
        kernel,
        grid=grid,
        in_specs=in_specs,
        out_specs=out_specs,
        out_shape=out_shape,
        scratch_shapes=list(scratch),
        compiler_params=grid_params(limit),
        cost_estimate=pl.CostEstimate(flops=1, bytes_accessed=1, transcendentals=0),
        name=name,
    )


def whole_spec(shape):
    return pl.BlockSpec(shape, lambda i: (0,) * len(shape))


def image_spec(rows, width):
    return pl.BlockSpec((1, rows, width), lambda i: (i, 0, 0))


def joint_kernel(
    own_ref, beside_ref, bias_ref, gain_ref, shift_ref, weight_ref, joint_bias_ref,
    embedded_ref, normed_ref, joint_ref,
):
    embedded = own_ref[0] + beside_ref[0] + bias_ref[0]
    embedded_ref[0] = embedded
    normed = norm_inside(embedded, block_eps)[0] * gain_ref[...] + shift_ref[...]
    normed = normed.astype(jnp.bfloat16)
    normed_ref[0] = normed
    joint = dot_nn(normed, weight_ref[...]) + joint_bias_ref[...]
    joint_ref[0] = joint.astype(jnp.bfloat16)


def make_joint(total, beside, image_bias, gain, shift, weight, joint_bias):
    images, rows, width = beside.shape
    triple = weight.shape[1]
    return small_call(
        joint_kernel,
        "make_joint",
        (images,),
        [image_spec(rows, width)] * 2
        + [image_spec(1, width), whole_spec((1, width)), whole_spec((1, width))]
        + [whole_spec(weight.shape), whole_spec((1, triple))],
        [image_spec(rows, width), image_spec(rows, width), image_spec(rows, triple)],
        [
            jax.ShapeDtypeStruct((images, rows, width), jnp.float32),
            jax.ShapeDtypeStruct((images, rows, width), jnp.bfloat16),
            jax.ShapeDtypeStruct((images, rows, triple), jnp.bfloat16),
        ],
    )(total, beside, image_bias[:, None], gain[None], shift[None], weight, joint_bias[None])


def residual_kernel(
    attended_ref, embedded_ref, weight_ref, bias_ref, gain_ref, shift_ref, residual_ref, normed_ref
):
    branch = dot_nn(attended_ref[0], weight_ref[...]) + bias_ref[...]
    residual = embedded_ref[0] + branch
    residual_ref[0] = residual
    normed = norm_inside(residual, block_eps)[0] * gain_ref[...] + shift_ref[...]
    normed_ref[0] = normed.astype(jnp.bfloat16)


def make_residual(attended, embedded, weight, bias, gain, shift):
    images, rows, width = embedded.shape
    return small_call(
        residual_kernel,
        "make_residual",
        (images,),
        [image_spec(rows, width)] * 2 + [whole_spec(weight.shape)] + [whole_spec((1, width))] * 3,
        [image_spec(rows, width)] * 2,
        [
            jax.ShapeDtypeStruct((images, rows, width), jnp.float32),
            jax.ShapeDtypeStruct((images, rows, width), jnp.bfloat16),
        ],
    )(attended, embedded, weight, bias[None], gain[None], shift[None])


def norm_back_inside(grad, values, gain, epsilon):
    normal, factor = norm_inside(values, epsilon)
    scaled = grad * gain
    back = factor * (
        scaled
        - jnp.mean(scaled, axis=-1, keepdims=True)
        - normal * jnp.mean(scaled * normal, axis=-1, keepdims=True)
    )
    return back, jnp.sum(grad * normal, axis=0, keepdims=True)


def add_rows(out_ref, rows):
    @pl.when(pl.program_id(0) == 0)
    def _():
        out_ref[...] = jnp.zeros_like(out_ref)

    out_ref[...] += jnp.concatenate(rows, axis=0)


def branch_back_kernel(
    grad_ref, residual_ref, out_grad_ref, gain_ref, weight_ref,
    resid_ref, branch_ref, att_ref, sum_ref,
):
    grad = grad_ref[0]
    out_grad = out_grad_ref[0].astype(jnp.float32)
    back, gain_grad = norm_back_inside(grad, residual_ref[0], gain_ref[...], block_eps)
    resid = out_grad + back
    resid_ref[0] = resid
    branch = resid.astype(jnp.bfloat16)
    branch_ref[0] = branch
    att_ref[0] = dot_nt(branch, weight_ref[...]).astype(jnp.bfloat16)
    add_rows(
        sum_ref,
        [
            gain_grad,
            jnp.sum(grad, axis=0, keepdims=True),
            jnp.sum(branch.astype(jnp.float32), axis=0, keepdims=True),
            jnp.sum(out_grad, axis=0, keepdims=True),
        ],
    )


def branch_back(grad, residual, out_grad, gain, weight):
    images, rows, width = residual.shape
    return small_call(
        branch_back_kernel,
        "branch_back",
        (images,),
        [image_spec(rows, width)] * 3 + [whole_spec((1, width)), whole_spec(weight.shape)],
        [image_spec(rows, width)] * 3 + [whole_spec((4, width))],
        [
            jax.ShapeDtypeStruct((images, rows, width), jnp.float32),
            jax.ShapeDtypeStruct((images, rows, width), jnp.bfloat16),
            jax.ShapeDtypeStruct((images, rows, width), jnp.bfloat16),
            jax.ShapeDtypeStruct((4, width), jnp.float32),
        ],
    )(grad, residual, out_grad, gain[None], weight)


def embed_back_kernel(
    joint_ref, weight_ref, embedded_ref, resid_ref, gain_ref, emb_ref, sum_ref, image_ref
):
    grad = dot_nt(joint_ref[0], weight_ref[...])
    back, gain_grad = norm_back_inside(grad, embedded_ref[0], gain_ref[...], block_eps)
    emb = (resid_ref[0] + back).astype(jnp.bfloat16)
    emb_ref[0] = emb
    image_ref[0] = jnp.sum(emb.astype(jnp.float32), axis=0, keepdims=True)
    add_rows(sum_ref, [gain_grad, jnp.sum(grad, axis=0, keepdims=True)])


def embed_back(joint_grad, weight, embedded, resid, gain):
    images, rows, width = embedded.shape
    return small_call(
        embed_back_kernel,
        "embed_back",
        (images,),
        [image_spec(rows, joint_grad.shape[2]), whole_spec(weight.shape)]
        + [image_spec(rows, width)] * 2
        + [whole_spec((1, width))],
        [image_spec(rows, width), whole_spec((2, width)), image_spec(1, width)],
        [
            jax.ShapeDtypeStruct((images, rows, width), jnp.bfloat16),
            jax.ShapeDtypeStruct((2, width), jnp.float32),
            jax.ShapeDtypeStruct((images, 1, width), jnp.float32),
        ],
    )(joint_grad, weight, embedded, resid, gain[None])


def mlp_kernel(
    normed_ref, residual_ref, grad_ref, up_ref, bias_ref, down_ref, down_bias_ref,
    out_ref, back_ref, up_grad_ref, down_grad_ref, bias_grad_ref, active, to_pre, turned, total,
):
    rows = normed_ref.shape[0]
    part = rows // 2

    @pl.when(pl.program_id(0) == 0)
    def _():
        total[...] = residual_ref[...] + down_bias_ref[...]
        back_ref[...] = jnp.zeros_like(back_ref)
        turned[...] = normed_ref[...].T

    up = up_ref[...]
    down = down_ref[...]
    bias_grad = jnp.zeros(bias_grad_ref.shape, jnp.float32)
    for at in range(0, rows, part):
        span = slice(at, at + part)
        pre = dot_nn(normed_ref[span], up) + bias_ref[...]
        share = 0.5 + 0.5 * lax.erf(pre * (0.5**0.5))
        slope = share + pre * (jnp.exp(-0.5 * pre * pre) * (0.5 / jnp.pi) ** 0.5)
        act = (pre * share).astype(jnp.bfloat16)
        grad = (slope * dot_nt(grad_ref[span], down)).astype(jnp.bfloat16)
        active[span] = act
        to_pre[span] = grad
        total[span] += dot_nn(act, down)
        back_ref[span] += dot_nt(grad, up)
        bias_grad += jnp.sum(grad.astype(jnp.float32), axis=0, keepdims=True)
    bias_grad_ref[...] = bias_grad
    up_grad_ref[...] = dot_nn(turned[...], to_pre[...]).astype(jnp.bfloat16)
    down_grad_ref[...] = dot_tn(active[...], grad_ref[...]).astype(jnp.bfloat16)

    @pl.when(pl.program_id(0) == pl.num_programs(0) - 1)
    def _():
        out_ref[...] = total[...].astype(jnp.bfloat16)


def mlp(normed, residual, grads, up, up_bias, down, down_bias):
    rows, width = normed.shape
    hidden = up.shape[1]
    part = 256
    whole = pl.BlockSpec((rows, width), lambda s: (0, 0))
    columns = pl.BlockSpec((width, part), lambda s: (0, s))
    lines = pl.BlockSpec((part, width), lambda s: (s, 0))
    vector = pl.BlockSpec((1, part), lambda s: (0, s))
    return pl.pallas_call(
        mlp_kernel,
        grid=(hidden // part,),
        in_specs=[
            whole, whole, whole, columns, vector, lines,
            pl.BlockSpec((1, width), lambda s: (0, 0)),
        ],
        out_specs=[whole, whole, columns, lines, vector],
        out_shape=[
            jax.ShapeDtypeStruct((rows, width), jnp.bfloat16),
            jax.ShapeDtypeStruct((rows, width), jnp.float32),
            jax.ShapeDtypeStruct((width, hidden), jnp.bfloat16),
            jax.ShapeDtypeStruct((hidden, width), jnp.bfloat16),
            jax.ShapeDtypeStruct((1, hidden), jnp.float32),
        ],
        scratch_shapes=[
            pltpu.VMEM((rows, part), jnp.bfloat16),
            pltpu.VMEM((rows, part), jnp.bfloat16),
            pltpu.VMEM((width, rows), jnp.bfloat16),
            pltpu.VMEM((rows, width), jnp.float32),
        ],
        compiler_params=grid_params(40),
        cost_estimate=pl.CostEstimate(flops=1, bytes_accessed=1, transcendentals=0),
        name="mlp",
    )(normed, residual, grads, up, up_bias[None], down, down_bias[None])


def per_device(
    pixels,
    band_count,
    band_bin,
    bin_wave,
    run_mean,
    run_var,
    weight_tokens,
    bias_token,
    hyper_in,
    hyper_qv_bias,
    hyper_out,
    hyper_out_bias,
    hyper_gain,
    hyper_shift,
    hyper_up,
    hyper_up_bias,
    hyper_down,
    hyper_down_bias,
    kernel_weight,
    bias_weight,
    bias_offset,
    norm_gain,
    norm_shift,
    w_qkv,
    qv_bias,
    w_out,
    out_bias,
    w_up,
    up_bias,
    w_down,
    down_bias,
    cotangent,
):
    pixel_data = pixels[0]
    images, band_slots, patches, pixel_cells = pixel_data.shape
    bin_total = bin_wave.shape[0]
    model_width = w_qkv.shape[0]
    head_size = model_width // HEADS
    padded = -(-patches // 16) * 16
    rows = images * padded
    cells = kernel_weight.shape[0]
    core = lax.axis_index("batch") & 1
    live_band = (
        lax.broadcasted_iota(jnp.int32, (images, band_slots), 1) < band_count[0][:, None]
    ).astype(jnp.float32)
    bin_onehot = (
        band_bin[0][..., None]
        == lax.broadcasted_iota(jnp.int32, (images, band_slots, bin_total), 2)
    ).astype(jnp.float32)
    chosen = bin_onehot * live_band[..., None]
    run_rstd = lax.rsqrt(run_var + stat_eps)
    band_mean = jnp.einsum("ibn,n->ib", chosen, run_mean, precision=highest)
    band_rstd = jnp.einsum("ibn,n->ib", chosen, run_rstd, precision=highest)
    values32 = pixel_data.astype(jnp.float32)
    band_total = jnp.sum(values32, axis=(2, 3))
    band_square = jnp.sum(values32 * values32, axis=(2, 3))
    bin_sums = jnp.einsum("ib,ibn->n", band_total, chosen, precision=highest)
    bin_squares = jnp.einsum("ib,ibn->n", band_square, chosen, precision=highest)
    bin_counts = jnp.sum(chosen, axis=(0, 1))

    grad_out = jnp.pad(cotangent[0], ((0, 0), (0, padded - patches), (0, 0)))
    band_wave = jnp.einsum("ibn,n->ib", bin_onehot, bin_wave, precision=highest)
    wave_emb = wave_embed(band_wave, hyper_in.shape[0])
    hyper_params = (
        weight_tokens,
        bias_token,
        hyper_in,
        hyper_qv_bias,
        hyper_out,
        hyper_out_bias,
        hyper_gain,
        hyper_shift,
        hyper_up,
        hyper_up_bias,
        hyper_down,
        hyper_down_bias,
    )

    def make_low():
        (band_vec, bias_vec), hyper_back = jax.vjp(
            partial(hypernet, wave_emb=wave_emb, live_band=live_band), hyper_params
        )
        band_low = band_vec.astype(jnp.bfloat16).reshape(images * band_slots, -1)
        return band_low, bias_vec, hyper_back

    def place(piece, *quarters):
        return jnp.stack([jnp.asarray(at, jnp.int32) for at in (piece,) + quarters])

    if not tuned_mesh():
        band_low, bias_vec, hyper_back = make_low()
        chip_low = jnp.concatenate([band_low, swap_batch(band_low, 1)])
        mine, other = split_pixels(pixel_data, band_mean, band_rstd, core, padded, cells)
        chip_pixels = (mine, swap_batch(other, 1))
        total, kernels = (None, None)
        for at, weight in enumerate(plain_weight_pieces(kernel_weight)):
            total, kernels = embed_piece(
                place(at, 0, 1, 2, 3), chip_low, [weight], chip_pixels, total, kernels
            )
        line_pixels = plain_line_cells(jnp.concatenate(chip_pixels, axis=1))
        line_low = lax.all_gather(
            chip_low, "batch", axis=0, axis_index_groups=same_core(), tiled=True
        )
    else:
        group = lax.axis_index("group")
        chip = lax.axis_index("batch") >> 1
        part = cells // 8
        quarter = part_of(kernel_weight, group, 4)

        def sides(block):
            return swap_group(block, 1), swap_group(block, 2)

        def corners(beside, above):
            return swap_group(beside[:part], 2), swap_group(above[part:], 1)

        def added(state, piece, weights, shifts):
            spots = place(piece, *[group ^ shift for shift in shifts])
            return embed_piece(spots, chip_low, weights, chip_pixels, *state)

        def pixel_block(hop, half):
            piece = lax.dynamic_index_in_dim(chip_pixels[half], chip ^ hop, 0, keepdims=False)
            return swap_batch(piece, 2 * hop) if hop else piece

        right1, left1 = (along_line(quarter, -1), along_line(quarter, 1))
        band_low, bias_vec, hyper_back = make_low()
        band_low, bias_vec, right1, left1, pixel_data = tie(
            band_low, bias_vec, right1, left1, pixel_data
        )
        block1 = jnp.where(chip == 3, left1, right1)
        right2, left2 = (along_line(right1, -1), along_line(left1, 1))
        beside1, above1 = sides(block1)
        mine, other = split_pixels(pixel_data, band_mean, band_rstd, core, padded, cells)
        chip_low = jnp.concatenate([band_low, swap_batch(band_low, 1)])
        mine, other, chip_low, right2, left2, beside1, above1 = tie(
            mine, other, chip_low, right2, left2, beside1, above1
        )
        block2 = jnp.where(chip == 0, right2, jnp.where(chip == 3, left2, left1))
        right3, left3 = (along_line(right2, -1), along_line(left2, 1))
        corner1 = corners(beside1, above1)
        beside2, above2 = sides(block2)
        chip_pixels = (mine, swap_batch(other, 1))
        pixels2 = [pixel_block(2, 0)]
        state = embed_piece(
            place(chip, 0, 1, 2, 3), chip_low, [kernel_weight], chip_pixels, None, None
        )
        weights1 = [block1, beside1, above1]
        spots1 = of_chip(chip, [1, 2, 3, 2])
        state = added(state, spots1, weights1, (0, 1, 2))
        state, chip_pixels, right3, left3, corner1, beside2, above2, pixels2 = tie(
            state, chip_pixels, right3, left3, corner1, beside2, above2, pixels2
        )
        block3 = jnp.where(
            chip == 0, right3, jnp.where(chip == 1, right2, jnp.where(chip == 2, left2, left3))
        )
        corner2 = corners(beside2, above2)
        beside3, above3 = sides(block3)
        pixels2.append(pixel_block(2, 1))
        pixels1 = [pixel_block(1, 0)]
        weights1.append(jnp.concatenate(corner1))
        state = added(state, spots1, weights1[3:], (3,))
        weights2 = [block2, beside2, above2]
        spots2 = of_chip(chip, [2, 0, 1, 1])
        state = added(state, spots2, weights2, (0, 1, 2))
        state, corner2, beside3, above3, pixels1, pixels2, chip_pixels, grad_out = tie(
            state, corner2, beside3, above3, pixels1, pixels2, chip_pixels, grad_out
        )
        corner3 = corners(beside3, above3)
        pixels1.append(pixel_block(1, 1))
        weights2.append(jnp.concatenate(corner2))
        state = added(state, spots2, weights2[3:], (3,))
        weights3 = [block3, beside3, above3]
        spots3 = of_chip(chip, [3, 3, 0, 0])
        state = added(state, spots3, weights3, (0, 1, 2))
        state, corner3, pixels1, chip_pixels = tie(state, corner3, pixels1, chip_pixels)
        pixels3 = [pixel_block(3, 0)]
        weights3.append(jnp.concatenate(corner3))
        total, kernels = added(state, spots3, weights3[3:], (3,))
        line_low = line_rows(chip_low)
    image_bias = jnp.dot(bias_vec, bias_weight, precision=highest) + bias_offset
    total_beside = swap_batch(total[images:], 1)
    joint_bias = jnp.concatenate([qv_bias[0], jnp.zeros_like(qv_bias[0]), qv_bias[1]])
    embedded, normed1, joint = make_joint(
        total, total_beside, image_bias, norm_gain[0], norm_shift[0], w_qkv, joint_bias
    )
    attended = attend(joint, patches, head_size)
    if tuned_mesh():
        attended, pixels3, chip_pixels = tie(attended, pixels3, chip_pixels)
        pixels3.append(pixel_block(3, 1))
    residual, normed2 = make_residual(
        attended, embedded, w_out, out_bias, norm_gain[1], norm_shift[1]
    )
    block_out, grad_n2, grad_w_up, grad_w_down, grad_up_bias = mlp(
        normed2.reshape(rows, model_width),
        residual.reshape(rows, model_width),
        grad_out.reshape(rows, model_width),
        w_up,
        up_bias,
        w_down,
        down_bias,
    )
    if tuned_mesh():
        grad_n2, pixels3, grad_w_up, grad_w_down = tie(grad_n2, pixels3, grad_w_up, grad_w_down)
    block_out = block_out.reshape(1, images, padded, model_width)[:, :, :patches]
    grad_resid, grad_branch, grad_att, branch_sum = branch_back(
        grad_n2.reshape(images, padded, model_width), residual, grad_out, norm_gain[1], w_out
    )
    grad_gain_two, grad_shift_two, grad_out_bias, grad_down_bias = branch_sum
    grad_joint, joint_sum = attend_back(joint, grad_att, patches, head_size)
    grad_emb, embed_sum, grad_image_bias = embed_back(
        grad_joint, w_qkv, embedded, grad_resid, norm_gain[0]
    )
    grad_gain_one, grad_shift_one = embed_sum
    grad_image_bias = grad_image_bias[:, 0]
    grad_qv_bias = joint_sum.reshape(3, model_width)[::2]
    attended = attended.reshape(rows, model_width)
    grad_branch = grad_branch.reshape(rows, model_width)
    half_up, half_down = core_sum(grad_w_up), core_sum(grad_w_down)
    share_up, share_down = row_share(half_up), row_share(half_down)
    grad_w_out = jnp.einsum("rd,re->de", attended, grad_branch, preferred_element_type=jnp.float32)
    grad_w_qkv = jnp.einsum(
        "rd,rj->dj",
        normed1.reshape(rows, model_width),
        grad_joint.reshape(rows, 3 * model_width),
        preferred_element_type=jnp.float32,
    )
    beside_emb = swap_batch(grad_emb, 1)
    if tuned_mesh():
        far_emb = [swap_batch(grad_emb, 2 * hop) for hop in (1, 2)]
    grad_bias_weight = jnp.einsum("ik,ie->ke", bias_vec, grad_image_bias, precision=highest)
    grad_bias_offset = jnp.sum(grad_image_bias, axis=0)
    grad_bias_vec = jnp.einsum("ie,ke->ik", grad_image_bias, bias_weight, precision=highest)

    def pack(hyper_grads):
        wide = (
            hyper_grads[0],
            hyper_grads[2],
            hyper_grads[4],
            hyper_grads[8],
            hyper_grads[10],
            grad_bias_weight,
        )
        narrow = (
            hyper_grads[1],
            hyper_grads[3],
            hyper_grads[5],
            hyper_grads[6],
            hyper_grads[7],
            hyper_grads[9],
            hyper_grads[11],
            bin_sums,
            bin_squares,
            bin_counts,
            grad_bias_offset,
            jnp.stack([grad_gain_one, grad_gain_two]),
            jnp.stack([grad_shift_one, grad_shift_two]),
            grad_qv_bias,
            grad_out_bias,
            grad_up_bias[0],
            grad_down_bias,
        )
        parts = [block_rows(part) for part in wide]
        thin = [part.reshape(-1, 128) for part in narrow]
        length = sum(part.shape[0] for part in thin)
        thin = jnp.concatenate(thin + [jnp.zeros((-length % 128, 128), jnp.float32)])
        (thin,) = tie(thin)
        parts.append(thin)
        length = sum(part.shape[0] for part in parts)
        parts.append(jnp.zeros((-length % 256, 128), jnp.float32))
        small = jnp.concatenate(parts)
        return wide, narrow, parts, small

    rates = jnp.tile(band_rstd, (1, pixel_cells // 8))
    rates = jnp.concatenate([rates, swap_batch(rates, 1)])[:, None, :]
    chip_emb = jnp.concatenate([grad_emb, beside_emb])

    def finish_low(grad_vectors):
        far = swap_batch(grad_vectors[images * band_slots :], 1)
        grad_vectors = grad_vectors[: images * band_slots] + far
        grad_vectors = grad_vectors.reshape(images, band_slots, -1)
        return hyper_back((grad_vectors, grad_bias_vec))[0]

    half_out = core_sum(grad_w_out.astype(jnp.bfloat16))
    half_qkv = core_sum(grad_w_qkv.astype(jnp.bfloat16))
    grad_vectors = None
    if tuned_mesh():
        plan = [
            (place(chip, 0, 1, 2, 3), [kernel_weight]),
            (place(spots1, group, group ^ 1, group ^ 2, group ^ 3), weights1),
            (place(spots2, group, group ^ 1, group ^ 2, group ^ 3), weights2),
            (place(spots3, group, group ^ 1, group ^ 2, group ^ 3), weights3),
        ]
        for spots, weights in plan:
            grad_vectors = band_piece(spots, chip_emb, weights, chip_pixels, grad_vectors)
        grad_vectors, far_emb, half_out, half_qkv, share_up, line_low, rates = tie(
            grad_vectors, far_emb, half_out, half_qkv, share_up, line_low, rates
        )
        far_emb.append(swap_batch(grad_emb, 6))
        share_out_rows, share_qkv = row_share(half_out), row_share(half_qkv)
        line_emb = [grad_emb, beside_emb]
        for far in far_emb[:2]:
            line_emb += [far, swap_batch(far, 1)]
        hyper_grads = finish_low(grad_vectors)
        wide, narrow, parts, small = pack(hyper_grads)
        small, block_out, far_emb, line_emb, share_down, share_out_rows, share_qkv, chip_emb = tie(
            small, block_out, far_emb, line_emb, share_down, share_out_rows, share_qkv, chip_emb
        )
        line_emb += [far_emb[2], swap_batch(far_emb[2], 1)]
        line_pixels = [pixel_block(0, 0), pixel_block(0, 1)] + pixels1 + pixels2 + pixels3
    else:
        for at, weight in enumerate(plain_weight_pieces(kernel_weight)):
            grad_vectors = band_piece(
                place(at, 0, 1, 2, 3), chip_emb, [weight], chip_pixels, grad_vectors
            )
        hyper_grads = finish_low(grad_vectors)
        wide, narrow, parts, small = pack(hyper_grads)
        share_out_rows, share_qkv = row_share(half_out), row_share(half_qkv)
        line_emb = plain_line_images(grad_emb, beside_emb)
    halves = 2 if cells % 32 == 0 else 1
    low_turned = line_low.T

    if not tuned_mesh():
        kernel_share = 0.0
        for at in range(0, line_pixels[0].shape[0], 32):
            columns = low_turned[:, at * band_slots : (at + 32) * band_slots]
            found = line_grads(
                columns, cells, [line_pixels[0][at : at + 32]], [line_emb[0][at : at + 32]], 0, 1
            )
            kernel_share += found.astype(jnp.float32)
        kernel_total = lax.psum(kernel_share.astype(jnp.bfloat16), "group").astype(jnp.float32)
        chip_back = pixel_grads(chip_emb, kernels, rates)
        other_back = swap_batch(chip_back[:, images:], 1)
        pixel_grad = join_pixels(
            chip_back[:, :images], other_back, core, patches, cells, pixel_cells, band_slots
        )
        small = lax.psum(small, ("group", "batch"))
        totals = [
            row_both(row_mine(share)) for share in (share_qkv, share_out_rows, share_up, share_down)
        ]
    else:
        def halved(value):
            rows_half = value.shape[0] // 2
            return [value[:rows_half], value[rows_half:]]

        kernel_one = line_grads(low_turned, cells, line_pixels, line_emb, 0, 2)
        small_came = swap_batch(part_of(small, 1 - core, 2), 1)
        kernel_one, small_came, line_emb = tie(kernel_one, small_came, line_emb)

        one = halved(kernel_one)
        one_came = sum_out(one, False)
        small = part_of(small, core, 2) + small_came
        small_came = [swap_batch(part_of(small, chip ^ hop, 4), 2 * hop) for hop in (1, 2, 3)]
        mine_up, mine_down = row_mine(share_up), row_mine(share_down)
        kernel_two = line_grads(low_turned, cells, line_pixels, line_emb, 1, 2)
        kernel_two, one_came, chip_emb, small_came = tie(
            kernel_two, one_came, chip_emb, small_came
        )

        one = sum_in(one, one_came, False)
        one_came = sum_out(one, True)
        two = halved(kernel_two)
        two_came = sum_out(two, False)
        small = sum(small_came, part_of(small, chip, 4))
        small_came = swap_group(small, 1)
        chip_back = pixel_grads(chip_emb, kernels, rates)
        chip_back, one_came, two_came, small_came, mine_up, mine_down, share_qkv = tie(
            chip_back, one_came, two_came, small_came, mine_up, mine_down, share_qkv
        )

        one = sum_in(one, one_came, True)
        one_came = share_out(one, True)
        two = sum_in(two, two_came, False)
        two_came = sum_out(two, True)
        small = small + small_came
        small_came = swap_group(small, 2)
        other_back = swap_batch(chip_back[:, images:], 1)
        mine_qkv, mine_out = row_mine(share_qkv), row_mine(share_out_rows)
        totals = [row_both(mine) for mine in (mine_up, mine_down)]
        other_back, one_came, two_came, small_came, totals = tie(
            other_back, one_came, two_came, small_came, totals
        )

        one = share_in(one, one_came, True)
        one_came = share_out(one, False)
        two = sum_in(two, two_came, True)
        two_came = share_out(two, True)
        small = small + small_came
        small_came = [swap_batch(small, 2 * hop) for hop in (1, 2, 3)]
        pixel_grad = join_pixels(
            chip_back[:, :images], other_back, core, patches, cells, pixel_cells, band_slots
        )
        pixel_grad, one_came, two_came, small_came, mine_qkv, mine_out = tie(
            pixel_grad, one_came, two_came, small_came, mine_qkv, mine_out
        )

        two = share_in(two, two_came, True)
        two_came = share_out(two, False)
        small = four_in_order(chip, [small] + small_came)
        small_came = swap_batch(small, 1)
        one = share_in(one, one_came, False)
        totals = [row_both(mine_qkv), row_both(mine_out)] + totals
        two_came, small_came, one, totals = tie(two_came, small_came, one, totals)
        small = in_order(core, small, small_came)
        kernel_total = jnp.concatenate(one + share_in(two, two_came, False)).astype(jnp.float32)
    pixel_grad = pixel_grad[None]

    found = []
    at = 0
    for part, like in zip(parts, wide):
        found.append(unblock_rows(small[at : at + part.shape[0]], like.shape[0]))
        at += part.shape[0]
    for like in narrow:
        count = like.size // 128
        found.append(small[at : at + count].reshape(like.shape))
        at += count
    batch_mean, batch_var = bin_stats(found[13], found[14], found[15], patches * pixel_cells)
    return (
        block_out,
        pixel_grad,
        batch_mean,
        batch_var,
        found[0],
        found[6],
        found[1],
        found[7],
        found[2],
        found[8],
        found[9],
        found[10],
        found[3],
        found[11],
        found[4],
        found[12],
        kernel_total,
        found[5],
        found[16],
        found[17],
        found[18],
        totals[0],
        found[19],
        totals[1],
        found[20],
        totals[2],
        found[21],
        totals[3],
        found[22],
    )


def solution(mesh):
    return jax.shard_map(
        per_device,
        mesh=mesh,
        in_specs=(
            P("group", "batch", None, None, None),
            P("group", "batch"),
            P("group", "batch", None),
            P(),
            P(),
            P(),
            P(),
            P(),
            P(),
            P(),
            P(),
            P(),
            P(),
            P(),
            P(),
            P(),
            P(),
            P(),
            P("batch", None, None),
            P(),
            P(),
            P(),
            P(),
            P(),
            P(),
            P(),
            P(),
            P(),
            P(),
            P(),
            P(),
            P("group", "batch", None, None),
        ),
        out_specs=(
            P("group", "batch", None, None),
            P("group", "batch", None, None, None),
            P(),
            P(),
            P(),
            P(),
            P(),
            P(),
            P(),
            P(),
            P(),
            P(),
            P(),
            P(),
            P(),
            P(),
            P("batch", None, None),
            P(),
            P(),
            P(),
            P(),
            P("group", None),
            P(),
            P("group", None),
            P(),
            P("group", None),
            P(),
            P("group", None),
            P(),
        ),
        check_vma=False,
    )
```

```python
from functools import partial

import jax
import jax.numpy as jnp
from jax import lax
from jax.experimental import pallas as pl
from jax.experimental.pallas import tpu as pltpu
from jax.sharding import PartitionSpec as P

HEADS = 12
HHEADS = 4


highest = lax.Precision.HIGHEST
high = lax.Precision.HIGH
stat_eps = 1e-05
hyper_eps = 1e-05
block_eps = 1e-06
wave_scale = 1000.0


def layer_norm(values, gain, shift, epsilon):
    center = values - jnp.mean(values, axis=-1, keepdims=True)
    return (
        center * lax.rsqrt(jnp.mean(center * center, axis=-1, keepdims=True) + epsilon) * gain
        + shift
    )


def norm_parts(values, epsilon):
    center = values - jnp.mean(values, axis=-1, keepdims=True)
    factor = lax.rsqrt(jnp.mean(center * center, axis=-1, keepdims=True) + epsilon)
    return (center * factor, factor)


def norm_back(grad_hat, normal_hat, factor):
    return factor * (
        grad_hat
        - jnp.mean(grad_hat, axis=-1, keepdims=True)
        - normal_hat * jnp.mean(grad_hat * normal_hat, axis=-1, keepdims=True)
    )


def wave_embed(band_wave, model_width):
    half_width = model_width // 2
    ladder = jnp.arange(half_width, dtype=jnp.float32) / half_width
    frequency = 1.0 / 10000.0**ladder
    phase_arg = band_wave[..., None] * wave_scale * frequency
    return jnp.concatenate([jnp.sin(phase_arg), jnp.cos(phase_arg)], axis=-1)


def bin_stats(total_sums, squares, counts, cell_count):
    scaled = jnp.maximum(counts * cell_count, 1.0)
    bin_mean = total_sums / scaled
    bin_var = squares / scaled - bin_mean * bin_mean
    return (bin_mean, bin_var)


def hypernet(params, wave_emb, live_band):
    (
        tokens_w,
        token_b,
        w_in,
        in_bias,
        w_proj,
        proj_bias,
        gain_pair,
        shifts,
        w_expand,
        expand_bias,
        w_reduce,
        reduce_bias,
    ) = params
    image_count = wave_emb.shape[0]
    band_slots = wave_emb.shape[1]
    model_width = wave_emb.shape[2]
    head_count = HHEADS
    head_size = model_width // head_count
    token_rows = tokens_w.shape[0]
    sequence = jnp.concatenate(
        [
            jnp.broadcast_to(tokens_w[None], (image_count, token_rows, model_width)),
            wave_emb,
            jnp.broadcast_to(token_b[None, None, :], (image_count, 1, model_width)),
        ],
        axis=1,
    )
    key_live = (
        jnp.concatenate(
            [
                jnp.ones((image_count, token_rows), jnp.float32),
                live_band,
                jnp.ones((image_count, 1), jnp.float32),
            ],
            axis=1,
        )
        > 0.5
    )
    projected = jnp.einsum("nsk,kj->nsj", sequence, w_in, precision=high)
    query_heads = (projected[..., :model_width] + in_bias[0]).reshape(
        image_count, -1, head_count, head_size
    )
    keyed = projected[..., model_width : 2 * model_width].reshape(
        image_count, -1, head_count, head_size
    )
    valued = (projected[..., 2 * model_width :] + in_bias[1]).reshape(
        image_count, -1, head_count, head_size
    )
    scores = jnp.einsum("nqhd,nkhd->nhqk", query_heads, keyed, precision=high) * head_size ** (
        -0.5
    )
    scores = jnp.where(key_live[:, None, None, :], scores, -1e30)
    attn_probs = jax.nn.softmax(scores, axis=-1)
    mixed_heads = jnp.einsum("nhqk,nkhd->nqhd", attn_probs, valued, precision=high).reshape(
        image_count, -1, model_width
    )
    first_out = layer_norm(
        sequence + jnp.einsum("nsk,kj->nsj", mixed_heads, w_proj, precision=high) + proj_bias,
        gain_pair[0],
        shifts[0],
        hyper_eps,
    )
    inner_act = jax.nn.gelu(
        jnp.einsum("nsk,kf->nsf", first_out, w_expand, precision=high) + expand_bias,
        approximate=False,
    )
    second_out = layer_norm(
        first_out + jnp.einsum("nsf,fk->nsk", inner_act, w_reduce, precision=high) + reduce_bias,
        gain_pair[1],
        shifts[1],
        hyper_eps,
    )
    return (
        second_out[:, token_rows : token_rows + band_slots] + wave_emb,
        second_out[:, token_rows + band_slots],
    )


def swap_group(value, bits):
    return lax.ppermute(value, "group", [(at, at ^ bits) for at in range(4)])


def swap_batch(value, bits):
    count = lax.axis_size("batch")
    return lax.ppermute(value, "batch", [(at, at ^ bits) for at in range(count)])


def tuned_mesh():
    return lax.axis_size("group") == 4 and lax.axis_size("batch") == 8


def same_core():
    count = lax.axis_size("batch")
    return [list(range(0, count, 2)), list(range(1, count, 2))]


def in_order(bit, first, second):
    return jnp.where(
        bit == 0, jnp.concatenate([first, second]), jnp.concatenate([second, first])
    )


def four_in_order(index, pieces):
    low, high = (index & 1, index >> 1)
    return in_order(
        high, in_order(low, pieces[0], pieces[1]), in_order(low, pieces[2], pieces[3])
    )


def part_of(value, index, parts):
    rows = value.shape[0] // parts
    return lax.dynamic_slice_in_dim(value, index * rows, rows)


def tie(*values):
    return lax.optimization_barrier(values)


def along_line(value, step, chips=(0, 1, 2, 3)):
    pairs = [
        (2 * at + core, 2 * (at + step) + core)
        for at in chips
        for core in (0, 1)
        if 0 <= at + step < 4
    ]
    return lax.ppermute(value, "batch", pairs)


def of_chip(chip, values):
    return jnp.array(values, jnp.int32)[chip]


def plain_weight_pieces(weight):
    core = lax.axis_index("batch") & 1
    shards = lax.all_gather(weight, "batch", axis=0)
    shards = shards.reshape((-1, 2) + weight.shape)
    mine = lax.dynamic_index_in_dim(shards, core, 1, keepdims=False)
    return mine.reshape((4, -1) + weight.shape[1:])


def plain_line_cells(pixels):
    pieces, images, rows, lanes = pixels.shape
    chips = lax.axis_size("batch") // 2
    parts = pixels.reshape(pieces, images, rows, chips // pieces, -1)
    parts = parts.transpose(0, 3, 1, 2, 4).reshape(chips, images, rows, -1)
    came = lax.all_to_all(parts, "batch", 0, 0, axis_index_groups=same_core(), tiled=True)
    return [came.reshape((chips * images,) + came.shape[2:])]


def plain_line_images(value, beside):
    both = jnp.concatenate([value, beside])
    return [lax.all_gather(both, "batch", axis=0, axis_index_groups=same_core(), tiled=True)]


def line_rows(low):
    if not tuned_mesh():
        return lax.all_gather(low, "batch", axis=0, axis_index_groups=same_core(), tiled=True)
    return jnp.concatenate([low] + [swap_batch(low, 2 * hop) for hop in (1, 2, 3)])


def core_sum(keep, send):
    return add_low(keep, swap_batch(send, 1))


def row_share(half):
    return lax.psum_scatter(half, "group", scatter_dimension=0, tiled=True)


def row_mine(share):
    return lax.psum(share, "batch", axis_index_groups=same_core())


def row_both(mine):
    core = lax.axis_index("batch") & 1
    return in_order(core, mine, swap_batch(mine, 1)).astype(jnp.float32)


def add_low(left, right):
    return (left.astype(jnp.float32) + right.astype(jnp.float32)).astype(left.dtype)


def ring_sides():
    group = lax.axis_index("group")
    side, level = (group & 1, group >> 1)
    return (1, side), (2, level)


def sum_out(parts, flip):
    order = ring_sides()[::-1] if flip else ring_sides()
    return [swap_group(part_of(part, 1 - bit, 2), way) for part, (way, bit) in zip(parts, order)]


def sum_in(parts, came, flip):
    order = ring_sides()[::-1] if flip else ring_sides()
    return [
        add_low(part_of(part, bit, 2), other)
        for part, other, (way, bit) in zip(parts, came, order)
    ]


def share_out(parts, flip):
    order = ring_sides()[::-1] if flip else ring_sides()
    return [swap_group(part, way) for part, (way, bit) in zip(parts, order)]


def share_in(parts, came, flip):
    order = ring_sides()[::-1] if flip else ring_sides()
    return [in_order(bit, part, other) for part, other, (way, bit) in zip(parts, came, order)]


def block_rows(value):
    rows, lanes = value.shape
    return value.reshape(rows, lanes // 128, 128).transpose(1, 0, 2).reshape(-1, 128)


def unblock_rows(value, rows):
    return value.reshape(-1, rows, 128).transpose(1, 0, 2).reshape(rows, -1)


def grid_params(mebibytes, semantics=1):
    return pltpu.CompilerParams(
        dimension_semantics=("arbitrary",) * semantics,
        vmem_limit_bytes=mebibytes * 1024 * 1024,
    )


def dot_nn(left, right):
    return lax.dot_general(
        left, right, (((1,), (0,)), ((), ())), preferred_element_type=jnp.float32
    )


def dot_nt(left, right):
    return lax.dot_general(
        left, right, (((1,), (1,)), ((), ())), preferred_element_type=jnp.float32
    )


def dot_tn(left, right):
    return lax.dot_general(
        left, right, (((0,), (0,)), ((), ())), preferred_element_type=jnp.float32
    )


def split_kernel(cells, core_ref, pixel_ref, mean_ref, rate_ref, *refs):
    out_refs, scratch = (refs[:2], refs[2:])
    patches, bands, lanes = pixel_ref.shape[1:]
    pieces, _, rows, _ = out_refs[0].shape
    share = lanes // (2 * pieces * cells)
    span = cells * bands
    tile = 128
    columns, tiles = (lanes // tile, -(-rows // tile))
    flat, turned = (scratch[:columns], scratch[columns:])
    values = (pixel_ref[0].astype(jnp.float32) - mean_ref[0]) * rate_ref[0]
    values = values.astype(jnp.bfloat16).astype(jnp.float32).reshape(patches * bands, lanes)
    for column in range(columns):
        flat[column][: patches * bands] = values[:, column * tile : (column + 1) * tile]
        flat[column][patches * bands :] = jnp.zeros(
            (flat[column].shape[0] - patches * bands, tile), jnp.float32
        )
    for band in range(bands):
        for column in range(columns):
            for at in range(tiles):
                block = flat[column][pl.ds(at * tile * bands + band, tile, stride=bands), :]
                turned[at][pl.ds(column * tile * bands + band, tile, stride=bands), :] = block.T
    for out_ref, side in zip(out_refs, (core_ref[0], 1 - core_ref[0])):
        for piece in range(pieces):
            for at in range(tiles):
                count = min(tile, rows - at * tile)
                parts = []
                for one in range(share):
                    first = ((piece * share + one) * 2 + side) * span
                    place = pl.ds(pl.multiple_of(first, span), span)
                    parts.append(turned[at][place, :].T[:count])
                block = parts[0] if share == 1 else jnp.concatenate(parts, axis=1)
                out_ref[piece, 0, at * tile : at * tile + count, :] = block.astype(jnp.bfloat16)


def turn_scratch(rows, bands, lanes):
    tiles = -(-rows // 128)
    return [pltpu.VMEM((tiles * 128 * bands, 128), jnp.float32)] * (lanes // 128) + [
        pltpu.VMEM((lanes * bands, 128), jnp.float32)
    ] * tiles


def split_pixels(pixels, means, rates, core, rows, cells):
    images, bands, patches, lanes = pixels.shape
    wide = bands * lanes // 8
    side = jax.ShapeDtypeStruct((4, images, rows, wide), jnp.bfloat16)
    return pl.pallas_call(
        partial(split_kernel, cells),
        grid_spec=pltpu.PrefetchScalarGridSpec(
            num_scalar_prefetch=1,
            grid=(images,),
            in_specs=[
                pl.BlockSpec((1, patches, bands, lanes), lambda i, core: (i, 0, 0, 0)),
                pl.BlockSpec((1, bands, 1), lambda i, core: (i, 0, 0)),
                pl.BlockSpec((1, bands, 1), lambda i, core: (i, 0, 0)),
            ],
            out_specs=[pl.BlockSpec((4, 1, rows, wide), lambda i, core: (0, i, 0, 0))] * 2,
            scratch_shapes=turn_scratch(rows, bands, lanes),
        ),
        out_shape=[side, side],
        compiler_params=grid_params(40),
        cost_estimate=pl.CostEstimate(flops=1, bytes_accessed=1, transcendentals=0),
        name="split_pixels",
    )(core.reshape(1), pixels.transpose(0, 2, 1, 3), means[:, :, None], rates[:, :, None])


def join_kernel(cells, patches, core_ref, mine_ref, other_ref, out_ref, *scratch):
    rows = mine_ref.shape[2]
    bands, lanes = out_ref.shape[2:]
    pieces = mine_ref.shape[0]
    share = lanes // (2 * pieces * cells)
    span = cells * bands
    tile = 128
    columns, tiles = (lanes // tile, -(-rows // tile))
    flat, turned = (scratch[:columns], scratch[columns:])
    core = core_ref[0]
    for piece in range(pieces):
        for ref, flip in ((mine_ref, core), (other_ref, 1 - core)):
            for one in range(share):
                first = ((piece * share + one) * 2 + flip) * span
                place = pl.ds(pl.multiple_of(first, span), span)
                for at in range(tiles):
                    count = min(tile, rows - at * tile)
                    block = ref[
                        piece, 0, at * tile : at * tile + count, one * span : (one + 1) * span
                    ].astype(jnp.float32)
                    if count < tile:
                        block = jnp.concatenate(
                            [block, jnp.zeros((tile - count, span), jnp.float32)]
                        )
                    turned[at][place, :] = block.T
    for band in range(bands):
        for column in range(columns):
            for at in range(tiles):
                block = turned[at][pl.ds(column * tile * bands + band, tile, stride=bands), :]
                flat[column][pl.ds(at * tile * bands + band, tile, stride=bands), :] = block.T
    for column in range(columns):
        out_ref[0, :, :, column * tile : (column + 1) * tile] = (
            flat[column][: patches * bands].reshape(patches, bands, tile).astype(jnp.bfloat16)
        )


def join_pixels(mine, other, core, patches, cells, lanes, bands):
    pieces, images, rows, wide = mine.shape
    block = pl.BlockSpec((pieces, 1, rows, wide), lambda i, core: (0, i, 0, 0))
    joined = pl.pallas_call(
        partial(join_kernel, cells, patches),
        grid_spec=pltpu.PrefetchScalarGridSpec(
            num_scalar_prefetch=1,
            grid=(images,),
            in_specs=[block, block],
            out_specs=pl.BlockSpec((1, patches, bands, lanes), lambda i, core: (i, 0, 0, 0)),
            scratch_shapes=turn_scratch(rows, bands, lanes),
        ),
        out_shape=jax.ShapeDtypeStruct((images, patches, bands, lanes), jnp.bfloat16),
        compiler_params=grid_params(40),
        cost_estimate=pl.CostEstimate(flops=1, bytes_accessed=1, transcendentals=0),
        name="join_pixels",
    )(core.reshape(1), mine, other)
    return joined.transpose(0, 2, 1, 3)


def embed_kernel(first, count, at_ref, low_ref, *refs):
    weight_refs, pixel_refs = refs[:count], refs[count : count + 2]
    if first:
        total_ref, kernel_ref, weight_now = refs[count + 2 :]
    else:
        before_ref, _, total_ref, kernel_ref, weight_now = refs[count + 2 :]
    share = pixel_refs[0].shape[1]
    images = 2 * share
    cells = weight_now.shape[0]
    bands = pixel_refs[0].shape[3] // cells

    @pl.when(pl.program_id(0) == 0)
    def _():
        if first:
            total_ref[...] = jnp.zeros_like(total_ref)
        else:
            total_ref[...] = before_ref[...]

    for at in range(count):

        @pl.when((pl.program_id(0) == at) | (count == 1))
        def _(at=at):
            weight_now[...] = weight_refs[at][...]

    low = low_ref[...]
    for cell in range(cells):
        made = dot_nt(low, weight_now[cell]).astype(jnp.bfloat16)
        for image in range(images):
            kernel_ref[0, image, cell * bands : (cell + 1) * bands, :] = made[
                image * bands : (image + 1) * bands
            ]
    for image in range(images):
        block = pixel_refs[image // share][0, image % share]
        total_ref[image] += dot_nn(block, kernel_ref[0, image])


def embed_piece(place, low, weights, pixels, total, kernels):
    pieces, share, rows, lanes = pixels[0].shape
    images = 2 * share
    cells, width, depth = weights[0].shape
    step = lanes // (4 * 16)
    count = len(weights)
    steps = max(count, cells // step)
    bands = lanes // (4 * step)
    first = total is None
    any_spec = pl.BlockSpec(memory_space=pl.ANY)
    whole_total = pl.BlockSpec((images, rows, width), lambda t, at: (0, 0, 0))
    if count == 1:
        weight_specs = [pl.BlockSpec((step, width, depth), lambda t, at: (t, 0, 0))]
    else:
        weight_specs = [pl.BlockSpec((step, width, depth), lambda t, at: (0, 0, 0))] * count
    return pl.pallas_call(
        partial(embed_kernel, first, count),
        grid_spec=pltpu.PrefetchScalarGridSpec(
            num_scalar_prefetch=1,
            grid=(steps,),
            in_specs=[pl.BlockSpec(low.shape, lambda t, at: (0, 0))]
            + weight_specs
            + [
                pl.BlockSpec(
                    (1, share, rows, step * bands), lambda t, at: (at[0], 0, 0, at[1 + t])
                ),
            ]
            * 2
            + ([] if first else [whole_total, any_spec]),
            out_specs=[
                whole_total,
                pl.BlockSpec(
                    (1, images, step * bands, width), lambda t, at: (at[0], 0, at[1 + t], 0)
                ),
            ],
            scratch_shapes=[pltpu.VMEM((step, width, depth), jnp.bfloat16)],
        ),
        out_shape=[
            jax.ShapeDtypeStruct((images, rows, width), jnp.float32),
            jax.ShapeDtypeStruct((pieces, images, lanes, width), jnp.bfloat16),
        ],
        input_output_aliases={} if first else {4 + count: 0, 5 + count: 1},
        compiler_params=grid_params(48),
        cost_estimate=pl.CostEstimate(flops=1, bytes_accessed=1, transcendentals=0),
        name="embed_piece",
    )(place, low, *weights, *pixels, *(() if first else (total, kernels)))


def pixel_grad_kernel(grad_ref, kernel_ref, rate_ref, out_ref):
    for image in range(grad_ref.shape[0]):
        out_ref[0, image] = (
            dot_nt(grad_ref[image], kernel_ref[0, image]) * rate_ref[image]
        ).astype(jnp.bfloat16)


def pixel_grads(grads, kernels, rates):
    pieces, images, lanes, width = kernels.shape
    rows = grads.shape[1]
    share = images // 2
    return pl.pallas_call(
        pixel_grad_kernel,
        grid=(2, pieces),
        in_specs=[
            pl.BlockSpec((share, rows, width), lambda i, j: (i, 0, 0)),
            pl.BlockSpec((1, share, lanes, width), lambda i, j: (j, i, 0, 0)),
            pl.BlockSpec((share, 1, lanes), lambda i, j: (i, 0, 0)),
        ],
        out_specs=pl.BlockSpec((1, share, rows, lanes), lambda i, j: (j, i, 0, 0)),
        out_shape=jax.ShapeDtypeStruct((pieces, images, rows, lanes), jnp.bfloat16),
        compiler_params=grid_params(40, 2),
        cost_estimate=pl.CostEstimate(flops=1, bytes_accessed=1, transcendentals=0),
        name="pixel_grads",
    )(grads, kernels, rates)


def line_kernel(half, halves, low_ref, pixel_refs, grad_refs, out_ref, made):
    cells = out_ref.shape[0]
    lanes = pixel_refs[0].shape[2] // halves
    bands = lanes // cells
    columns = slice(half * lanes, (half + 1) * lanes)
    spots = [(ref, at) for ref in grad_refs for at in range(ref.shape[0])]
    image = 0
    for pixel_ref in pixel_refs:
        for at in range(pixel_ref.shape[0]):
            grad_ref, where = spots[image]
            grads = dot_tn(pixel_ref[at, :, columns], grad_ref[where]).astype(jnp.bfloat16)
            for cell in range(cells):
                made[cell, image * bands : (image + 1) * bands, :] = grads[
                    cell * bands : (cell + 1) * bands
                ]
            image += 1

    @pl.loop(0, cells, unroll=4)
    def _(cell):
        out_ref[cell] = dot_nn(low_ref[...], made[cell]).T.astype(jnp.bfloat16)


def line_grads(low_turned, cells, pixels, grads, half, halves):
    step_cells = cells // halves
    depth = low_turned.shape[0]
    width = grads[0].shape[2]
    bands = pixels[0].shape[2] // cells
    images = sum(piece.shape[0] for piece in pixels)
    vmem = pl.BlockSpec(memory_space=pltpu.VMEM)

    def body(*refs):
        pixel_refs = refs[1 : 1 + len(pixels)]
        grad_refs = refs[1 + len(pixels) : 1 + len(pixels) + len(grads)]
        line_kernel(half, halves, refs[0], pixel_refs, grad_refs, *refs[-2:])

    return pl.pallas_call(
        body,
        in_specs=[vmem] * (1 + len(pixels) + len(grads)),
        out_specs=vmem,
        out_shape=jax.ShapeDtypeStruct((step_cells, width, depth), jnp.bfloat16),
        scratch_shapes=[pltpu.VMEM((step_cells, images * bands, width), jnp.bfloat16)],
        compiler_params=pltpu.CompilerParams(vmem_limit_bytes=48 * 1024 * 1024),
        cost_estimate=pl.CostEstimate(flops=1, bytes_accessed=1, transcendentals=0),
        name="line_grads",
    )(low_turned, *pixels, *grads)


def band_kernel(first, count, at_ref, grad_ref, *refs):
    weight_refs, pixel_refs = refs[:count], refs[count : count + 2]
    if first:
        total_ref, weight_now, made = refs[count + 2 :]
    else:
        before_ref, total_ref, weight_now, made = refs[count + 2 :]
    share = pixel_refs[0].shape[1]
    images = 2 * share
    cells = weight_now.shape[0]
    bands = pixel_refs[0].shape[3] // cells

    @pl.when(pl.program_id(0) == 0)
    def _():
        if first:
            total_ref[...] = jnp.zeros_like(total_ref)
        else:
            total_ref[...] = before_ref[...]

    for at in range(count):

        @pl.when((pl.program_id(0) == at) | (count == 1))
        def _(at=at):
            weight_now[...] = weight_refs[at][...]

    for image in range(images):
        block = pixel_refs[image // share][0, image % share]
        grads = dot_tn(block, grad_ref[image]).astype(jnp.bfloat16)
        for cell in range(cells):
            made[cell, image * bands : (image + 1) * bands, :] = grads[
                cell * bands : (cell + 1) * bands
            ]
    for cell in range(cells):
        total_ref[...] += dot_nn(made[cell], weight_now[cell])


def band_piece(place, grads, weights, pixels, total):
    pieces, share, rows, lanes = pixels[0].shape
    images = 2 * share
    cells, width, depth = weights[0].shape
    step = lanes // (4 * 16)
    count = len(weights)
    steps = max(count, cells // step)
    bands = lanes // (4 * step)
    first = total is None
    whole_total = pl.BlockSpec((images * bands, depth), lambda t, at: (0, 0))
    if count == 1:
        weight_specs = [pl.BlockSpec((step, width, depth), lambda t, at: (t, 0, 0))]
    else:
        weight_specs = [pl.BlockSpec((step, width, depth), lambda t, at: (0, 0, 0))] * count
    return pl.pallas_call(
        partial(band_kernel, first, count),
        grid_spec=pltpu.PrefetchScalarGridSpec(
            num_scalar_prefetch=1,
            grid=(steps,),
            in_specs=[pl.BlockSpec(grads.shape, lambda t, at: (0, 0, 0))]
            + weight_specs
            + [
                pl.BlockSpec(
                    (1, share, rows, step * bands), lambda t, at: (at[0], 0, 0, at[1 + t])
                ),
            ]
            * 2
            + ([] if first else [whole_total]),
            out_specs=whole_total,
            scratch_shapes=[
                pltpu.VMEM((step, width, depth), jnp.bfloat16),
                pltpu.VMEM((step, images * bands, width), jnp.bfloat16),
            ],
        ),
        out_shape=jax.ShapeDtypeStruct((images * bands, depth), jnp.float32),
        compiler_params=grid_params(40),
        cost_estimate=pl.CostEstimate(flops=1, bytes_accessed=1, transcendentals=0),
        name="band_piece",
    )(place, grads, *weights, *pixels, *(() if first else (total,)))


def head_probs(patches, query, keyed, mine):
    rows = query.shape[0]
    scores = dot_nt(jnp.where(mine, query, jnp.zeros_like(query)), keyed)
    column = lax.broadcasted_iota(jnp.int32, (1, rows), 1)
    scores = jnp.where(column < patches, scores, -1e30)
    powers = jnp.exp(scores - jnp.max(scores, axis=-1, keepdims=True))
    return powers * (1.0 / jnp.sum(powers, axis=-1, keepdims=True))


def attend_kernel(patches, head_size, joint_ref, out_ref):
    width = out_ref.shape[2]
    pair = 2 * head_size
    lane = lax.broadcasted_iota(jnp.int32, (1, pair), 1)
    scale = jnp.asarray(head_size ** (-0.5), jnp.bfloat16)
    for at in range(0, width, pair):
        query = joint_ref[0, :, at : at + pair] * scale
        keyed = joint_ref[0, :, width + at : width + at + pair]
        valued = joint_ref[0, :, 2 * width + at : 2 * width + at + pair]
        mixed = []
        for head in range(2):
            mine = (lane >= head * head_size) & (lane < (head + 1) * head_size)
            probs = head_probs(patches, query, keyed, mine)
            mixed.append(dot_nn(probs.astype(jnp.bfloat16), valued))
        out_ref[0, :, at : at + pair] = jnp.where(lane < head_size, mixed[0], mixed[1]).astype(
            jnp.bfloat16
        )


def attend(joint, patches, head_size):
    images, rows, triple = joint.shape
    width = triple // 3
    return pl.pallas_call(
        partial(attend_kernel, patches, head_size),
        grid=(images,),
        in_specs=[pl.BlockSpec((1, rows, triple), lambda i: (i, 0, 0))],
        out_specs=pl.BlockSpec((1, rows, width), lambda i: (i, 0, 0)),
        out_shape=jax.ShapeDtypeStruct((images, rows, width), jnp.bfloat16),
        compiler_params=grid_params(24),
        cost_estimate=pl.CostEstimate(flops=1, bytes_accessed=1, transcendentals=0),
        name="attend",
    )(joint)


def attend_back_kernel(patches, head_size, joint_ref, grad_ref, out_ref, sum_ref):
    width = grad_ref.shape[2]
    pair = 2 * head_size
    lane = lax.broadcasted_iota(jnp.int32, (1, pair), 1)
    scale = jnp.asarray(head_size ** (-0.5), jnp.bfloat16)

    @pl.when(pl.program_id(0) == 0)
    def _():
        sum_ref[...] = jnp.zeros_like(sum_ref)

    for at in range(0, width, pair):
        query = joint_ref[0, :, at : at + pair] * scale
        keyed = joint_ref[0, :, width + at : width + at + pair]
        valued = joint_ref[0, :, 2 * width + at : 2 * width + at + pair]
        grads = grad_ref[0, :, at : at + pair]
        none = jnp.zeros_like(grads)
        parts = []
        for head in range(2):
            mine = (lane >= head * head_size) & (lane < (head + 1) * head_size)
            probs = head_probs(patches, query, keyed, mine)
            grad = jnp.where(mine, grads, none)
            to_probs = dot_nt(grad, valued)
            inner = jnp.sum(probs * to_probs, axis=-1, keepdims=True)
            to_scores = (probs * (to_probs - inner)).astype(jnp.bfloat16)
            parts.append(
                (
                    dot_nn(to_scores, jnp.where(mine, keyed, none)),
                    dot_tn(to_scores, jnp.where(mine, query, none)),
                    dot_tn(probs.astype(jnp.bfloat16), grad),
                )
            )
        to_query = (parts[0][0] + parts[1][0]) * (head_size ** (-0.5))
        to_keyed = parts[0][1] + parts[1][1]
        to_valued = parts[0][2] + parts[1][2]
        for slot, value in enumerate((to_query, to_keyed, to_valued)):
            value = value.astype(jnp.bfloat16)
            out_ref[0, :, slot * width + at : slot * width + at + pair] = value
            sum_ref[:, slot * width + at : slot * width + at + pair] += jnp.sum(
                value.astype(jnp.float32), axis=0, keepdims=True
            )


def attend_back(joint, grads, patches, head_size):
    images, rows, triple = joint.shape
    width = triple // 3
    return pl.pallas_call(
        partial(attend_back_kernel, patches, head_size),
        grid=(images,),
        in_specs=[
            pl.BlockSpec((1, rows, triple), lambda i: (i, 0, 0)),
            pl.BlockSpec((1, rows, width), lambda i: (i, 0, 0)),
        ],
        out_specs=[
            pl.BlockSpec((1, rows, triple), lambda i: (i, 0, 0)),
            pl.BlockSpec((1, triple), lambda i: (0, 0)),
        ],
        out_shape=[
            jax.ShapeDtypeStruct((images, rows, triple), jnp.bfloat16),
            jax.ShapeDtypeStruct((1, triple), jnp.float32),
        ],
        compiler_params=grid_params(24),
        cost_estimate=pl.CostEstimate(flops=1, bytes_accessed=1, transcendentals=0),
        name="attend_back",
    )(joint, grads)


def norm_inside(values, epsilon):
    center = values - jnp.mean(values, axis=-1, keepdims=True)
    factor = lax.rsqrt(jnp.mean(center * center, axis=-1, keepdims=True) + epsilon)
    return center * factor, factor


def small_call(kernel, name, grid, in_specs, out_specs, out_shape, scratch=(), limit=40):
    return pl.pallas_call(
        kernel,
        grid=grid,
        in_specs=in_specs,
        out_specs=out_specs,
        out_shape=out_shape,
        scratch_shapes=list(scratch),
        compiler_params=grid_params(limit),
        cost_estimate=pl.CostEstimate(flops=1, bytes_accessed=1, transcendentals=0),
        name=name,
    )


def whole_spec(shape):
    return pl.BlockSpec(shape, lambda i: (0,) * len(shape))


def image_spec(rows, width):
    return pl.BlockSpec((1, rows, width), lambda i: (i, 0, 0))


def joint_kernel(
    own_ref, beside_ref, bias_ref, gain_ref, shift_ref, weight_ref, joint_bias_ref,
    embedded_ref, normed_ref, joint_ref,
):
    embedded = own_ref[0] + beside_ref[0] + bias_ref[0]
    embedded_ref[0] = embedded
    normed = norm_inside(embedded, block_eps)[0] * gain_ref[...] + shift_ref[...]
    normed = normed.astype(jnp.bfloat16)
    normed_ref[0] = normed
    joint = dot_nn(normed, weight_ref[...]) + joint_bias_ref[...]
    joint_ref[0] = joint.astype(jnp.bfloat16)


def make_joint(total, beside, image_bias, gain, shift, weight, joint_bias):
    images, rows, width = beside.shape
    triple = weight.shape[1]
    return small_call(
        joint_kernel,
        "make_joint",
        (images,),
        [image_spec(rows, width)] * 2
        + [image_spec(1, width), whole_spec((1, width)), whole_spec((1, width))]
        + [whole_spec(weight.shape), whole_spec((1, triple))],
        [image_spec(rows, width), image_spec(rows, width), image_spec(rows, triple)],
        [
            jax.ShapeDtypeStruct((images, rows, width), jnp.float32),
            jax.ShapeDtypeStruct((images, rows, width), jnp.bfloat16),
            jax.ShapeDtypeStruct((images, rows, triple), jnp.bfloat16),
        ],
    )(total, beside, image_bias[:, None], gain[None], shift[None], weight, joint_bias[None])


def residual_kernel(
    attended_ref, embedded_ref, weight_ref, bias_ref, gain_ref, shift_ref, residual_ref, normed_ref
):
    branch = dot_nn(attended_ref[0], weight_ref[...]) + bias_ref[...]
    residual = embedded_ref[0] + branch
    residual_ref[0] = residual
    normed = norm_inside(residual, block_eps)[0] * gain_ref[...] + shift_ref[...]
    normed_ref[0] = normed.astype(jnp.bfloat16)


def make_residual(attended, embedded, weight, bias, gain, shift):
    images, rows, width = embedded.shape
    return small_call(
        residual_kernel,
        "make_residual",
        (images,),
        [image_spec(rows, width)] * 2 + [whole_spec(weight.shape)] + [whole_spec((1, width))] * 3,
        [image_spec(rows, width)] * 2,
        [
            jax.ShapeDtypeStruct((images, rows, width), jnp.float32),
            jax.ShapeDtypeStruct((images, rows, width), jnp.bfloat16),
        ],
    )(attended, embedded, weight, bias[None], gain[None], shift[None])


def norm_back_inside(grad, values, gain, epsilon):
    normal, factor = norm_inside(values, epsilon)
    scaled = grad * gain
    back = factor * (
        scaled
        - jnp.mean(scaled, axis=-1, keepdims=True)
        - normal * jnp.mean(scaled * normal, axis=-1, keepdims=True)
    )
    return back, jnp.sum(grad * normal, axis=0, keepdims=True)


def add_rows(out_ref, rows):
    @pl.when(pl.program_id(0) == 0)
    def _():
        out_ref[...] = jnp.zeros_like(out_ref)

    out_ref[...] += jnp.concatenate(rows, axis=0)


def branch_back_kernel(
    grad_ref, residual_ref, out_grad_ref, gain_ref, weight_ref,
    resid_ref, branch_ref, att_ref, sum_ref,
):
    grad = grad_ref[0]
    out_grad = out_grad_ref[0].astype(jnp.float32)
    back, gain_grad = norm_back_inside(grad, residual_ref[0], gain_ref[...], block_eps)
    resid = out_grad + back
    resid_ref[0] = resid
    branch = resid.astype(jnp.bfloat16)
    branch_ref[0] = branch
    att_ref[0] = dot_nt(branch, weight_ref[...]).astype(jnp.bfloat16)
    add_rows(
        sum_ref,
        [
            gain_grad,
            jnp.sum(grad, axis=0, keepdims=True),
            jnp.sum(branch.astype(jnp.float32), axis=0, keepdims=True),
            jnp.sum(out_grad, axis=0, keepdims=True),
        ],
    )


def branch_back(grad, residual, out_grad, gain, weight):
    images, rows, width = residual.shape
    return small_call(
        branch_back_kernel,
        "branch_back",
        (images,),
        [image_spec(rows, width)] * 3 + [whole_spec((1, width)), whole_spec(weight.shape)],
        [image_spec(rows, width)] * 3 + [whole_spec((4, width))],
        [
            jax.ShapeDtypeStruct((images, rows, width), jnp.float32),
            jax.ShapeDtypeStruct((images, rows, width), jnp.bfloat16),
            jax.ShapeDtypeStruct((images, rows, width), jnp.bfloat16),
            jax.ShapeDtypeStruct((4, width), jnp.float32),
        ],
    )(grad, residual, out_grad, gain[None], weight)


def embed_back_kernel(
    joint_ref, weight_ref, embedded_ref, resid_ref, gain_ref, emb_ref, sum_ref, image_ref
):
    grad = dot_nt(joint_ref[0], weight_ref[...])
    back, gain_grad = norm_back_inside(grad, embedded_ref[0], gain_ref[...], block_eps)
    emb = (resid_ref[0] + back).astype(jnp.bfloat16)
    emb_ref[0] = emb
    image_ref[0] = jnp.sum(emb.astype(jnp.float32), axis=0, keepdims=True)
    add_rows(sum_ref, [gain_grad, jnp.sum(grad, axis=0, keepdims=True)])


def embed_back(joint_grad, weight, embedded, resid, gain):
    images, rows, width = embedded.shape
    return small_call(
        embed_back_kernel,
        "embed_back",
        (images,),
        [image_spec(rows, joint_grad.shape[2]), whole_spec(weight.shape)]
        + [image_spec(rows, width)] * 2
        + [whole_spec((1, width))],
        [image_spec(rows, width), whole_spec((2, width)), image_spec(1, width)],
        [
            jax.ShapeDtypeStruct((images, rows, width), jnp.bfloat16),
            jax.ShapeDtypeStruct((2, width), jnp.float32),
            jax.ShapeDtypeStruct((images, 1, width), jnp.float32),
        ],
    )(joint_grad, weight, embedded, resid, gain[None])


def split_rows(core, value, count, keep_ref, send_ref):
    size = value.shape[0] // (2 * count)
    for at in range(count):
        first = value[2 * at * size : (2 * at + 1) * size]
        second = value[(2 * at + 1) * size : (2 * at + 2) * size]
        keep = jnp.where(core == 0, first, second).astype(jnp.bfloat16)
        send = jnp.where(core == 0, second, first).astype(jnp.bfloat16)
        keep_ref[at * size : (at + 1) * size] = keep
        send_ref[at * size : (at + 1) * size] = send


def rows_kernel(count, core_ref, left_ref, right_ref, keep_ref, send_ref, turned):
    @pl.when(pl.program_id(0) == 0)
    def _():
        turned[...] = left_ref[...].T

    split_rows(core_ref[0], dot_nn(turned[...], right_ref[...]), count, keep_ref, send_ref)


def rows_grad(core, left, right, count=4):
    rows, width = left.shape
    columns = right.shape[1]
    part = min(columns, 768)
    half = jax.ShapeDtypeStruct((width // 2, columns), jnp.bfloat16)
    return pl.pallas_call(
        partial(rows_kernel, count),
        grid_spec=pltpu.PrefetchScalarGridSpec(
            num_scalar_prefetch=1,
            grid=(columns // part,),
            in_specs=[
                pl.BlockSpec((rows, width), lambda s, core: (0, 0)),
                pl.BlockSpec((rows, part), lambda s, core: (0, s)),
            ],
            out_specs=[pl.BlockSpec((width // 2, part), lambda s, core: (0, s))] * 2,
            scratch_shapes=[pltpu.VMEM((width, rows), jnp.bfloat16)],
        ),
        out_shape=[half, half],
        compiler_params=grid_params(32),
        cost_estimate=pl.CostEstimate(flops=1, bytes_accessed=1, transcendentals=0),
        name="rows_grad",
    )(core.reshape(1), left, right)


def mlp_kernel(
    core_ref, normed_ref, residual_ref, grad_ref, up_ref, bias_ref, down_ref, down_bias_ref,
    out_ref, back_ref, up_keep_ref, up_send_ref, down_keep_ref, down_send_ref, bias_grad_ref,
    active, to_pre, turned, total,
):
    rows = normed_ref.shape[0]
    part = rows // MLP_PARTS

    @pl.when(pl.program_id(0) == 0)
    def _():
        total[...] = residual_ref[...] + down_bias_ref[...]
        back_ref[...] = jnp.zeros_like(back_ref)
        turned[...] = normed_ref[...].T

    up = up_ref[...]
    down = down_ref[...]
    bias_grad = jnp.zeros(bias_grad_ref.shape, jnp.float32)
    for at in range(0, rows, part):
        span = slice(at, at + part)
        pre = dot_nn(normed_ref[span], up) + bias_ref[...]
        share = 0.5 + 0.5 * lax.erf(pre * (0.5**0.5))
        slope = share + pre * (jnp.exp(-0.5 * pre * pre) * (0.5 / jnp.pi) ** 0.5)
        act = (pre * share).astype(jnp.bfloat16)
        grad = (slope * dot_nt(grad_ref[span], down)).astype(jnp.bfloat16)
        active[span] = act
        to_pre[span] = grad
        total[span] += dot_nn(act, down)
        back_ref[span] += dot_nt(grad, up)
        bias_grad += jnp.sum(grad.astype(jnp.float32), axis=0, keepdims=True)
    bias_grad_ref[...] = bias_grad
    core = core_ref[0]
    split_rows(core, dot_nn(turned[...], to_pre[...]), 4, up_keep_ref, up_send_ref)
    split_rows(core, dot_tn(active[...], grad_ref[...]), 1, down_keep_ref, down_send_ref)

    @pl.when(pl.program_id(0) == pl.num_programs(0) - 1)
    def _():
        out_ref[...] = total[...].astype(jnp.bfloat16)


MLP_PARTS = 2


def mlp(core, normed, residual, grads, up, up_bias, down, down_bias):
    rows, width = normed.shape
    hidden = up.shape[1]
    part = hidden // 4
    whole = pl.BlockSpec((rows, width), lambda s, core: (0, 0))
    columns = pl.BlockSpec((width, part), lambda s, core: (0, s))
    lines = pl.BlockSpec((part, width), lambda s, core: (s, 0))
    vector = pl.BlockSpec((1, part), lambda s, core: (0, s))
    up_half = jax.ShapeDtypeStruct((width // 2, hidden), jnp.bfloat16)
    down_half = jax.ShapeDtypeStruct((hidden // 2, width), jnp.bfloat16)
    return pl.pallas_call(
        mlp_kernel,
        grid_spec=pltpu.PrefetchScalarGridSpec(
            num_scalar_prefetch=1,
            grid=(hidden // part,),
            in_specs=[
                whole, whole, whole, columns, vector, lines,
                pl.BlockSpec((1, width), lambda s, core: (0, 0)),
            ],
            out_specs=[whole, whole]
            + [pl.BlockSpec((width // 2, part), lambda s, core: (0, s))] * 2
            + [pl.BlockSpec((part // 2, width), lambda s, core: (s, 0))] * 2
            + [vector],
            scratch_shapes=[
                pltpu.VMEM((rows, part), jnp.bfloat16),
                pltpu.VMEM((rows, part), jnp.bfloat16),
                pltpu.VMEM((width, rows), jnp.bfloat16),
                pltpu.VMEM((rows, width), jnp.float32),
            ],
        ),
        out_shape=[
            jax.ShapeDtypeStruct((rows, width), jnp.bfloat16),
            jax.ShapeDtypeStruct((rows, width), jnp.float32),
            up_half,
            up_half,
            down_half,
            down_half,
            jax.ShapeDtypeStruct((1, hidden), jnp.float32),
        ],
        compiler_params=grid_params(52),
        cost_estimate=pl.CostEstimate(flops=1, bytes_accessed=1, transcendentals=0),
        name="mlp",
    )(core.reshape(1), normed, residual, grads, up, up_bias[None], down, down_bias[None])


def per_device(
    pixels,
    band_count,
    band_bin,
    bin_wave,
    run_mean,
    run_var,
    weight_tokens,
    bias_token,
    hyper_in,
    hyper_qv_bias,
    hyper_out,
    hyper_out_bias,
    hyper_gain,
    hyper_shift,
    hyper_up,
    hyper_up_bias,
    hyper_down,
    hyper_down_bias,
    kernel_weight,
    bias_weight,
    bias_offset,
    norm_gain,
    norm_shift,
    w_qkv,
    qv_bias,
    w_out,
    out_bias,
    w_up,
    up_bias,
    w_down,
    down_bias,
    cotangent,
):
    pixel_data = pixels[0]
    images, band_slots, patches, pixel_cells = pixel_data.shape
    bin_total = bin_wave.shape[0]
    model_width = w_qkv.shape[0]
    head_size = model_width // HEADS
    padded = -(-patches // 16) * 16
    rows = images * padded
    cells = kernel_weight.shape[0]
    core = lax.axis_index("batch") & 1
    live_band = (
        lax.broadcasted_iota(jnp.int32, (images, band_slots), 1) < band_count[0][:, None]
    ).astype(jnp.float32)
    bin_onehot = (
        band_bin[0][..., None]
        == lax.broadcasted_iota(jnp.int32, (images, band_slots, bin_total), 2)
    ).astype(jnp.float32)
    chosen = bin_onehot * live_band[..., None]
    run_rstd = lax.rsqrt(run_var + stat_eps)
    band_mean = jnp.einsum("ibn,n->ib", chosen, run_mean, precision=highest)
    band_rstd = jnp.einsum("ibn,n->ib", chosen, run_rstd, precision=highest)
    values32 = pixel_data.astype(jnp.float32)
    band_total = jnp.sum(values32, axis=(2, 3))
    band_square = jnp.sum(values32 * values32, axis=(2, 3))
    bin_sums = jnp.einsum("ib,ibn->n", band_total, chosen, precision=highest)
    bin_squares = jnp.einsum("ib,ibn->n", band_square, chosen, precision=highest)
    bin_counts = jnp.sum(chosen, axis=(0, 1))

    grad_out = jnp.pad(cotangent[0], ((0, 0), (0, padded - patches), (0, 0)))
    band_wave = jnp.einsum("ibn,n->ib", bin_onehot, bin_wave, precision=highest)
    wave_emb = wave_embed(band_wave, hyper_in.shape[0])
    hyper_params = (
        weight_tokens,
        bias_token,
        hyper_in,
        hyper_qv_bias,
        hyper_out,
        hyper_out_bias,
        hyper_gain,
        hyper_shift,
        hyper_up,
        hyper_up_bias,
        hyper_down,
        hyper_down_bias,
    )

    def make_low():
        (band_vec, bias_vec), hyper_back = jax.vjp(
            partial(hypernet, wave_emb=wave_emb, live_band=live_band), hyper_params
        )
        band_low = band_vec.astype(jnp.bfloat16).reshape(images * band_slots, -1)
        return band_low, bias_vec, hyper_back

    def place(piece, *quarters):
        return jnp.stack([jnp.asarray(at, jnp.int32) for at in (piece,) + quarters])

    if not tuned_mesh():
        band_low, bias_vec, hyper_back = make_low()
        chip_low = jnp.concatenate([band_low, swap_batch(band_low, 1)])
        mine, other = split_pixels(pixel_data, band_mean, band_rstd, core, padded, cells)
        chip_pixels = (mine, swap_batch(other, 1))
        total, kernels = (None, None)
        for at, weight in enumerate(plain_weight_pieces(kernel_weight)):
            total, kernels = embed_piece(
                place(at, 0, 1, 2, 3), chip_low, [weight], chip_pixels, total, kernels
            )
        line_pixels = plain_line_cells(jnp.concatenate(chip_pixels, axis=1))
        line_low = lax.all_gather(
            chip_low, "batch", axis=0, axis_index_groups=same_core(), tiled=True
        )
    else:
        group = lax.axis_index("group")
        chip = lax.axis_index("batch") >> 1
        part = cells // 8
        quarter = part_of(kernel_weight, group, 4)

        def sides(block):
            return swap_group(block, 1), swap_group(block, 2)

        def corners(beside, above):
            return swap_group(beside[:part], 2), swap_group(above[part : 2 * part], 1)

        def sides_and_corner(block, beside, above):
            return (
                swap_group(jnp.concatenate([block, above[part : 2 * part]]), 1),
                swap_group(jnp.concatenate([block, beside[:part]]), 2),
            )

        def added(state, piece, weights, shifts):
            spots = place(piece, *[group ^ shift for shift in shifts])
            return embed_piece(spots, chip_low, weights, chip_pixels, *state)

        def pixel_block(hop, half):
            piece = lax.dynamic_index_in_dim(chip_pixels[half], chip ^ hop, 0, keepdims=False)
            return swap_batch(piece, 2 * hop) if hop else piece

        right1, left1 = (along_line(quarter, -1), along_line(quarter, 1))
        band_low, bias_vec, hyper_back = make_low()
        band_low, bias_vec, right1, left1, pixel_data = tie(
            band_low, bias_vec, right1, left1, pixel_data
        )
        block1 = jnp.where(chip == 3, left1, right1)
        right2, left2 = (along_line(right1, -1, (1, 2)), along_line(left1, 1, (1, 2)))
        beside1, above1 = sides(block1)
        mine, other = split_pixels(pixel_data, band_mean, band_rstd, core, padded, cells)
        chip_low = jnp.concatenate([band_low, swap_batch(band_low, 1)])
        mine, other, chip_low, right2, left2, beside1, above1 = tie(
            mine, other, chip_low, right2, left2, beside1, above1
        )
        block2 = jnp.where(chip == 0, right2, jnp.where(chip == 3, left2, left1))
        end3 = lax.ppermute(
            jnp.where(chip == 1, right2, left2),
            "batch",
            [(2 + at, at) for at in range(2)] + [(4 + at, 6 + at) for at in range(2)],
        )
        across2, up2 = sides_and_corner(block2, beside1, above1)
        chip_pixels = (mine, swap_batch(other, 1))
        pixels2 = [pixel_block(2, 0)]
        state = embed_piece(
            place(chip, 0, 1, 2, 3), chip_low, [kernel_weight], chip_pixels, None, None
        )
        weights1 = [block1, beside1, above1]
        spots1 = of_chip(chip, [1, 2, 3, 2])
        state = added(state, spots1, weights1, (0, 1, 2))
        state, chip_pixels, end3, across2, up2, pixels2, bin_sums, bin_squares = tie(
            state, chip_pixels, end3, across2, up2, pixels2, bin_sums, bin_squares
        )
        block3 = jnp.where(chip == 1, right2, jnp.where(chip == 2, left2, end3))
        across3, up3 = sides_and_corner(block3, across2, up2)
        pixels2.append(pixel_block(2, 1))
        pixels1 = [pixel_block(1, 0)]
        weights1.append(jnp.concatenate([up2[2 * part :], across2[2 * part :]]))
        state = added(state, spots1, weights1[3:], (3,))
        weights2 = [block2, across2, up2]
        spots2 = of_chip(chip, [2, 0, 1, 1])
        state = added(state, spots2, weights2, (0, 1, 2))
        state, across3, up3, pixels1, pixels2, chip_pixels, grad_out = tie(
            state, across3, up3, pixels1, pixels2, chip_pixels, grad_out
        )
        corner3 = corners(across3, up3)
        pixels1.append(pixel_block(1, 1))
        weights2.append(jnp.concatenate([up3[2 * part :], across3[2 * part :]]))
        state = added(state, spots2, weights2[3:], (3,))
        weights3 = [block3, across3, up3]
        spots3 = of_chip(chip, [3, 3, 0, 0])
        state = added(state, spots3, weights3, (0, 1, 2))
        state, corner3, pixels1, chip_pixels = tie(state, corner3, pixels1, chip_pixels)
        pixels3 = [pixel_block(3, 0)]
        weights3.append(jnp.concatenate(corner3))
        total, kernels = added(state, spots3, weights3[3:], (3,))
    image_bias = jnp.dot(bias_vec, bias_weight, precision=highest) + bias_offset
    total_beside = swap_batch(total[images:], 1)
    joint_bias = jnp.concatenate([qv_bias[0], jnp.zeros_like(qv_bias[0]), qv_bias[1]])
    embedded, normed1, joint = make_joint(
        total, total_beside, image_bias, norm_gain[0], norm_shift[0], w_qkv, joint_bias
    )
    attended = attend(joint, patches, head_size)
    rates = jnp.tile(band_rstd, (1, pixel_cells // 8))
    if tuned_mesh():
        attended, chip_pixels, chip_low, rates = tie(attended, chip_pixels, chip_low, rates)
        line_low = line_rows(chip_low)
    residual, normed2 = make_residual(
        attended, embedded, w_out, out_bias, norm_gain[1], norm_shift[1]
    )
    block_out, grad_n2, up_keep, up_send, down_keep, down_send, grad_up_bias = mlp(
        core,
        normed2.reshape(rows, model_width),
        residual.reshape(rows, model_width),
        grad_out.reshape(rows, model_width),
        w_up,
        up_bias,
        w_down,
        down_bias,
    )
    if tuned_mesh():
        rates_beside = swap_batch(rates, 1)
        grad_n2, pixels3, chip_pixels, line_low, rates_beside, up_send, down_send = tie(
            grad_n2, pixels3, chip_pixels, line_low, rates_beside, up_send, down_send
        )
        pixels3.append(pixel_block(3, 1))
    else:
        rates_beside = swap_batch(rates, 1)
    rates = jnp.concatenate([rates, rates_beside])[:, None, :]
    up_came, down_came = swap_batch(up_send, 1), swap_batch(down_send, 1)
    block_out = block_out.reshape(1, images, padded, model_width)[:, :, :patches]
    grad_resid, grad_branch, grad_att, branch_sum = branch_back(
        grad_n2.reshape(images, padded, model_width), residual, grad_out, norm_gain[1], w_out
    )
    grad_gain_two, grad_shift_two, grad_out_bias, grad_down_bias = branch_sum
    grad_joint, joint_sum = attend_back(joint, grad_att, patches, head_size)
    grad_emb, embed_sum, grad_image_bias = embed_back(
        grad_joint, w_qkv, embedded, grad_resid, norm_gain[0]
    )
    if tuned_mesh():
        grad_emb, pixels3, up_keep, up_came, down_keep, down_came = tie(
            grad_emb, pixels3, up_keep, up_came, down_keep, down_came
        )
    grad_gain_one, grad_shift_one = embed_sum
    grad_image_bias = grad_image_bias[:, 0]
    grad_qv_bias = joint_sum.reshape(3, model_width)[::2]
    attended = attended.reshape(rows, model_width)
    grad_branch = grad_branch.reshape(rows, model_width)
    share_up = row_share(add_low(up_keep, up_came))
    share_down = row_share(add_low(down_keep, down_came))

    def late_rows(attended, grad_branch, normed1, grad_joint):
        out_keep, out_send = rows_grad(core, attended, grad_branch)
        qkv_keep, qkv_send = rows_grad(core, normed1, grad_joint)
        return core_sum(out_keep, out_send), core_sum(qkv_keep, qkv_send)

    late = (
        attended,
        grad_branch,
        normed1.reshape(rows, model_width),
        grad_joint.reshape(rows, 3 * model_width),
    )
    beside_emb = swap_batch(grad_emb, 1)
    if tuned_mesh():
        far_emb = [swap_batch(grad_emb, 2), swap_batch(grad_emb, 4)]
    grad_bias_weight = jnp.einsum("ik,ie->ke", bias_vec, grad_image_bias, precision=highest)
    grad_bias_offset = jnp.sum(grad_image_bias, axis=0)
    grad_bias_vec = jnp.einsum("ie,ke->ik", grad_image_bias, bias_weight, precision=highest)

    def pack(hyper_grads):
        wide = (
            hyper_grads[0],
            hyper_grads[2],
            hyper_grads[4],
            hyper_grads[8],
            hyper_grads[10],
            grad_bias_weight,
        )
        narrow = (
            hyper_grads[1],
            hyper_grads[3],
            hyper_grads[5],
            hyper_grads[6],
            hyper_grads[7],
            hyper_grads[9],
            hyper_grads[11],
            bin_sums,
            bin_squares,
            bin_counts,
            grad_bias_offset,
            jnp.stack([grad_gain_one, grad_gain_two]),
            jnp.stack([grad_shift_one, grad_shift_two]),
            grad_qv_bias,
            grad_out_bias,
            grad_up_bias[0],
            grad_down_bias,
        )
        parts = [block_rows(part) for part in wide]
        thin = [part.reshape(-1, 128) for part in narrow]
        length = sum(part.shape[0] for part in thin)
        thin = jnp.concatenate(thin + [jnp.zeros((-length % 128, 128), jnp.float32)])
        (thin,) = tie(thin)
        parts.append(thin)
        length = sum(part.shape[0] for part in parts)
        parts.append(jnp.zeros((-length % 256, 128), jnp.float32))
        small = jnp.concatenate(parts)
        return wide, narrow, parts, small

    chip_emb = jnp.concatenate([grad_emb, beside_emb])

    def finish_low(grad_vectors):
        far = swap_batch(grad_vectors[images * band_slots :], 1)
        grad_vectors = grad_vectors[: images * band_slots] + far
        grad_vectors = grad_vectors.reshape(images, band_slots, -1)
        return hyper_back((grad_vectors, grad_bias_vec))[0]

    grad_vectors = None
    if tuned_mesh():
        plan = [
            (place(chip, 0, 1, 2, 3), [kernel_weight]),
            (place(spots1, group, group ^ 1, group ^ 2, group ^ 3), weights1),
            (place(spots2, group, group ^ 1, group ^ 2, group ^ 3), weights2),
            (place(spots3, group, group ^ 1, group ^ 2, group ^ 3), weights3),
        ]
        for spots, weights in plan:
            grad_vectors = band_piece(spots, chip_emb, weights, chip_pixels, grad_vectors)
        half_out, half_qkv = late_rows(*late)
        grad_vectors, far_emb, half_out, half_qkv, grad_emb, share_up = tie(
            grad_vectors, far_emb, half_out, half_qkv, grad_emb, share_up
        )
        far_emb.append(swap_batch(grad_emb, 6))
        share_out_rows, share_qkv = row_share(half_out), row_share(half_qkv)
        line_emb = [grad_emb, beside_emb]
        for far in far_emb[:2]:
            line_emb += [far, swap_batch(far, 1)]
        hyper_grads = finish_low(grad_vectors)
        wide, narrow, parts, small = pack(hyper_grads)
        (
            small, block_out, far_emb, line_emb, share_up, share_down, share_out_rows, share_qkv,
            chip_emb,
        ) = tie(
            small, block_out, far_emb, line_emb, share_up, share_down, share_out_rows, share_qkv,
            chip_emb,
        )
        small_came = swap_batch(part_of(small, 1 - core, 2), 1)
        line_emb += [far_emb[2], swap_batch(far_emb[2], 1)]
        small, small_came, line_emb = tie(small, small_came, line_emb)
        line_pixels = [pixel_block(0, 0), pixel_block(0, 1)] + pixels1 + pixels2 + pixels3
    else:
        for at, weight in enumerate(plain_weight_pieces(kernel_weight)):
            grad_vectors = band_piece(
                place(at, 0, 1, 2, 3), chip_emb, [weight], chip_pixels, grad_vectors
            )
        half_out, half_qkv = late_rows(*late)
        hyper_grads = finish_low(grad_vectors)
        wide, narrow, parts, small = pack(hyper_grads)
        share_out_rows, share_qkv = row_share(half_out), row_share(half_qkv)
        line_emb = plain_line_images(grad_emb, beside_emb)
    halves = 2 if cells % 32 == 0 else 1
    low_turned = line_low.T

    if not tuned_mesh():
        kernel_share = 0.0
        for at in range(0, line_pixels[0].shape[0], 32):
            columns = low_turned[:, at * band_slots : (at + 32) * band_slots]
            found = line_grads(
                columns, cells, [line_pixels[0][at : at + 32]], [line_emb[0][at : at + 32]], 0, 1
            )
            kernel_share += found.astype(jnp.float32)
        kernel_total = lax.psum(kernel_share.astype(jnp.bfloat16), "group").astype(jnp.float32)
        chip_back = pixel_grads(chip_emb, kernels, rates)
        other_back = swap_batch(chip_back[:, images:], 1)
        pixel_grad = join_pixels(
            chip_back[:, :images], other_back, core, patches, cells, pixel_cells, band_slots
        )
        small = lax.psum(small, ("group", "batch"))
        totals = [
            row_both(row_mine(share)) for share in (share_qkv, share_out_rows, share_up, share_down)
        ]
    else:
        small = part_of(small, core, 2) + small_came
        small_came = [swap_batch(part_of(small, chip ^ hop, 4), 2 * hop) for hop in (1, 2, 3)]
        kernel_one = line_grads(low_turned, cells, line_pixels, line_emb, 0, 2)
        kernel_one, line_emb, small_came = tie(kernel_one, line_emb, small_came)

        kernel_two = line_grads(low_turned, cells, line_pixels, line_emb, 1, 2)
        sums = [kernel_one, kernel_two]
        came = sum_out(sums, False)
        small = sum(small_came, part_of(small, chip, 4))
        small = small + swap_group(small, 1)
        (small,) = tie(small)
        small_came = swap_group(small, 2)
        chip_back = pixel_grads(chip_emb, kernels, rates)
        totals = [row_mine(share) for share in (share_qkv, share_out_rows, share_up, share_down)]
        chip_back, came, small, small_came = tie(chip_back, came, small, small_came)

        sums = sum_in(sums, came, False)
        came = sum_out(sums, True)
        small = small + small_came
        small_came = [swap_batch(small, 2 * hop) for hop in (1, 2, 3)]
        own_back, other_back = chip_back[:, :images], chip_back[:, images:]
        came, own_back, other_back, totals = tie(came, own_back, other_back, totals)

        sums = sum_in(sums, came, True)
        came = share_out(sums, True)
        other_back = swap_batch(other_back, 1)
        came, small_came, other_back = tie(came, small_came, other_back)

        sums = share_in(sums, came, True)
        came = share_out(sums, False)
        small = four_in_order(chip, [small] + small_came)
        small = in_order(core, small, swap_batch(small, 1))
        pixel_grad = join_pixels(
            own_back, other_back, core, patches, cells, pixel_cells, band_slots
        )
        (totals,) = tie(totals)
        widths = [mine.shape[1] for mine in totals[:3]]
        wide_mine = jnp.concatenate(totals[:3], axis=1)
        wide_both = row_both(wide_mine)
        ends = [0, widths[0], widths[0] + widths[1], sum(widths)]
        totals = [wide_both[:, ends[at] : ends[at + 1]] for at in range(3)] + [row_both(totals[3])]
    pixel_grad = pixel_grad[None]

    found = []
    at = 0
    for part, like in zip(parts, wide):
        found.append(unblock_rows(small[at : at + part.shape[0]], like.shape[0]))
        at += part.shape[0]
    for like in narrow:
        count = like.size // 128
        found.append(small[at : at + count].reshape(like.shape))
        at += count
    batch_mean, batch_var = bin_stats(found[13], found[14], found[15], patches * pixel_cells)
    if tuned_mesh():
        came, pixel_grad, found, totals, batch_mean, batch_var = tie(
            came, pixel_grad, found, totals, batch_mean, batch_var
        )
        kernel_total = jnp.concatenate(share_in(sums, came, False)).astype(jnp.float32)
    return (
        block_out,
        pixel_grad,
        batch_mean,
        batch_var,
        found[0],
        found[6],
        found[1],
        found[7],
        found[2],
        found[8],
        found[9],
        found[10],
        found[3],
        found[11],
        found[4],
        found[12],
        kernel_total,
        found[5],
        found[16],
        found[17],
        found[18],
        totals[0],
        found[19],
        totals[1],
        found[20],
        totals[2],
        found[21],
        totals[3],
        found[22],
    )


def solution(mesh):
    return jax.shard_map(
        per_device,
        mesh=mesh,
        in_specs=(
            P("group", "batch", None, None, None),
            P("group", "batch"),
            P("group", "batch", None),
            P(),
            P(),
            P(),
            P(),
            P(),
            P(),
            P(),
            P(),
            P(),
            P(),
            P(),
            P(),
            P(),
            P(),
            P(),
            P("batch", None, None),
            P(),
            P(),
            P(),
            P(),
            P(),
            P(),
            P(),
            P(),
            P(),
            P(),
            P(),
            P(),
            P("group", "batch", None, None),
        ),
        out_specs=(
            P("group", "batch", None, None),
            P("group", "batch", None, None, None),
            P(),
            P(),
            P(),
            P(),
            P(),
            P(),
            P(),
            P(),
            P(),
            P(),
            P(),
            P(),
            P(),
            P(),
            P("batch", None, None),
            P(),
            P(),
            P(),
            P(),
            P("group", None),
            P(),
            P("group", None),
            P(),
            P("group", None),
            P(),
            P("group", None),
            P(),
        ),
        check_vma=False,
    )
```

```python
from functools import partial

import jax
import jax.numpy as jnp
from jax import lax
from jax.experimental import pallas as pl
from jax.experimental.pallas import tpu as pltpu
from jax.sharding import PartitionSpec as P

HEADS = 12
HHEADS = 4


highest = lax.Precision.HIGHEST
high = lax.Precision.HIGH
stat_eps = 1e-05
hyper_eps = 1e-05
block_eps = 1e-06
wave_scale = 1000.0


def layer_norm(values, gain, shift, epsilon):
    center = values - jnp.mean(values, axis=-1, keepdims=True)
    return (
        center * lax.rsqrt(jnp.mean(center * center, axis=-1, keepdims=True) + epsilon) * gain
        + shift
    )


def norm_parts(values, epsilon):
    center = values - jnp.mean(values, axis=-1, keepdims=True)
    factor = lax.rsqrt(jnp.mean(center * center, axis=-1, keepdims=True) + epsilon)
    return (center * factor, factor)


def norm_back(grad_hat, normal_hat, factor):
    return factor * (
        grad_hat
        - jnp.mean(grad_hat, axis=-1, keepdims=True)
        - normal_hat * jnp.mean(grad_hat * normal_hat, axis=-1, keepdims=True)
    )


def wave_embed(band_wave, model_width):
    half_width = model_width // 2
    ladder = jnp.arange(half_width, dtype=jnp.float32) / half_width
    frequency = 1.0 / 10000.0**ladder
    phase_arg = band_wave[..., None] * wave_scale * frequency
    return jnp.concatenate([jnp.sin(phase_arg), jnp.cos(phase_arg)], axis=-1)


def bin_stats(total_sums, squares, counts, cell_count):
    scaled = jnp.maximum(counts * cell_count, 1.0)
    bin_mean = total_sums / scaled
    bin_var = squares / scaled - bin_mean * bin_mean
    return (bin_mean, bin_var)


def hypernet(params, wave_emb, live_band):
    (
        tokens_w,
        token_b,
        w_in,
        in_bias,
        w_proj,
        proj_bias,
        gain_pair,
        shifts,
        w_expand,
        expand_bias,
        w_reduce,
        reduce_bias,
    ) = params
    image_count = wave_emb.shape[0]
    band_slots = wave_emb.shape[1]
    model_width = wave_emb.shape[2]
    head_count = HHEADS
    head_size = model_width // head_count
    token_rows = tokens_w.shape[0]
    sequence = jnp.concatenate(
        [
            jnp.broadcast_to(tokens_w[None], (image_count, token_rows, model_width)),
            wave_emb,
            jnp.broadcast_to(token_b[None, None, :], (image_count, 1, model_width)),
        ],
        axis=1,
    )
    key_live = (
        jnp.concatenate(
            [
                jnp.ones((image_count, token_rows), jnp.float32),
                live_band,
                jnp.ones((image_count, 1), jnp.float32),
            ],
            axis=1,
        )
        > 0.5
    )
    projected = jnp.einsum("nsk,kj->nsj", sequence, w_in[:, model_width:], precision=high)
    asking = sequence[:, token_rows:]
    query_heads = (
        jnp.einsum("nsk,kj->nsj", asking, w_in[:, :model_width], precision=high) + in_bias[0]
    ).reshape(image_count, -1, head_count, head_size)
    keyed = projected[..., :model_width].reshape(
        image_count, -1, head_count, head_size
    )
    valued = (projected[..., model_width:] + in_bias[1]).reshape(
        image_count, -1, head_count, head_size
    )
    scores = jnp.einsum("nqhd,nkhd->nhqk", query_heads, keyed, precision=high) * head_size ** (
        -0.5
    )
    scores = jnp.where(key_live[:, None, None, :], scores, -1e30)
    attn_probs = jax.nn.softmax(scores, axis=-1)
    mixed_heads = jnp.einsum("nhqk,nkhd->nqhd", attn_probs, valued, precision=high).reshape(
        image_count, -1, model_width
    )
    first_out = layer_norm(
        asking + jnp.einsum("nsk,kj->nsj", mixed_heads, w_proj, precision=high) + proj_bias,
        gain_pair[0],
        shifts[0],
        hyper_eps,
    )
    inner_act = jax.nn.gelu(
        jnp.einsum("nsk,kf->nsf", first_out, w_expand, precision=high) + expand_bias,
        approximate=False,
    )
    second_out = layer_norm(
        first_out + jnp.einsum("nsf,fk->nsk", inner_act, w_reduce, precision=high) + reduce_bias,
        gain_pair[1],
        shifts[1],
        hyper_eps,
    )
    return (
        second_out[:, :band_slots] + wave_emb,
        second_out[:, band_slots],
    )


def swap_group(value, bits):
    return lax.ppermute(value, "group", [(at, at ^ bits) for at in range(4)])


def swap_batch(value, bits):
    count = lax.axis_size("batch")
    return lax.ppermute(value, "batch", [(at, at ^ bits) for at in range(count)])


def tuned_mesh():
    return lax.axis_size("group") == 4 and lax.axis_size("batch") == 8


def same_core():
    count = lax.axis_size("batch")
    return [list(range(0, count, 2)), list(range(1, count, 2))]


def in_order(bit, first, second):
    return jnp.where(
        bit == 0, jnp.concatenate([first, second]), jnp.concatenate([second, first])
    )


def four_in_order(index, pieces):
    low, high = (index & 1, index >> 1)
    return in_order(
        high, in_order(low, pieces[0], pieces[1]), in_order(low, pieces[2], pieces[3])
    )


def part_of(value, index, parts):
    rows = value.shape[0] // parts
    return lax.dynamic_slice_in_dim(value, index * rows, rows)


def tie(*values):
    return lax.optimization_barrier(values)


def along_line(value, step, chips=(0, 1, 2, 3)):
    pairs = [
        (2 * at + core, 2 * (at + step) + core)
        for at in chips
        for core in (0, 1)
        if 0 <= at + step < 4
    ]
    return lax.ppermute(value, "batch", pairs)


def line_ends(value):
    pairs = [(2 + at, at) for at in range(2)] + [(4 + at, 6 + at) for at in range(2)]
    return lax.ppermute(value, "batch", pairs)


def of_chip(chip, values):
    return jnp.array(values, jnp.int32)[chip]


def plain_weight_pieces(weight):
    core = lax.axis_index("batch") & 1
    shards = lax.all_gather(weight, "batch", axis=0)
    shards = shards.reshape((-1, 2) + weight.shape)
    mine = lax.dynamic_index_in_dim(shards, core, 1, keepdims=False)
    return mine.reshape((4, -1) + weight.shape[1:])


def plain_line_cells(pixels):
    pieces, images, rows, lanes = pixels.shape
    chips = lax.axis_size("batch") // 2
    parts = pixels.reshape(pieces, images, rows, chips // pieces, -1)
    parts = parts.transpose(0, 3, 1, 2, 4).reshape(chips, images, rows, -1)
    came = lax.all_to_all(parts, "batch", 0, 0, axis_index_groups=same_core(), tiled=True)
    return [came.reshape((chips * images,) + came.shape[2:])]


def plain_line_images(value, beside):
    both = jnp.concatenate([value, beside])
    return [lax.all_gather(both, "batch", axis=0, axis_index_groups=same_core(), tiled=True)]


def line_rows(low):
    if not tuned_mesh():
        return lax.all_gather(low, "batch", axis=0, axis_index_groups=same_core(), tiled=True)
    return jnp.concatenate([low] + [swap_batch(low, 2 * hop) for hop in (1, 2, 3)])


def core_sum(keep, send):
    return add_low(keep, swap_batch(send, 1))


def row_share(half):
    return lax.psum_scatter(half, "group", scatter_dimension=0, tiled=True)


def row_mine(share):
    return lax.psum(share, "batch", axis_index_groups=same_core())


def row_both(mine):
    core = lax.axis_index("batch") & 1
    return in_order(core, mine, swap_batch(mine, 1)).astype(jnp.float32)


def add_low(left, right):
    return (left.astype(jnp.float32) + right.astype(jnp.float32)).astype(left.dtype)


def ring_sides():
    group = lax.axis_index("group")
    side, level = (group & 1, group >> 1)
    return (1, side), (2, level)


def sum_out(parts, flip):
    order = ring_sides()[::-1] if flip else ring_sides()
    return [swap_group(part_of(part, 1 - bit, 2), way) for part, (way, bit) in zip(parts, order)]


def sum_in(parts, came, flip):
    order = ring_sides()[::-1] if flip else ring_sides()
    return [
        add_low(part_of(part, bit, 2), other)
        for part, other, (way, bit) in zip(parts, came, order)
    ]


def share_out(parts, flip):
    order = ring_sides()[::-1] if flip else ring_sides()
    return [swap_group(part, way) for part, (way, bit) in zip(parts, order)]


def share_in(parts, came, flip):
    order = ring_sides()[::-1] if flip else ring_sides()
    return [in_order(bit, part, other) for part, other, (way, bit) in zip(parts, came, order)]


def block_rows(value):
    rows, lanes = value.shape
    return value.reshape(rows, lanes // 128, 128).transpose(1, 0, 2).reshape(-1, 128)


def unblock_rows(value, rows):
    return value.reshape(-1, rows, 128).transpose(1, 0, 2).reshape(rows, -1)


def grid_params(mebibytes, semantics=1):
    return pltpu.CompilerParams(
        dimension_semantics=("arbitrary",) * semantics,
        vmem_limit_bytes=mebibytes * 1024 * 1024,
    )


def dot_nn(left, right):
    return lax.dot_general(
        left, right, (((1,), (0,)), ((), ())), preferred_element_type=jnp.float32
    )


def dot_nt(left, right):
    return lax.dot_general(
        left, right, (((1,), (1,)), ((), ())), preferred_element_type=jnp.float32
    )


def dot_tn(left, right):
    return lax.dot_general(
        left, right, (((0,), (0,)), ((), ())), preferred_element_type=jnp.float32
    )


def split_kernel(cells, core_ref, pixel_ref, mean_ref, rate_ref, *refs):
    out_refs, scratch = (refs[:2], refs[2:])
    patches, bands, lanes = pixel_ref.shape[1:]
    pieces, _, rows, _ = out_refs[0].shape
    share = lanes // (2 * pieces * cells)
    span = cells * bands
    tile = 128
    columns, tiles = (lanes // tile, -(-rows // tile))
    flat, turned = (scratch[:columns], scratch[columns:])
    values = (pixel_ref[0].astype(jnp.float32) - mean_ref[0]) * rate_ref[0]
    values = values.astype(jnp.bfloat16).astype(jnp.float32).reshape(patches * bands, lanes)
    for column in range(columns):
        flat[column][: patches * bands] = values[:, column * tile : (column + 1) * tile]
        flat[column][patches * bands :] = jnp.zeros(
            (flat[column].shape[0] - patches * bands, tile), jnp.float32
        )
    for band in range(bands):
        for column in range(columns):
            for at in range(tiles):
                block = flat[column][pl.ds(at * tile * bands + band, tile, stride=bands), :]
                turned[at][pl.ds(column * tile * bands + band, tile, stride=bands), :] = block.T
    for out_ref, side in zip(out_refs, (core_ref[0], 1 - core_ref[0])):
        for piece in range(pieces):
            for at in range(tiles):
                count = min(tile, rows - at * tile)
                parts = []
                for one in range(share):
                    first = ((piece * share + one) * 2 + side) * span
                    place = pl.ds(pl.multiple_of(first, span), span)
                    parts.append(turned[at][place, :].T[:count])
                block = parts[0] if share == 1 else jnp.concatenate(parts, axis=1)
                out_ref[piece, 0, at * tile : at * tile + count, :] = block.astype(jnp.bfloat16)


def turn_scratch(rows, bands, lanes):
    tiles = -(-rows // 128)
    return [pltpu.VMEM((tiles * 128 * bands, 128), jnp.float32)] * (lanes // 128) + [
        pltpu.VMEM((lanes * bands, 128), jnp.float32)
    ] * tiles


def split_pixels(pixels, means, rates, core, rows, cells):
    images, bands, patches, lanes = pixels.shape
    wide = bands * lanes // 8
    side = jax.ShapeDtypeStruct((4, images, rows, wide), jnp.bfloat16)
    return pl.pallas_call(
        partial(split_kernel, cells),
        grid_spec=pltpu.PrefetchScalarGridSpec(
            num_scalar_prefetch=1,
            grid=(images,),
            in_specs=[
                pl.BlockSpec((1, patches, bands, lanes), lambda i, core: (i, 0, 0, 0)),
                pl.BlockSpec((1, bands, 1), lambda i, core: (i, 0, 0)),
                pl.BlockSpec((1, bands, 1), lambda i, core: (i, 0, 0)),
            ],
            out_specs=[pl.BlockSpec((4, 1, rows, wide), lambda i, core: (0, i, 0, 0))] * 2,
            scratch_shapes=turn_scratch(rows, bands, lanes),
        ),
        out_shape=[side, side],
        compiler_params=grid_params(60),
        cost_estimate=pl.CostEstimate(flops=1, bytes_accessed=1, transcendentals=0),
        name="split_pixels",
    )(core.reshape(1), pixels.transpose(0, 2, 1, 3), means[:, :, None], rates[:, :, None])


def join_kernel(cells, patches, core_ref, mine_ref, other_ref, out_ref, *scratch):
    rows = mine_ref.shape[2]
    bands, lanes = out_ref.shape[2:]
    pieces = mine_ref.shape[0]
    share = lanes // (2 * pieces * cells)
    span = cells * bands
    tile = 128
    columns, tiles = (lanes // tile, -(-rows // tile))
    flat, turned = (scratch[:columns], scratch[columns:])
    core = core_ref[0]
    for piece in range(pieces):
        for ref, flip in ((mine_ref, core), (other_ref, 1 - core)):
            for one in range(share):
                first = ((piece * share + one) * 2 + flip) * span
                place = pl.ds(pl.multiple_of(first, span), span)
                for at in range(tiles):
                    count = min(tile, rows - at * tile)
                    block = ref[
                        piece, 0, at * tile : at * tile + count, one * span : (one + 1) * span
                    ].astype(jnp.float32)
                    if count < tile:
                        block = jnp.concatenate(
                            [block, jnp.zeros((tile - count, span), jnp.float32)]
                        )
                    turned[at][place, :] = block.T
    for band in range(bands):
        for column in range(columns):
            for at in range(tiles):
                block = turned[at][pl.ds(column * tile * bands + band, tile, stride=bands), :]
                flat[column][pl.ds(at * tile * bands + band, tile, stride=bands), :] = block.T
    for column in range(columns):
        out_ref[0, :, :, column * tile : (column + 1) * tile] = (
            flat[column][: patches * bands].reshape(patches, bands, tile).astype(jnp.bfloat16)
        )


def join_pixels(mine, other, core, patches, cells, lanes, bands):
    pieces, images, rows, wide = mine.shape
    block = pl.BlockSpec((pieces, 1, rows, wide), lambda i, core: (0, i, 0, 0))
    joined = pl.pallas_call(
        partial(join_kernel, cells, patches),
        grid_spec=pltpu.PrefetchScalarGridSpec(
            num_scalar_prefetch=1,
            grid=(images,),
            in_specs=[block, block],
            out_specs=pl.BlockSpec((1, patches, bands, lanes), lambda i, core: (i, 0, 0, 0)),
            scratch_shapes=turn_scratch(rows, bands, lanes),
        ),
        out_shape=jax.ShapeDtypeStruct((images, patches, bands, lanes), jnp.bfloat16),
        compiler_params=grid_params(60),
        cost_estimate=pl.CostEstimate(flops=1, bytes_accessed=1, transcendentals=0),
        name="join_pixels",
    )(core.reshape(1), mine, other)
    return joined.transpose(0, 2, 1, 3)


def embed_kernel(first, count, at_ref, low_ref, *refs):
    weight_refs, pixel_refs = refs[:count], refs[count : count + 2]
    if first:
        total_ref, kernel_ref, weight_now = refs[count + 2 :]
    else:
        before_ref, _, total_ref, kernel_ref, weight_now = refs[count + 2 :]
    share = pixel_refs[0].shape[1]
    images = 2 * share
    cells = weight_now.shape[0]
    bands = pixel_refs[0].shape[3] // cells

    @pl.when(pl.program_id(0) == 0)
    def _():
        if first:
            total_ref[...] = jnp.zeros_like(total_ref)
        else:
            total_ref[...] = before_ref[...]

    for at in range(count):

        @pl.when((pl.program_id(0) == at) | (count == 1))
        def _(at=at):
            weight_now[...] = weight_refs[at][...]

    low = low_ref[...]
    for cell in range(cells):
        made = dot_nt(low, weight_now[cell]).astype(jnp.bfloat16)
        for image in range(images):
            kernel_ref[0, image, cell * bands : (cell + 1) * bands, :] = made[
                image * bands : (image + 1) * bands
            ]
    for image in range(images):
        block = pixel_refs[image // share][0, image % share]
        total_ref[image] += dot_nn(block, kernel_ref[0, image])


def embed_piece(place, low, weights, pixels, total, kernels):
    pieces, share, rows, lanes = pixels[0].shape
    images = 2 * share
    cells, width, depth = weights[0].shape
    step = lanes // (4 * 16)
    count = len(weights)
    steps = max(count, cells // step)
    bands = lanes // (4 * step)
    first = total is None
    any_spec = pl.BlockSpec(memory_space=pl.ANY)
    whole_total = pl.BlockSpec((images, rows, width), lambda t, at: (0, 0, 0))
    if count == 1:
        weight_specs = [pl.BlockSpec((step, width, depth), lambda t, at: (t, 0, 0))]
    else:
        weight_specs = [pl.BlockSpec((step, width, depth), lambda t, at: (0, 0, 0))] * count
    return pl.pallas_call(
        partial(embed_kernel, first, count),
        grid_spec=pltpu.PrefetchScalarGridSpec(
            num_scalar_prefetch=1,
            grid=(steps,),
            in_specs=[pl.BlockSpec(low.shape, lambda t, at: (0, 0))]
            + weight_specs
            + [
                pl.BlockSpec(
                    (1, share, rows, step * bands), lambda t, at: (at[0], 0, 0, at[1 + t])
                ),
            ]
            * 2
            + ([] if first else [whole_total, any_spec]),
            out_specs=[
                whole_total,
                pl.BlockSpec(
                    (1, images, step * bands, width), lambda t, at: (at[0], 0, at[1 + t], 0)
                ),
            ],
            scratch_shapes=[pltpu.VMEM((step, width, depth), jnp.bfloat16)],
        ),
        out_shape=[
            jax.ShapeDtypeStruct((images, rows, width), jnp.float32),
            jax.ShapeDtypeStruct((pieces, images, lanes, width), jnp.bfloat16),
        ],
        input_output_aliases={} if first else {4 + count: 0, 5 + count: 1},
        compiler_params=grid_params(60),
        cost_estimate=pl.CostEstimate(flops=1, bytes_accessed=1, transcendentals=0),
        name="embed_piece",
    )(place, low, *weights, *pixels, *(() if first else (total, kernels)))


def pixel_grad_kernel(grad_ref, kernel_ref, rate_ref, out_ref):
    for image in range(grad_ref.shape[0]):
        out_ref[0, image] = (
            dot_nt(grad_ref[image], kernel_ref[0, image]) * rate_ref[image]
        ).astype(jnp.bfloat16)


def pixel_grads(grads, kernels, rates):
    pieces, images, lanes, width = kernels.shape
    rows = grads.shape[1]
    share = images // 2
    return pl.pallas_call(
        pixel_grad_kernel,
        grid=(2, pieces),
        in_specs=[
            pl.BlockSpec((share, rows, width), lambda i, j: (i, 0, 0)),
            pl.BlockSpec((1, share, lanes, width), lambda i, j: (j, i, 0, 0)),
            pl.BlockSpec((share, 1, lanes), lambda i, j: (i, 0, 0)),
        ],
        out_specs=pl.BlockSpec((1, share, rows, lanes), lambda i, j: (j, i, 0, 0)),
        out_shape=jax.ShapeDtypeStruct((pieces, images, rows, lanes), jnp.bfloat16),
        compiler_params=grid_params(60, 2),
        cost_estimate=pl.CostEstimate(flops=1, bytes_accessed=1, transcendentals=0),
        name="pixel_grads",
    )(grads, kernels, rates)


def line_kernel(half, halves, low_ref, pixel_refs, grad_refs, out_ref, made):
    cells = out_ref.shape[0]
    lanes = pixel_refs[0].shape[2] // halves
    bands = lanes // cells
    columns = slice(half * lanes, (half + 1) * lanes)
    spots = [(ref, at) for ref in grad_refs for at in range(ref.shape[0])]
    image = 0
    for pixel_ref in pixel_refs:
        for at in range(pixel_ref.shape[0]):
            grad_ref, where = spots[image]
            grads = dot_tn(pixel_ref[at, :, columns], grad_ref[where]).astype(jnp.bfloat16)
            for cell in range(cells):
                made[cell, image * bands : (image + 1) * bands, :] = grads[
                    cell * bands : (cell + 1) * bands
                ]
            image += 1

    @pl.loop(0, cells, unroll=4)
    def _(cell):
        out_ref[cell] = dot_nn(low_ref[...], made[cell]).T.astype(jnp.bfloat16)


def line_grads(low_turned, cells, pixels, grads, half, halves):
    step_cells = cells // halves
    depth = low_turned.shape[0]
    width = grads[0].shape[2]
    bands = pixels[0].shape[2] // cells
    images = sum(piece.shape[0] for piece in pixels)
    vmem = pl.BlockSpec(memory_space=pltpu.VMEM)

    def body(*refs):
        pixel_refs = refs[1 : 1 + len(pixels)]
        grad_refs = refs[1 + len(pixels) : 1 + len(pixels) + len(grads)]
        line_kernel(half, halves, refs[0], pixel_refs, grad_refs, *refs[-2:])

    return pl.pallas_call(
        body,
        in_specs=[vmem] * (1 + len(pixels) + len(grads)),
        out_specs=vmem,
        out_shape=jax.ShapeDtypeStruct((step_cells, width, depth), jnp.bfloat16),
        scratch_shapes=[pltpu.VMEM((step_cells, images * bands, width), jnp.bfloat16)],
        compiler_params=pltpu.CompilerParams(vmem_limit_bytes=60 * 1024 * 1024),
        cost_estimate=pl.CostEstimate(flops=1, bytes_accessed=1, transcendentals=0),
        name="line_grads",
    )(low_turned, *pixels, *grads)


def band_kernel(first, count, at_ref, grad_ref, *refs):
    weight_refs, pixel_refs = refs[:count], refs[count : count + 2]
    if first:
        total_ref, weight_now, made = refs[count + 2 :]
    else:
        before_ref, total_ref, weight_now, made = refs[count + 2 :]
    share = pixel_refs[0].shape[1]
    images = 2 * share
    cells = weight_now.shape[0]
    bands = pixel_refs[0].shape[3] // cells

    @pl.when(pl.program_id(0) == 0)
    def _():
        if first:
            total_ref[...] = jnp.zeros_like(total_ref)
        else:
            total_ref[...] = before_ref[...]

    for at in range(count):

        @pl.when((pl.program_id(0) == at) | (count == 1))
        def _(at=at):
            weight_now[...] = weight_refs[at][...]

    for image in range(images):
        block = pixel_refs[image // share][0, image % share]
        grads = dot_tn(block, grad_ref[image]).astype(jnp.bfloat16)
        for cell in range(cells):
            made[cell, image * bands : (image + 1) * bands, :] = grads[
                cell * bands : (cell + 1) * bands
            ]
    for cell in range(cells):
        total_ref[...] += dot_nn(made[cell], weight_now[cell])


def band_piece(place, grads, weights, pixels, total):
    pieces, share, rows, lanes = pixels[0].shape
    images = 2 * share
    cells, width, depth = weights[0].shape
    step = lanes // (4 * 16)
    count = len(weights)
    steps = max(count, cells // step)
    bands = lanes // (4 * step)
    first = total is None
    whole_total = pl.BlockSpec((images * bands, depth), lambda t, at: (0, 0))
    if count == 1:
        weight_specs = [pl.BlockSpec((step, width, depth), lambda t, at: (t, 0, 0))]
    else:
        weight_specs = [pl.BlockSpec((step, width, depth), lambda t, at: (0, 0, 0))] * count
    return pl.pallas_call(
        partial(band_kernel, first, count),
        grid_spec=pltpu.PrefetchScalarGridSpec(
            num_scalar_prefetch=1,
            grid=(steps,),
            in_specs=[pl.BlockSpec(grads.shape, lambda t, at: (0, 0, 0))]
            + weight_specs
            + [
                pl.BlockSpec(
                    (1, share, rows, step * bands), lambda t, at: (at[0], 0, 0, at[1 + t])
                ),
            ]
            * 2
            + ([] if first else [whole_total]),
            out_specs=whole_total,
            scratch_shapes=[
                pltpu.VMEM((step, width, depth), jnp.bfloat16),
                pltpu.VMEM((step, images * bands, width), jnp.bfloat16),
            ],
        ),
        out_shape=jax.ShapeDtypeStruct((images * bands, depth), jnp.float32),
        compiler_params=grid_params(60),
        cost_estimate=pl.CostEstimate(flops=1, bytes_accessed=1, transcendentals=0),
        name="band_piece",
    )(place, grads, *weights, *pixels, *(() if first else (total,)))


def head_probs(patches, query, keyed, mine):
    rows = query.shape[0]
    scores = dot_nt(jnp.where(mine, query, jnp.zeros_like(query)), keyed)
    column = lax.broadcasted_iota(jnp.int32, (1, rows), 1)
    scores = jnp.where(column < patches, scores, -1e30)
    powers = jnp.exp(scores - jnp.max(scores, axis=-1, keepdims=True))
    return powers * (1.0 / jnp.sum(powers, axis=-1, keepdims=True))


def attend_kernel(patches, head_size, joint_ref, out_ref):
    width = out_ref.shape[2]
    pair = 2 * head_size
    lane = lax.broadcasted_iota(jnp.int32, (1, pair), 1)
    scale = jnp.asarray(head_size ** (-0.5), jnp.bfloat16)
    for at in range(0, width, pair):
        query = joint_ref[0, :, at : at + pair] * scale
        keyed = joint_ref[0, :, width + at : width + at + pair]
        valued = joint_ref[0, :, 2 * width + at : 2 * width + at + pair]
        mixed = []
        for head in range(2):
            mine = (lane >= head * head_size) & (lane < (head + 1) * head_size)
            probs = head_probs(patches, query, keyed, mine)
            mixed.append(dot_nn(probs.astype(jnp.bfloat16), valued))
        out_ref[0, :, at : at + pair] = jnp.where(lane < head_size, mixed[0], mixed[1]).astype(
            jnp.bfloat16
        )


def attend(joint, patches, head_size):
    images, rows, triple = joint.shape
    width = triple // 3
    return pl.pallas_call(
        partial(attend_kernel, patches, head_size),
        grid=(images,),
        in_specs=[pl.BlockSpec((1, rows, triple), lambda i: (i, 0, 0))],
        out_specs=pl.BlockSpec((1, rows, width), lambda i: (i, 0, 0)),
        out_shape=jax.ShapeDtypeStruct((images, rows, width), jnp.bfloat16),
        compiler_params=grid_params(60),
        cost_estimate=pl.CostEstimate(flops=1, bytes_accessed=1, transcendentals=0),
        name="attend",
    )(joint)


def attend_back_kernel(patches, head_size, joint_ref, grad_ref, out_ref, sum_ref):
    width = grad_ref.shape[2]
    pair = 2 * head_size
    lane = lax.broadcasted_iota(jnp.int32, (1, pair), 1)
    scale = jnp.asarray(head_size ** (-0.5), jnp.bfloat16)

    @pl.when(pl.program_id(0) == 0)
    def _():
        sum_ref[...] = jnp.zeros_like(sum_ref)

    for at in range(0, width, pair):
        query = joint_ref[0, :, at : at + pair] * scale
        keyed = joint_ref[0, :, width + at : width + at + pair]
        valued = joint_ref[0, :, 2 * width + at : 2 * width + at + pair]
        grads = grad_ref[0, :, at : at + pair]
        none = jnp.zeros_like(grads)
        parts = []
        for head in range(2):
            mine = (lane >= head * head_size) & (lane < (head + 1) * head_size)
            probs = head_probs(patches, query, keyed, mine)
            grad = jnp.where(mine, grads, none)
            to_probs = dot_nt(grad, valued)
            inner = jnp.sum(probs * to_probs, axis=-1, keepdims=True)
            to_scores = (probs * (to_probs - inner)).astype(jnp.bfloat16)
            parts.append(
                (
                    dot_nn(to_scores, jnp.where(mine, keyed, none)),
                    dot_tn(to_scores, jnp.where(mine, query, none)),
                    dot_tn(probs.astype(jnp.bfloat16), grad),
                )
            )
        to_query = (parts[0][0] + parts[1][0]) * (head_size ** (-0.5))
        to_keyed = parts[0][1] + parts[1][1]
        to_valued = parts[0][2] + parts[1][2]
        for slot, value in enumerate((to_query, to_keyed, to_valued)):
            value = value.astype(jnp.bfloat16)
            out_ref[0, :, slot * width + at : slot * width + at + pair] = value
            sum_ref[:, slot * width + at : slot * width + at + pair] += jnp.sum(
                value.astype(jnp.float32), axis=0, keepdims=True
            )


def attend_back(joint, grads, patches, head_size):
    images, rows, triple = joint.shape
    width = triple // 3
    return pl.pallas_call(
        partial(attend_back_kernel, patches, head_size),
        grid=(images,),
        in_specs=[
            pl.BlockSpec((1, rows, triple), lambda i: (i, 0, 0)),
            pl.BlockSpec((1, rows, width), lambda i: (i, 0, 0)),
        ],
        out_specs=[
            pl.BlockSpec((1, rows, triple), lambda i: (i, 0, 0)),
            pl.BlockSpec((1, triple), lambda i: (0, 0)),
        ],
        out_shape=[
            jax.ShapeDtypeStruct((images, rows, triple), jnp.bfloat16),
            jax.ShapeDtypeStruct((1, triple), jnp.float32),
        ],
        compiler_params=grid_params(60),
        cost_estimate=pl.CostEstimate(flops=1, bytes_accessed=1, transcendentals=0),
        name="attend_back",
    )(joint, grads)


def norm_inside(values, epsilon):
    center = values - jnp.mean(values, axis=-1, keepdims=True)
    factor = lax.rsqrt(jnp.mean(center * center, axis=-1, keepdims=True) + epsilon)
    return center * factor, factor


def small_call(kernel, name, grid, in_specs, out_specs, out_shape, scratch=(), limit=60):
    return pl.pallas_call(
        kernel,
        grid=grid,
        in_specs=in_specs,
        out_specs=out_specs,
        out_shape=out_shape,
        scratch_shapes=list(scratch),
        compiler_params=grid_params(limit),
        cost_estimate=pl.CostEstimate(flops=1, bytes_accessed=1, transcendentals=0),
        name=name,
    )


def whole_spec(shape):
    return pl.BlockSpec(shape, lambda i: (0,) * len(shape))


def image_spec(rows, width):
    return pl.BlockSpec((1, rows, width), lambda i: (i, 0, 0))


def joint_kernel(
    own_ref, beside_ref, bias_ref, gain_ref, shift_ref, weight_ref, joint_bias_ref,
    embedded_ref, normed_ref, joint_ref,
):
    embedded = own_ref[0] + beside_ref[0] + bias_ref[0]
    embedded_ref[0] = embedded
    normed = norm_inside(embedded, block_eps)[0] * gain_ref[...] + shift_ref[...]
    normed = normed.astype(jnp.bfloat16)
    normed_ref[0] = normed
    joint = dot_nn(normed, weight_ref[...]) + joint_bias_ref[...]
    joint_ref[0] = joint.astype(jnp.bfloat16)


def make_joint(total, beside, image_bias, gain, shift, weight, joint_bias):
    images, rows, width = beside.shape
    triple = weight.shape[1]
    return small_call(
        joint_kernel,
        "make_joint",
        (images,),
        [image_spec(rows, width)] * 2
        + [image_spec(1, width), whole_spec((1, width)), whole_spec((1, width))]
        + [whole_spec(weight.shape), whole_spec((1, triple))],
        [image_spec(rows, width), image_spec(rows, width), image_spec(rows, triple)],
        [
            jax.ShapeDtypeStruct((images, rows, width), jnp.float32),
            jax.ShapeDtypeStruct((images, rows, width), jnp.bfloat16),
            jax.ShapeDtypeStruct((images, rows, triple), jnp.bfloat16),
        ],
    )(total, beside, image_bias[:, None], gain[None], shift[None], weight, joint_bias[None])


def residual_kernel(
    attended_ref, embedded_ref, weight_ref, bias_ref, gain_ref, shift_ref, residual_ref, normed_ref
):
    branch = dot_nn(attended_ref[0], weight_ref[...]) + bias_ref[...]
    residual = embedded_ref[0] + branch
    residual_ref[0] = residual
    normed = norm_inside(residual, block_eps)[0] * gain_ref[...] + shift_ref[...]
    normed_ref[0] = normed.astype(jnp.bfloat16)


def make_residual(attended, embedded, weight, bias, gain, shift):
    images, rows, width = embedded.shape
    return small_call(
        residual_kernel,
        "make_residual",
        (images,),
        [image_spec(rows, width)] * 2 + [whole_spec(weight.shape)] + [whole_spec((1, width))] * 3,
        [image_spec(rows, width)] * 2,
        [
            jax.ShapeDtypeStruct((images, rows, width), jnp.float32),
            jax.ShapeDtypeStruct((images, rows, width), jnp.bfloat16),
        ],
    )(attended, embedded, weight, bias[None], gain[None], shift[None])


def norm_back_inside(grad, values, gain, epsilon):
    normal, factor = norm_inside(values, epsilon)
    scaled = grad * gain
    back = factor * (
        scaled
        - jnp.mean(scaled, axis=-1, keepdims=True)
        - normal * jnp.mean(scaled * normal, axis=-1, keepdims=True)
    )
    return back, jnp.sum(grad * normal, axis=0, keepdims=True)


def add_rows(out_ref, rows):
    @pl.when(pl.program_id(0) == 0)
    def _():
        out_ref[...] = jnp.zeros_like(out_ref)

    out_ref[...] += jnp.concatenate(rows, axis=0)


def branch_back_kernel(
    grad_ref, residual_ref, out_grad_ref, gain_ref, weight_ref,
    resid_ref, branch_ref, att_ref, sum_ref,
):
    grad = grad_ref[0]
    out_grad = out_grad_ref[0].astype(jnp.float32)
    back, gain_grad = norm_back_inside(grad, residual_ref[0], gain_ref[...], block_eps)
    resid = out_grad + back
    resid_ref[0] = resid
    branch = resid.astype(jnp.bfloat16)
    branch_ref[0] = branch
    att_ref[0] = dot_nt(branch, weight_ref[...]).astype(jnp.bfloat16)
    add_rows(
        sum_ref,
        [
            gain_grad,
            jnp.sum(grad, axis=0, keepdims=True),
            jnp.sum(branch.astype(jnp.float32), axis=0, keepdims=True),
            jnp.sum(out_grad, axis=0, keepdims=True),
        ],
    )


def branch_back(grad, residual, out_grad, gain, weight):
    images, rows, width = residual.shape
    return small_call(
        branch_back_kernel,
        "branch_back",
        (images,),
        [image_spec(rows, width)] * 3 + [whole_spec((1, width)), whole_spec(weight.shape)],
        [image_spec(rows, width)] * 3 + [whole_spec((4, width))],
        [
            jax.ShapeDtypeStruct((images, rows, width), jnp.float32),
            jax.ShapeDtypeStruct((images, rows, width), jnp.bfloat16),
            jax.ShapeDtypeStruct((images, rows, width), jnp.bfloat16),
            jax.ShapeDtypeStruct((4, width), jnp.float32),
        ],
    )(grad, residual, out_grad, gain[None], weight)


def embed_back_kernel(
    joint_ref, weight_ref, embedded_ref, resid_ref, gain_ref, emb_ref, sum_ref, image_ref
):
    grad = dot_nt(joint_ref[0], weight_ref[...])
    back, gain_grad = norm_back_inside(grad, embedded_ref[0], gain_ref[...], block_eps)
    emb = (resid_ref[0] + back).astype(jnp.bfloat16)
    emb_ref[0] = emb
    image_ref[0] = jnp.sum(emb.astype(jnp.float32), axis=0, keepdims=True)
    add_rows(sum_ref, [gain_grad, jnp.sum(grad, axis=0, keepdims=True)])


def embed_back(joint_grad, weight, embedded, resid, gain):
    images, rows, width = embedded.shape
    return small_call(
        embed_back_kernel,
        "embed_back",
        (images,),
        [image_spec(rows, joint_grad.shape[2]), whole_spec(weight.shape)]
        + [image_spec(rows, width)] * 2
        + [whole_spec((1, width))],
        [image_spec(rows, width), whole_spec((2, width)), image_spec(1, width)],
        [
            jax.ShapeDtypeStruct((images, rows, width), jnp.bfloat16),
            jax.ShapeDtypeStruct((2, width), jnp.float32),
            jax.ShapeDtypeStruct((images, 1, width), jnp.float32),
        ],
    )(joint_grad, weight, embedded, resid, gain[None])


def split_rows(core, value, count, keep_ref, send_ref):
    size = value.shape[0] // (2 * count)
    for at in range(count):
        first = value[2 * at * size : (2 * at + 1) * size]
        second = value[(2 * at + 1) * size : (2 * at + 2) * size]
        keep = jnp.where(core == 0, first, second).astype(jnp.bfloat16)
        send = jnp.where(core == 0, second, first).astype(jnp.bfloat16)
        keep_ref[at * size : (at + 1) * size] = keep
        send_ref[at * size : (at + 1) * size] = send


def rows_kernel(count, core_ref, left_ref, right_ref, keep_ref, send_ref, turned):
    @pl.when(pl.program_id(0) == 0)
    def _():
        turned[...] = left_ref[...].T

    split_rows(core_ref[0], dot_nn(turned[...], right_ref[...]), count, keep_ref, send_ref)


def rows_grad(core, left, right, count=4):
    rows, width = left.shape
    columns = right.shape[1]
    part = min(columns, 768)
    half = jax.ShapeDtypeStruct((width // 2, columns), jnp.bfloat16)
    return pl.pallas_call(
        partial(rows_kernel, count),
        grid_spec=pltpu.PrefetchScalarGridSpec(
            num_scalar_prefetch=1,
            grid=(columns // part,),
            in_specs=[
                pl.BlockSpec((rows, width), lambda s, core: (0, 0)),
                pl.BlockSpec((rows, part), lambda s, core: (0, s)),
            ],
            out_specs=[pl.BlockSpec((width // 2, part), lambda s, core: (0, s))] * 2,
            scratch_shapes=[pltpu.VMEM((width, rows), jnp.bfloat16)],
        ),
        out_shape=[half, half],
        compiler_params=grid_params(60),
        cost_estimate=pl.CostEstimate(flops=1, bytes_accessed=1, transcendentals=0),
        name="rows_grad",
    )(core.reshape(1), left, right)


def mlp_kernel(
    core_ref, normed_ref, residual_ref, grad_ref, up_ref, bias_ref, down_ref, down_bias_ref,
    out_ref, back_ref, up_keep_ref, up_send_ref, down_keep_ref, down_send_ref, bias_grad_ref,
    active, to_pre, turned, total,
):
    rows = normed_ref.shape[0]
    part = rows // MLP_PARTS

    @pl.when(pl.program_id(0) == 0)
    def _():
        total[...] = residual_ref[...] + down_bias_ref[...]
        back_ref[...] = jnp.zeros_like(back_ref)
        turned[...] = normed_ref[...].T

    up = up_ref[...]
    down = down_ref[...]
    bias_grad = jnp.zeros(bias_grad_ref.shape, jnp.float32)
    for at in range(0, rows, part):
        span = slice(at, at + part)
        pre = dot_nn(normed_ref[span], up) + bias_ref[...]
        share = 0.5 + 0.5 * lax.erf(pre * (0.5**0.5))
        slope = share + pre * (jnp.exp(-0.5 * pre * pre) * (0.5 / jnp.pi) ** 0.5)
        act = (pre * share).astype(jnp.bfloat16)
        grad = (slope * dot_nt(grad_ref[span], down)).astype(jnp.bfloat16)
        active[span] = act
        to_pre[span] = grad
        total[span] += dot_nn(act, down)
        back_ref[span] += dot_nt(grad, up)
        bias_grad += jnp.sum(grad.astype(jnp.float32), axis=0, keepdims=True)
    bias_grad_ref[...] = bias_grad
    core = core_ref[0]
    split_rows(core, dot_nn(turned[...], to_pre[...]), 4, up_keep_ref, up_send_ref)
    split_rows(core, dot_tn(active[...], grad_ref[...]), 1, down_keep_ref, down_send_ref)

    @pl.when(pl.program_id(0) == pl.num_programs(0) - 1)
    def _():
        out_ref[...] = total[...].astype(jnp.bfloat16)


MLP_PARTS = 2


def mlp(core, normed, residual, grads, up, up_bias, down, down_bias):
    rows, width = normed.shape
    hidden = up.shape[1]
    part = hidden // 4
    whole = pl.BlockSpec((rows, width), lambda s, core: (0, 0))
    columns = pl.BlockSpec((width, part), lambda s, core: (0, s))
    lines = pl.BlockSpec((part, width), lambda s, core: (s, 0))
    vector = pl.BlockSpec((1, part), lambda s, core: (0, s))
    up_half = jax.ShapeDtypeStruct((width // 2, hidden), jnp.bfloat16)
    down_half = jax.ShapeDtypeStruct((hidden // 2, width), jnp.bfloat16)
    return pl.pallas_call(
        mlp_kernel,
        grid_spec=pltpu.PrefetchScalarGridSpec(
            num_scalar_prefetch=1,
            grid=(hidden // part,),
            in_specs=[
                whole, whole, whole, columns, vector, lines,
                pl.BlockSpec((1, width), lambda s, core: (0, 0)),
            ],
            out_specs=[whole, whole]
            + [pl.BlockSpec((width // 2, part), lambda s, core: (0, s))] * 2
            + [pl.BlockSpec((part // 2, width), lambda s, core: (s, 0))] * 2
            + [vector],
            scratch_shapes=[
                pltpu.VMEM((rows, part), jnp.bfloat16),
                pltpu.VMEM((rows, part), jnp.bfloat16),
                pltpu.VMEM((width, rows), jnp.bfloat16),
                pltpu.VMEM((rows, width), jnp.float32),
            ],
        ),
        out_shape=[
            jax.ShapeDtypeStruct((rows, width), jnp.bfloat16),
            jax.ShapeDtypeStruct((rows, width), jnp.float32),
            up_half,
            up_half,
            down_half,
            down_half,
            jax.ShapeDtypeStruct((1, hidden), jnp.float32),
        ],
        compiler_params=grid_params(60),
        cost_estimate=pl.CostEstimate(flops=1, bytes_accessed=1, transcendentals=0),
        name="mlp",
    )(core.reshape(1), normed, residual, grads, up, up_bias[None], down, down_bias[None])


def assemble_kernel(bits_ref, one_mine, one_came, two_mine, two_came, out_ref):
    for at, ref in enumerate((one_mine, one_came, two_mine, two_came)):

        @pl.when(pl.program_id(0) == at)
        def _(ref=ref):
            out_ref[...] = ref[...].astype(jnp.float32)


def assemble(bits, one_mine, one_came, two_mine, two_came):
    cells, width, depth = one_mine.shape
    whole = pl.BlockSpec((cells, width, depth), lambda t, bits: (0, 0, 0))
    return pl.pallas_call(
        assemble_kernel,
        grid_spec=pltpu.PrefetchScalarGridSpec(
            num_scalar_prefetch=1,
            grid=(4,),
            in_specs=[whole] * 4,
            out_specs=pl.BlockSpec(
                (cells, width, depth), lambda t, bits: (t // 2 * 2 + (bits[t // 2] ^ (t % 2)), 0, 0)
            ),
        ),
        out_shape=jax.ShapeDtypeStruct((4 * cells, width, depth), jnp.float32),
        compiler_params=grid_params(60),
        cost_estimate=pl.CostEstimate(flops=1, bytes_accessed=1, transcendentals=0),
        name="assemble",
    )(bits, one_mine, one_came, two_mine, two_came)


def per_device(
    pixels,
    band_count,
    band_bin,
    bin_wave,
    run_mean,
    run_var,
    weight_tokens,
    bias_token,
    hyper_in,
    hyper_qv_bias,
    hyper_out,
    hyper_out_bias,
    hyper_gain,
    hyper_shift,
    hyper_up,
    hyper_up_bias,
    hyper_down,
    hyper_down_bias,
    kernel_weight,
    bias_weight,
    bias_offset,
    norm_gain,
    norm_shift,
    w_qkv,
    qv_bias,
    w_out,
    out_bias,
    w_up,
    up_bias,
    w_down,
    down_bias,
    cotangent,
):
    pixel_data = pixels[0]
    images, band_slots, patches, pixel_cells = pixel_data.shape
    bin_total = bin_wave.shape[0]
    model_width = w_qkv.shape[0]
    head_size = model_width // HEADS
    padded = -(-patches // 16) * 16
    rows = images * padded
    cells = kernel_weight.shape[0]
    core = lax.axis_index("batch") & 1
    live_band = (
        lax.broadcasted_iota(jnp.int32, (images, band_slots), 1) < band_count[0][:, None]
    ).astype(jnp.float32)
    bin_onehot = (
        band_bin[0][..., None]
        == lax.broadcasted_iota(jnp.int32, (images, band_slots, bin_total), 2)
    ).astype(jnp.float32)
    chosen = bin_onehot * live_band[..., None]
    run_rstd = lax.rsqrt(run_var + stat_eps)
    band_mean = jnp.einsum("ibn,n->ib", chosen, run_mean, precision=highest)
    band_rstd = jnp.einsum("ibn,n->ib", chosen, run_rstd, precision=highest)
    values32 = pixel_data.astype(jnp.float32)
    band_total = jnp.sum(values32, axis=(2, 3))
    band_square = jnp.sum(values32 * values32, axis=(2, 3))
    bin_sums = jnp.einsum("ib,ibn->n", band_total, chosen, precision=highest)
    bin_squares = jnp.einsum("ib,ibn->n", band_square, chosen, precision=highest)
    bin_counts = jnp.sum(chosen, axis=(0, 1))

    grad_out = jnp.pad(cotangent[0], ((0, 0), (0, padded - patches), (0, 0)))
    band_wave = jnp.einsum("ibn,n->ib", bin_onehot, bin_wave, precision=highest)
    wave_emb = wave_embed(band_wave, hyper_in.shape[0])
    hyper_params = (
        weight_tokens,
        bias_token,
        hyper_in,
        hyper_qv_bias,
        hyper_out,
        hyper_out_bias,
        hyper_gain,
        hyper_shift,
        hyper_up,
        hyper_up_bias,
        hyper_down,
        hyper_down_bias,
    )

    def make_low():
        (band_vec, bias_vec), hyper_back = jax.vjp(
            partial(hypernet, wave_emb=wave_emb, live_band=live_band), hyper_params
        )
        band_low = band_vec.astype(jnp.bfloat16).reshape(images * band_slots, -1)
        return band_low, bias_vec, hyper_back

    def place(piece, *quarters):
        return jnp.stack([jnp.asarray(at, jnp.int32) for at in (piece,) + quarters])

    if not tuned_mesh():
        band_low, bias_vec, hyper_back = make_low()
        chip_low = jnp.concatenate([band_low, swap_batch(band_low, 1)])
        mine, other = split_pixels(pixel_data, band_mean, band_rstd, core, padded, cells)
        chip_pixels = (mine, swap_batch(other, 1))
        total, kernels = (None, None)
        for at, weight in enumerate(plain_weight_pieces(kernel_weight)):
            total, kernels = embed_piece(
                place(at, 0, 1, 2, 3), chip_low, [weight], chip_pixels, total, kernels
            )
        line_pixels = plain_line_cells(jnp.concatenate(chip_pixels, axis=1))
        line_low = lax.all_gather(
            chip_low, "batch", axis=0, axis_index_groups=same_core(), tiled=True
        )
    else:
        group = lax.axis_index("group")
        chip = lax.axis_index("batch") >> 1
        part = cells // 8
        quarter = part_of(kernel_weight, group, 4)

        def sides(block):
            return swap_group(block, 1), swap_group(block, 2)

        def corners(beside, above):
            return swap_group(beside[:part], 2), swap_group(above[part : 2 * part], 1)

        def sides_and_corner(block, beside, above):
            return (
                swap_group(jnp.concatenate([block, above[part : 2 * part]]), 1),
                swap_group(jnp.concatenate([block, beside[:part]]), 2),
            )

        def added(state, piece, weights, shifts):
            spots = place(piece, *[group ^ shift for shift in shifts])
            return embed_piece(spots, chip_low, weights, chip_pixels, *state)

        def pixel_block(hop, half):
            piece = lax.dynamic_index_in_dim(chip_pixels[half], chip ^ hop, 0, keepdims=False)
            return swap_batch(piece, 2 * hop) if hop else piece

        right1, left1 = (along_line(quarter, -1), along_line(quarter, 1))
        band_low, bias_vec, hyper_back = make_low()
        band_low, bias_vec, right1, left1, pixel_data = tie(
            band_low, bias_vec, right1, left1, pixel_data
        )
        block1 = jnp.where(chip == 3, left1, right1)
        right2, left2 = (along_line(right1, -1, (1, 2)), along_line(left1, 1, (1, 2)))
        beside1, above1 = sides(block1)
        mine, other = split_pixels(pixel_data, band_mean, band_rstd, core, padded, cells)
        chip_low = jnp.concatenate([band_low, swap_batch(band_low, 1)])
        mine, other, chip_low, right2, left2, beside1, above1 = tie(
            mine, other, chip_low, right2, left2, beside1, above1
        )
        block2 = jnp.where(chip == 0, right2, jnp.where(chip == 3, left2, left1))
        end3 = line_ends(jnp.where(chip == 1, right2, left2))
        across2, up2 = sides_and_corner(block2, beside1, above1)
        chip_pixels = (mine, swap_batch(other, 1))
        pixels2 = [pixel_block(2, 0)]
        state = embed_piece(
            place(chip, 0, 1, 2, 3), chip_low, [kernel_weight], chip_pixels, None, None
        )
        weights1 = [block1, beside1, above1]
        spots1 = of_chip(chip, [1, 2, 3, 2])
        state = added(state, spots1, weights1, (0, 1, 2))
        state, chip_pixels, end3, across2, up2, pixels2, bin_sums, bin_squares = tie(
            state, chip_pixels, end3, across2, up2, pixels2, bin_sums, bin_squares
        )
        block3 = jnp.where(chip == 1, right2, jnp.where(chip == 2, left2, end3))
        across3, up3 = sides_and_corner(block3, across2, up2)
        pixels2.append(pixel_block(2, 1))
        pixels1 = [pixel_block(1, 0)]
        weights1.append(jnp.concatenate([up2[2 * part :], across2[2 * part :]]))
        state = added(state, spots1, weights1[3:], (3,))
        weights2 = [block2, across2, up2]
        spots2 = of_chip(chip, [2, 0, 1, 1])
        state = added(state, spots2, weights2, (0, 1, 2))
        state, across3, up3, pixels1, pixels2, chip_pixels, grad_out = tie(
            state, across3, up3, pixels1, pixels2, chip_pixels, grad_out
        )
        corner3 = corners(across3, up3)
        pixels1.append(pixel_block(1, 1))
        weights2.append(jnp.concatenate([up3[2 * part :], across3[2 * part :]]))
        state = added(state, spots2, weights2[3:], (3,))
        weights3 = [block3, across3, up3]
        spots3 = of_chip(chip, [3, 3, 0, 0])
        state = added(state, spots3, weights3, (0, 1, 2))
        state, corner3, pixels1, chip_pixels = tie(state, corner3, pixels1, chip_pixels)
        pixels3 = [pixel_block(3, 0)]
        weights3.append(jnp.concatenate(corner3))
        total, kernels = added(state, spots3, weights3[3:], (3,))
    image_bias = jnp.dot(bias_vec, bias_weight, precision=highest) + bias_offset
    total_beside = swap_batch(total[images:], 1)
    joint_bias = jnp.concatenate([qv_bias[0], jnp.zeros_like(qv_bias[0]), qv_bias[1]])
    embedded, normed1, joint = make_joint(
        total, total_beside, image_bias, norm_gain[0], norm_shift[0], w_qkv, joint_bias
    )
    attended = attend(joint, patches, head_size)
    rates = jnp.tile(band_rstd, (1, pixel_cells // 8))
    if tuned_mesh():
        attended, chip_pixels, chip_low, rates = tie(attended, chip_pixels, chip_low, rates)
        line_low = line_rows(chip_low)
    residual, normed2 = make_residual(
        attended, embedded, w_out, out_bias, norm_gain[1], norm_shift[1]
    )
    block_out, grad_n2, up_keep, up_send, down_keep, down_send, grad_up_bias = mlp(
        core,
        normed2.reshape(rows, model_width),
        residual.reshape(rows, model_width),
        grad_out.reshape(rows, model_width),
        w_up,
        up_bias,
        w_down,
        down_bias,
    )
    if tuned_mesh():
        rates_beside = swap_batch(rates, 1)
        grad_n2, pixels3, chip_pixels, line_low, rates_beside, up_send, down_send = tie(
            grad_n2, pixels3, chip_pixels, line_low, rates_beside, up_send, down_send
        )
        pixels3.append(pixel_block(3, 1))
    else:
        rates_beside = swap_batch(rates, 1)
    rates = jnp.concatenate([rates, rates_beside])[:, None, :]
    up_came, down_came = swap_batch(up_send, 1), swap_batch(down_send, 1)
    block_out = block_out.reshape(1, images, padded, model_width)[:, :, :patches]
    grad_resid, grad_branch, grad_att, branch_sum = branch_back(
        grad_n2.reshape(images, padded, model_width), residual, grad_out, norm_gain[1], w_out
    )
    grad_gain_two, grad_shift_two, grad_out_bias, grad_down_bias = branch_sum
    grad_joint, joint_sum = attend_back(joint, grad_att, patches, head_size)
    grad_emb, embed_sum, grad_image_bias = embed_back(
        grad_joint, w_qkv, embedded, grad_resid, norm_gain[0]
    )
    if tuned_mesh():
        grad_emb, pixels3, up_keep, up_came, down_keep, down_came = tie(
            grad_emb, pixels3, up_keep, up_came, down_keep, down_came
        )
    grad_gain_one, grad_shift_one = embed_sum
    grad_image_bias = grad_image_bias[:, 0]
    grad_qv_bias = joint_sum.reshape(3, model_width)[::2]
    attended = attended.reshape(rows, model_width)
    grad_branch = grad_branch.reshape(rows, model_width)
    share_up = row_share(add_low(up_keep, up_came))
    share_down = row_share(add_low(down_keep, down_came))

    def late_rows(attended, grad_branch, normed1, grad_joint):
        return rows_grad(core, attended, grad_branch), rows_grad(core, normed1, grad_joint)

    late = (
        attended,
        grad_branch,
        normed1.reshape(rows, model_width),
        grad_joint.reshape(rows, 3 * model_width),
    )
    beside_emb = swap_batch(grad_emb, 1)
    if tuned_mesh():
        right1, left1 = (along_line(grad_emb, -1), along_line(grad_emb, 1))
    grad_bias_weight = jnp.einsum("ik,ie->ke", bias_vec, grad_image_bias, precision=highest)
    grad_bias_offset = jnp.sum(grad_image_bias, axis=0)
    grad_bias_vec = jnp.einsum("ie,ke->ik", grad_image_bias, bias_weight, precision=highest)

    def pack(hyper_grads):
        wide = (
            hyper_grads[0],
            hyper_grads[2],
            hyper_grads[4],
            hyper_grads[8],
            hyper_grads[10],
            grad_bias_weight,
        )
        narrow = (
            hyper_grads[1],
            hyper_grads[3],
            hyper_grads[5],
            hyper_grads[6],
            hyper_grads[7],
            hyper_grads[9],
            hyper_grads[11],
            bin_sums,
            bin_squares,
            bin_counts,
            grad_bias_offset,
            jnp.stack([grad_gain_one, grad_gain_two]),
            jnp.stack([grad_shift_one, grad_shift_two]),
            grad_qv_bias,
            grad_out_bias,
            grad_up_bias[0],
            grad_down_bias,
        )
        parts = [block_rows(part) for part in wide]
        thin = [part.reshape(-1, 128) for part in narrow]
        length = sum(part.shape[0] for part in thin)
        thin = jnp.concatenate(thin + [jnp.zeros((-length % 128, 128), jnp.float32)])
        (thin,) = tie(thin)
        parts.append(thin)
        length = sum(part.shape[0] for part in parts)
        parts.append(jnp.zeros((-length % 256, 128), jnp.float32))
        small = jnp.concatenate(parts)
        return wide, narrow, parts, small

    chip_emb = jnp.concatenate([grad_emb, beside_emb])

    def finish_low(grad_vectors):
        far = swap_batch(grad_vectors[images * band_slots :], 1)
        grad_vectors = grad_vectors[: images * band_slots] + far
        grad_vectors = grad_vectors.reshape(images, band_slots, -1)
        return hyper_back((grad_vectors, grad_bias_vec))[0]

    grad_vectors = None
    if tuned_mesh():
        plan = [
            (place(chip, 0, 1, 2, 3), [kernel_weight]),
            (place(spots1, group, group ^ 1, group ^ 2, group ^ 3), weights1),
            (place(spots2, group, group ^ 1, group ^ 2, group ^ 3), weights2),
            (place(spots3, group, group ^ 1, group ^ 2, group ^ 3), weights3),
        ]
        for spots, weights in plan[:2]:
            grad_vectors = band_piece(spots, chip_emb, weights, chip_pixels, grad_vectors)
        grad_vectors, right1, left1, beside_emb, share_up, late = tie(
            grad_vectors, right1, left1, beside_emb, share_up, late
        )
        right2, left2 = (along_line(right1, -1, (1, 2)), along_line(left1, 1, (1, 2)))
        pair_out, pair_qkv = late_rows(*late)
        far = jnp.where((chip & 1) == 0, right1, left1)
        line_emb = [grad_emb, beside_emb, far, swap_batch(far, 1)]
        for spots, weights in plan[2:]:
            grad_vectors = band_piece(spots, chip_emb, weights, chip_pixels, grad_vectors)
        grad_vectors, right2, left2, line_emb, share_down, pair_out, pair_qkv = tie(
            grad_vectors, right2, left2, line_emb, share_down, pair_out, pair_qkv
        )
        half_out, half_qkv = core_sum(*pair_out), core_sum(*pair_qkv)
        share_out_rows, share_qkv = row_share(half_out), row_share(half_qkv)
        end3 = line_ends(jnp.where(chip == 1, right2, left2))
        far = jnp.where(chip < 2, right2, left2)
        line_emb += [far, swap_batch(far, 1)]
        hyper_grads = finish_low(grad_vectors)
        wide, narrow, parts, small = pack(hyper_grads)
        small, block_out, end3, line_emb, chip_emb = tie(
            small, block_out, end3, line_emb, chip_emb
        )
        small_came = swap_batch(part_of(small, 1 - core, 2), 1)
        far = jnp.where(chip == 1, right1, jnp.where(chip == 2, left1, end3))
        line_emb += [far, swap_batch(far, 1)]
        small, small_came, line_emb = tie(small, small_came, line_emb)
        line_pixels = [pixel_block(0, 0), pixel_block(0, 1)] + pixels1 + pixels2 + pixels3
    else:
        for at, weight in enumerate(plain_weight_pieces(kernel_weight)):
            grad_vectors = band_piece(
                place(at, 0, 1, 2, 3), chip_emb, [weight], chip_pixels, grad_vectors
            )
        half_out, half_qkv = [core_sum(*pair) for pair in late_rows(*late)]
        hyper_grads = finish_low(grad_vectors)
        wide, narrow, parts, small = pack(hyper_grads)
        share_out_rows, share_qkv = row_share(half_out), row_share(half_qkv)
        line_emb = plain_line_images(grad_emb, beside_emb)
    halves = 2 if cells % 32 == 0 else 1
    low_turned = line_low.T

    if not tuned_mesh():
        kernel_share = 0.0
        for at in range(0, line_pixels[0].shape[0], 32):
            columns = low_turned[:, at * band_slots : (at + 32) * band_slots]
            found = line_grads(
                columns, cells, [line_pixels[0][at : at + 32]], [line_emb[0][at : at + 32]], 0, 1
            )
            kernel_share += found.astype(jnp.float32)
        kernel_total = lax.psum(kernel_share.astype(jnp.bfloat16), "group").astype(jnp.float32)
        chip_back = pixel_grads(chip_emb, kernels, rates)
        other_back = swap_batch(chip_back[:, images:], 1)
        pixel_grad = join_pixels(
            chip_back[:, :images], other_back, core, patches, cells, pixel_cells, band_slots
        )
        small = lax.psum(small, ("group", "batch"))
        totals = [
            row_both(row_mine(share)) for share in (share_qkv, share_out_rows, share_up, share_down)
        ]
    else:
        small = part_of(small, core, 2) + small_came
        small_came = [swap_batch(part_of(small, chip ^ hop, 4), 2 * hop) for hop in (1, 2, 3)]
        kernel_one = line_grads(low_turned, cells, line_pixels, line_emb, 0, 2)
        mine_up, mine_down = row_mine(share_up), row_mine(share_down)
        kernel_one, line_emb, small_came, mine_up, mine_down, share_qkv, share_out_rows = tie(
            kernel_one, line_emb, small_came, mine_up, mine_down, share_qkv, share_out_rows
        )

        small = sum(small_came, part_of(small, chip, 4))
        small_came = swap_group(small, 1)
        kernel_two = line_grads(low_turned, cells, line_pixels, line_emb, 1, 2)
        kernel_two, small_came = tie(kernel_two, small_came)

        sums = [kernel_one, kernel_two]
        came = sum_out(sums, False)
        small = small + small_came
        small_came = swap_group(small, 2)
        mine_qkv, mine_out = row_mine(share_qkv), row_mine(share_out_rows)
        chip_back = pixel_grads(chip_emb, kernels, rates)
        chip_back, came, small_came, mine_qkv, mine_out = tie(
            chip_back, came, small_came, mine_qkv, mine_out
        )

        sums = sum_in(sums, came, False)
        came = sum_out(sums, True)
        small = small + small_came
        small_came = [swap_batch(small, 2 * hop) for hop in (1, 2, 3)]
        own_back, other_back = chip_back[:, :images], chip_back[:, images:]
        came, own_back, other_back = tie(came, own_back, other_back)

        sums = sum_in(sums, came, True)
        came = share_out(sums, True)
        other_back = swap_batch(other_back, 1)
        came, small_came, other_back = tie(came, small_came, other_back)

        sums = share_in(sums, came, True)
        came = share_out(sums, False)
        small = four_in_order(chip, [small] + small_came)
        small = in_order(core, small, swap_batch(small, 1))
        pixel_grad = join_pixels(
            own_back, other_back, core, patches, cells, pixel_cells, band_slots
        )
        totals = [mine_qkv, mine_out, mine_up, mine_down]
        widths = [mine.shape[1] for mine in totals[:3]]
        wide_mine = jnp.concatenate(totals[:3], axis=1)
        wide_both = row_both(wide_mine)
        ends = [0, widths[0], widths[0] + widths[1], sum(widths)]
        totals = [wide_both[:, ends[at] : ends[at + 1]] for at in range(3)] + [row_both(totals[3])]
    pixel_grad = pixel_grad[None]

    found = []
    at = 0
    for part, like in zip(parts, wide):
        found.append(unblock_rows(small[at : at + part.shape[0]], like.shape[0]))
        at += part.shape[0]
    for like in narrow:
        count = like.size // 128
        found.append(small[at : at + count].reshape(like.shape))
        at += count
    batch_mean, batch_var = bin_stats(found[13], found[14], found[15], patches * pixel_cells)
    if tuned_mesh():
        came, pixel_grad, found, totals, batch_mean, batch_var = tie(
            came, pixel_grad, found, totals, batch_mean, batch_var
        )
        bits = jnp.stack([group & 1, group >> 1])
        kernel_total = assemble(bits, sums[0], came[0], sums[1], came[1])
    return (
        block_out,
        pixel_grad,
        batch_mean,
        batch_var,
        found[0],
        found[6],
        found[1],
        found[7],
        found[2],
        found[8],
        found[9],
        found[10],
        found[3],
        found[11],
        found[4],
        found[12],
        kernel_total,
        found[5],
        found[16],
        found[17],
        found[18],
        totals[0],
        found[19],
        totals[1],
        found[20],
        totals[2],
        found[21],
        totals[3],
        found[22],
    )


def solution(mesh):
    return jax.shard_map(
        per_device,
        mesh=mesh,
        in_specs=(
            P("group", "batch", None, None, None),
            P("group", "batch"),
            P("group", "batch", None),
            P(),
            P(),
            P(),
            P(),
            P(),
            P(),
            P(),
            P(),
            P(),
            P(),
            P(),
            P(),
            P(),
            P(),
            P(),
            P("batch", None, None),
            P(),
            P(),
            P(),
            P(),
            P(),
            P(),
            P(),
            P(),
            P(),
            P(),
            P(),
            P(),
            P("group", "batch", None, None),
        ),
        out_specs=(
            P("group", "batch", None, None),
            P("group", "batch", None, None, None),
            P(),
            P(),
            P(),
            P(),
            P(),
            P(),
            P(),
            P(),
            P(),
            P(),
            P(),
            P(),
            P(),
            P(),
            P("batch", None, None),
            P(),
            P(),
            P(),
            P(),
            P("group", None),
            P(),
            P("group", None),
            P(),
            P("group", None),
            P(),
            P("group", None),
            P(),
        ),
        check_vma=False,
    )
```

```python
from functools import partial

import jax
import jax.numpy as jnp
from jax import lax
from jax.experimental import pallas as pl
from jax.experimental.pallas import tpu as pltpu
from jax.sharding import PartitionSpec as P

HEADS = 12
HHEADS = 4


highest = lax.Precision.HIGHEST
high = lax.Precision.HIGH
stat_eps = 1e-05
hyper_eps = 1e-05
block_eps = 1e-06
wave_scale = 1000.0


def layer_norm(values, gain, shift, epsilon):
    center = values - jnp.mean(values, axis=-1, keepdims=True)
    return (
        center * lax.rsqrt(jnp.mean(center * center, axis=-1, keepdims=True) + epsilon) * gain
        + shift
    )


def norm_parts(values, epsilon):
    center = values - jnp.mean(values, axis=-1, keepdims=True)
    factor = lax.rsqrt(jnp.mean(center * center, axis=-1, keepdims=True) + epsilon)
    return (center * factor, factor)


def norm_back(grad_hat, normal_hat, factor):
    return factor * (
        grad_hat
        - jnp.mean(grad_hat, axis=-1, keepdims=True)
        - normal_hat * jnp.mean(grad_hat * normal_hat, axis=-1, keepdims=True)
    )


def wave_embed(band_wave, model_width):
    half_width = model_width // 2
    ladder = jnp.arange(half_width, dtype=jnp.float32) / half_width
    frequency = 1.0 / 10000.0**ladder
    phase_arg = band_wave[..., None] * wave_scale * frequency
    return jnp.concatenate([jnp.sin(phase_arg), jnp.cos(phase_arg)], axis=-1)


def bin_stats(total_sums, squares, counts, cell_count):
    scaled = jnp.maximum(counts * cell_count, 1.0)
    bin_mean = total_sums / scaled
    bin_var = squares / scaled - bin_mean * bin_mean
    return (bin_mean, bin_var)


def hypernet(params, wave_emb, live_band):
    (
        tokens_w,
        token_b,
        w_in,
        in_bias,
        w_proj,
        proj_bias,
        gain_pair,
        shifts,
        w_expand,
        expand_bias,
        w_reduce,
        reduce_bias,
    ) = params
    image_count = wave_emb.shape[0]
    band_slots = wave_emb.shape[1]
    model_width = wave_emb.shape[2]
    head_count = HHEADS
    head_size = model_width // head_count
    token_rows = tokens_w.shape[0]
    sequence = jnp.concatenate(
        [
            jnp.broadcast_to(tokens_w[None], (image_count, token_rows, model_width)),
            wave_emb,
            jnp.broadcast_to(token_b[None, None, :], (image_count, 1, model_width)),
        ],
        axis=1,
    )
    key_live = (
        jnp.concatenate(
            [
                jnp.ones((image_count, token_rows), jnp.float32),
                live_band,
                jnp.ones((image_count, 1), jnp.float32),
            ],
            axis=1,
        )
        > 0.5
    )
    projected = jnp.einsum("nsk,kj->nsj", sequence, w_in[:, model_width:], precision=high)
    asking = sequence[:, token_rows:]
    query_heads = (
        jnp.einsum("nsk,kj->nsj", asking, w_in[:, :model_width], precision=high) + in_bias[0]
    ).reshape(image_count, -1, head_count, head_size)
    keyed = projected[..., :model_width].reshape(
        image_count, -1, head_count, head_size
    )
    valued = (projected[..., model_width:] + in_bias[1]).reshape(
        image_count, -1, head_count, head_size
    )
    scores = jnp.einsum("nqhd,nkhd->nhqk", query_heads, keyed, precision=high) * head_size ** (
        -0.5
    )
    scores = jnp.where(key_live[:, None, None, :], scores, -1e30)
    attn_probs = jax.nn.softmax(scores, axis=-1)
    mixed_heads = jnp.einsum("nhqk,nkhd->nqhd", attn_probs, valued, precision=high).reshape(
        image_count, -1, model_width
    )
    first_out = layer_norm(
        asking + jnp.einsum("nsk,kj->nsj", mixed_heads, w_proj, precision=high) + proj_bias,
        gain_pair[0],
        shifts[0],
        hyper_eps,
    )
    inner_act = jax.nn.gelu(
        jnp.einsum("nsk,kf->nsf", first_out, w_expand, precision=high) + expand_bias,
        approximate=False,
    )
    second_out = layer_norm(
        first_out + jnp.einsum("nsf,fk->nsk", inner_act, w_reduce, precision=high) + reduce_bias,
        gain_pair[1],
        shifts[1],
        hyper_eps,
    )
    return (
        second_out[:, :band_slots] + wave_emb,
        second_out[:, band_slots],
    )


def swap_group(value, bits):
    return lax.ppermute(value, "group", [(at, at ^ bits) for at in range(4)])


def swap_batch(value, bits):
    count = lax.axis_size("batch")
    return lax.ppermute(value, "batch", [(at, at ^ bits) for at in range(count)])


def tuned_mesh():
    return lax.axis_size("group") == 4 and lax.axis_size("batch") == 8


def same_core():
    count = lax.axis_size("batch")
    return [list(range(0, count, 2)), list(range(1, count, 2))]


def in_order(bit, first, second):
    return jnp.where(
        bit == 0, jnp.concatenate([first, second]), jnp.concatenate([second, first])
    )


def four_in_order(index, pieces):
    low, high = (index & 1, index >> 1)
    return in_order(
        high, in_order(low, pieces[0], pieces[1]), in_order(low, pieces[2], pieces[3])
    )


def part_of(value, index, parts):
    rows = value.shape[0] // parts
    return lax.dynamic_slice_in_dim(value, index * rows, rows)


def tie(*values):
    return lax.optimization_barrier(values)


def along_line(value, step, chips=(0, 1, 2, 3)):
    pairs = [
        (2 * at + core, 2 * (at + step) + core)
        for at in chips
        for core in (0, 1)
        if 0 <= at + step < 4
    ]
    return lax.ppermute(value, "batch", pairs)


def line_ends(value):
    pairs = [(2 + at, at) for at in range(2)] + [(4 + at, 6 + at) for at in range(2)]
    return lax.ppermute(value, "batch", pairs)


def of_chip(chip, values):
    return jnp.array(values, jnp.int32)[chip]


def plain_weight_pieces(weight):
    core = lax.axis_index("batch") & 1
    shards = lax.all_gather(weight, "batch", axis=0)
    shards = shards.reshape((-1, 2) + weight.shape)
    mine = lax.dynamic_index_in_dim(shards, core, 1, keepdims=False)
    return mine.reshape((4, -1) + weight.shape[1:])


def plain_line_cells(pixels):
    pieces, images, rows, lanes = pixels.shape
    chips = lax.axis_size("batch") // 2
    parts = pixels.reshape(pieces, images, rows, chips // pieces, -1)
    parts = parts.transpose(0, 3, 1, 2, 4).reshape(chips, images, rows, -1)
    came = lax.all_to_all(parts, "batch", 0, 0, axis_index_groups=same_core(), tiled=True)
    return [came.reshape((chips * images,) + came.shape[2:])]


def plain_line_images(value, beside):
    both = jnp.concatenate([value, beside])
    return [lax.all_gather(both, "batch", axis=0, axis_index_groups=same_core(), tiled=True)]


def line_rows(low):
    if not tuned_mesh():
        return lax.all_gather(low, "batch", axis=0, axis_index_groups=same_core(), tiled=True)
    return jnp.concatenate([low] + [swap_batch(low, 2 * hop) for hop in (1, 2, 3)])


def core_sum(keep, send):
    return add_low(keep, swap_batch(send, 1))


def row_share(half):
    return lax.psum_scatter(half, "group", scatter_dimension=0, tiled=True)


def row_mine(share):
    return lax.psum(share, "batch", axis_index_groups=same_core())


def row_both(mine):
    core = lax.axis_index("batch") & 1
    return in_order(core, mine, swap_batch(mine, 1)).astype(jnp.float32)


def add_low(left, right):
    return (left.astype(jnp.float32) + right.astype(jnp.float32)).astype(left.dtype)


def ring_sides():
    group = lax.axis_index("group")
    side, level = (group & 1, group >> 1)
    return (1, side), (2, level)


def sum_out(parts, flip):
    order = ring_sides()[::-1] if flip else ring_sides()
    return [swap_group(part_of(part, 1 - bit, 2), way) for part, (way, bit) in zip(parts, order)]


def sum_in(parts, came, flip):
    order = ring_sides()[::-1] if flip else ring_sides()
    return [
        add_low(part_of(part, bit, 2), other)
        for part, other, (way, bit) in zip(parts, came, order)
    ]


def share_out(parts, flip):
    order = ring_sides()[::-1] if flip else ring_sides()
    return [swap_group(part, way) for part, (way, bit) in zip(parts, order)]


def share_in(parts, came, flip):
    order = ring_sides()[::-1] if flip else ring_sides()
    return [in_order(bit, part, other) for part, other, (way, bit) in zip(parts, came, order)]


def block_rows(value):
    rows, lanes = value.shape
    return value.reshape(rows, lanes // 128, 128).transpose(1, 0, 2).reshape(-1, 128)


def unblock_rows(value, rows):
    return value.reshape(-1, rows, 128).transpose(1, 0, 2).reshape(rows, -1)


def grid_params(mebibytes, semantics=1):
    return pltpu.CompilerParams(
        dimension_semantics=("arbitrary",) * semantics,
        vmem_limit_bytes=mebibytes * 1024 * 1024,
    )


def dot_nn(left, right):
    return lax.dot_general(
        left, right, (((1,), (0,)), ((), ())), preferred_element_type=jnp.float32
    )


def dot_nt(left, right):
    return lax.dot_general(
        left, right, (((1,), (1,)), ((), ())), preferred_element_type=jnp.float32
    )


def dot_tn(left, right):
    return lax.dot_general(
        left, right, (((0,), (0,)), ((), ())), preferred_element_type=jnp.float32
    )


def split_kernel(cells, core_ref, pixel_ref, mean_ref, rate_ref, *refs):
    out_refs, scratch = (refs[:2], refs[2:])
    patches, bands, lanes = pixel_ref.shape[1:]
    pieces, _, rows, _ = out_refs[0].shape
    share = lanes // (2 * pieces * cells)
    span = cells * bands
    tile = 128
    columns, tiles = (lanes // tile, -(-rows // tile))
    flat, turned = (scratch[:columns], scratch[columns:])
    values = (pixel_ref[0].astype(jnp.float32) - mean_ref[0]) * rate_ref[0]
    values = values.astype(jnp.bfloat16).astype(jnp.float32).reshape(patches * bands, lanes)
    for column in range(columns):
        flat[column][: patches * bands] = values[:, column * tile : (column + 1) * tile]
        flat[column][patches * bands :] = jnp.zeros(
            (flat[column].shape[0] - patches * bands, tile), jnp.float32
        )
    for band in range(bands):
        for column in range(columns):
            for at in range(tiles):
                block = flat[column][pl.ds(at * tile * bands + band, tile, stride=bands), :]
                turned[at][pl.ds(column * tile * bands + band, tile, stride=bands), :] = block.T
    for out_ref, side in zip(out_refs, (core_ref[0], 1 - core_ref[0])):
        for piece in range(pieces):
            for at in range(tiles):
                count = min(tile, rows - at * tile)
                parts = []
                for one in range(share):
                    first = ((piece * share + one) * 2 + side) * span
                    place = pl.ds(pl.multiple_of(first, span), span)
                    parts.append(turned[at][place, :].T[:count])
                block = parts[0] if share == 1 else jnp.concatenate(parts, axis=1)
                out_ref[piece, 0, at * tile : at * tile + count, :] = block.astype(jnp.bfloat16)


def turn_scratch(rows, bands, lanes):
    tiles = -(-rows // 128)
    return [pltpu.VMEM((tiles * 128 * bands, 128), jnp.float32)] * (lanes // 128) + [
        pltpu.VMEM((lanes * bands, 128), jnp.float32)
    ] * tiles


def split_pixels(pixels, means, rates, core, rows, cells):
    images, bands, patches, lanes = pixels.shape
    wide = bands * lanes // 8
    side = jax.ShapeDtypeStruct((4, images, rows, wide), jnp.bfloat16)
    return pl.pallas_call(
        partial(split_kernel, cells),
        grid_spec=pltpu.PrefetchScalarGridSpec(
            num_scalar_prefetch=1,
            grid=(images,),
            in_specs=[
                pl.BlockSpec((1, patches, bands, lanes), lambda i, core: (i, 0, 0, 0)),
                pl.BlockSpec((1, bands, 1), lambda i, core: (i, 0, 0)),
                pl.BlockSpec((1, bands, 1), lambda i, core: (i, 0, 0)),
            ],
            out_specs=[pl.BlockSpec((4, 1, rows, wide), lambda i, core: (0, i, 0, 0))] * 2,
            scratch_shapes=turn_scratch(rows, bands, lanes),
        ),
        out_shape=[side, side],
        compiler_params=grid_params(40),
        cost_estimate=pl.CostEstimate(flops=1, bytes_accessed=1, transcendentals=0),
        name="split_pixels",
    )(core.reshape(1), pixels.transpose(0, 2, 1, 3), means[:, :, None], rates[:, :, None])


def join_kernel(cells, patches, core_ref, mine_ref, other_ref, out_ref, *scratch):
    rows = mine_ref.shape[2]
    bands, lanes = out_ref.shape[2:]
    pieces = mine_ref.shape[0]
    share = lanes // (2 * pieces * cells)
    span = cells * bands
    tile = 128
    columns, tiles = (lanes // tile, -(-rows // tile))
    flat, turned = (scratch[:columns], scratch[columns:])
    core = core_ref[0]
    for piece in range(pieces):
        for ref, flip in ((mine_ref, core), (other_ref, 1 - core)):
            for one in range(share):
                first = ((piece * share + one) * 2 + flip) * span
                place = pl.ds(pl.multiple_of(first, span), span)
                for at in range(tiles):
                    count = min(tile, rows - at * tile)
                    block = ref[
                        piece, 0, at * tile : at * tile + count, one * span : (one + 1) * span
                    ].astype(jnp.float32)
                    if count < tile:
                        block = jnp.concatenate(
                            [block, jnp.zeros((tile - count, span), jnp.float32)]
                        )
                    turned[at][place, :] = block.T
    for band in range(bands):
        for column in range(columns):
            for at in range(tiles):
                block = turned[at][pl.ds(column * tile * bands + band, tile, stride=bands), :]
                flat[column][pl.ds(at * tile * bands + band, tile, stride=bands), :] = block.T
    for column in range(columns):
        out_ref[0, :, :, column * tile : (column + 1) * tile] = (
            flat[column][: patches * bands].reshape(patches, bands, tile).astype(jnp.bfloat16)
        )


def join_pixels(mine, other, core, patches, cells, lanes, bands):
    pieces, images, rows, wide = mine.shape
    block = pl.BlockSpec((pieces, 1, rows, wide), lambda i, core: (0, i, 0, 0))
    joined = pl.pallas_call(
        partial(join_kernel, cells, patches),
        grid_spec=pltpu.PrefetchScalarGridSpec(
            num_scalar_prefetch=1,
            grid=(images,),
            in_specs=[block, block],
            out_specs=pl.BlockSpec((1, patches, bands, lanes), lambda i, core: (i, 0, 0, 0)),
            scratch_shapes=turn_scratch(rows, bands, lanes),
        ),
        out_shape=jax.ShapeDtypeStruct((images, patches, bands, lanes), jnp.bfloat16),
        compiler_params=grid_params(40),
        cost_estimate=pl.CostEstimate(flops=1, bytes_accessed=1, transcendentals=0),
        name="join_pixels",
    )(core.reshape(1), mine, other)
    return joined.transpose(0, 2, 1, 3)


def embed_kernel(first, count, at_ref, low_ref, *refs):
    weight_refs, pixel_refs = refs[:count], refs[count : count + 2]
    if first:
        total_ref, kernel_ref, weight_now = refs[count + 2 :]
    else:
        before_ref, _, total_ref, kernel_ref, weight_now = refs[count + 2 :]
    share = pixel_refs[0].shape[1]
    images = 2 * share
    cells = weight_now.shape[0]
    bands = pixel_refs[0].shape[3] // cells

    @pl.when(pl.program_id(0) == 0)
    def _():
        if first:
            total_ref[...] = jnp.zeros_like(total_ref)
        else:
            total_ref[...] = before_ref[...]

    for at in range(count):

        @pl.when((pl.program_id(0) == at) | (count == 1))
        def _(at=at):
            weight_now[...] = weight_refs[at][...]

    low = low_ref[...]
    for cell in range(cells):
        made = dot_nt(low, weight_now[cell]).astype(jnp.bfloat16)
        for image in range(images):
            kernel_ref[0, image, cell * bands : (cell + 1) * bands, :] = made[
                image * bands : (image + 1) * bands
            ]
    for image in range(images):
        block = pixel_refs[image // share][0, image % share]
        total_ref[image] += dot_nn(block, kernel_ref[0, image])


def embed_piece(place, low, weights, pixels, total, kernels):
    pieces, share, rows, lanes = pixels[0].shape
    images = 2 * share
    cells, width, depth = weights[0].shape
    step = lanes // (4 * 16)
    count = len(weights)
    steps = max(count, cells // step)
    bands = lanes // (4 * step)
    first = total is None
    any_spec = pl.BlockSpec(memory_space=pl.ANY)
    whole_total = pl.BlockSpec((images, rows, width), lambda t, at: (0, 0, 0))
    if count == 1:
        weight_specs = [pl.BlockSpec((step, width, depth), lambda t, at: (t, 0, 0))]
    else:
        weight_specs = [pl.BlockSpec((step, width, depth), lambda t, at: (0, 0, 0))] * count
    return pl.pallas_call(
        partial(embed_kernel, first, count),
        grid_spec=pltpu.PrefetchScalarGridSpec(
            num_scalar_prefetch=1,
            grid=(steps,),
            in_specs=[pl.BlockSpec(low.shape, lambda t, at: (0, 0))]
            + weight_specs
            + [
                pl.BlockSpec(
                    (1, share, rows, step * bands), lambda t, at: (at[0], 0, 0, at[1 + t])
                ),
            ]
            * 2
            + ([] if first else [whole_total, any_spec]),
            out_specs=[
                whole_total,
                pl.BlockSpec(
                    (1, images, step * bands, width), lambda t, at: (at[0], 0, at[1 + t], 0)
                ),
            ],
            scratch_shapes=[pltpu.VMEM((step, width, depth), jnp.bfloat16)],
        ),
        out_shape=[
            jax.ShapeDtypeStruct((images, rows, width), jnp.float32),
            jax.ShapeDtypeStruct((pieces, images, lanes, width), jnp.bfloat16),
        ],
        input_output_aliases={} if first else {4 + count: 0, 5 + count: 1},
        compiler_params=grid_params(48),
        cost_estimate=pl.CostEstimate(flops=1, bytes_accessed=1, transcendentals=0),
        name="embed_piece",
    )(place, low, *weights, *pixels, *(() if first else (total, kernels)))


def pixel_grad_kernel(grad_ref, kernel_ref, rate_ref, out_ref):
    for image in range(grad_ref.shape[0]):
        out_ref[0, image] = (
            dot_nt(grad_ref[image], kernel_ref[0, image]) * rate_ref[image]
        ).astype(jnp.bfloat16)


def pixel_grads(grads, kernels, rates):
    pieces, images, lanes, width = kernels.shape
    rows = grads.shape[1]
    share = images // 2
    return pl.pallas_call(
        pixel_grad_kernel,
        grid=(2, pieces),
        in_specs=[
            pl.BlockSpec((share, rows, width), lambda i, j: (i, 0, 0)),
            pl.BlockSpec((1, share, lanes, width), lambda i, j: (j, i, 0, 0)),
            pl.BlockSpec((share, 1, lanes), lambda i, j: (i, 0, 0)),
        ],
        out_specs=pl.BlockSpec((1, share, rows, lanes), lambda i, j: (j, i, 0, 0)),
        out_shape=jax.ShapeDtypeStruct((pieces, images, rows, lanes), jnp.bfloat16),
        compiler_params=grid_params(40, 2),
        cost_estimate=pl.CostEstimate(flops=1, bytes_accessed=1, transcendentals=0),
        name="pixel_grads",
    )(grads, kernels, rates)


def line_kernel(half, halves, low_ref, pixel_refs, grad_refs, out_ref, made):
    cells = out_ref.shape[0]
    lanes = pixel_refs[0].shape[2] // halves
    bands = lanes // cells
    columns = slice(half * lanes, (half + 1) * lanes)
    spots = [(ref, at) for ref in grad_refs for at in range(ref.shape[0])]
    image = 0
    for pixel_ref in pixel_refs:
        for at in range(pixel_ref.shape[0]):
            grad_ref, where = spots[image]
            grads = dot_tn(pixel_ref[at, :, columns], grad_ref[where]).astype(jnp.bfloat16)
            for cell in range(cells):
                made[cell, image * bands : (image + 1) * bands, :] = grads[
                    cell * bands : (cell + 1) * bands
                ]
            image += 1

    @pl.loop(0, cells, unroll=4)
    def _(cell):
        out_ref[cell] = dot_nn(low_ref[...], made[cell]).T.astype(jnp.bfloat16)


def line_grads(low_turned, cells, pixels, grads, half, halves):
    step_cells = cells // halves
    depth = low_turned.shape[0]
    width = grads[0].shape[2]
    bands = pixels[0].shape[2] // cells
    images = sum(piece.shape[0] for piece in pixels)
    vmem = pl.BlockSpec(memory_space=pltpu.VMEM)

    def body(*refs):
        pixel_refs = refs[1 : 1 + len(pixels)]
        grad_refs = refs[1 + len(pixels) : 1 + len(pixels) + len(grads)]
        line_kernel(half, halves, refs[0], pixel_refs, grad_refs, *refs[-2:])

    return pl.pallas_call(
        body,
        in_specs=[vmem] * (1 + len(pixels) + len(grads)),
        out_specs=vmem,
        out_shape=jax.ShapeDtypeStruct((step_cells, width, depth), jnp.bfloat16),
        scratch_shapes=[pltpu.VMEM((step_cells, images * bands, width), jnp.bfloat16)],
        compiler_params=pltpu.CompilerParams(vmem_limit_bytes=48 * 1024 * 1024),
        cost_estimate=pl.CostEstimate(flops=1, bytes_accessed=1, transcendentals=0),
        name="line_grads",
    )(low_turned, *pixels, *grads)


def band_kernel(first, count, at_ref, grad_ref, *refs):
    weight_refs, pixel_refs = refs[:count], refs[count : count + 2]
    if first:
        total_ref, weight_now, made = refs[count + 2 :]
    else:
        before_ref, total_ref, weight_now, made = refs[count + 2 :]
    share = pixel_refs[0].shape[1]
    images = 2 * share
    cells = weight_now.shape[0]
    bands = pixel_refs[0].shape[3] // cells

    @pl.when(pl.program_id(0) == 0)
    def _():
        if first:
            total_ref[...] = jnp.zeros_like(total_ref)
        else:
            total_ref[...] = before_ref[...]

    for at in range(count):

        @pl.when((pl.program_id(0) == at) | (count == 1))
        def _(at=at):
            weight_now[...] = weight_refs[at][...]

    for image in range(images):
        block = pixel_refs[image // share][0, image % share]
        grads = dot_tn(block, grad_ref[image]).astype(jnp.bfloat16)
        for cell in range(cells):
            made[cell, image * bands : (image + 1) * bands, :] = grads[
                cell * bands : (cell + 1) * bands
            ]
    for cell in range(cells):
        total_ref[...] += dot_nn(made[cell], weight_now[cell])


def band_piece(place, grads, weights, pixels, total):
    pieces, share, rows, lanes = pixels[0].shape
    images = 2 * share
    cells, width, depth = weights[0].shape
    step = lanes // (4 * 16)
    count = len(weights)
    steps = max(count, cells // step)
    bands = lanes // (4 * step)
    first = total is None
    whole_total = pl.BlockSpec((images * bands, depth), lambda t, at: (0, 0))
    if count == 1:
        weight_specs = [pl.BlockSpec((step, width, depth), lambda t, at: (t, 0, 0))]
    else:
        weight_specs = [pl.BlockSpec((step, width, depth), lambda t, at: (0, 0, 0))] * count
    return pl.pallas_call(
        partial(band_kernel, first, count),
        grid_spec=pltpu.PrefetchScalarGridSpec(
            num_scalar_prefetch=1,
            grid=(steps,),
            in_specs=[pl.BlockSpec(grads.shape, lambda t, at: (0, 0, 0))]
            + weight_specs
            + [
                pl.BlockSpec(
                    (1, share, rows, step * bands), lambda t, at: (at[0], 0, 0, at[1 + t])
                ),
            ]
            * 2
            + ([] if first else [whole_total]),
            out_specs=whole_total,
            scratch_shapes=[
                pltpu.VMEM((step, width, depth), jnp.bfloat16),
                pltpu.VMEM((step, images * bands, width), jnp.bfloat16),
            ],
        ),
        out_shape=jax.ShapeDtypeStruct((images * bands, depth), jnp.float32),
        compiler_params=grid_params(40),
        cost_estimate=pl.CostEstimate(flops=1, bytes_accessed=1, transcendentals=0),
        name="band_piece",
    )(place, grads, *weights, *pixels, *(() if first else (total,)))


def head_probs(patches, query, keyed, mine):
    rows = query.shape[0]
    scores = dot_nt(jnp.where(mine, query, jnp.zeros_like(query)), keyed)
    column = lax.broadcasted_iota(jnp.int32, (1, rows), 1)
    scores = jnp.where(column < patches, scores, -1e30)
    powers = jnp.exp(scores - jnp.max(scores, axis=-1, keepdims=True))
    return powers * (1.0 / jnp.sum(powers, axis=-1, keepdims=True))


def attend_kernel(patches, head_size, joint_ref, out_ref):
    width = out_ref.shape[2]
    pair = 2 * head_size
    lane = lax.broadcasted_iota(jnp.int32, (1, pair), 1)
    scale = jnp.asarray(head_size ** (-0.5), jnp.bfloat16)
    for at in range(0, width, pair):
        query = joint_ref[0, :, at : at + pair] * scale
        keyed = joint_ref[0, :, width + at : width + at + pair]
        valued = joint_ref[0, :, 2 * width + at : 2 * width + at + pair]
        mixed = []
        for head in range(2):
            mine = (lane >= head * head_size) & (lane < (head + 1) * head_size)
            probs = head_probs(patches, query, keyed, mine)
            mixed.append(dot_nn(probs.astype(jnp.bfloat16), valued))
        out_ref[0, :, at : at + pair] = jnp.where(lane < head_size, mixed[0], mixed[1]).astype(
            jnp.bfloat16
        )


def attend(joint, patches, head_size):
    images, rows, triple = joint.shape
    width = triple // 3
    return pl.pallas_call(
        partial(attend_kernel, patches, head_size),
        grid=(images,),
        in_specs=[pl.BlockSpec((1, rows, triple), lambda i: (i, 0, 0))],
        out_specs=pl.BlockSpec((1, rows, width), lambda i: (i, 0, 0)),
        out_shape=jax.ShapeDtypeStruct((images, rows, width), jnp.bfloat16),
        compiler_params=grid_params(24),
        cost_estimate=pl.CostEstimate(flops=1, bytes_accessed=1, transcendentals=0),
        name="attend",
    )(joint)


def attend_back_kernel(patches, head_size, joint_ref, grad_ref, out_ref, sum_ref):
    width = grad_ref.shape[2]
    pair = 2 * head_size
    lane = lax.broadcasted_iota(jnp.int32, (1, pair), 1)
    scale = jnp.asarray(head_size ** (-0.5), jnp.bfloat16)

    @pl.when(pl.program_id(0) == 0)
    def _():
        sum_ref[...] = jnp.zeros_like(sum_ref)

    for at in range(0, width, pair):
        query = joint_ref[0, :, at : at + pair] * scale
        keyed = joint_ref[0, :, width + at : width + at + pair]
        valued = joint_ref[0, :, 2 * width + at : 2 * width + at + pair]
        grads = grad_ref[0, :, at : at + pair]
        none = jnp.zeros_like(grads)
        parts = []
        for head in range(2):
            mine = (lane >= head * head_size) & (lane < (head + 1) * head_size)
            probs = head_probs(patches, query, keyed, mine)
            grad = jnp.where(mine, grads, none)
            to_probs = dot_nt(grad, valued)
            inner = jnp.sum(probs * to_probs, axis=-1, keepdims=True)
            to_scores = (probs * (to_probs - inner)).astype(jnp.bfloat16)
            parts.append(
                (
                    dot_nn(to_scores, jnp.where(mine, keyed, none)),
                    dot_tn(to_scores, jnp.where(mine, query, none)),
                    dot_tn(probs.astype(jnp.bfloat16), grad),
                )
            )
        to_query = (parts[0][0] + parts[1][0]) * (head_size ** (-0.5))
        to_keyed = parts[0][1] + parts[1][1]
        to_valued = parts[0][2] + parts[1][2]
        for slot, value in enumerate((to_query, to_keyed, to_valued)):
            value = value.astype(jnp.bfloat16)
            out_ref[0, :, slot * width + at : slot * width + at + pair] = value
            sum_ref[:, slot * width + at : slot * width + at + pair] += jnp.sum(
                value.astype(jnp.float32), axis=0, keepdims=True
            )


def attend_back(joint, grads, patches, head_size):
    images, rows, triple = joint.shape
    width = triple // 3
    return pl.pallas_call(
        partial(attend_back_kernel, patches, head_size),
        grid=(images,),
        in_specs=[
            pl.BlockSpec((1, rows, triple), lambda i: (i, 0, 0)),
            pl.BlockSpec((1, rows, width), lambda i: (i, 0, 0)),
        ],
        out_specs=[
            pl.BlockSpec((1, rows, triple), lambda i: (i, 0, 0)),
            pl.BlockSpec((1, triple), lambda i: (0, 0)),
        ],
        out_shape=[
            jax.ShapeDtypeStruct((images, rows, triple), jnp.bfloat16),
            jax.ShapeDtypeStruct((1, triple), jnp.float32),
        ],
        compiler_params=grid_params(24),
        cost_estimate=pl.CostEstimate(flops=1, bytes_accessed=1, transcendentals=0),
        name="attend_back",
    )(joint, grads)


def norm_inside(values, epsilon):
    center = values - jnp.mean(values, axis=-1, keepdims=True)
    factor = lax.rsqrt(jnp.mean(center * center, axis=-1, keepdims=True) + epsilon)
    return center * factor, factor


def small_call(kernel, name, grid, in_specs, out_specs, out_shape, scratch=(), limit=40):
    return pl.pallas_call(
        kernel,
        grid=grid,
        in_specs=in_specs,
        out_specs=out_specs,
        out_shape=out_shape,
        scratch_shapes=list(scratch),
        compiler_params=grid_params(limit),
        cost_estimate=pl.CostEstimate(flops=1, bytes_accessed=1, transcendentals=0),
        name=name,
    )


def whole_spec(shape):
    return pl.BlockSpec(shape, lambda i: (0,) * len(shape))


def image_spec(rows, width):
    return pl.BlockSpec((1, rows, width), lambda i: (i, 0, 0))


def joint_kernel(
    own_ref, beside_ref, bias_ref, gain_ref, shift_ref, weight_ref, joint_bias_ref,
    embedded_ref, normed_ref, joint_ref,
):
    embedded = own_ref[0] + beside_ref[0] + bias_ref[0]
    embedded_ref[0] = embedded
    normed = norm_inside(embedded, block_eps)[0] * gain_ref[...] + shift_ref[...]
    normed = normed.astype(jnp.bfloat16)
    normed_ref[0] = normed
    joint = dot_nn(normed, weight_ref[...]) + joint_bias_ref[...]
    joint_ref[0] = joint.astype(jnp.bfloat16)


def make_joint(total, beside, image_bias, gain, shift, weight, joint_bias):
    images, rows, width = beside.shape
    triple = weight.shape[1]
    return small_call(
        joint_kernel,
        "make_joint",
        (images,),
        [image_spec(rows, width)] * 2
        + [image_spec(1, width), whole_spec((1, width)), whole_spec((1, width))]
        + [whole_spec(weight.shape), whole_spec((1, triple))],
        [image_spec(rows, width), image_spec(rows, width), image_spec(rows, triple)],
        [
            jax.ShapeDtypeStruct((images, rows, width), jnp.float32),
            jax.ShapeDtypeStruct((images, rows, width), jnp.bfloat16),
            jax.ShapeDtypeStruct((images, rows, triple), jnp.bfloat16),
        ],
    )(total, beside, image_bias[:, None], gain[None], shift[None], weight, joint_bias[None])


def residual_kernel(
    attended_ref, embedded_ref, weight_ref, bias_ref, gain_ref, shift_ref, residual_ref, normed_ref
):
    branch = dot_nn(attended_ref[0], weight_ref[...]) + bias_ref[...]
    residual = embedded_ref[0] + branch
    residual_ref[0] = residual
    normed = norm_inside(residual, block_eps)[0] * gain_ref[...] + shift_ref[...]
    normed_ref[0] = normed.astype(jnp.bfloat16)


def make_residual(attended, embedded, weight, bias, gain, shift):
    images, rows, width = embedded.shape
    return small_call(
        residual_kernel,
        "make_residual",
        (images,),
        [image_spec(rows, width)] * 2 + [whole_spec(weight.shape)] + [whole_spec((1, width))] * 3,
        [image_spec(rows, width)] * 2,
        [
            jax.ShapeDtypeStruct((images, rows, width), jnp.float32),
            jax.ShapeDtypeStruct((images, rows, width), jnp.bfloat16),
        ],
    )(attended, embedded, weight, bias[None], gain[None], shift[None])


def norm_back_inside(grad, values, gain, epsilon):
    normal, factor = norm_inside(values, epsilon)
    scaled = grad * gain
    back = factor * (
        scaled
        - jnp.mean(scaled, axis=-1, keepdims=True)
        - normal * jnp.mean(scaled * normal, axis=-1, keepdims=True)
    )
    return back, jnp.sum(grad * normal, axis=0, keepdims=True)


def add_rows(out_ref, rows):
    @pl.when(pl.program_id(0) == 0)
    def _():
        out_ref[...] = jnp.zeros_like(out_ref)

    out_ref[...] += jnp.concatenate(rows, axis=0)


def branch_back_kernel(
    grad_ref, residual_ref, out_grad_ref, gain_ref, weight_ref,
    resid_ref, branch_ref, att_ref, sum_ref,
):
    grad = grad_ref[0]
    out_grad = out_grad_ref[0].astype(jnp.float32)
    back, gain_grad = norm_back_inside(grad, residual_ref[0], gain_ref[...], block_eps)
    resid = out_grad + back
    resid_ref[0] = resid
    branch = resid.astype(jnp.bfloat16)
    branch_ref[0] = branch
    att_ref[0] = dot_nt(branch, weight_ref[...]).astype(jnp.bfloat16)
    add_rows(
        sum_ref,
        [
            gain_grad,
            jnp.sum(grad, axis=0, keepdims=True),
            jnp.sum(branch.astype(jnp.float32), axis=0, keepdims=True),
            jnp.sum(out_grad, axis=0, keepdims=True),
        ],
    )


def branch_back(grad, residual, out_grad, gain, weight):
    images, rows, width = residual.shape
    return small_call(
        branch_back_kernel,
        "branch_back",
        (images,),
        [image_spec(rows, width)] * 3 + [whole_spec((1, width)), whole_spec(weight.shape)],
        [image_spec(rows, width)] * 3 + [whole_spec((4, width))],
        [
            jax.ShapeDtypeStruct((images, rows, width), jnp.float32),
            jax.ShapeDtypeStruct((images, rows, width), jnp.bfloat16),
            jax.ShapeDtypeStruct((images, rows, width), jnp.bfloat16),
            jax.ShapeDtypeStruct((4, width), jnp.float32),
        ],
    )(grad, residual, out_grad, gain[None], weight)


def embed_back_kernel(
    joint_ref, weight_ref, embedded_ref, resid_ref, gain_ref, emb_ref, sum_ref, image_ref
):
    grad = dot_nt(joint_ref[0], weight_ref[...])
    back, gain_grad = norm_back_inside(grad, embedded_ref[0], gain_ref[...], block_eps)
    emb = (resid_ref[0] + back).astype(jnp.bfloat16)
    emb_ref[0] = emb
    image_ref[0] = jnp.sum(emb.astype(jnp.float32), axis=0, keepdims=True)
    add_rows(sum_ref, [gain_grad, jnp.sum(grad, axis=0, keepdims=True)])


def embed_back(joint_grad, weight, embedded, resid, gain):
    images, rows, width = embedded.shape
    return small_call(
        embed_back_kernel,
        "embed_back",
        (images,),
        [image_spec(rows, joint_grad.shape[2]), whole_spec(weight.shape)]
        + [image_spec(rows, width)] * 2
        + [whole_spec((1, width))],
        [image_spec(rows, width), whole_spec((2, width)), image_spec(1, width)],
        [
            jax.ShapeDtypeStruct((images, rows, width), jnp.bfloat16),
            jax.ShapeDtypeStruct((2, width), jnp.float32),
            jax.ShapeDtypeStruct((images, 1, width), jnp.float32),
        ],
    )(joint_grad, weight, embedded, resid, gain[None])


def split_rows(core, value, count, keep_ref, send_ref):
    size = value.shape[0] // (2 * count)
    for at in range(count):
        first = value[2 * at * size : (2 * at + 1) * size]
        second = value[(2 * at + 1) * size : (2 * at + 2) * size]
        keep = jnp.where(core == 0, first, second).astype(jnp.bfloat16)
        send = jnp.where(core == 0, second, first).astype(jnp.bfloat16)
        keep_ref[at * size : (at + 1) * size] = keep
        send_ref[at * size : (at + 1) * size] = send


def rows_kernel(count, core_ref, left_ref, right_ref, keep_ref, send_ref, turned):
    @pl.when(pl.program_id(0) == 0)
    def _():
        turned[...] = left_ref[...].T

    split_rows(core_ref[0], dot_nn(turned[...], right_ref[...]), count, keep_ref, send_ref)


def rows_grad(core, left, right, count=4):
    rows, width = left.shape
    columns = right.shape[1]
    part = min(columns, 768)
    half = jax.ShapeDtypeStruct((width // 2, columns), jnp.bfloat16)
    return pl.pallas_call(
        partial(rows_kernel, count),
        grid_spec=pltpu.PrefetchScalarGridSpec(
            num_scalar_prefetch=1,
            grid=(columns // part,),
            in_specs=[
                pl.BlockSpec((rows, width), lambda s, core: (0, 0)),
                pl.BlockSpec((rows, part), lambda s, core: (0, s)),
            ],
            out_specs=[pl.BlockSpec((width // 2, part), lambda s, core: (0, s))] * 2,
            scratch_shapes=[pltpu.VMEM((width, rows), jnp.bfloat16)],
        ),
        out_shape=[half, half],
        compiler_params=grid_params(32),
        cost_estimate=pl.CostEstimate(flops=1, bytes_accessed=1, transcendentals=0),
        name="rows_grad",
    )(core.reshape(1), left, right)


def mlp_kernel(
    core_ref, normed_ref, residual_ref, grad_ref, up_ref, bias_ref, down_ref, down_bias_ref,
    out_ref, back_ref, up_keep_ref, up_send_ref, down_keep_ref, down_send_ref, bias_grad_ref,
    active, to_pre, turned, total,
):
    rows = normed_ref.shape[0]
    part = rows // MLP_PARTS

    @pl.when(pl.program_id(0) == 0)
    def _():
        total[...] = residual_ref[...] + down_bias_ref[...]
        back_ref[...] = jnp.zeros_like(back_ref)
        turned[...] = normed_ref[...].T

    up = up_ref[...]
    down = down_ref[...]
    bias_grad = jnp.zeros(bias_grad_ref.shape, jnp.float32)
    for at in range(0, rows, part):
        span = slice(at, at + part)
        pre = dot_nn(normed_ref[span], up) + bias_ref[...]
        share = 0.5 + 0.5 * lax.erf(pre * (0.5**0.5))
        slope = share + pre * (jnp.exp(-0.5 * pre * pre) * (0.5 / jnp.pi) ** 0.5)
        act = (pre * share).astype(jnp.bfloat16)
        grad = (slope * dot_nt(grad_ref[span], down)).astype(jnp.bfloat16)
        active[span] = act
        to_pre[span] = grad
        total[span] += dot_nn(act, down)
        back_ref[span] += dot_nt(grad, up)
        bias_grad += jnp.sum(grad.astype(jnp.float32), axis=0, keepdims=True)
    bias_grad_ref[...] = bias_grad
    core = core_ref[0]
    split_rows(core, dot_nn(turned[...], to_pre[...]), 4, up_keep_ref, up_send_ref)
    split_rows(core, dot_tn(active[...], grad_ref[...]), 1, down_keep_ref, down_send_ref)

    @pl.when(pl.program_id(0) == pl.num_programs(0) - 1)
    def _():
        out_ref[...] = total[...].astype(jnp.bfloat16)


MLP_PARTS = 2


def mlp(core, normed, residual, grads, up, up_bias, down, down_bias):
    rows, width = normed.shape
    hidden = up.shape[1]
    part = hidden // 4
    whole = pl.BlockSpec((rows, width), lambda s, core: (0, 0))
    columns = pl.BlockSpec((width, part), lambda s, core: (0, s))
    lines = pl.BlockSpec((part, width), lambda s, core: (s, 0))
    vector = pl.BlockSpec((1, part), lambda s, core: (0, s))
    up_half = jax.ShapeDtypeStruct((width // 2, hidden), jnp.bfloat16)
    down_half = jax.ShapeDtypeStruct((hidden // 2, width), jnp.bfloat16)
    return pl.pallas_call(
        mlp_kernel,
        grid_spec=pltpu.PrefetchScalarGridSpec(
            num_scalar_prefetch=1,
            grid=(hidden // part,),
            in_specs=[
                whole, whole, whole, columns, vector, lines,
                pl.BlockSpec((1, width), lambda s, core: (0, 0)),
            ],
            out_specs=[whole, whole]
            + [pl.BlockSpec((width // 2, part), lambda s, core: (0, s))] * 2
            + [pl.BlockSpec((part // 2, width), lambda s, core: (s, 0))] * 2
            + [vector],
            scratch_shapes=[
                pltpu.VMEM((rows, part), jnp.bfloat16),
                pltpu.VMEM((rows, part), jnp.bfloat16),
                pltpu.VMEM((width, rows), jnp.bfloat16),
                pltpu.VMEM((rows, width), jnp.float32),
            ],
        ),
        out_shape=[
            jax.ShapeDtypeStruct((rows, width), jnp.bfloat16),
            jax.ShapeDtypeStruct((rows, width), jnp.float32),
            up_half,
            up_half,
            down_half,
            down_half,
            jax.ShapeDtypeStruct((1, hidden), jnp.float32),
        ],
        compiler_params=grid_params(52),
        cost_estimate=pl.CostEstimate(flops=1, bytes_accessed=1, transcendentals=0),
        name="mlp",
    )(core.reshape(1), normed, residual, grads, up, up_bias[None], down, down_bias[None])


def assemble_kernel(bits_ref, *refs):
    out_ref = refs[-1]
    count = out_ref.shape[0]
    pieces = []
    for part in range(2):
        mine, early, late = refs[part], refs[2 + part], refs[4 + part]
        pieces += [(mine, 0), (mine, count), (early, 0), (late, 0)]
    for at, (ref, first) in enumerate(pieces):

        @pl.when(pl.program_id(0) == at)
        def _(ref=ref, first=first):
            out_ref[...] = ref[first : first + count].astype(jnp.float32)


def assemble(bits, mine, early, late):
    cells, width, depth = mine[0].shape
    half = cells // 2

    def whole(count):
        return pl.BlockSpec((count, width, depth), lambda t, bits: (0, 0, 0))

    return pl.pallas_call(
        assemble_kernel,
        grid_spec=pltpu.PrefetchScalarGridSpec(
            num_scalar_prefetch=1,
            grid=(8,),
            in_specs=[whole(cells)] * 2 + [whole(half)] * 4,
            out_specs=pl.BlockSpec(
                (half, width, depth),
                lambda t, bits: (t // 4 * 4 + (bits[t // 4] ^ (t // 2 % 2)) * 2 + t % 2, 0, 0),
            ),
        ),
        out_shape=jax.ShapeDtypeStruct((4 * cells, width, depth), jnp.float32),
        compiler_params=grid_params(40),
        cost_estimate=pl.CostEstimate(flops=1, bytes_accessed=1, transcendentals=0),
        name="assemble",
    )(bits, *mine, *early, *late)


def per_device(
    pixels,
    band_count,
    band_bin,
    bin_wave,
    run_mean,
    run_var,
    weight_tokens,
    bias_token,
    hyper_in,
    hyper_qv_bias,
    hyper_out,
    hyper_out_bias,
    hyper_gain,
    hyper_shift,
    hyper_up,
    hyper_up_bias,
    hyper_down,
    hyper_down_bias,
    kernel_weight,
    bias_weight,
    bias_offset,
    norm_gain,
    norm_shift,
    w_qkv,
    qv_bias,
    w_out,
    out_bias,
    w_up,
    up_bias,
    w_down,
    down_bias,
    cotangent,
):
    pixel_data = pixels[0]
    images, band_slots, patches, pixel_cells = pixel_data.shape
    bin_total = bin_wave.shape[0]
    model_width = w_qkv.shape[0]
    head_size = model_width // HEADS
    padded = -(-patches // 16) * 16
    rows = images * padded
    cells = kernel_weight.shape[0]
    core = lax.axis_index("batch") & 1
    live_band = (
        lax.broadcasted_iota(jnp.int32, (images, band_slots), 1) < band_count[0][:, None]
    ).astype(jnp.float32)
    bin_onehot = (
        band_bin[0][..., None]
        == lax.broadcasted_iota(jnp.int32, (images, band_slots, bin_total), 2)
    ).astype(jnp.float32)
    chosen = bin_onehot * live_band[..., None]
    run_rstd = lax.rsqrt(run_var + stat_eps)
    band_mean = jnp.einsum("ibn,n->ib", chosen, run_mean, precision=highest)
    band_rstd = jnp.einsum("ibn,n->ib", chosen, run_rstd, precision=highest)
    values32 = pixel_data.astype(jnp.float32)
    band_total = jnp.sum(values32, axis=(2, 3))
    band_square = jnp.sum(values32 * values32, axis=(2, 3))
    bin_sums = jnp.einsum("ib,ibn->n", band_total, chosen, precision=highest)
    bin_squares = jnp.einsum("ib,ibn->n", band_square, chosen, precision=highest)
    bin_counts = jnp.sum(chosen, axis=(0, 1))

    grad_out = jnp.pad(cotangent[0], ((0, 0), (0, padded - patches), (0, 0)))
    band_wave = jnp.einsum("ibn,n->ib", bin_onehot, bin_wave, precision=highest)
    wave_emb = wave_embed(band_wave, hyper_in.shape[0])
    hyper_params = (
        weight_tokens,
        bias_token,
        hyper_in,
        hyper_qv_bias,
        hyper_out,
        hyper_out_bias,
        hyper_gain,
        hyper_shift,
        hyper_up,
        hyper_up_bias,
        hyper_down,
        hyper_down_bias,
    )

    def make_low():
        (band_vec, bias_vec), hyper_back = jax.vjp(
            partial(hypernet, wave_emb=wave_emb, live_band=live_band), hyper_params
        )
        band_low = band_vec.astype(jnp.bfloat16).reshape(images * band_slots, -1)
        return band_low, bias_vec, hyper_back

    def place(piece, *quarters):
        return jnp.stack([jnp.asarray(at, jnp.int32) for at in (piece,) + quarters])

    if not tuned_mesh():
        band_low, bias_vec, hyper_back = make_low()
        chip_low = jnp.concatenate([band_low, swap_batch(band_low, 1)])
        mine, other = split_pixels(pixel_data, band_mean, band_rstd, core, padded, cells)
        chip_pixels = (mine, swap_batch(other, 1))
        total, kernels = (None, None)
        for at, weight in enumerate(plain_weight_pieces(kernel_weight)):
            total, kernels = embed_piece(
                place(at, 0, 1, 2, 3), chip_low, [weight], chip_pixels, total, kernels
            )
        line_pixels = plain_line_cells(jnp.concatenate(chip_pixels, axis=1))
        line_low = lax.all_gather(
            chip_low, "batch", axis=0, axis_index_groups=same_core(), tiled=True
        )
    else:
        group = lax.axis_index("group")
        chip = lax.axis_index("batch") >> 1
        part = cells // 8
        quarter = part_of(kernel_weight, group, 4)

        def sides(block):
            return swap_group(block, 1), swap_group(block, 2)

        def corners(beside, above):
            return swap_group(beside[:part], 2), swap_group(above[part : 2 * part], 1)

        def sides_and_corner(block, beside, above):
            return (
                swap_group(jnp.concatenate([block, above[part : 2 * part]]), 1),
                swap_group(jnp.concatenate([block, beside[:part]]), 2),
            )

        def added(state, piece, weights, shifts):
            spots = place(piece, *[group ^ shift for shift in shifts])
            return embed_piece(spots, chip_low, weights, chip_pixels, *state)

        def pixel_block(hop, half):
            piece = lax.dynamic_index_in_dim(chip_pixels[half], chip ^ hop, 0, keepdims=False)
            return swap_batch(piece, 2 * hop) if hop else piece

        right1, left1 = (along_line(quarter, -1), along_line(quarter, 1))
        band_low, bias_vec, hyper_back = make_low()
        band_low, bias_vec, right1, left1, pixel_data = tie(
            band_low, bias_vec, right1, left1, pixel_data
        )
        block1 = jnp.where(chip == 3, left1, right1)
        right2, left2 = (along_line(right1, -1, (1, 2)), along_line(left1, 1, (1, 2)))
        beside1, above1 = sides(block1)
        mine, other = split_pixels(pixel_data, band_mean, band_rstd, core, padded, cells)
        chip_low = jnp.concatenate([band_low, swap_batch(band_low, 1)])
        mine, other, chip_low, right2, left2, beside1, above1 = tie(
            mine, other, chip_low, right2, left2, beside1, above1
        )
        block2 = jnp.where(chip == 0, right2, jnp.where(chip == 3, left2, left1))
        end3 = line_ends(jnp.where(chip == 1, right2, left2))
        across2, up2 = sides_and_corner(block2, beside1, above1)
        chip_pixels = (mine, swap_batch(other, 1))
        pixels2 = [pixel_block(2, 0)]
        state = embed_piece(
            place(chip, 0, 1, 2, 3), chip_low, [kernel_weight], chip_pixels, None, None
        )
        weights1 = [block1, beside1, above1]
        spots1 = of_chip(chip, [1, 2, 3, 2])
        state = added(state, spots1, weights1, (0, 1, 2))
        state, chip_pixels, end3, across2, up2, pixels2, bin_sums, bin_squares = tie(
            state, chip_pixels, end3, across2, up2, pixels2, bin_sums, bin_squares
        )
        block3 = jnp.where(chip == 1, right2, jnp.where(chip == 2, left2, end3))
        across3, up3 = sides_and_corner(block3, across2, up2)
        pixels2.append(pixel_block(2, 1))
        pixels1 = [pixel_block(1, 0)]
        weights1.append(jnp.concatenate([up2[2 * part :], across2[2 * part :]]))
        state = added(state, spots1, weights1[3:], (3,))
        weights2 = [block2, across2, up2]
        spots2 = of_chip(chip, [2, 0, 1, 1])
        state = added(state, spots2, weights2, (0, 1, 2))
        state, across3, up3, pixels1, pixels2, chip_pixels, grad_out = tie(
            state, across3, up3, pixels1, pixels2, chip_pixels, grad_out
        )
        corner3 = corners(across3, up3)
        pixels1.append(pixel_block(1, 1))
        weights2.append(jnp.concatenate([up3[2 * part :], across3[2 * part :]]))
        state = added(state, spots2, weights2[3:], (3,))
        weights3 = [block3, across3, up3]
        spots3 = of_chip(chip, [3, 3, 0, 0])
        state = added(state, spots3, weights3, (0, 1, 2))
        state, corner3, pixels1, chip_pixels = tie(state, corner3, pixels1, chip_pixels)
        pixels3 = [pixel_block(3, 0)]
        weights3.append(jnp.concatenate(corner3))
        total, kernels = added(state, spots3, weights3[3:], (3,))
    image_bias = jnp.dot(bias_vec, bias_weight, precision=highest) + bias_offset
    total_beside = swap_batch(total[images:], 1)
    joint_bias = jnp.concatenate([qv_bias[0], jnp.zeros_like(qv_bias[0]), qv_bias[1]])
    embedded, normed1, joint = make_joint(
        total, total_beside, image_bias, norm_gain[0], norm_shift[0], w_qkv, joint_bias
    )
    attended = attend(joint, patches, head_size)
    rates = jnp.tile(band_rstd, (1, pixel_cells // 8))
    if tuned_mesh():
        attended, chip_pixels, chip_low, rates = tie(attended, chip_pixels, chip_low, rates)
        line_low = line_rows(chip_low)
    residual, normed2 = make_residual(
        attended, embedded, w_out, out_bias, norm_gain[1], norm_shift[1]
    )
    block_out, grad_n2, up_keep, up_send, down_keep, down_send, grad_up_bias = mlp(
        core,
        normed2.reshape(rows, model_width),
        residual.reshape(rows, model_width),
        grad_out.reshape(rows, model_width),
        w_up,
        up_bias,
        w_down,
        down_bias,
    )
    if tuned_mesh():
        rates_beside = swap_batch(rates, 1)
        grad_n2, pixels3, chip_pixels, line_low, rates_beside, up_send, down_send = tie(
            grad_n2, pixels3, chip_pixels, line_low, rates_beside, up_send, down_send
        )
        pixels3.append(pixel_block(3, 1))
    else:
        rates_beside = swap_batch(rates, 1)
    rates = jnp.concatenate([rates, rates_beside])[:, None, :]
    up_came, down_came = swap_batch(up_send, 1), swap_batch(down_send, 1)
    block_out = block_out.reshape(1, images, padded, model_width)[:, :, :patches]
    grad_resid, grad_branch, grad_att, branch_sum = branch_back(
        grad_n2.reshape(images, padded, model_width), residual, grad_out, norm_gain[1], w_out
    )
    grad_gain_two, grad_shift_two, grad_out_bias, grad_down_bias = branch_sum
    grad_joint, joint_sum = attend_back(joint, grad_att, patches, head_size)
    grad_emb, embed_sum, grad_image_bias = embed_back(
        grad_joint, w_qkv, embedded, grad_resid, norm_gain[0]
    )
    if tuned_mesh():
        grad_emb, pixels3, up_keep, up_came, down_keep, down_came = tie(
            grad_emb, pixels3, up_keep, up_came, down_keep, down_came
        )
    grad_gain_one, grad_shift_one = embed_sum
    grad_image_bias = grad_image_bias[:, 0]
    grad_qv_bias = joint_sum.reshape(3, model_width)[::2]
    attended = attended.reshape(rows, model_width)
    grad_branch = grad_branch.reshape(rows, model_width)
    share_up = row_share(add_low(up_keep, up_came))
    share_down = row_share(add_low(down_keep, down_came))

    def late_rows(attended, grad_branch, normed1, grad_joint):
        return rows_grad(core, attended, grad_branch), rows_grad(core, normed1, grad_joint)

    late = (
        attended,
        grad_branch,
        normed1.reshape(rows, model_width),
        grad_joint.reshape(rows, 3 * model_width),
    )
    beside_emb = swap_batch(grad_emb, 1)
    if tuned_mesh():
        right1, left1 = (along_line(grad_emb, -1), along_line(grad_emb, 1))
    grad_bias_weight = jnp.einsum("ik,ie->ke", bias_vec, grad_image_bias, precision=highest)
    grad_bias_offset = jnp.sum(grad_image_bias, axis=0)
    grad_bias_vec = jnp.einsum("ie,ke->ik", grad_image_bias, bias_weight, precision=highest)

    def pack(hyper_grads):
        wide = (
            hyper_grads[0],
            hyper_grads[2],
            hyper_grads[4],
            hyper_grads[8],
            hyper_grads[10],
            grad_bias_weight,
        )
        narrow = (
            hyper_grads[1],
            hyper_grads[3],
            hyper_grads[5],
            hyper_grads[6],
            hyper_grads[7],
            hyper_grads[9],
            hyper_grads[11],
            bin_sums,
            bin_squares,
            bin_counts,
            grad_bias_offset,
            jnp.stack([grad_gain_one, grad_gain_two]),
            jnp.stack([grad_shift_one, grad_shift_two]),
            grad_qv_bias,
            grad_out_bias,
            grad_up_bias[0],
            grad_down_bias,
        )
        parts = [block_rows(part) for part in wide]
        thin = [part.reshape(-1, 128) for part in narrow]
        length = sum(part.shape[0] for part in thin)
        thin = jnp.concatenate(thin + [jnp.zeros((-length % 128, 128), jnp.float32)])
        (thin,) = tie(thin)
        parts.append(thin)
        length = sum(part.shape[0] for part in parts)
        parts.append(jnp.zeros((-length % 256, 128), jnp.float32))
        small = jnp.concatenate(parts)
        return wide, narrow, parts, small

    chip_emb = jnp.concatenate([grad_emb, beside_emb])

    def finish_low(grad_vectors):
        far = swap_batch(grad_vectors[images * band_slots :], 1)
        grad_vectors = grad_vectors[: images * band_slots] + far
        grad_vectors = grad_vectors.reshape(images, band_slots, -1)
        return hyper_back((grad_vectors, grad_bias_vec))[0]

    grad_vectors = None
    if tuned_mesh():
        plan = [
            (place(chip, 0, 1, 2, 3), [kernel_weight]),
            (place(spots1, group, group ^ 1, group ^ 2, group ^ 3), weights1),
            (place(spots2, group, group ^ 1, group ^ 2, group ^ 3), weights2),
            (place(spots3, group, group ^ 1, group ^ 2, group ^ 3), weights3),
        ]
        pair_out, pair_qkv = late_rows(*late)
        for spots, weights in plan[:2]:
            grad_vectors = band_piece(spots, chip_emb, weights, chip_pixels, grad_vectors)
        grad_vectors, right1, left1, beside_emb, share_up, pair_out, pair_qkv = tie(
            grad_vectors, right1, left1, beside_emb, share_up, pair_out, pair_qkv
        )
        right2, left2 = (along_line(right1, -1, (1, 2)), along_line(left1, 1, (1, 2)))
        half_out, half_qkv = core_sum(*pair_out), core_sum(*pair_qkv)
        far = jnp.where((chip & 1) == 0, right1, left1)
        line_emb = [grad_emb, beside_emb, far, swap_batch(far, 1)]
        for spots, weights in plan[2:]:
            grad_vectors = band_piece(spots, chip_emb, weights, chip_pixels, grad_vectors)
        grad_vectors, right2, left2, line_emb, share_down, half_out, half_qkv = tie(
            grad_vectors, right2, left2, line_emb, share_down, half_out, half_qkv
        )
        share_out_rows, share_qkv = row_share(half_out), row_share(half_qkv)
        end3 = line_ends(jnp.where(chip == 1, right2, left2))
        far = jnp.where(chip < 2, right2, left2)
        line_emb += [far, swap_batch(far, 1)]
        hyper_grads = finish_low(grad_vectors)
        wide, narrow, parts, small = pack(hyper_grads)
        small, block_out, end3, line_emb, chip_emb, share_out_rows, share_qkv = tie(
            small, block_out, end3, line_emb, chip_emb, share_out_rows, share_qkv
        )
        small_came = swap_batch(part_of(small, 1 - core, 2), 1)
        far = jnp.where(chip == 1, right1, jnp.where(chip == 2, left1, end3))
        line_emb += [far, swap_batch(far, 1)]
        small, small_came, line_emb = tie(small, small_came, line_emb)
        line_pixels = [pixel_block(0, 0), pixel_block(0, 1)] + pixels1 + pixels2 + pixels3
    else:
        for at, weight in enumerate(plain_weight_pieces(kernel_weight)):
            grad_vectors = band_piece(
                place(at, 0, 1, 2, 3), chip_emb, [weight], chip_pixels, grad_vectors
            )
        half_out, half_qkv = [core_sum(*pair) for pair in late_rows(*late)]
        hyper_grads = finish_low(grad_vectors)
        wide, narrow, parts, small = pack(hyper_grads)
        share_out_rows, share_qkv = row_share(half_out), row_share(half_qkv)
        line_emb = plain_line_images(grad_emb, beside_emb)
    halves = 2 if cells % 32 == 0 else 1
    low_turned = line_low.T

    if not tuned_mesh():
        kernel_share = 0.0
        for at in range(0, line_pixels[0].shape[0], 32):
            columns = low_turned[:, at * band_slots : (at + 32) * band_slots]
            found = line_grads(
                columns, cells, [line_pixels[0][at : at + 32]], [line_emb[0][at : at + 32]], 0, 1
            )
            kernel_share += found.astype(jnp.float32)
        kernel_total = lax.psum(kernel_share.astype(jnp.bfloat16), "group").astype(jnp.float32)
        chip_back = pixel_grads(chip_emb, kernels, rates)
        other_back = swap_batch(chip_back[:, images:], 1)
        pixel_grad = join_pixels(
            chip_back[:, :images], other_back, core, patches, cells, pixel_cells, band_slots
        )
        small = lax.psum(small, ("group", "batch"))
        totals = [
            row_both(row_mine(share)) for share in (share_qkv, share_out_rows, share_up, share_down)
        ]
    else:
        def small_hop(hop):
            return swap_batch(part_of(small, chip ^ hop, 4), 2 * hop)

        small = part_of(small, core, 2) + small_came
        small_came = [small_hop(1), small_hop(2)]
        kernel_one = line_grads(low_turned, cells, line_pixels, line_emb, 0, 2)
        kernel_one, line_emb, small, small_came = tie(kernel_one, line_emb, small, small_came)

        small_came.append(small_hop(3))
        kernel_two = line_grads(low_turned, cells, line_pixels, line_emb, 1, 2)
        mine_up, mine_out = row_mine(share_up), row_mine(share_out_rows)
        kernel_two, small_came, mine_up, mine_out, share_down, share_qkv = tie(
            kernel_two, small_came, mine_up, mine_out, share_down, share_qkv
        )

        sums = [kernel_one, kernel_two]
        mine_down, mine_qkv = row_mine(share_down), row_mine(share_qkv)
        came = sum_out(sums, False)
        small = sum(small_came, part_of(small, chip, 4))
        small_came = swap_group(small, 1)
        chip_back = pixel_grads(chip_emb, kernels, rates)
        chip_back, came, small_came, mine_down, mine_qkv = tie(
            chip_back, came, small_came, mine_down, mine_qkv
        )

        sums = sum_in(sums, came, False)
        came = sum_out(sums, True)
        small = small + small_came
        small_came = swap_group(small, 2)
        own_back, other_back = chip_back[:, :images], swap_batch(chip_back[:, images:], 1)
        came, own_back, other_back, small_came = tie(came, own_back, other_back, small_came)

        sums = sum_in(sums, came, True)
        came = share_out(sums, True)
        small = small + small_came
        small_came = [swap_batch(small, 2), swap_batch(small, 4)]
        pixel_grad = join_pixels(
            own_back, other_back, core, patches, cells, pixel_cells, band_slots
        )
        came, small, small_came, pixel_grad = tie(came, small, small_came, pixel_grad)

        sums = share_in(sums, came, True)
        early, late = ([value[: cells // 8] for value in sums], [value[cells // 8 :] for value in sums])
        early = share_out(early, False)
        small_came.append(swap_batch(small, 6))
        wide_mine = jnp.concatenate([mine_qkv, mine_out, mine_up], axis=1)
        wide_came, down_came = swap_batch(wide_mine, 1), swap_batch(mine_down, 1)
        early, late, small_came, wide_came, down_came = tie(
            early, late, small_came, wide_came, down_came
        )
        late = share_out(late, False)
        small = four_in_order(chip, [small] + small_came)
        small = in_order(core, small, swap_batch(small, 1))
        widths = [mine.shape[1] for mine in (mine_qkv, mine_out, mine_up)]
        wide_both = in_order(core, wide_mine, wide_came).astype(jnp.float32)
        ends = [0, widths[0], widths[0] + widths[1], sum(widths)]
        totals = [wide_both[:, ends[at] : ends[at + 1]] for at in range(3)]
        totals.append(in_order(core, mine_down, down_came).astype(jnp.float32))
    pixel_grad = pixel_grad[None]

    found = []
    at = 0
    for part, like in zip(parts, wide):
        found.append(unblock_rows(small[at : at + part.shape[0]], like.shape[0]))
        at += part.shape[0]
    for like in narrow:
        count = like.size // 128
        found.append(small[at : at + count].reshape(like.shape))
        at += count
    batch_mean, batch_var = bin_stats(found[13], found[14], found[15], patches * pixel_cells)
    if tuned_mesh():
        late, found, totals, batch_mean, batch_var = tie(
            late, found, totals, batch_mean, batch_var
        )
        bits = jnp.stack([group & 1, group >> 1])
        kernel_total = assemble(bits, sums, early, late)
    return (
        block_out,
        pixel_grad,
        batch_mean,
        batch_var,
        found[0],
        found[6],
        found[1],
        found[7],
        found[2],
        found[8],
        found[9],
        found[10],
        found[3],
        found[11],
        found[4],
        found[12],
        kernel_total,
        found[5],
        found[16],
        found[17],
        found[18],
        totals[0],
        found[19],
        totals[1],
        found[20],
        totals[2],
        found[21],
        totals[3],
        found[22],
    )


def solution(mesh):
    return jax.shard_map(
        per_device,
        mesh=mesh,
        in_specs=(
            P("group", "batch", None, None, None),
            P("group", "batch"),
            P("group", "batch", None),
            P(),
            P(),
            P(),
            P(),
            P(),
            P(),
            P(),
            P(),
            P(),
            P(),
            P(),
            P(),
            P(),
            P(),
            P(),
            P("batch", None, None),
            P(),
            P(),
            P(),
            P(),
            P(),
            P(),
            P(),
            P(),
            P(),
            P(),
            P(),
            P(),
            P("group", "batch", None, None),
        ),
        out_specs=(
            P("group", "batch", None, None),
            P("group", "batch", None, None, None),
            P(),
            P(),
            P(),
            P(),
            P(),
            P(),
            P(),
            P(),
            P(),
            P(),
            P(),
            P(),
            P(),
            P(),
            P("batch", None, None),
            P(),
            P(),
            P(),
            P(),
            P("group", None),
            P(),
            P("group", None),
            P(),
            P("group", None),
            P(),
            P("group", None),
            P(),
        ),
        check_vma=False,
    )
```

```python
from functools import partial

import jax
import jax.numpy as jnp
from jax import lax
from jax.experimental import pallas as pl
from jax.experimental.pallas import tpu as pltpu
from jax.sharding import PartitionSpec as P

HEADS = 12
HHEADS = 4


highest = lax.Precision.HIGHEST
high = lax.Precision.HIGH
stat_eps = 1e-05
hyper_eps = 1e-05
block_eps = 1e-06
wave_scale = 1000.0


def layer_norm(values, gain, shift, epsilon):
    center = values - jnp.mean(values, axis=-1, keepdims=True)
    return (
        center * lax.rsqrt(jnp.mean(center * center, axis=-1, keepdims=True) + epsilon) * gain
        + shift
    )


def norm_parts(values, epsilon):
    center = values - jnp.mean(values, axis=-1, keepdims=True)
    factor = lax.rsqrt(jnp.mean(center * center, axis=-1, keepdims=True) + epsilon)
    return (center * factor, factor)


def norm_back(grad_hat, normal_hat, factor):
    return factor * (
        grad_hat
        - jnp.mean(grad_hat, axis=-1, keepdims=True)
        - normal_hat * jnp.mean(grad_hat * normal_hat, axis=-1, keepdims=True)
    )


def wave_embed(band_wave, model_width):
    half_width = model_width // 2
    ladder = jnp.arange(half_width, dtype=jnp.float32) / half_width
    frequency = 1.0 / 10000.0**ladder
    phase_arg = band_wave[..., None] * wave_scale * frequency
    return jnp.concatenate([jnp.sin(phase_arg), jnp.cos(phase_arg)], axis=-1)


def bin_stats(total_sums, squares, counts, cell_count):
    scaled = jnp.maximum(counts * cell_count, 1.0)
    bin_mean = total_sums / scaled
    bin_var = squares / scaled - bin_mean * bin_mean
    return (bin_mean, bin_var)


def hypernet(params, wave_emb, live_band):
    (
        tokens_w,
        token_b,
        w_in,
        in_bias,
        w_proj,
        proj_bias,
        gain_pair,
        shifts,
        w_expand,
        expand_bias,
        w_reduce,
        reduce_bias,
    ) = params
    image_count = wave_emb.shape[0]
    band_slots = wave_emb.shape[1]
    model_width = wave_emb.shape[2]
    head_count = HHEADS
    head_size = model_width // head_count
    token_rows = tokens_w.shape[0]
    sequence = jnp.concatenate(
        [
            jnp.broadcast_to(tokens_w[None], (image_count, token_rows, model_width)),
            wave_emb,
            jnp.broadcast_to(token_b[None, None, :], (image_count, 1, model_width)),
        ],
        axis=1,
    )
    key_live = (
        jnp.concatenate(
            [
                jnp.ones((image_count, token_rows), jnp.float32),
                live_band,
                jnp.ones((image_count, 1), jnp.float32),
            ],
            axis=1,
        )
        > 0.5
    )
    projected = jnp.einsum("nsk,kj->nsj", sequence, w_in[:, model_width:], precision=high)
    asking = sequence[:, token_rows:]
    query_heads = (
        jnp.einsum("nsk,kj->nsj", asking, w_in[:, :model_width], precision=high) + in_bias[0]
    ).reshape(image_count, -1, head_count, head_size)
    keyed = projected[..., :model_width].reshape(
        image_count, -1, head_count, head_size
    )
    valued = (projected[..., model_width:] + in_bias[1]).reshape(
        image_count, -1, head_count, head_size
    )
    scores = jnp.einsum("nqhd,nkhd->nhqk", query_heads, keyed, precision=high) * head_size ** (
        -0.5
    )
    scores = jnp.where(key_live[:, None, None, :], scores, -1e30)
    attn_probs = jax.nn.softmax(scores, axis=-1)
    mixed_heads = jnp.einsum("nhqk,nkhd->nqhd", attn_probs, valued, precision=high).reshape(
        image_count, -1, model_width
    )
    first_out = layer_norm(
        asking + jnp.einsum("nsk,kj->nsj", mixed_heads, w_proj, precision=high) + proj_bias,
        gain_pair[0],
        shifts[0],
        hyper_eps,
    )
    inner_act = jax.nn.gelu(
        jnp.einsum("nsk,kf->nsf", first_out, w_expand, precision=high) + expand_bias,
        approximate=False,
    )
    second_out = layer_norm(
        first_out + jnp.einsum("nsf,fk->nsk", inner_act, w_reduce, precision=high) + reduce_bias,
        gain_pair[1],
        shifts[1],
        hyper_eps,
    )
    return (
        second_out[:, :band_slots] + wave_emb,
        second_out[:, band_slots],
    )


def swap_group(value, bits):
    return lax.ppermute(value, "group", [(at, at ^ bits) for at in range(4)])


def swap_batch(value, bits):
    count = lax.axis_size("batch")
    return lax.ppermute(value, "batch", [(at, at ^ bits) for at in range(count)])


def tuned_mesh():
    return lax.axis_size("group") == 4 and lax.axis_size("batch") == 8


def same_core():
    count = lax.axis_size("batch")
    return [list(range(0, count, 2)), list(range(1, count, 2))]


def in_order(bit, first, second):
    return jnp.where(
        bit == 0, jnp.concatenate([first, second]), jnp.concatenate([second, first])
    )


def four_in_order(index, pieces):
    low, high = (index & 1, index >> 1)
    return in_order(
        high, in_order(low, pieces[0], pieces[1]), in_order(low, pieces[2], pieces[3])
    )


def part_of(value, index, parts):
    rows = value.shape[0] // parts
    return lax.dynamic_slice_in_dim(value, index * rows, rows)


def tie(*values):
    return lax.optimization_barrier(values)


def along_line(value, step, chips=(0, 1, 2, 3)):
    pairs = [
        (2 * at + core, 2 * (at + step) + core)
        for at in chips
        for core in (0, 1)
        if 0 <= at + step < 4
    ]
    return lax.ppermute(value, "batch", pairs)


def line_ends(value):
    pairs = [(2 + at, at) for at in range(2)] + [(4 + at, 6 + at) for at in range(2)]
    return lax.ppermute(value, "batch", pairs)


def of_chip(chip, values):
    return jnp.array(values, jnp.int32)[chip]


def plain_weight_pieces(weight):
    core = lax.axis_index("batch") & 1
    shards = lax.all_gather(weight, "batch", axis=0)
    shards = shards.reshape((-1, 2) + weight.shape)
    mine = lax.dynamic_index_in_dim(shards, core, 1, keepdims=False)
    return mine.reshape((4, -1) + weight.shape[1:])


def plain_line_cells(pixels):
    pieces, images, rows, lanes = pixels.shape
    chips = lax.axis_size("batch") // 2
    parts = pixels.reshape(pieces, images, rows, chips // pieces, -1)
    parts = parts.transpose(0, 3, 1, 2, 4).reshape(chips, images, rows, -1)
    came = lax.all_to_all(parts, "batch", 0, 0, axis_index_groups=same_core(), tiled=True)
    return [came.reshape((chips * images,) + came.shape[2:])]


def plain_line_images(value, beside):
    both = jnp.concatenate([value, beside])
    return [lax.all_gather(both, "batch", axis=0, axis_index_groups=same_core(), tiled=True)]


def line_rows(low):
    if not tuned_mesh():
        return lax.all_gather(low, "batch", axis=0, axis_index_groups=same_core(), tiled=True)
    return jnp.concatenate([low] + [swap_batch(low, 2 * hop) for hop in (1, 2, 3)])


def core_sum(keep, send):
    return add_low(keep, swap_batch(send, 1))


def row_share(half):
    return lax.psum_scatter(half, "group", scatter_dimension=0, tiled=True)


def row_mine(share):
    return lax.psum(share, "batch", axis_index_groups=same_core())


def row_both(mine):
    core = lax.axis_index("batch") & 1
    return in_order(core, mine, swap_batch(mine, 1)).astype(jnp.float32)


def add_low(left, right):
    return (left.astype(jnp.float32) + right.astype(jnp.float32)).astype(left.dtype)


def ring_sides():
    group = lax.axis_index("group")
    side, level = (group & 1, group >> 1)
    return (1, side), (2, level)


def sum_out(parts, flip):
    order = ring_sides()[::-1] if flip else ring_sides()
    return [swap_group(part_of(part, 1 - bit, 2), way) for part, (way, bit) in zip(parts, order)]


def sum_in(parts, came, flip):
    order = ring_sides()[::-1] if flip else ring_sides()
    return [
        add_low(part_of(part, bit, 2), other)
        for part, other, (way, bit) in zip(parts, came, order)
    ]


def share_out(parts, flip):
    order = ring_sides()[::-1] if flip else ring_sides()
    return [swap_group(part, way) for part, (way, bit) in zip(parts, order)]


def share_in(parts, came, flip):
    order = ring_sides()[::-1] if flip else ring_sides()
    return [in_order(bit, part, other) for part, other, (way, bit) in zip(parts, came, order)]


def block_rows(value):
    rows, lanes = value.shape
    return value.reshape(rows, lanes // 128, 128).transpose(1, 0, 2).reshape(-1, 128)


def unblock_rows(value, rows):
    return value.reshape(-1, rows, 128).transpose(1, 0, 2).reshape(rows, -1)


def grid_params(mebibytes, semantics=1):
    return pltpu.CompilerParams(
        dimension_semantics=("arbitrary",) * semantics,
        vmem_limit_bytes=mebibytes * 1024 * 1024,
    )


def dot_nn(left, right):
    return lax.dot_general(
        left, right, (((1,), (0,)), ((), ())), preferred_element_type=jnp.float32
    )


def dot_nt(left, right):
    return lax.dot_general(
        left, right, (((1,), (1,)), ((), ())), preferred_element_type=jnp.float32
    )


def dot_tn(left, right):
    return lax.dot_general(
        left, right, (((0,), (0,)), ((), ())), preferred_element_type=jnp.float32
    )


def split_kernel(cells, core_ref, pixel_ref, mean_ref, rate_ref, *refs):
    out_refs, scratch = (refs[:2], refs[2:])
    patches, bands, lanes = pixel_ref.shape[1:]
    pieces, _, rows, _ = out_refs[0].shape
    share = lanes // (2 * pieces * cells)
    span = cells * bands
    tile = 128
    columns, tiles = (lanes // tile, -(-rows // tile))
    flat, turned = (scratch[:columns], scratch[columns:])
    values = (pixel_ref[0].astype(jnp.float32) - mean_ref[0]) * rate_ref[0]
    values = values.astype(jnp.bfloat16).astype(jnp.float32).reshape(patches * bands, lanes)
    for column in range(columns):
        flat[column][: patches * bands] = values[:, column * tile : (column + 1) * tile]
        flat[column][patches * bands :] = jnp.zeros(
            (flat[column].shape[0] - patches * bands, tile), jnp.float32
        )
    for band in range(bands):
        for column in range(columns):
            for at in range(tiles):
                block = flat[column][pl.ds(at * tile * bands + band, tile, stride=bands), :]
                turned[at][pl.ds(column * tile * bands + band, tile, stride=bands), :] = block.T
    for out_ref, side in zip(out_refs, (core_ref[0], 1 - core_ref[0])):
        for piece in range(pieces):
            for at in range(tiles):
                count = min(tile, rows - at * tile)
                parts = []
                for one in range(share):
                    first = ((piece * share + one) * 2 + side) * span
                    place = pl.ds(pl.multiple_of(first, span), span)
                    parts.append(turned[at][place, :].T[:count])
                block = parts[0] if share == 1 else jnp.concatenate(parts, axis=1)
                out_ref[piece, 0, at * tile : at * tile + count, :] = block.astype(jnp.bfloat16)


def turn_scratch(rows, bands, lanes):
    tiles = -(-rows // 128)
    return [pltpu.VMEM((tiles * 128 * bands, 128), jnp.float32)] * (lanes // 128) + [
        pltpu.VMEM((lanes * bands, 128), jnp.float32)
    ] * tiles


def split_pixels(pixels, means, rates, core, rows, cells):
    images, bands, patches, lanes = pixels.shape
    wide = bands * lanes // 8
    side = jax.ShapeDtypeStruct((4, images, rows, wide), jnp.bfloat16)
    return pl.pallas_call(
        partial(split_kernel, cells),
        grid_spec=pltpu.PrefetchScalarGridSpec(
            num_scalar_prefetch=1,
            grid=(images,),
            in_specs=[
                pl.BlockSpec((1, patches, bands, lanes), lambda i, core: (i, 0, 0, 0)),
                pl.BlockSpec((1, bands, 1), lambda i, core: (i, 0, 0)),
                pl.BlockSpec((1, bands, 1), lambda i, core: (i, 0, 0)),
            ],
            out_specs=[pl.BlockSpec((4, 1, rows, wide), lambda i, core: (0, i, 0, 0))] * 2,
            scratch_shapes=turn_scratch(rows, bands, lanes),
        ),
        out_shape=[side, side],
        compiler_params=grid_params(40),
        cost_estimate=pl.CostEstimate(flops=1, bytes_accessed=1, transcendentals=0),
        name="split_pixels",
    )(core.reshape(1), pixels.transpose(0, 2, 1, 3), means[:, :, None], rates[:, :, None])


def join_kernel(cells, patches, core_ref, mine_ref, other_ref, out_ref, *scratch):
    rows = mine_ref.shape[2]
    bands, lanes = out_ref.shape[2:]
    pieces = mine_ref.shape[0]
    share = lanes // (2 * pieces * cells)
    span = cells * bands
    tile = 128
    columns, tiles = (lanes // tile, -(-rows // tile))
    flat, turned = (scratch[:columns], scratch[columns:])
    core = core_ref[0]
    for piece in range(pieces):
        for ref, flip in ((mine_ref, core), (other_ref, 1 - core)):
            for one in range(share):
                first = ((piece * share + one) * 2 + flip) * span
                place = pl.ds(pl.multiple_of(first, span), span)
                for at in range(tiles):
                    count = min(tile, rows - at * tile)
                    block = ref[
                        piece, 0, at * tile : at * tile + count, one * span : (one + 1) * span
                    ].astype(jnp.float32)
                    if count < tile:
                        block = jnp.concatenate(
                            [block, jnp.zeros((tile - count, span), jnp.float32)]
                        )
                    turned[at][place, :] = block.T
    for band in range(bands):
        for column in range(columns):
            for at in range(tiles):
                block = turned[at][pl.ds(column * tile * bands + band, tile, stride=bands), :]
                flat[column][pl.ds(at * tile * bands + band, tile, stride=bands), :] = block.T
    for column in range(columns):
        out_ref[0, :, :, column * tile : (column + 1) * tile] = (
            flat[column][: patches * bands].reshape(patches, bands, tile).astype(jnp.bfloat16)
        )


def join_pixels(mine, other, core, patches, cells, lanes, bands):
    pieces, images, rows, wide = mine.shape
    block = pl.BlockSpec((pieces, 1, rows, wide), lambda i, core: (0, i, 0, 0))
    joined = pl.pallas_call(
        partial(join_kernel, cells, patches),
        grid_spec=pltpu.PrefetchScalarGridSpec(
            num_scalar_prefetch=1,
            grid=(images,),
            in_specs=[block, block],
            out_specs=pl.BlockSpec((1, patches, bands, lanes), lambda i, core: (i, 0, 0, 0)),
            scratch_shapes=turn_scratch(rows, bands, lanes),
        ),
        out_shape=jax.ShapeDtypeStruct((images, patches, bands, lanes), jnp.bfloat16),
        compiler_params=grid_params(40),
        cost_estimate=pl.CostEstimate(flops=1, bytes_accessed=1, transcendentals=0),
        name="join_pixels",
    )(core.reshape(1), mine, other)
    return joined.transpose(0, 2, 1, 3)


def embed_kernel(first, count, at_ref, low_ref, *refs):
    weight_refs, pixel_refs = refs[:count], refs[count : count + 2]
    if first:
        total_refs, kernel_ref, weight_now = refs[count + 2 : count + 4], *refs[count + 4 :]
    else:
        before_refs = refs[count + 2 : count + 4]
        total_refs, kernel_ref, weight_now = refs[count + 5 : count + 7], *refs[count + 7 :]
    share = pixel_refs[0].shape[1]
    images = 2 * share
    cells = weight_now.shape[0]
    bands = pixel_refs[0].shape[3] // cells

    @pl.when(pl.program_id(0) == 0)
    def _():
        for at, total_ref in enumerate(total_refs):
            if first:
                total_ref[...] = jnp.zeros_like(total_ref)
            else:
                total_ref[...] = before_refs[at][...]

    for at in range(count):

        @pl.when((pl.program_id(0) == at) | (count == 1))
        def _(at=at):
            weight_now[...] = weight_refs[at][...]

    low = low_ref[...]
    for cell in range(cells):
        made = dot_nt(low, weight_now[cell]).astype(jnp.bfloat16)
        for image in range(images):
            kernel_ref[0, image, cell * bands : (cell + 1) * bands, :] = made[
                image * bands : (image + 1) * bands
            ]
    for image in range(images):
        block = pixel_refs[image // share][0, image % share]
        total_refs[image // share][image % share] += dot_nn(block, kernel_ref[0, image])


def embed_piece(place, low, weights, pixels, total, kernels):
    pieces, share, rows, lanes = pixels[0].shape
    images = 2 * share
    cells, width, depth = weights[0].shape
    step = lanes // (4 * 16)
    count = len(weights)
    steps = max(count, cells // step)
    bands = lanes // (4 * step)
    first = total is None
    any_spec = pl.BlockSpec(memory_space=pl.ANY)
    whole_total = pl.BlockSpec((share, rows, width), lambda t, at: (0, 0, 0))
    if count == 1:
        weight_specs = [pl.BlockSpec((step, width, depth), lambda t, at: (t, 0, 0))]
    else:
        weight_specs = [pl.BlockSpec((step, width, depth), lambda t, at: (0, 0, 0))] * count
    own, other, kernels = pl.pallas_call(
        partial(embed_kernel, first, count),
        grid_spec=pltpu.PrefetchScalarGridSpec(
            num_scalar_prefetch=1,
            grid=(steps,),
            in_specs=[pl.BlockSpec(low.shape, lambda t, at: (0, 0))]
            + weight_specs
            + [
                pl.BlockSpec(
                    (1, share, rows, step * bands), lambda t, at: (at[0], 0, 0, at[1 + t])
                ),
            ]
            * 2
            + ([] if first else [whole_total, whole_total, any_spec]),
            out_specs=[
                whole_total,
                whole_total,
                pl.BlockSpec(
                    (1, images, step * bands, width), lambda t, at: (at[0], 0, at[1 + t], 0)
                ),
            ],
            scratch_shapes=[pltpu.VMEM((step, width, depth), jnp.bfloat16)],
        ),
        out_shape=[
            jax.ShapeDtypeStruct((share, rows, width), jnp.float32),
            jax.ShapeDtypeStruct((share, rows, width), jnp.float32),
            jax.ShapeDtypeStruct((pieces, images, lanes, width), jnp.bfloat16),
        ],
        input_output_aliases={} if first else {4 + count: 0, 5 + count: 1, 6 + count: 2},
        compiler_params=grid_params(48),
        cost_estimate=pl.CostEstimate(flops=1, bytes_accessed=1, transcendentals=0),
        name="embed_piece",
    )(place, low, *weights, *pixels, *(() if first else (*total, kernels)))
    return (own, other), kernels


def pixel_grad_kernel(grad_ref, kernel_ref, rate_ref, out_ref):
    for image in range(grad_ref.shape[0]):
        out_ref[0, image] = (
            dot_nt(grad_ref[image], kernel_ref[0, image]) * rate_ref[image]
        ).astype(jnp.bfloat16)


def pixel_grads(grads, kernels, rates, half):
    pieces, images, lanes, width = kernels.shape
    rows = grads.shape[1]
    share = images // 2
    return pl.pallas_call(
        pixel_grad_kernel,
        grid=(pieces,),
        in_specs=[
            pl.BlockSpec((share, rows, width), lambda j: (half, 0, 0)),
            pl.BlockSpec((1, share, lanes, width), lambda j: (j, half, 0, 0)),
            pl.BlockSpec((share, 1, lanes), lambda j: (half, 0, 0)),
        ],
        out_specs=pl.BlockSpec((1, share, rows, lanes), lambda j: (j, 0, 0, 0)),
        out_shape=jax.ShapeDtypeStruct((pieces, share, rows, lanes), jnp.bfloat16),
        compiler_params=grid_params(40),
        cost_estimate=pl.CostEstimate(flops=1, bytes_accessed=1, transcendentals=0),
        name="pixel_grads",
    )(grads, kernels, rates)


def line_kernel(half, halves, low_ref, pixel_refs, grad_refs, out_ref, made):
    cells = out_ref.shape[0]
    lanes = pixel_refs[0].shape[2] // halves
    bands = lanes // cells
    columns = slice(half * lanes, (half + 1) * lanes)
    spots = [(ref, at) for ref in grad_refs for at in range(ref.shape[0])]
    image = 0
    for pixel_ref in pixel_refs:
        for at in range(pixel_ref.shape[0]):
            grad_ref, where = spots[image]
            grads = dot_tn(pixel_ref[at, :, columns], grad_ref[where]).astype(jnp.bfloat16)
            for cell in range(cells):
                made[cell, image * bands : (image + 1) * bands, :] = grads[
                    cell * bands : (cell + 1) * bands
                ]
            image += 1

    @pl.loop(0, cells, unroll=4)
    def _(cell):
        out_ref[cell] = dot_nn(low_ref[...], made[cell]).T.astype(jnp.bfloat16)


def line_grads(low_turned, cells, pixels, grads, half, halves):
    step_cells = cells // halves
    depth = low_turned.shape[0]
    width = grads[0].shape[2]
    bands = pixels[0].shape[2] // cells
    images = sum(piece.shape[0] for piece in pixels)
    vmem = pl.BlockSpec(memory_space=pltpu.VMEM)

    def body(*refs):
        pixel_refs = refs[1 : 1 + len(pixels)]
        grad_refs = refs[1 + len(pixels) : 1 + len(pixels) + len(grads)]
        line_kernel(half, halves, refs[0], pixel_refs, grad_refs, *refs[-2:])

    return pl.pallas_call(
        body,
        in_specs=[vmem] * (1 + len(pixels) + len(grads)),
        out_specs=vmem,
        out_shape=jax.ShapeDtypeStruct((step_cells, width, depth), jnp.bfloat16),
        scratch_shapes=[pltpu.VMEM((step_cells, images * bands, width), jnp.bfloat16)],
        compiler_params=pltpu.CompilerParams(vmem_limit_bytes=48 * 1024 * 1024),
        cost_estimate=pl.CostEstimate(flops=1, bytes_accessed=1, transcendentals=0),
        name="line_grads",
    )(low_turned, *pixels, *grads)


def band_kernel(first, count, at_ref, grad_ref, *refs):
    weight_refs, pixel_refs = refs[:count], refs[count : count + 2]
    if first:
        total_ref, weight_now, made = refs[count + 2 :]
    else:
        before_ref, total_ref, weight_now, made = refs[count + 2 :]
    share = pixel_refs[0].shape[1]
    images = 2 * share
    cells = weight_now.shape[0]
    bands = pixel_refs[0].shape[3] // cells

    @pl.when(pl.program_id(0) == 0)
    def _():
        if first:
            total_ref[...] = jnp.zeros_like(total_ref)
        else:
            total_ref[...] = before_ref[...]

    for at in range(count):

        @pl.when((pl.program_id(0) == at) | (count == 1))
        def _(at=at):
            weight_now[...] = weight_refs[at][...]

    for image in range(images):
        block = pixel_refs[image // share][0, image % share]
        grads = dot_tn(block, grad_ref[image]).astype(jnp.bfloat16)
        for cell in range(cells):
            made[cell, image * bands : (image + 1) * bands, :] = grads[
                cell * bands : (cell + 1) * bands
            ]
    for cell in range(cells):
        total_ref[...] += dot_nn(made[cell], weight_now[cell])


def band_piece(place, grads, weights, pixels, total):
    pieces, share, rows, lanes = pixels[0].shape
    images = 2 * share
    cells, width, depth = weights[0].shape
    step = lanes // (4 * 16)
    count = len(weights)
    steps = max(count, cells // step)
    bands = lanes // (4 * step)
    first = total is None
    whole_total = pl.BlockSpec((images * bands, depth), lambda t, at: (0, 0))
    if count == 1:
        weight_specs = [pl.BlockSpec((step, width, depth), lambda t, at: (t, 0, 0))]
    else:
        weight_specs = [pl.BlockSpec((step, width, depth), lambda t, at: (0, 0, 0))] * count
    return pl.pallas_call(
        partial(band_kernel, first, count),
        grid_spec=pltpu.PrefetchScalarGridSpec(
            num_scalar_prefetch=1,
            grid=(steps,),
            in_specs=[pl.BlockSpec(grads.shape, lambda t, at: (0, 0, 0))]
            + weight_specs
            + [
                pl.BlockSpec(
                    (1, share, rows, step * bands), lambda t, at: (at[0], 0, 0, at[1 + t])
                ),
            ]
            * 2
            + ([] if first else [whole_total]),
            out_specs=whole_total,
            scratch_shapes=[
                pltpu.VMEM((step, width, depth), jnp.bfloat16),
                pltpu.VMEM((step, images * bands, width), jnp.bfloat16),
            ],
        ),
        out_shape=jax.ShapeDtypeStruct((images * bands, depth), jnp.float32),
        compiler_params=grid_params(40),
        cost_estimate=pl.CostEstimate(flops=1, bytes_accessed=1, transcendentals=0),
        name="band_piece",
    )(place, grads, *weights, *pixels, *(() if first else (total,)))


def head_probs(patches, query, keyed, mine):
    rows = query.shape[0]
    scores = dot_nt(jnp.where(mine, query, jnp.zeros_like(query)), keyed)
    column = lax.broadcasted_iota(jnp.int32, (1, rows), 1)
    scores = jnp.where(column < patches, scores, -1e30)
    powers = jnp.exp(scores - jnp.max(scores, axis=-1, keepdims=True))
    return powers * (1.0 / jnp.sum(powers, axis=-1, keepdims=True))


def attend_kernel(patches, head_size, joint_ref, out_ref):
    width = out_ref.shape[2]
    pair = 2 * head_size
    lane = lax.broadcasted_iota(jnp.int32, (1, pair), 1)
    scale = jnp.asarray(head_size ** (-0.5), jnp.bfloat16)
    for at in range(0, width, pair):
        query = joint_ref[0, :, at : at + pair] * scale
        keyed = joint_ref[0, :, width + at : width + at + pair]
        valued = joint_ref[0, :, 2 * width + at : 2 * width + at + pair]
        mixed = []
        for head in range(2):
            mine = (lane >= head * head_size) & (lane < (head + 1) * head_size)
            probs = head_probs(patches, query, keyed, mine)
            mixed.append(dot_nn(probs.astype(jnp.bfloat16), valued))
        out_ref[0, :, at : at + pair] = jnp.where(lane < head_size, mixed[0], mixed[1]).astype(
            jnp.bfloat16
        )


def attend(joint, patches, head_size):
    images, rows, triple = joint.shape
    width = triple // 3
    return pl.pallas_call(
        partial(attend_kernel, patches, head_size),
        grid=(images,),
        in_specs=[pl.BlockSpec((1, rows, triple), lambda i: (i, 0, 0))],
        out_specs=pl.BlockSpec((1, rows, width), lambda i: (i, 0, 0)),
        out_shape=jax.ShapeDtypeStruct((images, rows, width), jnp.bfloat16),
        compiler_params=grid_params(24),
        cost_estimate=pl.CostEstimate(flops=1, bytes_accessed=1, transcendentals=0),
        name="attend",
    )(joint)


def attend_back_kernel(patches, head_size, joint_ref, grad_ref, out_ref, sum_ref):
    width = grad_ref.shape[2]
    pair = 2 * head_size
    lane = lax.broadcasted_iota(jnp.int32, (1, pair), 1)
    scale = jnp.asarray(head_size ** (-0.5), jnp.bfloat16)

    @pl.when(pl.program_id(0) == 0)
    def _():
        sum_ref[...] = jnp.zeros_like(sum_ref)

    for at in range(0, width, pair):
        query = joint_ref[0, :, at : at + pair] * scale
        keyed = joint_ref[0, :, width + at : width + at + pair]
        valued = joint_ref[0, :, 2 * width + at : 2 * width + at + pair]
        grads = grad_ref[0, :, at : at + pair]
        none = jnp.zeros_like(grads)
        parts = []
        for head in range(2):
            mine = (lane >= head * head_size) & (lane < (head + 1) * head_size)
            probs = head_probs(patches, query, keyed, mine)
            grad = jnp.where(mine, grads, none)
            to_probs = dot_nt(grad, valued)
            inner = jnp.sum(probs * to_probs, axis=-1, keepdims=True)
            to_scores = (probs * (to_probs - inner)).astype(jnp.bfloat16)
            parts.append(
                (
                    dot_nn(to_scores, jnp.where(mine, keyed, none)),
                    dot_tn(to_scores, jnp.where(mine, query, none)),
                    dot_tn(probs.astype(jnp.bfloat16), grad),
                )
            )
        to_query = (parts[0][0] + parts[1][0]) * (head_size ** (-0.5))
        to_keyed = parts[0][1] + parts[1][1]
        to_valued = parts[0][2] + parts[1][2]
        for slot, value in enumerate((to_query, to_keyed, to_valued)):
            value = value.astype(jnp.bfloat16)
            out_ref[0, :, slot * width + at : slot * width + at + pair] = value
            sum_ref[:, slot * width + at : slot * width + at + pair] += jnp.sum(
                value.astype(jnp.float32), axis=0, keepdims=True
            )


def attend_back(joint, grads, patches, head_size):
    images, rows, triple = joint.shape
    width = triple // 3
    return pl.pallas_call(
        partial(attend_back_kernel, patches, head_size),
        grid=(images,),
        in_specs=[
            pl.BlockSpec((1, rows, triple), lambda i: (i, 0, 0)),
            pl.BlockSpec((1, rows, width), lambda i: (i, 0, 0)),
        ],
        out_specs=[
            pl.BlockSpec((1, rows, triple), lambda i: (i, 0, 0)),
            pl.BlockSpec((1, triple), lambda i: (0, 0)),
        ],
        out_shape=[
            jax.ShapeDtypeStruct((images, rows, triple), jnp.bfloat16),
            jax.ShapeDtypeStruct((1, triple), jnp.float32),
        ],
        compiler_params=grid_params(24),
        cost_estimate=pl.CostEstimate(flops=1, bytes_accessed=1, transcendentals=0),
        name="attend_back",
    )(joint, grads)


def norm_inside(values, epsilon):
    center = values - jnp.mean(values, axis=-1, keepdims=True)
    factor = lax.rsqrt(jnp.mean(center * center, axis=-1, keepdims=True) + epsilon)
    return center * factor, factor


def small_call(kernel, name, grid, in_specs, out_specs, out_shape, scratch=(), limit=40):
    return pl.pallas_call(
        kernel,
        grid=grid,
        in_specs=in_specs,
        out_specs=out_specs,
        out_shape=out_shape,
        scratch_shapes=list(scratch),
        compiler_params=grid_params(limit),
        cost_estimate=pl.CostEstimate(flops=1, bytes_accessed=1, transcendentals=0),
        name=name,
    )


def whole_spec(shape):
    return pl.BlockSpec(shape, lambda i: (0,) * len(shape))


def image_spec(rows, width):
    return pl.BlockSpec((1, rows, width), lambda i: (i, 0, 0))


def joint_kernel(
    own_ref, beside_ref, bias_ref, gain_ref, shift_ref, weight_ref, joint_bias_ref,
    embedded_ref, normed_ref, joint_ref,
):
    embedded = own_ref[0] + beside_ref[0] + bias_ref[0]
    embedded_ref[0] = embedded
    normed = norm_inside(embedded, block_eps)[0] * gain_ref[...] + shift_ref[...]
    normed = normed.astype(jnp.bfloat16)
    normed_ref[0] = normed
    joint = dot_nn(normed, weight_ref[...]) + joint_bias_ref[...]
    joint_ref[0] = joint.astype(jnp.bfloat16)


def make_joint(total, beside, image_bias, gain, shift, weight, joint_bias):
    images, rows, width = beside.shape
    triple = weight.shape[1]
    return small_call(
        joint_kernel,
        "make_joint",
        (images,),
        [image_spec(rows, width)] * 2
        + [image_spec(1, width), whole_spec((1, width)), whole_spec((1, width))]
        + [whole_spec(weight.shape), whole_spec((1, triple))],
        [image_spec(rows, width), image_spec(rows, width), image_spec(rows, triple)],
        [
            jax.ShapeDtypeStruct((images, rows, width), jnp.float32),
            jax.ShapeDtypeStruct((images, rows, width), jnp.bfloat16),
            jax.ShapeDtypeStruct((images, rows, triple), jnp.bfloat16),
        ],
    )(total, beside, image_bias[:, None], gain[None], shift[None], weight, joint_bias[None])


def residual_kernel(
    attended_ref, embedded_ref, weight_ref, bias_ref, gain_ref, shift_ref, residual_ref, normed_ref
):
    branch = dot_nn(attended_ref[0], weight_ref[...]) + bias_ref[...]
    residual = embedded_ref[0] + branch
    residual_ref[0] = residual
    normed = norm_inside(residual, block_eps)[0] * gain_ref[...] + shift_ref[...]
    normed_ref[0] = normed.astype(jnp.bfloat16)


def make_residual(attended, embedded, weight, bias, gain, shift):
    images, rows, width = embedded.shape
    return small_call(
        residual_kernel,
        "make_residual",
        (images,),
        [image_spec(rows, width)] * 2 + [whole_spec(weight.shape)] + [whole_spec((1, width))] * 3,
        [image_spec(rows, width)] * 2,
        [
            jax.ShapeDtypeStruct((images, rows, width), jnp.float32),
            jax.ShapeDtypeStruct((images, rows, width), jnp.bfloat16),
        ],
    )(attended, embedded, weight, bias[None], gain[None], shift[None])


def norm_back_inside(grad, values, gain, epsilon):
    normal, factor = norm_inside(values, epsilon)
    scaled = grad * gain
    back = factor * (
        scaled
        - jnp.mean(scaled, axis=-1, keepdims=True)
        - normal * jnp.mean(scaled * normal, axis=-1, keepdims=True)
    )
    return back, jnp.sum(grad * normal, axis=0, keepdims=True)


def add_rows(out_ref, rows):
    @pl.when(pl.program_id(0) == 0)
    def _():
        out_ref[...] = jnp.zeros_like(out_ref)

    out_ref[...] += jnp.concatenate(rows, axis=0)


def branch_back_kernel(
    grad_ref, residual_ref, out_grad_ref, gain_ref, weight_ref,
    resid_ref, branch_ref, att_ref, sum_ref,
):
    grad = grad_ref[0]
    out_grad = out_grad_ref[0].astype(jnp.float32)
    back, gain_grad = norm_back_inside(grad, residual_ref[0], gain_ref[...], block_eps)
    resid = out_grad + back
    resid_ref[0] = resid
    branch = resid.astype(jnp.bfloat16)
    branch_ref[0] = branch
    att_ref[0] = dot_nt(branch, weight_ref[...]).astype(jnp.bfloat16)
    add_rows(
        sum_ref,
        [
            gain_grad,
            jnp.sum(grad, axis=0, keepdims=True),
            jnp.sum(branch.astype(jnp.float32), axis=0, keepdims=True),
            jnp.sum(out_grad, axis=0, keepdims=True),
        ],
    )


def branch_back(grad, residual, out_grad, gain, weight):
    images, rows, width = residual.shape
    return small_call(
        branch_back_kernel,
        "branch_back",
        (images,),
        [image_spec(rows, width)] * 3 + [whole_spec((1, width)), whole_spec(weight.shape)],
        [image_spec(rows, width)] * 3 + [whole_spec((4, width))],
        [
            jax.ShapeDtypeStruct((images, rows, width), jnp.float32),
            jax.ShapeDtypeStruct((images, rows, width), jnp.bfloat16),
            jax.ShapeDtypeStruct((images, rows, width), jnp.bfloat16),
            jax.ShapeDtypeStruct((4, width), jnp.float32),
        ],
    )(grad, residual, out_grad, gain[None], weight)


def embed_back_kernel(
    joint_ref, weight_ref, embedded_ref, resid_ref, gain_ref, emb_ref, sum_ref, image_ref
):
    grad = dot_nt(joint_ref[0], weight_ref[...])
    back, gain_grad = norm_back_inside(grad, embedded_ref[0], gain_ref[...], block_eps)
    emb = (resid_ref[0] + back).astype(jnp.bfloat16)
    emb_ref[0] = emb
    image_ref[0] = jnp.sum(emb.astype(jnp.float32), axis=0, keepdims=True)
    add_rows(sum_ref, [gain_grad, jnp.sum(grad, axis=0, keepdims=True)])


def embed_back(joint_grad, weight, embedded, resid, gain):
    images, rows, width = embedded.shape
    return small_call(
        embed_back_kernel,
        "embed_back",
        (images,),
        [image_spec(rows, joint_grad.shape[2]), whole_spec(weight.shape)]
        + [image_spec(rows, width)] * 2
        + [whole_spec((1, width))],
        [image_spec(rows, width), whole_spec((2, width)), image_spec(1, width)],
        [
            jax.ShapeDtypeStruct((images, rows, width), jnp.bfloat16),
            jax.ShapeDtypeStruct((2, width), jnp.float32),
            jax.ShapeDtypeStruct((images, 1, width), jnp.float32),
        ],
    )(joint_grad, weight, embedded, resid, gain[None])


def split_rows(core, value, count, keep_ref, send_ref):
    size = value.shape[0] // (2 * count)
    for at in range(count):
        first = value[2 * at * size : (2 * at + 1) * size]
        second = value[(2 * at + 1) * size : (2 * at + 2) * size]
        keep = jnp.where(core == 0, first, second).astype(jnp.bfloat16)
        send = jnp.where(core == 0, second, first).astype(jnp.bfloat16)
        keep_ref[at * size : (at + 1) * size] = keep
        send_ref[at * size : (at + 1) * size] = send


def rows_kernel(count, core_ref, left_ref, right_ref, keep_ref, send_ref, turned):
    @pl.when(pl.program_id(0) == 0)
    def _():
        turned[...] = left_ref[...].T

    split_rows(core_ref[0], dot_nn(turned[...], right_ref[...]), count, keep_ref, send_ref)


def rows_grad(core, left, right, count=4):
    rows, width = left.shape
    columns = right.shape[1]
    part = min(columns, 768)
    half = jax.ShapeDtypeStruct((width // 2, columns), jnp.bfloat16)
    return pl.pallas_call(
        partial(rows_kernel, count),
        grid_spec=pltpu.PrefetchScalarGridSpec(
            num_scalar_prefetch=1,
            grid=(columns // part,),
            in_specs=[
                pl.BlockSpec((rows, width), lambda s, core: (0, 0)),
                pl.BlockSpec((rows, part), lambda s, core: (0, s)),
            ],
            out_specs=[pl.BlockSpec((width // 2, part), lambda s, core: (0, s))] * 2,
            scratch_shapes=[pltpu.VMEM((width, rows), jnp.bfloat16)],
        ),
        out_shape=[half, half],
        compiler_params=grid_params(32),
        cost_estimate=pl.CostEstimate(flops=1, bytes_accessed=1, transcendentals=0),
        name="rows_grad",
    )(core.reshape(1), left, right)


def mlp_kernel(
    core_ref, normed_ref, residual_ref, grad_ref, up_ref, bias_ref, down_ref, down_bias_ref,
    out_ref, back_ref, up_keep_ref, up_send_ref, down_keep_ref, down_send_ref, bias_grad_ref,
    active, to_pre, turned, total,
):
    rows = normed_ref.shape[0]
    part = rows // MLP_PARTS

    @pl.when(pl.program_id(0) == 0)
    def _():
        total[...] = residual_ref[...] + down_bias_ref[...]
        back_ref[...] = jnp.zeros_like(back_ref)
        turned[...] = normed_ref[...].T

    up = up_ref[...]
    down = down_ref[...]
    bias_grad = jnp.zeros(bias_grad_ref.shape, jnp.float32)
    for at in range(0, rows, part):
        span = slice(at, at + part)
        pre = dot_nn(normed_ref[span], up) + bias_ref[...]
        share = 0.5 + 0.5 * lax.erf(pre * (0.5**0.5))
        slope = share + pre * (jnp.exp(-0.5 * pre * pre) * (0.5 / jnp.pi) ** 0.5)
        act = (pre * share).astype(jnp.bfloat16)
        grad = (slope * dot_nt(grad_ref[span], down)).astype(jnp.bfloat16)
        active[span] = act
        to_pre[span] = grad
        total[span] += dot_nn(act, down)
        back_ref[span] += dot_nt(grad, up)
        bias_grad += jnp.sum(grad.astype(jnp.float32), axis=0, keepdims=True)
    bias_grad_ref[...] = bias_grad
    core = core_ref[0]
    split_rows(core, dot_nn(turned[...], to_pre[...]), 4, up_keep_ref, up_send_ref)
    split_rows(core, dot_tn(active[...], grad_ref[...]), 1, down_keep_ref, down_send_ref)

    @pl.when(pl.program_id(0) == pl.num_programs(0) - 1)
    def _():
        out_ref[...] = total[...].astype(jnp.bfloat16)


MLP_PARTS = 2


def mlp(core, normed, residual, grads, up, up_bias, down, down_bias):
    rows, width = normed.shape
    hidden = up.shape[1]
    part = hidden // 4
    whole = pl.BlockSpec((rows, width), lambda s, core: (0, 0))
    columns = pl.BlockSpec((width, part), lambda s, core: (0, s))
    lines = pl.BlockSpec((part, width), lambda s, core: (s, 0))
    vector = pl.BlockSpec((1, part), lambda s, core: (0, s))
    up_half = jax.ShapeDtypeStruct((width // 2, hidden), jnp.bfloat16)
    down_half = jax.ShapeDtypeStruct((hidden // 2, width), jnp.bfloat16)
    return pl.pallas_call(
        mlp_kernel,
        grid_spec=pltpu.PrefetchScalarGridSpec(
            num_scalar_prefetch=1,
            grid=(hidden // part,),
            in_specs=[
                whole, whole, whole, columns, vector, lines,
                pl.BlockSpec((1, width), lambda s, core: (0, 0)),
            ],
            out_specs=[whole, whole]
            + [pl.BlockSpec((width // 2, part), lambda s, core: (0, s))] * 2
            + [pl.BlockSpec((part // 2, width), lambda s, core: (s, 0))] * 2
            + [vector],
            scratch_shapes=[
                pltpu.VMEM((rows, part), jnp.bfloat16),
                pltpu.VMEM((rows, part), jnp.bfloat16),
                pltpu.VMEM((width, rows), jnp.bfloat16),
                pltpu.VMEM((rows, width), jnp.float32),
            ],
        ),
        out_shape=[
            jax.ShapeDtypeStruct((rows, width), jnp.bfloat16),
            jax.ShapeDtypeStruct((rows, width), jnp.float32),
            up_half,
            up_half,
            down_half,
            down_half,
            jax.ShapeDtypeStruct((1, hidden), jnp.float32),
        ],
        compiler_params=grid_params(52),
        cost_estimate=pl.CostEstimate(flops=1, bytes_accessed=1, transcendentals=0),
        name="mlp",
    )(core.reshape(1), normed, residual, grads, up, up_bias[None], down, down_bias[None])


def assemble_kernel(bits_ref, *refs):
    out_ref = refs[-1]
    count = out_ref.shape[0]
    pieces = []
    for part in range(2):
        mine, early, late = refs[part], refs[2 + part], refs[4 + part]
        pieces += [(mine, 0), (mine, count), (early, 0), (late, 0)]
    for at, (ref, first) in enumerate(pieces):

        @pl.when(pl.program_id(0) == at)
        def _(ref=ref, first=first):
            out_ref[...] = ref[first : first + count].astype(jnp.float32)


def assemble(bits, mine, early, late):
    cells, width, depth = mine[0].shape
    half = cells // 2

    def whole(count):
        return pl.BlockSpec((count, width, depth), lambda t, bits: (0, 0, 0))

    return pl.pallas_call(
        assemble_kernel,
        grid_spec=pltpu.PrefetchScalarGridSpec(
            num_scalar_prefetch=1,
            grid=(8,),
            in_specs=[whole(cells)] * 2 + [whole(half)] * 4,
            out_specs=pl.BlockSpec(
                (half, width, depth),
                lambda t, bits: (t // 4 * 4 + (bits[t // 4] ^ (t // 2 % 2)) * 2 + t % 2, 0, 0),
            ),
        ),
        out_shape=jax.ShapeDtypeStruct((4 * cells, width, depth), jnp.float32),
        compiler_params=grid_params(40),
        cost_estimate=pl.CostEstimate(flops=1, bytes_accessed=1, transcendentals=0),
        name="assemble",
    )(bits, *mine, *early, *late)


def per_device(
    pixels,
    band_count,
    band_bin,
    bin_wave,
    run_mean,
    run_var,
    weight_tokens,
    bias_token,
    hyper_in,
    hyper_qv_bias,
    hyper_out,
    hyper_out_bias,
    hyper_gain,
    hyper_shift,
    hyper_up,
    hyper_up_bias,
    hyper_down,
    hyper_down_bias,
    kernel_weight,
    bias_weight,
    bias_offset,
    norm_gain,
    norm_shift,
    w_qkv,
    qv_bias,
    w_out,
    out_bias,
    w_up,
    up_bias,
    w_down,
    down_bias,
    cotangent,
):
    pixel_data = pixels[0]
    images, band_slots, patches, pixel_cells = pixel_data.shape
    bin_total = bin_wave.shape[0]
    model_width = w_qkv.shape[0]
    head_size = model_width // HEADS
    padded = -(-patches // 16) * 16
    rows = images * padded
    cells = kernel_weight.shape[0]
    core = lax.axis_index("batch") & 1
    live_band = (
        lax.broadcasted_iota(jnp.int32, (images, band_slots), 1) < band_count[0][:, None]
    ).astype(jnp.float32)
    bin_onehot = (
        band_bin[0][..., None]
        == lax.broadcasted_iota(jnp.int32, (images, band_slots, bin_total), 2)
    ).astype(jnp.float32)
    chosen = bin_onehot * live_band[..., None]
    run_rstd = lax.rsqrt(run_var + stat_eps)
    band_mean = jnp.einsum("ibn,n->ib", chosen, run_mean, precision=highest)
    band_rstd = jnp.einsum("ibn,n->ib", chosen, run_rstd, precision=highest)
    values32 = pixel_data.astype(jnp.float32)
    band_total = jnp.sum(values32, axis=(2, 3))
    band_square = jnp.sum(values32 * values32, axis=(2, 3))
    bin_sums = jnp.einsum("ib,ibn->n", band_total, chosen, precision=highest)
    bin_squares = jnp.einsum("ib,ibn->n", band_square, chosen, precision=highest)
    bin_counts = jnp.sum(chosen, axis=(0, 1))

    grad_out = jnp.pad(cotangent[0], ((0, 0), (0, padded - patches), (0, 0)))
    band_wave = jnp.einsum("ibn,n->ib", bin_onehot, bin_wave, precision=highest)
    wave_emb = wave_embed(band_wave, hyper_in.shape[0])
    hyper_params = (
        weight_tokens,
        bias_token,
        hyper_in,
        hyper_qv_bias,
        hyper_out,
        hyper_out_bias,
        hyper_gain,
        hyper_shift,
        hyper_up,
        hyper_up_bias,
        hyper_down,
        hyper_down_bias,
    )

    def make_low():
        (band_vec, bias_vec), hyper_back = jax.vjp(
            partial(hypernet, wave_emb=wave_emb, live_band=live_band), hyper_params
        )
        band_low = band_vec.astype(jnp.bfloat16).reshape(images * band_slots, -1)
        return band_low, bias_vec, hyper_back

    def place(piece, *quarters):
        return jnp.stack([jnp.asarray(at, jnp.int32) for at in (piece,) + quarters])

    if not tuned_mesh():
        band_low, bias_vec, hyper_back = make_low()
        chip_low = jnp.concatenate([band_low, swap_batch(band_low, 1)])
        mine, other = split_pixels(pixel_data, band_mean, band_rstd, core, padded, cells)
        chip_pixels = (mine, swap_batch(other, 1))
        total, kernels = (None, None)
        for at, weight in enumerate(plain_weight_pieces(kernel_weight)):
            total, kernels = embed_piece(
                place(at, 0, 1, 2, 3), chip_low, [weight], chip_pixels, total, kernels
            )
        line_pixels = plain_line_cells(jnp.concatenate(chip_pixels, axis=1))
        line_low = lax.all_gather(
            chip_low, "batch", axis=0, axis_index_groups=same_core(), tiled=True
        )
    else:
        group = lax.axis_index("group")
        chip = lax.axis_index("batch") >> 1
        part = cells // 8
        quarter = part_of(kernel_weight, group, 4)

        def sides(block):
            return swap_group(block, 1), swap_group(block, 2)

        def corners(beside, above):
            return swap_group(beside[:part], 2), swap_group(above[part : 2 * part], 1)

        def sides_and_corner(block, beside, above):
            return (
                swap_group(jnp.concatenate([block, above[part : 2 * part]]), 1),
                swap_group(jnp.concatenate([block, beside[:part]]), 2),
            )

        def added(state, piece, weights, shifts):
            spots = place(piece, *[group ^ shift for shift in shifts])
            return embed_piece(spots, chip_low, weights, chip_pixels, *state)

        def pixel_block(hop, half):
            piece = lax.dynamic_index_in_dim(chip_pixels[half], chip ^ hop, 0, keepdims=False)
            return swap_batch(piece, 2 * hop) if hop else piece

        right1, left1 = (along_line(quarter, -1), along_line(quarter, 1))
        band_low, bias_vec, hyper_back = make_low()
        band_low, bias_vec, right1, left1, pixel_data = tie(
            band_low, bias_vec, right1, left1, pixel_data
        )
        block1 = jnp.where(chip == 3, left1, right1)
        right2, left2 = (along_line(right1, -1, (1, 2)), along_line(left1, 1, (1, 2)))
        beside1, above1 = sides(block1)
        mine, other = split_pixels(pixel_data, band_mean, band_rstd, core, padded, cells)
        chip_low = jnp.concatenate([band_low, swap_batch(band_low, 1)])
        mine, other, chip_low, right2, left2, beside1, above1 = tie(
            mine, other, chip_low, right2, left2, beside1, above1
        )
        block2 = jnp.where(chip == 0, right2, jnp.where(chip == 3, left2, left1))
        end3 = line_ends(jnp.where(chip == 1, right2, left2))
        across2, up2 = sides_and_corner(block2, beside1, above1)
        chip_pixels = (mine, swap_batch(other, 1))
        pixels2 = [pixel_block(2, 0)]
        state = embed_piece(
            place(chip, 0, 1, 2, 3), chip_low, [kernel_weight], chip_pixels, None, None
        )
        weights1 = [block1, beside1, above1]
        spots1 = of_chip(chip, [1, 2, 3, 2])
        state = added(state, spots1, weights1, (0, 1, 2))
        state, chip_pixels, end3, across2, up2, pixels2, bin_sums, bin_squares = tie(
            state, chip_pixels, end3, across2, up2, pixels2, bin_sums, bin_squares
        )
        block3 = jnp.where(chip == 1, right2, jnp.where(chip == 2, left2, end3))
        across3, up3 = sides_and_corner(block3, across2, up2)
        pixels2.append(pixel_block(2, 1))
        pixels1 = [pixel_block(1, 0)]
        weights1.append(jnp.concatenate([up2[2 * part :], across2[2 * part :]]))
        state = added(state, spots1, weights1[3:], (3,))
        weights2 = [block2, across2, up2]
        spots2 = of_chip(chip, [2, 0, 1, 1])
        state = added(state, spots2, weights2, (0, 1, 2))
        state, across3, up3, pixels1, pixels2, chip_pixels, grad_out = tie(
            state, across3, up3, pixels1, pixels2, chip_pixels, grad_out
        )
        corner3 = corners(across3, up3)
        pixels1.append(pixel_block(1, 1))
        weights2.append(jnp.concatenate([up3[2 * part :], across3[2 * part :]]))
        state = added(state, spots2, weights2[3:], (3,))
        weights3 = [block3, across3, up3]
        spots3 = of_chip(chip, [3, 3, 0, 0])
        state = added(state, spots3, weights3, (0, 1, 2))
        state, corner3, pixels1, chip_pixels = tie(state, corner3, pixels1, chip_pixels)
        pixels3 = [pixel_block(3, 0)]
        weights3.append(jnp.concatenate(corner3))
        total, kernels = added(state, spots3, weights3[3:], (3,))
    image_bias = jnp.dot(bias_vec, bias_weight, precision=highest) + bias_offset
    total, total_other = total
    total_beside = swap_batch(total_other, 1)
    joint_bias = jnp.concatenate([qv_bias[0], jnp.zeros_like(qv_bias[0]), qv_bias[1]])
    embedded, normed1, joint = make_joint(
        total, total_beside, image_bias, norm_gain[0], norm_shift[0], w_qkv, joint_bias
    )
    attended = attend(joint, patches, head_size)
    rates = jnp.tile(band_rstd, (1, pixel_cells // 8))
    if tuned_mesh():
        attended, chip_pixels, chip_low, rates = tie(attended, chip_pixels, chip_low, rates)
        line_low = line_rows(chip_low)
    residual, normed2 = make_residual(
        attended, embedded, w_out, out_bias, norm_gain[1], norm_shift[1]
    )
    block_out, grad_n2, up_keep, up_send, down_keep, down_send, grad_up_bias = mlp(
        core,
        normed2.reshape(rows, model_width),
        residual.reshape(rows, model_width),
        grad_out.reshape(rows, model_width),
        w_up,
        up_bias,
        w_down,
        down_bias,
    )
    if tuned_mesh():
        rates_beside = swap_batch(rates, 1)
        grad_n2, pixels3, chip_pixels, line_low, rates_beside, up_send, down_send = tie(
            grad_n2, pixels3, chip_pixels, line_low, rates_beside, up_send, down_send
        )
        pixels3.append(pixel_block(3, 1))
    else:
        rates_beside = swap_batch(rates, 1)
    rates = jnp.concatenate([rates, rates_beside])[:, None, :]
    up_came, down_came = swap_batch(up_send, 1), swap_batch(down_send, 1)
    block_out = block_out.reshape(1, images, padded, model_width)[:, :, :patches]
    grad_resid, grad_branch, grad_att, branch_sum = branch_back(
        grad_n2.reshape(images, padded, model_width), residual, grad_out, norm_gain[1], w_out
    )
    grad_gain_two, grad_shift_two, grad_out_bias, grad_down_bias = branch_sum
    grad_joint, joint_sum = attend_back(joint, grad_att, patches, head_size)
    grad_emb, embed_sum, grad_image_bias = embed_back(
        grad_joint, w_qkv, embedded, grad_resid, norm_gain[0]
    )
    if tuned_mesh():
        grad_emb, pixels3, up_keep, up_came, down_keep, down_came = tie(
            grad_emb, pixels3, up_keep, up_came, down_keep, down_came
        )
    grad_gain_one, grad_shift_one = embed_sum
    grad_image_bias = grad_image_bias[:, 0]
    grad_qv_bias = joint_sum.reshape(3, model_width)[::2]
    attended = attended.reshape(rows, model_width)
    grad_branch = grad_branch.reshape(rows, model_width)
    beside_emb = swap_batch(grad_emb, 1)
    if tuned_mesh():
        right1, left1 = (along_line(grad_emb, -1), along_line(grad_emb, 1))
    share_up = row_share(add_low(up_keep, up_came))
    share_down = row_share(add_low(down_keep, down_came))

    def late_rows(attended, grad_branch, normed1, grad_joint):
        return rows_grad(core, attended, grad_branch), rows_grad(core, normed1, grad_joint)

    late = (
        attended,
        grad_branch,
        normed1.reshape(rows, model_width),
        grad_joint.reshape(rows, 3 * model_width),
    )
    grad_bias_weight = jnp.einsum("ik,ie->ke", bias_vec, grad_image_bias, precision=highest)
    grad_bias_offset = jnp.sum(grad_image_bias, axis=0)
    grad_bias_vec = jnp.einsum("ie,ke->ik", grad_image_bias, bias_weight, precision=highest)

    def pack(hyper_grads):
        wide = (
            hyper_grads[0],
            hyper_grads[2],
            hyper_grads[4],
            hyper_grads[8],
            hyper_grads[10],
            grad_bias_weight,
        )
        narrow = (
            hyper_grads[1],
            hyper_grads[3],
            hyper_grads[5],
            hyper_grads[6],
            hyper_grads[7],
            hyper_grads[9],
            hyper_grads[11],
            bin_sums,
            bin_squares,
            bin_counts,
            grad_bias_offset,
            jnp.stack([grad_gain_one, grad_gain_two]),
            jnp.stack([grad_shift_one, grad_shift_two]),
            grad_qv_bias,
            grad_out_bias,
            grad_up_bias[0],
            grad_down_bias,
        )
        parts = [block_rows(part) for part in wide]
        thin = [part.reshape(-1, 128) for part in narrow]
        length = sum(part.shape[0] for part in thin)
        thin = jnp.concatenate(thin + [jnp.zeros((-length % 128, 128), jnp.float32)])
        (thin,) = tie(thin)
        parts.append(thin)
        length = sum(part.shape[0] for part in parts)
        parts.append(jnp.zeros((-length % 256, 128), jnp.float32))
        small = jnp.concatenate(parts)
        return wide, narrow, parts, small

    chip_emb = jnp.concatenate([grad_emb, beside_emb])

    def finish_low(grad_vectors):
        far = swap_batch(grad_vectors[images * band_slots :], 1)
        grad_vectors = grad_vectors[: images * band_slots] + far
        grad_vectors = grad_vectors.reshape(images, band_slots, -1)
        return hyper_back((grad_vectors, grad_bias_vec))[0]

    grad_vectors = None
    if tuned_mesh():
        plan = [
            (place(chip, 0, 1, 2, 3), [kernel_weight]),
            (place(spots1, group, group ^ 1, group ^ 2, group ^ 3), weights1),
            (place(spots2, group, group ^ 1, group ^ 2, group ^ 3), weights2),
            (place(spots3, group, group ^ 1, group ^ 2, group ^ 3), weights3),
        ]
        pair_out, pair_qkv = late_rows(*late)
        for spots, weights in plan[:2]:
            grad_vectors = band_piece(spots, chip_emb, weights, chip_pixels, grad_vectors)
        grad_vectors, right1, left1, beside_emb, share_up, pair_out, pair_qkv = tie(
            grad_vectors, right1, left1, beside_emb, share_up, pair_out, pair_qkv
        )
        right2, left2 = (along_line(right1, -1, (1, 2)), along_line(left1, 1, (1, 2)))
        half_out, half_qkv = core_sum(*pair_out), core_sum(*pair_qkv)
        far = jnp.where((chip & 1) == 0, right1, left1)
        line_emb = [grad_emb, beside_emb, far, swap_batch(far, 1)]
        for spots, weights in plan[2:]:
            grad_vectors = band_piece(spots, chip_emb, weights, chip_pixels, grad_vectors)
        grad_vectors, right2, left2, line_emb, share_down, half_out, half_qkv = tie(
            grad_vectors, right2, left2, line_emb, share_down, half_out, half_qkv
        )
        share_out_rows, share_qkv = row_share(half_out), row_share(half_qkv)
        end3 = line_ends(jnp.where(chip == 1, right2, left2))
        far = jnp.where(chip < 2, right2, left2)
        line_emb += [far, swap_batch(far, 1)]
        hyper_grads = finish_low(grad_vectors)
        wide, narrow, parts, small = pack(hyper_grads)
        line_pixels = [pixel_block(0, 0), pixel_block(0, 1)]
        small, end3, line_emb, line_pixels = tie(small, end3, line_emb, line_pixels)
        small_came = swap_batch(part_of(small, 1 - core, 2), 1)
        far = jnp.where(chip == 1, right1, jnp.where(chip == 2, left1, end3))
        line_emb += [far, swap_batch(far, 1)]
        small, small_came, line_emb = tie(small, small_came, line_emb)
        line_pixels += pixels1 + pixels2 + pixels3
    else:
        for at, weight in enumerate(plain_weight_pieces(kernel_weight)):
            grad_vectors = band_piece(
                place(at, 0, 1, 2, 3), chip_emb, [weight], chip_pixels, grad_vectors
            )
        half_out, half_qkv = [core_sum(*pair) for pair in late_rows(*late)]
        hyper_grads = finish_low(grad_vectors)
        wide, narrow, parts, small = pack(hyper_grads)
        share_out_rows, share_qkv = row_share(half_out), row_share(half_qkv)
        line_emb = plain_line_images(grad_emb, beside_emb)
    halves = 2 if cells % 32 == 0 else 1
    low_turned = line_low.T

    if not tuned_mesh():
        kernel_share = 0.0
        for at in range(0, line_pixels[0].shape[0], 32):
            columns = low_turned[:, at * band_slots : (at + 32) * band_slots]
            found = line_grads(
                columns, cells, [line_pixels[0][at : at + 32]], [line_emb[0][at : at + 32]], 0, 1
            )
            kernel_share += found.astype(jnp.float32)
        kernel_total = lax.psum(kernel_share.astype(jnp.bfloat16), "group").astype(jnp.float32)
        own_back = pixel_grads(chip_emb, kernels, rates, 0)
        other_back = swap_batch(pixel_grads(chip_emb, kernels, rates, 1), 1)
        pixel_grad = join_pixels(
            own_back, other_back, core, patches, cells, pixel_cells, band_slots
        )
        small = lax.psum(small, ("group", "batch"))
        totals = [
            row_both(row_mine(share)) for share in (share_qkv, share_out_rows, share_up, share_down)
        ]
    else:
        def small_hop(hop):
            return swap_batch(part_of(small, chip ^ hop, 4), 2 * hop)

        small = part_of(small, core, 2) + small_came
        small_came = [small_hop(1), small_hop(2)]
        kernel_one = line_grads(low_turned, cells, line_pixels, line_emb, 0, 2)
        kernel_one, line_emb, small, small_came, share_out_rows, share_qkv = tie(
            kernel_one, line_emb, small, small_came, share_out_rows, share_qkv
        )

        small_came.append(small_hop(3))
        kernel_two = line_grads(low_turned, cells, line_pixels, line_emb, 1, 2)
        kernel_two, small_came = tie(kernel_two, small_came)

        sums = [kernel_one, kernel_two]
        mine_qkv, mine_out, mine_up, mine_down = [
            row_mine(share) for share in (share_qkv, share_out_rows, share_up, share_down)
        ]
        came = sum_out(sums, False)
        small = sum(small_came, part_of(small, chip, 4))
        small_came = swap_group(small, 1)
        own_back = pixel_grads(chip_emb, kernels, rates, 0)
        other_back = pixel_grads(chip_emb, kernels, rates, 1)
        own_back, other_back, came, small_came, mine_qkv, mine_out, mine_up, mine_down = tie(
            own_back, other_back, came, small_came, mine_qkv, mine_out, mine_up, mine_down
        )

        sums = sum_in(sums, came, False)
        came = sum_out(sums, True)
        small = small + small_came
        small_came = swap_group(small, 2)
        other_back = swap_batch(other_back, 1)
        wide_mine = jnp.concatenate([mine_qkv, mine_out, mine_up], axis=1)
        wide_came = swap_batch(wide_mine, 1)
        came, other_back, small_came, wide_came, block_out = tie(
            came, other_back, small_came, wide_came, block_out
        )

        sums = sum_in(sums, came, True)
        came = share_out(sums, True)
        small = small + small_came
        small_came = [swap_batch(small, 2), swap_batch(small, 4)]
        pixel_grad = join_pixels(
            own_back, other_back, core, patches, cells, pixel_cells, band_slots
        )
        down_came = swap_batch(mine_down, 1)
        came, small, small_came, pixel_grad, down_came = tie(
            came, small, small_came, pixel_grad, down_came
        )

        sums = share_in(sums, came, True)
        early, late = ([value[: cells // 8] for value in sums], [value[cells // 8 :] for value in sums])
        early = share_out(early, False)
        small_came.append(swap_batch(small, 6))
        widths = [mine.shape[1] for mine in (mine_qkv, mine_out, mine_up)]
        wide_both = in_order(core, wide_mine, wide_came).astype(jnp.float32)
        ends = [0, widths[0], widths[0] + widths[1], sum(widths)]
        totals = [wide_both[:, ends[at] : ends[at + 1]] for at in range(3)]
        totals.append(in_order(core, mine_down, down_came).astype(jnp.float32))
        early, late, small_came, totals = tie(early, late, small_came, totals)
        late = share_out(late, False)
        small = four_in_order(chip, [small] + small_came)
        small = in_order(core, small, swap_batch(small, 1))
    pixel_grad = pixel_grad[None]

    found = []
    at = 0
    for part, like in zip(parts, wide):
        found.append(unblock_rows(small[at : at + part.shape[0]], like.shape[0]))
        at += part.shape[0]
    for like in narrow:
        count = like.size // 128
        found.append(small[at : at + count].reshape(like.shape))
        at += count
    batch_mean, batch_var = bin_stats(found[13], found[14], found[15], patches * pixel_cells)
    if tuned_mesh():
        late, found, batch_mean, batch_var = tie(late, found, batch_mean, batch_var)
        bits = jnp.stack([group & 1, group >> 1])
        kernel_total = assemble(bits, sums, early, late)
    return (
        block_out,
        pixel_grad,
        batch_mean,
        batch_var,
        found[0],
        found[6],
        found[1],
        found[7],
        found[2],
        found[8],
        found[9],
        found[10],
        found[3],
        found[11],
        found[4],
        found[12],
        kernel_total,
        found[5],
        found[16],
        found[17],
        found[18],
        totals[0],
        found[19],
        totals[1],
        found[20],
        totals[2],
        found[21],
        totals[3],
        found[22],
    )


def solution(mesh):
    return jax.shard_map(
        per_device,
        mesh=mesh,
        in_specs=(
            P("group", "batch", None, None, None),
            P("group", "batch"),
            P("group", "batch", None),
            P(),
            P(),
            P(),
            P(),
            P(),
            P(),
            P(),
            P(),
            P(),
            P(),
            P(),
            P(),
            P(),
            P(),
            P(),
            P("batch", None, None),
            P(),
            P(),
            P(),
            P(),
            P(),
            P(),
            P(),
            P(),
            P(),
            P(),
            P(),
            P(),
            P("group", "batch", None, None),
        ),
        out_specs=(
            P("group", "batch", None, None),
            P("group", "batch", None, None, None),
            P(),
            P(),
            P(),
            P(),
            P(),
            P(),
            P(),
            P(),
            P(),
            P(),
            P(),
            P(),
            P(),
            P(),
            P("batch", None, None),
            P(),
            P(),
            P(),
            P(),
            P("group", None),
            P(),
            P("group", None),
            P(),
            P("group", None),
            P(),
            P("group", None),
            P(),
        ),
        check_vma=False,
    )
```

```python
from functools import partial

import jax
import jax.numpy as jnp
from jax import lax
from jax.experimental import pallas as pl
from jax.experimental.pallas import tpu as pltpu
from jax.sharding import PartitionSpec as P

HEADS = 12
HHEADS = 4


highest = lax.Precision.HIGHEST
high = lax.Precision.HIGH
stat_eps = 1e-05
hyper_eps = 1e-05
block_eps = 1e-06
wave_scale = 1000.0


def layer_norm(values, gain, shift, epsilon):
    center = values - jnp.mean(values, axis=-1, keepdims=True)
    return (
        center * lax.rsqrt(jnp.mean(center * center, axis=-1, keepdims=True) + epsilon) * gain
        + shift
    )


def norm_parts(values, epsilon):
    center = values - jnp.mean(values, axis=-1, keepdims=True)
    factor = lax.rsqrt(jnp.mean(center * center, axis=-1, keepdims=True) + epsilon)
    return (center * factor, factor)


def norm_back(grad_hat, normal_hat, factor):
    return factor * (
        grad_hat
        - jnp.mean(grad_hat, axis=-1, keepdims=True)
        - normal_hat * jnp.mean(grad_hat * normal_hat, axis=-1, keepdims=True)
    )


def wave_embed(band_wave, model_width):
    half_width = model_width // 2
    ladder = jnp.arange(half_width, dtype=jnp.float32) / half_width
    frequency = 1.0 / 10000.0**ladder
    phase_arg = band_wave[..., None] * wave_scale * frequency
    return jnp.concatenate([jnp.sin(phase_arg), jnp.cos(phase_arg)], axis=-1)


def bin_stats(total_sums, squares, counts, cell_count):
    scaled = jnp.maximum(counts * cell_count, 1.0)
    bin_mean = total_sums / scaled
    bin_var = squares / scaled - bin_mean * bin_mean
    return (bin_mean, bin_var)


def hypernet(params, wave_emb, live_band):
    (
        tokens_w,
        token_b,
        w_in,
        in_bias,
        w_proj,
        proj_bias,
        gain_pair,
        shifts,
        w_expand,
        expand_bias,
        w_reduce,
        reduce_bias,
    ) = params
    image_count = wave_emb.shape[0]
    band_slots = wave_emb.shape[1]
    model_width = wave_emb.shape[2]
    head_count = HHEADS
    head_size = model_width // head_count
    token_rows = tokens_w.shape[0]
    sequence = jnp.concatenate(
        [
            jnp.broadcast_to(tokens_w[None], (image_count, token_rows, model_width)),
            wave_emb,
            jnp.broadcast_to(token_b[None, None, :], (image_count, 1, model_width)),
        ],
        axis=1,
    )
    key_live = (
        jnp.concatenate(
            [
                jnp.ones((image_count, token_rows), jnp.float32),
                live_band,
                jnp.ones((image_count, 1), jnp.float32),
            ],
            axis=1,
        )
        > 0.5
    )
    projected = jnp.einsum("nsk,kj->nsj", sequence, w_in[:, model_width:], precision=high)
    asking = sequence[:, token_rows:]
    query_heads = (
        jnp.einsum("nsk,kj->nsj", asking, w_in[:, :model_width], precision=high) + in_bias[0]
    ).reshape(image_count, -1, head_count, head_size)
    keyed = projected[..., :model_width].reshape(
        image_count, -1, head_count, head_size
    )
    valued = (projected[..., model_width:] + in_bias[1]).reshape(
        image_count, -1, head_count, head_size
    )
    scores = jnp.einsum("nqhd,nkhd->nhqk", query_heads, keyed, precision=high) * head_size ** (
        -0.5
    )
    scores = jnp.where(key_live[:, None, None, :], scores, -1e30)
    attn_probs = jax.nn.softmax(scores, axis=-1)
    mixed_heads = jnp.einsum("nhqk,nkhd->nqhd", attn_probs, valued, precision=high).reshape(
        image_count, -1, model_width
    )
    first_out = layer_norm(
        asking + jnp.einsum("nsk,kj->nsj", mixed_heads, w_proj, precision=high) + proj_bias,
        gain_pair[0],
        shifts[0],
        hyper_eps,
    )
    inner_act = jax.nn.gelu(
        jnp.einsum("nsk,kf->nsf", first_out, w_expand, precision=high) + expand_bias,
        approximate=False,
    )
    second_out = layer_norm(
        first_out + jnp.einsum("nsf,fk->nsk", inner_act, w_reduce, precision=high) + reduce_bias,
        gain_pair[1],
        shifts[1],
        hyper_eps,
    )
    return (
        second_out[:, :band_slots] + wave_emb,
        second_out[:, band_slots],
    )


def swap_group(value, bits):
    return lax.ppermute(value, "group", [(at, at ^ bits) for at in range(4)])


def swap_batch(value, bits):
    count = lax.axis_size("batch")
    return lax.ppermute(value, "batch", [(at, at ^ bits) for at in range(count)])


def tuned_mesh():
    return lax.axis_size("group") == 4 and lax.axis_size("batch") == 8


def same_core():
    count = lax.axis_size("batch")
    return [list(range(0, count, 2)), list(range(1, count, 2))]


def in_order(bit, first, second):
    return jnp.where(
        bit == 0, jnp.concatenate([first, second]), jnp.concatenate([second, first])
    )


def four_in_order(index, pieces):
    low, high = (index & 1, index >> 1)
    return in_order(
        high, in_order(low, pieces[0], pieces[1]), in_order(low, pieces[2], pieces[3])
    )


def part_of(value, index, parts):
    rows = value.shape[0] // parts
    return lax.dynamic_slice_in_dim(value, index * rows, rows)


def tie(*values):
    return lax.optimization_barrier(values)


def along_line(value, step, chips=(0, 1, 2, 3)):
    pairs = [
        (2 * at + core, 2 * (at + step) + core)
        for at in chips
        for core in (0, 1)
        if 0 <= at + step < 4
    ]
    return lax.ppermute(value, "batch", pairs)


def line_ends(value):
    pairs = [(2 + at, at) for at in range(2)] + [(4 + at, 6 + at) for at in range(2)]
    return lax.ppermute(value, "batch", pairs)


def of_chip(chip, values):
    return jnp.array(values, jnp.int32)[chip]


def plain_weight_pieces(weight):
    core = lax.axis_index("batch") & 1
    shards = lax.all_gather(weight, "batch", axis=0)
    shards = shards.reshape((-1, 2) + weight.shape)
    mine = lax.dynamic_index_in_dim(shards, core, 1, keepdims=False)
    return mine.reshape((4, -1) + weight.shape[1:])


def plain_line_cells(pixels):
    pieces, images, rows, lanes = pixels.shape
    chips = lax.axis_size("batch") // 2
    parts = pixels.reshape(pieces, images, rows, chips // pieces, -1)
    parts = parts.transpose(0, 3, 1, 2, 4).reshape(chips, images, rows, -1)
    came = lax.all_to_all(parts, "batch", 0, 0, axis_index_groups=same_core(), tiled=True)
    return [came.reshape((chips * images,) + came.shape[2:])]


def plain_line_images(value, beside):
    both = jnp.concatenate([value, beside])
    return [lax.all_gather(both, "batch", axis=0, axis_index_groups=same_core(), tiled=True)]


def line_rows(low):
    if not tuned_mesh():
        return lax.all_gather(low, "batch", axis=0, axis_index_groups=same_core(), tiled=True)
    return jnp.concatenate([low] + [swap_batch(low, 2 * hop) for hop in (1, 2, 3)])


def core_sum(keep, send):
    return add_low(keep, swap_batch(send, 1))


def row_share(half):
    return lax.psum_scatter(half, "group", scatter_dimension=0, tiled=True)


def row_mine(share):
    return lax.psum(share, "batch", axis_index_groups=same_core())


def row_both(mine):
    core = lax.axis_index("batch") & 1
    return in_order(core, mine, swap_batch(mine, 1)).astype(jnp.float32)


def add_low(left, right):
    return (left.astype(jnp.float32) + right.astype(jnp.float32)).astype(left.dtype)


def ring_sides():
    group = lax.axis_index("group")
    side, level = (group & 1, group >> 1)
    return (1, side), (2, level)


def sum_out(parts, flip):
    order = ring_sides()[::-1] if flip else ring_sides()
    return [swap_group(part_of(part, 1 - bit, 2), way) for part, (way, bit) in zip(parts, order)]


def sum_in(parts, came, flip):
    order = ring_sides()[::-1] if flip else ring_sides()
    return [
        add_low(part_of(part, bit, 2), other)
        for part, other, (way, bit) in zip(parts, came, order)
    ]


def share_out(parts, flip):
    order = ring_sides()[::-1] if flip else ring_sides()
    return [swap_group(part, way) for part, (way, bit) in zip(parts, order)]


def share_in(parts, came, flip):
    order = ring_sides()[::-1] if flip else ring_sides()
    return [in_order(bit, part, other) for part, other, (way, bit) in zip(parts, came, order)]


def block_rows(value):
    rows, lanes = value.shape
    return value.reshape(rows, lanes // 128, 128).transpose(1, 0, 2).reshape(-1, 128)


def unblock_rows(value, rows):
    return value.reshape(-1, rows, 128).transpose(1, 0, 2).reshape(rows, -1)


THIN_ROWS = 16


def encode(values):
    wide = lax.reduce_precision(values[:, :-THIN_ROWS], 8, 7)
    thin = values[:, -THIN_ROWS:]
    first = lax.reduce_precision(thin, 8, 7)
    second = lax.reduce_precision(thin - first, 8, 7)
    third = lax.reduce_precision(thin - first - second, 8, 7)
    return jnp.concatenate([wide, first, second, third], axis=1).astype(jnp.bfloat16)


def decode(values):
    values = values.astype(jnp.float32)
    rows = values.shape[1] - 3 * THIN_ROWS
    ends = [rows + at * THIN_ROWS for at in range(4)]
    first, second, third = [values[:, ends[at] : ends[at + 1]] for at in range(3)]
    return jnp.concatenate([values[:, :rows], first + second + third], axis=1)


def grid_params(mebibytes, semantics=1):
    return pltpu.CompilerParams(
        dimension_semantics=("arbitrary",) * semantics,
        vmem_limit_bytes=mebibytes * 1024 * 1024,
    )


def dot_nn(left, right):
    return lax.dot_general(
        left, right, (((1,), (0,)), ((), ())), preferred_element_type=jnp.float32
    )


def dot_nt(left, right):
    return lax.dot_general(
        left, right, (((1,), (1,)), ((), ())), preferred_element_type=jnp.float32
    )


def dot_tn(left, right):
    return lax.dot_general(
        left, right, (((0,), (0,)), ((), ())), preferred_element_type=jnp.float32
    )


def split_kernel(cells, core_ref, pixel_ref, mean_ref, rate_ref, *refs):
    out_refs, scratch = (refs[:2], refs[2:])
    patches, bands, lanes = pixel_ref.shape[1:]
    pieces, _, rows, _ = out_refs[0].shape
    share = lanes // (2 * pieces * cells)
    span = cells * bands
    tile = 128
    columns, tiles = (lanes // tile, -(-rows // tile))
    flat, turned = (scratch[:columns], scratch[columns:])
    values = (pixel_ref[0].astype(jnp.float32) - mean_ref[0]) * rate_ref[0]
    values = values.astype(jnp.bfloat16).astype(jnp.float32).reshape(patches * bands, lanes)
    for column in range(columns):
        flat[column][: patches * bands] = values[:, column * tile : (column + 1) * tile]
        flat[column][patches * bands :] = jnp.zeros(
            (flat[column].shape[0] - patches * bands, tile), jnp.float32
        )
    for band in range(bands):
        for column in range(columns):
            for at in range(tiles):
                block = flat[column][pl.ds(at * tile * bands + band, tile, stride=bands), :]
                turned[at][pl.ds(column * tile * bands + band, tile, stride=bands), :] = block.T
    for out_ref, side in zip(out_refs, (core_ref[0], 1 - core_ref[0])):
        for piece in range(pieces):
            for at in range(tiles):
                count = min(tile, rows - at * tile)
                parts = []
                for one in range(share):
                    first = ((piece * share + one) * 2 + side) * span
                    place = pl.ds(pl.multiple_of(first, span), span)
                    parts.append(turned[at][place, :].T[:count])
                block = parts[0] if share == 1 else jnp.concatenate(parts, axis=1)
                out_ref[piece, 0, at * tile : at * tile + count, :] = block.astype(jnp.bfloat16)


def turn_scratch(rows, bands, lanes):
    tiles = -(-rows // 128)
    return [pltpu.VMEM((tiles * 128 * bands, 128), jnp.float32)] * (lanes // 128) + [
        pltpu.VMEM((lanes * bands, 128), jnp.float32)
    ] * tiles


def split_pixels(pixels, means, rates, core, rows, cells):
    images, bands, patches, lanes = pixels.shape
    wide = bands * lanes // 8
    side = jax.ShapeDtypeStruct((4, images, rows, wide), jnp.bfloat16)
    return pl.pallas_call(
        partial(split_kernel, cells),
        grid_spec=pltpu.PrefetchScalarGridSpec(
            num_scalar_prefetch=1,
            grid=(images,),
            in_specs=[
                pl.BlockSpec((1, patches, bands, lanes), lambda i, core: (i, 0, 0, 0)),
                pl.BlockSpec((1, bands, 1), lambda i, core: (i, 0, 0)),
                pl.BlockSpec((1, bands, 1), lambda i, core: (i, 0, 0)),
            ],
            out_specs=[pl.BlockSpec((4, 1, rows, wide), lambda i, core: (0, i, 0, 0))] * 2,
            scratch_shapes=turn_scratch(rows, bands, lanes),
        ),
        out_shape=[side, side],
        compiler_params=grid_params(40),
        cost_estimate=pl.CostEstimate(flops=1, bytes_accessed=1, transcendentals=0),
        name="split_pixels",
    )(core.reshape(1), pixels.transpose(0, 2, 1, 3), means[:, :, None], rates[:, :, None])


def join_kernel(cells, patches, core_ref, mine_ref, other_ref, out_ref, *scratch):
    rows = mine_ref.shape[2]
    bands, lanes = out_ref.shape[2:]
    pieces = mine_ref.shape[0]
    share = lanes // (2 * pieces * cells)
    span = cells * bands
    tile = 128
    columns, tiles = (lanes // tile, -(-rows // tile))
    flat, turned = (scratch[:columns], scratch[columns:])
    core = core_ref[0]
    for piece in range(pieces):
        for ref, flip in ((mine_ref, core), (other_ref, 1 - core)):
            for one in range(share):
                first = ((piece * share + one) * 2 + flip) * span
                place = pl.ds(pl.multiple_of(first, span), span)
                for at in range(tiles):
                    count = min(tile, rows - at * tile)
                    block = ref[
                        piece, 0, at * tile : at * tile + count, one * span : (one + 1) * span
                    ].astype(jnp.float32)
                    if count < tile:
                        block = jnp.concatenate(
                            [block, jnp.zeros((tile - count, span), jnp.float32)]
                        )
                    turned[at][place, :] = block.T
    for band in range(bands):
        for column in range(columns):
            for at in range(tiles):
                block = turned[at][pl.ds(column * tile * bands + band, tile, stride=bands), :]
                flat[column][pl.ds(at * tile * bands + band, tile, stride=bands), :] = block.T
    for column in range(columns):
        out_ref[0, :, :, column * tile : (column + 1) * tile] = (
            flat[column][: patches * bands].reshape(patches, bands, tile).astype(jnp.bfloat16)
        )


def join_pixels(mine, other, core, patches, cells, lanes, bands):
    pieces, images, rows, wide = mine.shape
    block = pl.BlockSpec((pieces, 1, rows, wide), lambda i, core: (0, i, 0, 0))
    joined = pl.pallas_call(
        partial(join_kernel, cells, patches),
        grid_spec=pltpu.PrefetchScalarGridSpec(
            num_scalar_prefetch=1,
            grid=(images,),
            in_specs=[block, block],
            out_specs=pl.BlockSpec((1, patches, bands, lanes), lambda i, core: (i, 0, 0, 0)),
            scratch_shapes=turn_scratch(rows, bands, lanes),
        ),
        out_shape=jax.ShapeDtypeStruct((images, patches, bands, lanes), jnp.bfloat16),
        compiler_params=grid_params(40),
        cost_estimate=pl.CostEstimate(flops=1, bytes_accessed=1, transcendentals=0),
        name="join_pixels",
    )(core.reshape(1), mine, other)
    return joined.transpose(0, 2, 1, 3)


def embed_kernel(first, count, at_ref, low_ref, *refs):
    weight_refs, pixel_refs = refs[:count], refs[count : count + 2]
    if first:
        total_refs, kernel_ref, weight_now = refs[count + 2 : count + 4], *refs[count + 4 :]
    else:
        before_refs = refs[count + 2 : count + 4]
        total_refs, kernel_ref, weight_now = refs[count + 5 : count + 7], *refs[count + 7 :]
    share = pixel_refs[0].shape[1]
    images = 2 * share
    cells = weight_now.shape[0]
    bands = pixel_refs[0].shape[3] // cells

    @pl.when(pl.program_id(0) == 0)
    def _():
        for at, total_ref in enumerate(total_refs):
            if first:
                total_ref[...] = jnp.zeros_like(total_ref)
            else:
                total_ref[...] = before_refs[at][...]

    for at in range(count):

        @pl.when((pl.program_id(0) == at) | (count == 1))
        def _(at=at):
            weight_now[...] = weight_refs[at][...]

    low = low_ref[...]
    for cell in range(cells):
        made = dot_nt(low, weight_now[cell]).astype(jnp.bfloat16)
        for image in range(images):
            kernel_ref[0, image, cell * bands : (cell + 1) * bands, :] = made[
                image * bands : (image + 1) * bands
            ]
    for image in range(images):
        block = pixel_refs[image // share][0, image % share]
        total_refs[image // share][image % share] += dot_nn(block, kernel_ref[0, image])


def embed_piece(place, low, weights, pixels, total, kernels):
    pieces, share, rows, lanes = pixels[0].shape
    images = 2 * share
    cells, width, depth = weights[0].shape
    step = lanes // (4 * 16)
    count = len(weights)
    steps = max(count, cells // step)
    bands = lanes // (4 * step)
    first = total is None
    any_spec = pl.BlockSpec(memory_space=pl.ANY)
    whole_total = pl.BlockSpec((share, rows, width), lambda t, at: (0, 0, 0))
    if count == 1:
        weight_specs = [pl.BlockSpec((step, width, depth), lambda t, at: (t, 0, 0))]
    else:
        weight_specs = [pl.BlockSpec((step, width, depth), lambda t, at: (0, 0, 0))] * count
    own, other, kernels = pl.pallas_call(
        partial(embed_kernel, first, count),
        grid_spec=pltpu.PrefetchScalarGridSpec(
            num_scalar_prefetch=1,
            grid=(steps,),
            in_specs=[pl.BlockSpec(low.shape, lambda t, at: (0, 0))]
            + weight_specs
            + [
                pl.BlockSpec(
                    (1, share, rows, step * bands), lambda t, at: (at[0], 0, 0, at[1 + t])
                ),
            ]
            * 2
            + ([] if first else [whole_total, whole_total, any_spec]),
            out_specs=[
                whole_total,
                whole_total,
                pl.BlockSpec(
                    (1, images, step * bands, width), lambda t, at: (at[0], 0, at[1 + t], 0)
                ),
            ],
            scratch_shapes=[pltpu.VMEM((step, width, depth), jnp.bfloat16)],
        ),
        out_shape=[
            jax.ShapeDtypeStruct((share, rows, width), jnp.float32),
            jax.ShapeDtypeStruct((share, rows, width), jnp.float32),
            jax.ShapeDtypeStruct((pieces, images, lanes, width), jnp.bfloat16),
        ],
        input_output_aliases={} if first else {4 + count: 0, 5 + count: 1, 6 + count: 2},
        compiler_params=grid_params(48),
        cost_estimate=pl.CostEstimate(flops=1, bytes_accessed=1, transcendentals=0),
        name="embed_piece",
    )(place, low, *weights, *pixels, *(() if first else (*total, kernels)))
    return (own, other), kernels


def pixel_grad_kernel(grad_ref, kernel_ref, rate_ref, out_ref):
    for image in range(grad_ref.shape[0]):
        out_ref[0, image] = (
            dot_nt(grad_ref[image], kernel_ref[0, image]) * rate_ref[image]
        ).astype(jnp.bfloat16)


def pixel_grads(grads, kernels, rates, half):
    pieces, images, lanes, width = kernels.shape
    rows = grads.shape[1]
    share = images // 2
    return pl.pallas_call(
        pixel_grad_kernel,
        grid=(pieces,),
        in_specs=[
            pl.BlockSpec((share, rows, width), lambda j: (half, 0, 0)),
            pl.BlockSpec((1, share, lanes, width), lambda j: (j, half, 0, 0)),
            pl.BlockSpec((share, 1, lanes), lambda j: (half, 0, 0)),
        ],
        out_specs=pl.BlockSpec((1, share, rows, lanes), lambda j: (j, 0, 0, 0)),
        out_shape=jax.ShapeDtypeStruct((pieces, share, rows, lanes), jnp.bfloat16),
        compiler_params=grid_params(40),
        cost_estimate=pl.CostEstimate(flops=1, bytes_accessed=1, transcendentals=0),
        name="pixel_grads",
    )(grads, kernels, rates)


def line_kernel(half, halves, low_ref, pixel_refs, grad_refs, out_ref, made):
    cells = out_ref.shape[0]
    lanes = pixel_refs[0].shape[2] // halves
    bands = lanes // cells
    columns = slice(half * lanes, (half + 1) * lanes)
    spots = [(ref, at) for ref in grad_refs for at in range(ref.shape[0])]
    image = 0
    for pixel_ref in pixel_refs:
        for at in range(pixel_ref.shape[0]):
            grad_ref, where = spots[image]
            grads = dot_tn(pixel_ref[at, :, columns], grad_ref[where]).astype(jnp.bfloat16)
            for cell in range(cells):
                made[cell, image * bands : (image + 1) * bands, :] = grads[
                    cell * bands : (cell + 1) * bands
                ]
            image += 1

    @pl.loop(0, cells, unroll=4)
    def _(cell):
        out_ref[cell] = dot_nn(low_ref[...], made[cell]).T.astype(jnp.bfloat16)


def line_grads(low_turned, cells, pixels, grads, half, halves):
    step_cells = cells // halves
    depth = low_turned.shape[0]
    width = grads[0].shape[2]
    bands = pixels[0].shape[2] // cells
    images = sum(piece.shape[0] for piece in pixels)
    vmem = pl.BlockSpec(memory_space=pltpu.VMEM)

    def body(*refs):
        pixel_refs = refs[1 : 1 + len(pixels)]
        grad_refs = refs[1 + len(pixels) : 1 + len(pixels) + len(grads)]
        line_kernel(half, halves, refs[0], pixel_refs, grad_refs, *refs[-2:])

    return pl.pallas_call(
        body,
        in_specs=[vmem] * (1 + len(pixels) + len(grads)),
        out_specs=vmem,
        out_shape=jax.ShapeDtypeStruct((step_cells, width, depth), jnp.bfloat16),
        scratch_shapes=[pltpu.VMEM((step_cells, images * bands, width), jnp.bfloat16)],
        compiler_params=pltpu.CompilerParams(vmem_limit_bytes=48 * 1024 * 1024),
        cost_estimate=pl.CostEstimate(flops=1, bytes_accessed=1, transcendentals=0),
        name="line_grads",
    )(low_turned, *pixels, *grads)


def band_kernel(first, count, at_ref, grad_ref, *refs):
    weight_refs, pixel_refs = refs[:count], refs[count : count + 2]
    if first:
        total_ref, weight_now, made = refs[count + 2 :]
    else:
        before_ref, total_ref, weight_now, made = refs[count + 2 :]
    share = pixel_refs[0].shape[1]
    images = 2 * share
    cells = weight_now.shape[0]
    bands = pixel_refs[0].shape[3] // cells

    @pl.when(pl.program_id(0) == 0)
    def _():
        if first:
            total_ref[...] = jnp.zeros_like(total_ref)
        else:
            total_ref[...] = before_ref[...]

    for at in range(count):

        @pl.when((pl.program_id(0) == at) | (count == 1))
        def _(at=at):
            weight_now[...] = weight_refs[at][...]

    for image in range(images):
        block = pixel_refs[image // share][0, image % share]
        grads = dot_tn(block, grad_ref[image]).astype(jnp.bfloat16)
        for cell in range(cells):
            made[cell, image * bands : (image + 1) * bands, :] = grads[
                cell * bands : (cell + 1) * bands
            ]
    for cell in range(cells):
        total_ref[...] += dot_nn(made[cell], weight_now[cell])


def band_piece(place, grads, weights, pixels, total):
    pieces, share, rows, lanes = pixels[0].shape
    images = 2 * share
    cells, width, depth = weights[0].shape
    step = lanes // (4 * 16)
    count = len(weights)
    steps = max(count, cells // step)
    bands = lanes // (4 * step)
    first = total is None
    whole_total = pl.BlockSpec((images * bands, depth), lambda t, at: (0, 0))
    if count == 1:
        weight_specs = [pl.BlockSpec((step, width, depth), lambda t, at: (t, 0, 0))]
    else:
        weight_specs = [pl.BlockSpec((step, width, depth), lambda t, at: (0, 0, 0))] * count
    return pl.pallas_call(
        partial(band_kernel, first, count),
        grid_spec=pltpu.PrefetchScalarGridSpec(
            num_scalar_prefetch=1,
            grid=(steps,),
            in_specs=[pl.BlockSpec(grads.shape, lambda t, at: (0, 0, 0))]
            + weight_specs
            + [
                pl.BlockSpec(
                    (1, share, rows, step * bands), lambda t, at: (at[0], 0, 0, at[1 + t])
                ),
            ]
            * 2
            + ([] if first else [whole_total]),
            out_specs=whole_total,
            scratch_shapes=[
                pltpu.VMEM((step, width, depth), jnp.bfloat16),
                pltpu.VMEM((step, images * bands, width), jnp.bfloat16),
            ],
        ),
        out_shape=jax.ShapeDtypeStruct((images * bands, depth), jnp.float32),
        compiler_params=grid_params(40),
        cost_estimate=pl.CostEstimate(flops=1, bytes_accessed=1, transcendentals=0),
        name="band_piece",
    )(place, grads, *weights, *pixels, *(() if first else (total,)))


def head_probs(patches, query, keyed, mine):
    rows = query.shape[0]
    scores = dot_nt(jnp.where(mine, query, jnp.zeros_like(query)), keyed)
    column = lax.broadcasted_iota(jnp.int32, (1, rows), 1)
    scores = jnp.where(column < patches, scores, -1e30)
    powers = jnp.exp(scores - jnp.max(scores, axis=-1, keepdims=True))
    return powers * (1.0 / jnp.sum(powers, axis=-1, keepdims=True))


def attend_kernel(patches, head_size, joint_ref, out_ref):
    width = out_ref.shape[2]
    pair = 2 * head_size
    lane = lax.broadcasted_iota(jnp.int32, (1, pair), 1)
    scale = jnp.asarray(head_size ** (-0.5), jnp.bfloat16)
    for at in range(0, width, pair):
        query = joint_ref[0, :, at : at + pair] * scale
        keyed = joint_ref[0, :, width + at : width + at + pair]
        valued = joint_ref[0, :, 2 * width + at : 2 * width + at + pair]
        mixed = []
        for head in range(2):
            mine = (lane >= head * head_size) & (lane < (head + 1) * head_size)
            probs = head_probs(patches, query, keyed, mine)
            mixed.append(dot_nn(probs.astype(jnp.bfloat16), valued))
        out_ref[0, :, at : at + pair] = jnp.where(lane < head_size, mixed[0], mixed[1]).astype(
            jnp.bfloat16
        )


def attend(joint, patches, head_size):
    images, rows, triple = joint.shape
    width = triple // 3
    return pl.pallas_call(
        partial(attend_kernel, patches, head_size),
        grid=(images,),
        in_specs=[pl.BlockSpec((1, rows, triple), lambda i: (i, 0, 0))],
        out_specs=pl.BlockSpec((1, rows, width), lambda i: (i, 0, 0)),
        out_shape=jax.ShapeDtypeStruct((images, rows, width), jnp.bfloat16),
        compiler_params=grid_params(24),
        cost_estimate=pl.CostEstimate(flops=1, bytes_accessed=1, transcendentals=0),
        name="attend",
    )(joint)


def attend_back_kernel(patches, head_size, joint_ref, grad_ref, out_ref, sum_ref):
    width = grad_ref.shape[2]
    pair = 2 * head_size
    lane = lax.broadcasted_iota(jnp.int32, (1, pair), 1)
    scale = jnp.asarray(head_size ** (-0.5), jnp.bfloat16)

    @pl.when(pl.program_id(0) == 0)
    def _():
        sum_ref[...] = jnp.zeros_like(sum_ref)

    for at in range(0, width, pair):
        query = joint_ref[0, :, at : at + pair] * scale
        keyed = joint_ref[0, :, width + at : width + at + pair]
        valued = joint_ref[0, :, 2 * width + at : 2 * width + at + pair]
        grads = grad_ref[0, :, at : at + pair]
        none = jnp.zeros_like(grads)
        parts = []
        for head in range(2):
            mine = (lane >= head * head_size) & (lane < (head + 1) * head_size)
            probs = head_probs(patches, query, keyed, mine)
            grad = jnp.where(mine, grads, none)
            to_probs = dot_nt(grad, valued)
            inner = jnp.sum(probs * to_probs, axis=-1, keepdims=True)
            to_scores = (probs * (to_probs - inner)).astype(jnp.bfloat16)
            parts.append(
                (
                    dot_nn(to_scores, jnp.where(mine, keyed, none)),
                    dot_tn(to_scores, jnp.where(mine, query, none)),
                    dot_tn(probs.astype(jnp.bfloat16), grad),
                )
            )
        to_query = (parts[0][0] + parts[1][0]) * (head_size ** (-0.5))
        to_keyed = parts[0][1] + parts[1][1]
        to_valued = parts[0][2] + parts[1][2]
        for slot, value in enumerate((to_query, to_keyed, to_valued)):
            value = value.astype(jnp.bfloat16)
            out_ref[0, :, slot * width + at : slot * width + at + pair] = value
            sum_ref[:, slot * width + at : slot * width + at + pair] += jnp.sum(
                value.astype(jnp.float32), axis=0, keepdims=True
            )


def attend_back(joint, grads, patches, head_size):
    images, rows, triple = joint.shape
    width = triple // 3
    return pl.pallas_call(
        partial(attend_back_kernel, patches, head_size),
        grid=(images,),
        in_specs=[
            pl.BlockSpec((1, rows, triple), lambda i: (i, 0, 0)),
            pl.BlockSpec((1, rows, width), lambda i: (i, 0, 0)),
        ],
        out_specs=[
            pl.BlockSpec((1, rows, triple), lambda i: (i, 0, 0)),
            pl.BlockSpec((1, triple), lambda i: (0, 0)),
        ],
        out_shape=[
            jax.ShapeDtypeStruct((images, rows, triple), jnp.bfloat16),
            jax.ShapeDtypeStruct((1, triple), jnp.float32),
        ],
        compiler_params=grid_params(24),
        cost_estimate=pl.CostEstimate(flops=1, bytes_accessed=1, transcendentals=0),
        name="attend_back",
    )(joint, grads)


def norm_inside(values, epsilon):
    center = values - jnp.mean(values, axis=-1, keepdims=True)
    factor = lax.rsqrt(jnp.mean(center * center, axis=-1, keepdims=True) + epsilon)
    return center * factor, factor


def small_call(kernel, name, grid, in_specs, out_specs, out_shape, scratch=(), limit=40):
    return pl.pallas_call(
        kernel,
        grid=grid,
        in_specs=in_specs,
        out_specs=out_specs,
        out_shape=out_shape,
        scratch_shapes=list(scratch),
        compiler_params=grid_params(limit),
        cost_estimate=pl.CostEstimate(flops=1, bytes_accessed=1, transcendentals=0),
        name=name,
    )


def whole_spec(shape):
    return pl.BlockSpec(shape, lambda i: (0,) * len(shape))


def image_spec(rows, width):
    return pl.BlockSpec((1, rows, width), lambda i: (i, 0, 0))


def joint_kernel(
    own_ref, beside_ref, bias_ref, gain_ref, shift_ref, weight_ref, joint_bias_ref,
    embedded_ref, normed_ref, joint_ref,
):
    embedded = own_ref[0] + beside_ref[0] + bias_ref[0]
    embedded_ref[0] = embedded
    normed = norm_inside(embedded, block_eps)[0] * gain_ref[...] + shift_ref[...]
    normed = normed.astype(jnp.bfloat16)
    normed_ref[0] = normed
    joint = dot_nn(normed, weight_ref[...]) + joint_bias_ref[...]
    joint_ref[0] = joint.astype(jnp.bfloat16)


def make_joint(total, beside, image_bias, gain, shift, weight, joint_bias):
    images, rows, width = beside.shape
    triple = weight.shape[1]
    return small_call(
        joint_kernel,
        "make_joint",
        (images,),
        [image_spec(rows, width)] * 2
        + [image_spec(1, width), whole_spec((1, width)), whole_spec((1, width))]
        + [whole_spec(weight.shape), whole_spec((1, triple))],
        [image_spec(rows, width), image_spec(rows, width), image_spec(rows, triple)],
        [
            jax.ShapeDtypeStruct((images, rows, width), jnp.float32),
            jax.ShapeDtypeStruct((images, rows, width), jnp.bfloat16),
            jax.ShapeDtypeStruct((images, rows, triple), jnp.bfloat16),
        ],
    )(total, beside, image_bias[:, None], gain[None], shift[None], weight, joint_bias[None])


def residual_kernel(
    attended_ref, embedded_ref, weight_ref, bias_ref, gain_ref, shift_ref, residual_ref, normed_ref
):
    branch = dot_nn(attended_ref[0], weight_ref[...]) + bias_ref[...]
    residual = embedded_ref[0] + branch
    residual_ref[0] = residual
    normed = norm_inside(residual, block_eps)[0] * gain_ref[...] + shift_ref[...]
    normed_ref[0] = normed.astype(jnp.bfloat16)


def make_residual(attended, embedded, weight, bias, gain, shift):
    images, rows, width = embedded.shape
    return small_call(
        residual_kernel,
        "make_residual",
        (images,),
        [image_spec(rows, width)] * 2 + [whole_spec(weight.shape)] + [whole_spec((1, width))] * 3,
        [image_spec(rows, width)] * 2,
        [
            jax.ShapeDtypeStruct((images, rows, width), jnp.float32),
            jax.ShapeDtypeStruct((images, rows, width), jnp.bfloat16),
        ],
    )(attended, embedded, weight, bias[None], gain[None], shift[None])


def norm_back_inside(grad, values, gain, epsilon):
    normal, factor = norm_inside(values, epsilon)
    scaled = grad * gain
    back = factor * (
        scaled
        - jnp.mean(scaled, axis=-1, keepdims=True)
        - normal * jnp.mean(scaled * normal, axis=-1, keepdims=True)
    )
    return back, jnp.sum(grad * normal, axis=0, keepdims=True)


def add_rows(out_ref, rows):
    @pl.when(pl.program_id(0) == 0)
    def _():
        out_ref[...] = jnp.zeros_like(out_ref)

    out_ref[...] += jnp.concatenate(rows, axis=0)


def branch_back_kernel(
    grad_ref, residual_ref, out_grad_ref, gain_ref, weight_ref,
    resid_ref, branch_ref, att_ref, sum_ref,
):
    grad = grad_ref[0]
    out_grad = out_grad_ref[0].astype(jnp.float32)
    back, gain_grad = norm_back_inside(grad, residual_ref[0], gain_ref[...], block_eps)
    resid = out_grad + back
    resid_ref[0] = resid
    branch = resid.astype(jnp.bfloat16)
    branch_ref[0] = branch
    att_ref[0] = dot_nt(branch, weight_ref[...]).astype(jnp.bfloat16)
    add_rows(
        sum_ref,
        [
            gain_grad,
            jnp.sum(grad, axis=0, keepdims=True),
            jnp.sum(branch.astype(jnp.float32), axis=0, keepdims=True),
            jnp.sum(out_grad, axis=0, keepdims=True),
        ],
    )


def branch_back(grad, residual, out_grad, gain, weight):
    images, rows, width = residual.shape
    return small_call(
        branch_back_kernel,
        "branch_back",
        (images,),
        [image_spec(rows, width)] * 3 + [whole_spec((1, width)), whole_spec(weight.shape)],
        [image_spec(rows, width)] * 3 + [whole_spec((4, width))],
        [
            jax.ShapeDtypeStruct((images, rows, width), jnp.float32),
            jax.ShapeDtypeStruct((images, rows, width), jnp.bfloat16),
            jax.ShapeDtypeStruct((images, rows, width), jnp.bfloat16),
            jax.ShapeDtypeStruct((4, width), jnp.float32),
        ],
    )(grad, residual, out_grad, gain[None], weight)


def embed_back_kernel(
    joint_ref, weight_ref, embedded_ref, resid_ref, gain_ref, emb_ref, sum_ref, image_ref
):
    grad = dot_nt(joint_ref[0], weight_ref[...])
    back, gain_grad = norm_back_inside(grad, embedded_ref[0], gain_ref[...], block_eps)
    emb = (resid_ref[0] + back).astype(jnp.bfloat16)
    emb_ref[0] = emb
    image_ref[0] = jnp.sum(emb.astype(jnp.float32), axis=0, keepdims=True)
    add_rows(sum_ref, [gain_grad, jnp.sum(grad, axis=0, keepdims=True)])


def embed_back(joint_grad, weight, embedded, resid, gain):
    images, rows, width = embedded.shape
    return small_call(
        embed_back_kernel,
        "embed_back",
        (images,),
        [image_spec(rows, joint_grad.shape[2]), whole_spec(weight.shape)]
        + [image_spec(rows, width)] * 2
        + [whole_spec((1, width))],
        [image_spec(rows, width), whole_spec((2, width)), image_spec(1, width)],
        [
            jax.ShapeDtypeStruct((images, rows, width), jnp.bfloat16),
            jax.ShapeDtypeStruct((2, width), jnp.float32),
            jax.ShapeDtypeStruct((images, 1, width), jnp.float32),
        ],
    )(joint_grad, weight, embedded, resid, gain[None])


def split_rows(core, value, count, keep_ref, send_ref):
    size = value.shape[0] // (2 * count)
    for at in range(count):
        first = value[2 * at * size : (2 * at + 1) * size]
        second = value[(2 * at + 1) * size : (2 * at + 2) * size]
        keep = jnp.where(core == 0, first, second).astype(jnp.bfloat16)
        send = jnp.where(core == 0, second, first).astype(jnp.bfloat16)
        keep_ref[at * size : (at + 1) * size] = keep
        send_ref[at * size : (at + 1) * size] = send


def rows_kernel(count, core_ref, left_ref, right_ref, keep_ref, send_ref, turned):
    @pl.when(pl.program_id(0) == 0)
    def _():
        turned[...] = left_ref[...].T

    split_rows(core_ref[0], dot_nn(turned[...], right_ref[...]), count, keep_ref, send_ref)


def rows_grad(core, left, right, count=4):
    rows, width = left.shape
    columns = right.shape[1]
    part = min(columns, 768)
    half = jax.ShapeDtypeStruct((width // 2, columns), jnp.bfloat16)
    return pl.pallas_call(
        partial(rows_kernel, count),
        grid_spec=pltpu.PrefetchScalarGridSpec(
            num_scalar_prefetch=1,
            grid=(columns // part,),
            in_specs=[
                pl.BlockSpec((rows, width), lambda s, core: (0, 0)),
                pl.BlockSpec((rows, part), lambda s, core: (0, s)),
            ],
            out_specs=[pl.BlockSpec((width // 2, part), lambda s, core: (0, s))] * 2,
            scratch_shapes=[pltpu.VMEM((width, rows), jnp.bfloat16)],
        ),
        out_shape=[half, half],
        compiler_params=grid_params(32),
        cost_estimate=pl.CostEstimate(flops=1, bytes_accessed=1, transcendentals=0),
        name="rows_grad",
    )(core.reshape(1), left, right)


def mlp_kernel(
    core_ref, normed_ref, residual_ref, grad_ref, up_ref, bias_ref, down_ref, down_bias_ref,
    out_ref, back_ref, up_keep_ref, up_send_ref, down_keep_ref, down_send_ref, bias_grad_ref,
    active, to_pre, turned, total,
):
    rows = normed_ref.shape[0]
    part = rows // MLP_PARTS

    @pl.when(pl.program_id(0) == 0)
    def _():
        total[...] = residual_ref[...] + down_bias_ref[...]
        back_ref[...] = jnp.zeros_like(back_ref)
        turned[...] = normed_ref[...].T

    up = up_ref[...]
    down = down_ref[...]
    bias_grad = jnp.zeros(bias_grad_ref.shape, jnp.float32)
    for at in range(0, rows, part):
        span = slice(at, at + part)
        pre = dot_nn(normed_ref[span], up) + bias_ref[...]
        share = 0.5 + 0.5 * lax.erf(pre * (0.5**0.5))
        slope = share + pre * (jnp.exp(-0.5 * pre * pre) * (0.5 / jnp.pi) ** 0.5)
        act = (pre * share).astype(jnp.bfloat16)
        grad = (slope * dot_nt(grad_ref[span], down)).astype(jnp.bfloat16)
        active[span] = act
        to_pre[span] = grad
        total[span] += dot_nn(act, down)
        back_ref[span] += dot_nt(grad, up)
        bias_grad += jnp.sum(grad.astype(jnp.float32), axis=0, keepdims=True)
    bias_grad_ref[...] = bias_grad
    core = core_ref[0]
    split_rows(core, dot_nn(turned[...], to_pre[...]), 4, up_keep_ref, up_send_ref)
    split_rows(core, dot_tn(active[...], grad_ref[...]), 1, down_keep_ref, down_send_ref)

    @pl.when(pl.program_id(0) == pl.num_programs(0) - 1)
    def _():
        out_ref[...] = total[...].astype(jnp.bfloat16)


MLP_PARTS = 2


def mlp(core, normed, residual, grads, up, up_bias, down, down_bias):
    rows, width = normed.shape
    hidden = up.shape[1]
    part = hidden // 4
    whole = pl.BlockSpec((rows, width), lambda s, core: (0, 0))
    columns = pl.BlockSpec((width, part), lambda s, core: (0, s))
    lines = pl.BlockSpec((part, width), lambda s, core: (s, 0))
    vector = pl.BlockSpec((1, part), lambda s, core: (0, s))
    up_half = jax.ShapeDtypeStruct((width // 2, hidden), jnp.bfloat16)
    down_half = jax.ShapeDtypeStruct((hidden // 2, width), jnp.bfloat16)
    return pl.pallas_call(
        mlp_kernel,
        grid_spec=pltpu.PrefetchScalarGridSpec(
            num_scalar_prefetch=1,
            grid=(hidden // part,),
            in_specs=[
                whole, whole, whole, columns, vector, lines,
                pl.BlockSpec((1, width), lambda s, core: (0, 0)),
            ],
            out_specs=[whole, whole]
            + [pl.BlockSpec((width // 2, part), lambda s, core: (0, s))] * 2
            + [pl.BlockSpec((part // 2, width), lambda s, core: (s, 0))] * 2
            + [vector],
            scratch_shapes=[
                pltpu.VMEM((rows, part), jnp.bfloat16),
                pltpu.VMEM((rows, part), jnp.bfloat16),
                pltpu.VMEM((width, rows), jnp.bfloat16),
                pltpu.VMEM((rows, width), jnp.float32),
            ],
        ),
        out_shape=[
            jax.ShapeDtypeStruct((rows, width), jnp.bfloat16),
            jax.ShapeDtypeStruct((rows, width), jnp.float32),
            up_half,
            up_half,
            down_half,
            down_half,
            jax.ShapeDtypeStruct((1, hidden), jnp.float32),
        ],
        compiler_params=grid_params(52),
        cost_estimate=pl.CostEstimate(flops=1, bytes_accessed=1, transcendentals=0),
        name="mlp",
    )(core.reshape(1), normed, residual, grads, up, up_bias[None], down, down_bias[None])


def assemble_kernel(bits_ref, *refs):
    out_ref = refs[-1]
    count = out_ref.shape[0]
    pieces = []
    for part in range(2):
        mine, early, late = refs[part], refs[2 + part], refs[4 + part]
        pieces += [(mine, 0), (mine, count), (early, 0), (late, 0)]
    for at, (ref, first) in enumerate(pieces):

        @pl.when(pl.program_id(0) == at)
        def _(ref=ref, first=first):
            out_ref[...] = ref[first : first + count].astype(jnp.float32)


def assemble(bits, mine, early, late):
    cells, width, depth = mine[0].shape
    half = cells // 2

    def whole(count):
        return pl.BlockSpec((count, width, depth), lambda t, bits: (0, 0, 0))

    return pl.pallas_call(
        assemble_kernel,
        grid_spec=pltpu.PrefetchScalarGridSpec(
            num_scalar_prefetch=1,
            grid=(8,),
            in_specs=[whole(cells)] * 2 + [whole(half)] * 4,
            out_specs=pl.BlockSpec(
                (half, width, depth),
                lambda t, bits: (t // 4 * 4 + (bits[t // 4] ^ (t // 2 % 2)) * 2 + t % 2, 0, 0),
            ),
        ),
        out_shape=jax.ShapeDtypeStruct((4 * cells, width, depth), jnp.float32),
        compiler_params=grid_params(40),
        cost_estimate=pl.CostEstimate(flops=1, bytes_accessed=1, transcendentals=0),
        name="assemble",
    )(bits, *mine, *early, *late)


def per_device(
    pixels,
    band_count,
    band_bin,
    bin_wave,
    run_mean,
    run_var,
    weight_tokens,
    bias_token,
    hyper_in,
    hyper_qv_bias,
    hyper_out,
    hyper_out_bias,
    hyper_gain,
    hyper_shift,
    hyper_up,
    hyper_up_bias,
    hyper_down,
    hyper_down_bias,
    kernel_weight,
    bias_weight,
    bias_offset,
    norm_gain,
    norm_shift,
    w_qkv,
    qv_bias,
    w_out,
    out_bias,
    w_up,
    up_bias,
    w_down,
    down_bias,
    cotangent,
):
    pixel_data = pixels[0]
    images, band_slots, patches, pixel_cells = pixel_data.shape
    bin_total = bin_wave.shape[0]
    model_width = w_qkv.shape[0]
    head_size = model_width // HEADS
    padded = -(-patches // 16) * 16
    rows = images * padded
    cells = kernel_weight.shape[0]
    core = lax.axis_index("batch") & 1
    live_band = (
        lax.broadcasted_iota(jnp.int32, (images, band_slots), 1) < band_count[0][:, None]
    ).astype(jnp.float32)
    bin_onehot = (
        band_bin[0][..., None]
        == lax.broadcasted_iota(jnp.int32, (images, band_slots, bin_total), 2)
    ).astype(jnp.float32)
    chosen = bin_onehot * live_band[..., None]
    run_rstd = lax.rsqrt(run_var + stat_eps)
    band_mean = jnp.einsum("ibn,n->ib", chosen, run_mean, precision=highest)
    band_rstd = jnp.einsum("ibn,n->ib", chosen, run_rstd, precision=highest)
    values32 = pixel_data.astype(jnp.float32)
    band_total = jnp.sum(values32, axis=(2, 3))
    band_square = jnp.sum(values32 * values32, axis=(2, 3))
    bin_sums = jnp.einsum("ib,ibn->n", band_total, chosen, precision=highest)
    bin_squares = jnp.einsum("ib,ibn->n", band_square, chosen, precision=highest)
    bin_counts = jnp.sum(chosen, axis=(0, 1))

    grad_out = jnp.pad(cotangent[0], ((0, 0), (0, padded - patches), (0, 0)))
    band_wave = jnp.einsum("ibn,n->ib", bin_onehot, bin_wave, precision=highest)
    wave_emb = wave_embed(band_wave, hyper_in.shape[0])
    hyper_params = (
        weight_tokens,
        bias_token,
        hyper_in,
        hyper_qv_bias,
        hyper_out,
        hyper_out_bias,
        hyper_gain,
        hyper_shift,
        hyper_up,
        hyper_up_bias,
        hyper_down,
        hyper_down_bias,
    )

    def make_low():
        (band_vec, bias_vec), hyper_back = jax.vjp(
            partial(hypernet, wave_emb=wave_emb, live_band=live_band), hyper_params
        )
        band_low = band_vec.astype(jnp.bfloat16).reshape(images * band_slots, -1)
        return band_low, bias_vec, hyper_back

    def place(piece, *quarters):
        return jnp.stack([jnp.asarray(at, jnp.int32) for at in (piece,) + quarters])

    if not tuned_mesh():
        band_low, bias_vec, hyper_back = make_low()
        chip_low = jnp.concatenate([band_low, swap_batch(band_low, 1)])
        mine, other = split_pixels(pixel_data, band_mean, band_rstd, core, padded, cells)
        chip_pixels = (mine, swap_batch(other, 1))
        total, kernels = (None, None)
        for at, weight in enumerate(plain_weight_pieces(kernel_weight)):
            total, kernels = embed_piece(
                place(at, 0, 1, 2, 3), chip_low, [weight], chip_pixels, total, kernels
            )
        line_pixels = plain_line_cells(jnp.concatenate(chip_pixels, axis=1))
        line_low = lax.all_gather(
            chip_low, "batch", axis=0, axis_index_groups=same_core(), tiled=True
        )
    else:
        group = lax.axis_index("group")
        chip = lax.axis_index("batch") >> 1
        part = cells // 8
        quarter = part_of(kernel_weight, group, 4)

        def sides(block):
            return swap_group(block, 1), swap_group(block, 2)

        def corners(beside, above):
            return swap_group(beside[:part], 2), swap_group(above[part : 2 * part], 1)

        def sides_and_corner(block, beside, above):
            return (
                swap_group(jnp.concatenate([block, above[part : 2 * part]]), 1),
                swap_group(jnp.concatenate([block, beside[:part]]), 2),
            )

        def added(state, piece, weights, shifts):
            spots = place(piece, *[group ^ shift for shift in shifts])
            return embed_piece(spots, chip_low, weights, chip_pixels, *state)

        def pixel_block(hop, half):
            piece = lax.dynamic_index_in_dim(chip_pixels[half], chip ^ hop, 0, keepdims=False)
            return swap_batch(piece, 2 * hop) if hop else piece

        right1, left1 = (along_line(quarter, -1), along_line(quarter, 1))
        band_low, bias_vec, hyper_back = make_low()
        band_low, bias_vec, right1, left1, pixel_data = tie(
            band_low, bias_vec, right1, left1, pixel_data
        )
        block1 = jnp.where(chip == 3, left1, right1)
        right2, left2 = (along_line(right1, -1, (1, 2)), along_line(left1, 1, (1, 2)))
        beside1, above1 = sides(block1)
        mine, other = split_pixels(pixel_data, band_mean, band_rstd, core, padded, cells)
        chip_low = jnp.concatenate([band_low, swap_batch(band_low, 1)])
        mine, other, chip_low, right2, left2, beside1, above1 = tie(
            mine, other, chip_low, right2, left2, beside1, above1
        )
        block2 = jnp.where(chip == 0, right2, jnp.where(chip == 3, left2, left1))
        end3 = line_ends(jnp.where(chip == 1, right2, left2))
        across2, up2 = sides_and_corner(block2, beside1, above1)
        chip_pixels = (mine, swap_batch(other, 1))
        pixels2 = [pixel_block(2, 0)]
        state = embed_piece(
            place(chip, 0, 1, 2, 3), chip_low, [kernel_weight], chip_pixels, None, None
        )
        weights1 = [block1, beside1, above1]
        spots1 = of_chip(chip, [1, 2, 3, 2])
        state = added(state, spots1, weights1, (0, 1, 2))
        state, chip_pixels, end3, across2, up2, pixels2, bin_sums, bin_squares = tie(
            state, chip_pixels, end3, across2, up2, pixels2, bin_sums, bin_squares
        )
        block3 = jnp.where(chip == 1, right2, jnp.where(chip == 2, left2, end3))
        across3, up3 = sides_and_corner(block3, across2, up2)
        pixels2.append(pixel_block(2, 1))
        pixels1 = [pixel_block(1, 0)]
        weights1.append(jnp.concatenate([up2[2 * part :], across2[2 * part :]]))
        state = added(state, spots1, weights1[3:], (3,))
        weights2 = [block2, across2, up2]
        spots2 = of_chip(chip, [2, 0, 1, 1])
        state = added(state, spots2, weights2, (0, 1, 2))
        state, across3, up3, pixels1, pixels2, chip_pixels, grad_out = tie(
            state, across3, up3, pixels1, pixels2, chip_pixels, grad_out
        )
        corner3 = corners(across3, up3)
        pixels1.append(pixel_block(1, 1))
        weights2.append(jnp.concatenate([up3[2 * part :], across3[2 * part :]]))
        state = added(state, spots2, weights2[3:], (3,))
        weights3 = [block3, across3, up3]
        spots3 = of_chip(chip, [3, 3, 0, 0])
        state = added(state, spots3, weights3, (0, 1, 2))
        state, corner3, pixels1, chip_pixels = tie(state, corner3, pixels1, chip_pixels)
        pixels3 = [pixel_block(3, 0)]
        weights3.append(jnp.concatenate(corner3))
        total, kernels = added(state, spots3, weights3[3:], (3,))
    image_bias = jnp.dot(bias_vec, bias_weight, precision=highest) + bias_offset
    total, total_other = total
    total_beside = swap_batch(total_other, 1)
    joint_bias = jnp.concatenate([qv_bias[0], jnp.zeros_like(qv_bias[0]), qv_bias[1]])
    embedded, normed1, joint = make_joint(
        total, total_beside, image_bias, norm_gain[0], norm_shift[0], w_qkv, joint_bias
    )
    attended = attend(joint, patches, head_size)
    rates = jnp.tile(band_rstd, (1, pixel_cells // 8))
    if tuned_mesh():
        attended, chip_pixels, chip_low, rates = tie(attended, chip_pixels, chip_low, rates)
        line_low = line_rows(chip_low)
    residual, normed2 = make_residual(
        attended, embedded, w_out, out_bias, norm_gain[1], norm_shift[1]
    )
    block_out, grad_n2, up_keep, up_send, down_keep, down_send, grad_up_bias = mlp(
        core,
        normed2.reshape(rows, model_width),
        residual.reshape(rows, model_width),
        grad_out.reshape(rows, model_width),
        w_up,
        up_bias,
        w_down,
        down_bias,
    )
    if tuned_mesh():
        rates_beside = swap_batch(rates, 1)
        grad_n2, pixels3, chip_pixels, line_low, rates_beside, up_send, down_send = tie(
            grad_n2, pixels3, chip_pixels, line_low, rates_beside, up_send, down_send
        )
        pixels3.append(pixel_block(3, 1))
    else:
        rates_beside = swap_batch(rates, 1)
    rates = jnp.concatenate([rates, rates_beside])[:, None, :]
    up_came, down_came = swap_batch(up_send, 1), swap_batch(down_send, 1)
    block_out = block_out.reshape(1, images, padded, model_width)[:, :, :patches]
    grad_resid, grad_branch, grad_att, branch_sum = branch_back(
        grad_n2.reshape(images, padded, model_width), residual, grad_out, norm_gain[1], w_out
    )
    grad_gain_two, grad_shift_two, grad_out_bias, grad_down_bias = branch_sum
    grad_joint, joint_sum = attend_back(joint, grad_att, patches, head_size)
    grad_emb, embed_sum, grad_image_bias = embed_back(
        grad_joint, w_qkv, embedded, grad_resid, norm_gain[0]
    )
    if tuned_mesh():
        grad_emb, pixels3, up_keep, up_came, down_keep, down_came = tie(
            grad_emb, pixels3, up_keep, up_came, down_keep, down_came
        )
    grad_gain_one, grad_shift_one = embed_sum
    grad_image_bias = grad_image_bias[:, 0]
    grad_qv_bias = joint_sum.reshape(3, model_width)[::2]
    attended = attended.reshape(rows, model_width)
    grad_branch = grad_branch.reshape(rows, model_width)
    beside_emb = swap_batch(grad_emb, 1)
    if tuned_mesh():
        right1, left1 = (along_line(grad_emb, -1), along_line(grad_emb, 1))
    share_up = row_share(add_low(up_keep, up_came))
    share_down = row_share(add_low(down_keep, down_came))

    def late_rows(attended, grad_branch, normed1, grad_joint):
        return rows_grad(core, attended, grad_branch), rows_grad(core, normed1, grad_joint)

    late = (
        attended,
        grad_branch,
        normed1.reshape(rows, model_width),
        grad_joint.reshape(rows, 3 * model_width),
    )
    grad_bias_weight = jnp.einsum("ik,ie->ke", bias_vec, grad_image_bias, precision=highest)
    grad_bias_offset = jnp.sum(grad_image_bias, axis=0)
    grad_bias_vec = jnp.einsum("ie,ke->ik", grad_image_bias, bias_weight, precision=highest)

    def pack(hyper_grads):
        wide = (
            hyper_grads[0],
            hyper_grads[2],
            hyper_grads[4],
            hyper_grads[8],
            hyper_grads[10],
            grad_bias_weight,
        )
        narrow = (
            hyper_grads[1],
            hyper_grads[3],
            hyper_grads[5],
            hyper_grads[6],
            hyper_grads[7],
            hyper_grads[9],
            hyper_grads[11],
            bin_sums,
            bin_squares,
            bin_counts,
            grad_bias_offset,
            jnp.stack([grad_gain_one, grad_gain_two]),
            jnp.stack([grad_shift_one, grad_shift_two]),
            grad_qv_bias,
            grad_out_bias,
            grad_up_bias[0],
            grad_down_bias,
        )
        parts = [block_rows(part) for part in wide]
        thin = [part.reshape(-1) for part in narrow]
        length = sum(part.shape[0] for part in thin)
        thin = jnp.concatenate(thin + [jnp.zeros((-length % 16384,), jnp.float32)])
        (thin,) = tie(thin)
        thin = thin.reshape(8, -1, 128)
        (thin,) = tie(thin)
        small = jnp.concatenate([jnp.concatenate(parts).reshape(8, -1, 128), thin], axis=1)
        return wide, narrow, parts, small

    chip_emb = jnp.concatenate([grad_emb, beside_emb])

    def finish_low(grad_vectors):
        far = swap_batch(grad_vectors[images * band_slots :], 1)
        grad_vectors = grad_vectors[: images * band_slots] + far
        grad_vectors = grad_vectors.reshape(images, band_slots, -1)
        return hyper_back((grad_vectors, grad_bias_vec))[0]

    grad_vectors = None
    if tuned_mesh():
        plan = [
            (place(chip, 0, 1, 2, 3), [kernel_weight]),
            (place(spots1, group, group ^ 1, group ^ 2, group ^ 3), weights1),
            (place(spots2, group, group ^ 1, group ^ 2, group ^ 3), weights2),
            (place(spots3, group, group ^ 1, group ^ 2, group ^ 3), weights3),
        ]
        pair_out, pair_qkv = late_rows(*late)
        for spots, weights in plan[:2]:
            grad_vectors = band_piece(spots, chip_emb, weights, chip_pixels, grad_vectors)
        grad_vectors, right1, left1, beside_emb, share_up, pair_out, pair_qkv = tie(
            grad_vectors, right1, left1, beside_emb, share_up, pair_out, pair_qkv
        )
        right2, left2 = (along_line(right1, -1, (1, 2)), along_line(left1, 1, (1, 2)))
        half_out, half_qkv = core_sum(*pair_out), core_sum(*pair_qkv)
        far = jnp.where((chip & 1) == 0, right1, left1)
        line_emb = [grad_emb, beside_emb, far, swap_batch(far, 1)]
        for spots, weights in plan[2:]:
            grad_vectors = band_piece(spots, chip_emb, weights, chip_pixels, grad_vectors)
        grad_vectors, right2, left2, line_emb, share_down, half_out, half_qkv = tie(
            grad_vectors, right2, left2, line_emb, share_down, half_out, half_qkv
        )
        share_out_rows, share_qkv = row_share(half_out), row_share(half_qkv)
        end3 = line_ends(jnp.where(chip == 1, right2, left2))
        far = jnp.where(chip < 2, right2, left2)
        line_emb += [far, swap_batch(far, 1)]
        hyper_grads = finish_low(grad_vectors)
        wide, narrow, parts, small = pack(hyper_grads)
        line_pixels = [pixel_block(0, 0), pixel_block(0, 1)]
        small, end3, line_emb, line_pixels = tie(small, end3, line_emb, line_pixels)
        small_came = swap_batch(encode(part_of(small, 1 - core, 2)), 1)
        far = jnp.where(chip == 1, right1, jnp.where(chip == 2, left1, end3))
        line_emb += [far, swap_batch(far, 1)]
        small, small_came, line_emb = tie(small, small_came, line_emb)
        line_pixels += pixels1 + pixels2 + pixels3
    else:
        for at, weight in enumerate(plain_weight_pieces(kernel_weight)):
            grad_vectors = band_piece(
                place(at, 0, 1, 2, 3), chip_emb, [weight], chip_pixels, grad_vectors
            )
        half_out, half_qkv = [core_sum(*pair) for pair in late_rows(*late)]
        hyper_grads = finish_low(grad_vectors)
        wide, narrow, parts, small = pack(hyper_grads)
        share_out_rows, share_qkv = row_share(half_out), row_share(half_qkv)
        line_emb = plain_line_images(grad_emb, beside_emb)
    halves = 2 if cells % 32 == 0 else 1
    low_turned = line_low.T

    if not tuned_mesh():
        kernel_share = 0.0
        for at in range(0, line_pixels[0].shape[0], 32):
            columns = low_turned[:, at * band_slots : (at + 32) * band_slots]
            found = line_grads(
                columns, cells, [line_pixels[0][at : at + 32]], [line_emb[0][at : at + 32]], 0, 1
            )
            kernel_share += found.astype(jnp.float32)
        kernel_total = lax.psum(kernel_share.astype(jnp.bfloat16), "group").astype(jnp.float32)
        own_back = pixel_grads(chip_emb, kernels, rates, 0)
        other_back = swap_batch(pixel_grads(chip_emb, kernels, rates, 1), 1)
        pixel_grad = join_pixels(
            own_back, other_back, core, patches, cells, pixel_cells, band_slots
        )
        small = lax.psum(small, ("group", "batch"))
        totals = [
            row_both(row_mine(share)) for share in (share_qkv, share_out_rows, share_up, share_down)
        ]
    else:
        def small_hop(hop):
            return swap_batch(encode(part_of(small, chip ^ hop, 4)), 2 * hop)

        small = part_of(small, core, 2) + decode(small_came)
        small_came = [small_hop(1), small_hop(2)]
        kernel_one = line_grads(low_turned, cells, line_pixels, line_emb, 0, 2)
        kernel_one, line_emb, small, small_came, share_out_rows, share_qkv = tie(
            kernel_one, line_emb, small, small_came, share_out_rows, share_qkv
        )

        small_came.append(small_hop(3))
        kernel_two = line_grads(low_turned, cells, line_pixels, line_emb, 1, 2)
        kernel_two, small_came = tie(kernel_two, small_came)

        sums = [kernel_one, kernel_two]
        mine_qkv, mine_out, mine_up, mine_down = [
            row_mine(share) for share in (share_qkv, share_out_rows, share_up, share_down)
        ]
        came = sum_out(sums, False)
        small = encode(sum([decode(one) for one in small_came], part_of(small, chip, 4)))
        small_came = swap_group(small, 1)
        own_back = pixel_grads(chip_emb, kernels, rates, 0)
        other_back = pixel_grads(chip_emb, kernels, rates, 1)
        own_back, other_back, came, small_came, mine_qkv, mine_out, mine_up, mine_down = tie(
            own_back, other_back, came, small_came, mine_qkv, mine_out, mine_up, mine_down
        )

        sums = sum_in(sums, came, False)
        came = sum_out(sums, True)
        small = encode(decode(small) + decode(small_came))
        small_came = swap_group(small, 2)
        other_back = swap_batch(other_back, 1)
        came, other_back, small_came, block_out, mine_qkv, mine_out, mine_up, mine_down = tie(
            came, other_back, small_came, block_out, mine_qkv, mine_out, mine_up, mine_down
        )

        sums = sum_in(sums, came, True)
        came = share_out(sums, True)
        small = encode(decode(small) + decode(small_came))
        small_came = [swap_batch(small, 2), swap_batch(small, 4)]
        pixel_grad = join_pixels(
            own_back, other_back, core, patches, cells, pixel_cells, band_slots
        )
        wide_mine = jnp.concatenate([mine_qkv, mine_out, mine_up], axis=1)
        wide_came = swap_batch(wide_mine, 1)
        came, small, small_came, pixel_grad, wide_came, mine_down = tie(
            came, small, small_came, pixel_grad, wide_came, mine_down
        )
        down_came = swap_batch(mine_down, 1)

        sums = share_in(sums, came, True)
        early, late = ([value[: cells // 8] for value in sums], [value[cells // 8 :] for value in sums])
        early = share_out(early, False)
        small_came.append(swap_batch(small, 6))
        widths = [mine.shape[1] for mine in (mine_qkv, mine_out, mine_up)]
        wide_both = in_order(core, wide_mine, wide_came).astype(jnp.float32)
        ends = [0, widths[0], widths[0] + widths[1], sum(widths)]
        totals = [wide_both[:, ends[at] : ends[at + 1]] for at in range(3)]
        totals.append(in_order(core, mine_down, down_came).astype(jnp.float32))
        early, late, small_came, totals = tie(early, late, small_came, totals)
        late = share_out(late, False)
        small = four_in_order(chip, [small] + small_came)
        small = decode(in_order(core, small, swap_batch(small, 1)))
    pixel_grad = pixel_grad[None]

    found = []
    at = 0
    wide_rows = small[:, :-THIN_ROWS].reshape(-1, 128)
    thin_flat = small[:, -THIN_ROWS:].reshape(-1)
    for part, like in zip(parts, wide):
        found.append(unblock_rows(wide_rows[at : at + part.shape[0]], like.shape[0]))
        at += part.shape[0]
    at = 0
    for like in narrow:
        found.append(thin_flat[at : at + like.size].reshape(like.shape))
        at += like.size
    batch_mean, batch_var = bin_stats(found[13], found[14], found[15], patches * pixel_cells)
    if tuned_mesh():
        late, found, batch_mean, batch_var = tie(late, found, batch_mean, batch_var)
        bits = jnp.stack([group & 1, group >> 1])
        kernel_total = assemble(bits, sums, early, late)
    return (
        block_out,
        pixel_grad,
        batch_mean,
        batch_var,
        found[0],
        found[6],
        found[1],
        found[7],
        found[2],
        found[8],
        found[9],
        found[10],
        found[3],
        found[11],
        found[4],
        found[12],
        kernel_total,
        found[5],
        found[16],
        found[17],
        found[18],
        totals[0],
        found[19],
        totals[1],
        found[20],
        totals[2],
        found[21],
        totals[3],
        found[22],
    )


def solution(mesh):
    return jax.shard_map(
        per_device,
        mesh=mesh,
        in_specs=(
            P("group", "batch", None, None, None),
            P("group", "batch"),
            P("group", "batch", None),
            P(),
            P(),
            P(),
            P(),
            P(),
            P(),
            P(),
            P(),
            P(),
            P(),
            P(),
            P(),
            P(),
            P(),
            P(),
            P("batch", None, None),
            P(),
            P(),
            P(),
            P(),
            P(),
            P(),
            P(),
            P(),
            P(),
            P(),
            P(),
            P(),
            P("group", "batch", None, None),
        ),
        out_specs=(
            P("group", "batch", None, None),
            P("group", "batch", None, None, None),
            P(),
            P(),
            P(),
            P(),
            P(),
            P(),
            P(),
            P(),
            P(),
            P(),
            P(),
            P(),
            P(),
            P(),
            P("batch", None, None),
            P(),
            P(),
            P(),
            P(),
            P("group", None),
            P(),
            P("group", None),
            P(),
            P("group", None),
            P(),
            P("group", None),
            P(),
        ),
        check_vma=False,
    )
```
